32 devices in a mesh: seq: 16 (over z, y, core), dp: 2 (over x).
Axes of the slice: x: 2, y: 2, z: 4, core: 2. Of those that a mesh axis runs over, the one named last changes fastest.
Arguments:
- tokens: bfloat16 [2, 4096, 1024], P('dp', 'seq'), may hold values from -6 to 6
- cotangent: bfloat16 [2, 4096, 1024], P('dp', 'seq'), may hold values from -6 to 6
- pre_gain: bfloat16 [1024], P('seq'), may hold values from 0.5 to 1.5
- pre_offset: bfloat16 [1024], P('seq'), may hold values from -1.25 to 1.25
- input_weight: bfloat16 [1024, 3072], P('seq'), may hold values from -0.1875 to 0.1875
- input_bias: bfloat16 [3072], P('seq'), may hold values from -1.25 to 1.25
- short_weight: bfloat16 [3, 3072], P(None, 'seq'), may hold values from -3.5 to 3.5
- short_bias: bfloat16 [3072], P('seq'), may hold values from -1.25 to 1.25
- skip_weight: bfloat16 [1024], P('seq'), may hold values from -6 to 6
- embed_weight: float32 [33, 64], replicated, may hold values from -1 to 1
- embed_bias: float32 [64], replicated, may hold values from -3 to 3
- hidden_weight: float32 [64, 64], replicated, may hold values from -0.75 to 0.75
- hidden_bias: float32 [64], replicated, may hold values from -3 to 3
- last_weight: float32 [64, 64], replicated, may hold values from -0.75 to 0.75
- last_bias: float32 [64], replicated, may hold values from -3 to 3
- frequency: float32 [64], replicated, may hold values from 0.5 to 1.5
- filter_weight: bfloat16 [64, 1024], P(None, 'seq'), may hold values from -0.02734375 to 0.02734375
- output_weight: bfloat16 [1024, 1024], P('seq'), may hold values from -0.1875 to 0.1875
- output_bias: bfloat16 [1024], P('seq'), may hold values from -1.25 to 1.25
- post_gain: bfloat16 [1024], P('seq'), may hold values from 0.5 to 1.5
- post_offset: bfloat16 [1024], P('seq'), may hold values from -1.25 to 1.25
- up_weight: bfloat16 [1024, 4096], P('seq'), may hold values from -0.1875 to 0.1875
- up_bias: bfloat16 [4096], P('seq'), may hold values from -1.25 to 1.25
- down_weight: bfloat16 [4096, 1024], P('seq'), may hold values from -0.09375 to 0.09375
- down_bias: bfloat16 [1024], P('seq'), may hold values from -1.25 to 1.25
Outputs:
- result: bfloat16 [2, 4096, 1024], P('dp', 'seq')
- tokens_grad: bfloat16 [2, 4096, 1024], P('dp', 'seq')
- pre_gain_grad: float32 [1024], P(('seq', 'dp'))
- pre_offset_grad: float32 [1024], P(('seq', 'dp'))
- input_weight_grad: float32 [1024, 3072], P(('seq', 'dp'))
- input_bias_grad: float32 [3072], P(('seq', 'dp'))
- short_weight_grad: float32 [3, 3072], P(None, ('seq', 'dp'))
- short_bias_grad: float32 [3072], P(('seq', 'dp'))
- skip_weight_grad: float32 [1024], P(('seq', 'dp'))
- embed_weight_grad: float32 [33, 64], replicated
- embed_bias_grad: float32 [64], replicated
- hidden_weight_grad: float32 [64, 64], replicated
- hidden_bias_grad: float32 [64], replicated
- last_weight_grad: float32 [64, 64], replicated
- last_bias_grad: float32 [64], replicated
- frequency_grad: float32 [64], replicated
- filter_weight_grad: float32 [64, 1024], P(None, ('seq', 'dp'))
- output_weight_grad: float32 [1024, 1024], P(('seq', 'dp'))
- output_bias_grad: float32 [1024], P(('seq', 'dp'))
- post_gain_grad: float32 [1024], P(('seq', 'dp'))
- post_offset_grad: float32 [1024], P(('seq', 'dp'))
- up_weight_grad: float32 [1024, 4096], P(('seq', 'dp'))
- up_bias_grad: float32 [4096], P(('seq', 'dp'))
- down_weight_grad: float32 [4096, 1024], P(('seq', 'dp'))
- down_bias_grad: float32 [1024], P(('seq', 'dp'))
The draws below stay inside these ranges and needn't reach their ends.
All inputs are finite; a program needn't handle non-finite values.
Results may differ from the reference program's by a relative error of at most 0.015.
Values may be sent and summed in bfloat16 or wider, within the bound.
No kernel may reach another device: no remote copies, remote signals or barrier semaphores. Data moves between devices by JAX's collectives and lax.ppermute only.
A program may use at most 256 MiB of HBM per device.

```python
import math
import jax
import jax.numpy as jnp
from jax import lax

D = 1024
FF = 4096
FILTER = 64
FEATURES = 33
TAPS = 3
LEN = 4096
SEQS = 2


def with_spikes(entries, own_key, source, target, shards_of, factor):
    def block_of(axis_at):
        return (jnp.arange(entries.shape[axis_at]) // (entries.shape[axis_at] // shards_of)).reshape((-1,) + (1,) * (entries.ndim - 1 - axis_at))

    one_side = jax.random.permutation(own_key, shards_of)[block_of(target)]
    other_side = (block_of(target) + shards_of // 2) % shards_of
    return jnp.where((block_of(source) == one_side) | (block_of(source) == other_side), factor * entries, entries)


def level_of(rng, dims, split, smallest, largest):
    level, own = 1.0, jax.random.fold_in(rng, 6)
    for axis_at, blocks in split:
        draws = jnp.exp(jax.random.uniform(jax.random.fold_in(own, axis_at), (blocks,), jnp.float32, smallest / len(split), largest / len(split)))
        level = level * jnp.repeat(draws, dims[axis_at] // blocks).reshape([-1 if axis == axis_at else 1 for axis in range(len(dims))])
    return level


def gaussian(rng, shape, scale, limit, pieces=(), kind=jnp.bfloat16):
    values = jax.random.normal(rng, shape, jnp.float32) * scale
    if len(pieces) > 0:
        values = level_of(rng, shape, pieces, -0.22, 0.18) * values
    return jnp.clip(values, min=-limit, max=limit).astype(kind)


def noise_with(own_key, shape, scale, reach, pieces, heavy, dtype=jnp.bfloat16):
    values = scale * jax.random.normal(own_key, shape, jnp.float32)
    if pieces:
        values = values * level_of(own_key, shape, pieces, -0.22, 0.18)
    return jnp.clip(with_spikes(values, jax.random.fold_in(own_key, 3), *heavy), -reach, reach).astype(dtype)


def setup_inputs(seed: int = 0) -> dict:
    seeds = jax.random.split(jax.random.key(seed), 26)
    return {
        "tokens": gaussian(seeds[0], (SEQS, LEN, D), 1.0, 6.0, ((0, 2), (1, 16))),
        "cotangent": noise_with(seeds[1], (SEQS, LEN, D), 1.0, 6.0, ((0, 2), (1, 16)), (1, 2, 16, 2.0)),
        "pre_gain": jnp.clip(1.0 + 0.1 * jax.random.normal(seeds[2], (D,), jnp.float32), 0.5, 1.5).astype(jnp.bfloat16),
        "pre_offset": gaussian(seeds[3], (D,), 0.2, 1.25, ((0, 16),)),
        "input_weight": gaussian(seeds[4], (D, 3 * D), D ** -0.5, 0.1875, ((0, 16),)),
        "input_bias": gaussian(seeds[5], (3 * D,), 0.2, 1.25, ((0, 16),)),
        "short_weight": gaussian(seeds[6], (TAPS, 3 * D), TAPS ** -0.5, 3.5, ((1, 16),)),
        "short_bias": gaussian(seeds[7], (3 * D,), 0.2, 1.25, ((0, 16),)),
        "skip_weight": gaussian(seeds[8], (D,), 1.0, 6.0, ((0, 16),)),
        "embed_weight": gaussian(seeds[9], (FEATURES, FILTER), FEATURES ** -0.5, 1.0, (), jnp.float32),
        "embed_bias": gaussian(seeds[10], (FILTER,), 0.5, 3.0, (), jnp.float32),
        "hidden_weight": gaussian(seeds[11], (FILTER, FILTER), FILTER ** -0.5, 0.75, (), jnp.float32),
        "hidden_bias": gaussian(seeds[12], (FILTER,), 0.5, 3.0, (), jnp.float32),
        "last_weight": gaussian(seeds[13], (FILTER, FILTER), FILTER ** -0.5, 0.75, (), jnp.float32),
        "last_bias": gaussian(seeds[14], (FILTER,), 0.5, 3.0, (), jnp.float32),
        "frequency": jnp.clip(1.0 + 0.1 * jax.random.normal(seeds[15], (FILTER,), jnp.float32), 0.5, 1.5),
        "filter_weight": gaussian(seeds[16], (FILTER, D), (12 * LEN) ** -0.5, 0.02734375, ((1, 16),)),
        "output_weight": gaussian(seeds[17], (D, D), D ** -0.5, 0.1875, ((0, 16),)),
        "output_bias": gaussian(seeds[18], (D,), 0.2, 1.25, ((0, 16),)),
        "post_gain": jnp.clip(1.0 + 0.1 * jax.random.normal(seeds[19], (D,), jnp.float32), 0.5, 1.5).astype(jnp.bfloat16),
        "post_offset": gaussian(seeds[20], (D,), 0.2, 1.25, ((0, 16),)),
        "up_weight": gaussian(seeds[21], (D, FF), D ** -0.5, 0.1875, ((0, 16),)),
        "up_bias": gaussian(seeds[22], (FF,), 0.2, 1.25, ((0, 16),)),
        "down_weight": gaussian(seeds[23], (FF, D), FF ** -0.5, 0.09375, ((0, 16),)),
        "down_bias": gaussian(seeds[24], (D,), 0.2, 1.25, ((0, 16),)),
    }


@jax.custom_vjp
def low(v):
    return lax.optimization_barrier(v.astype(jnp.bfloat16)).astype(jnp.float32)

@jax.custom_vjp
def low_back(v):
    return v

def low_keep(v):
    return (low(v), None)

def low_pass(kept, grad):
    return (grad,)

def back_keep(v):
    return (v, None)

def back_low(kept, grad):
    return (low(grad),)
low.defvjp(low_keep, low_pass)
low_back.defvjp(back_keep, back_low)

def matmul(left_side, right_side):
    return jnp.dot(left_side, right_side, precision=lax.Precision.HIGHEST, preferred_element_type=jnp.float32)

def layer_norm(values, norm_gain, norm_offset):
    center = values - lax.optimization_barrier(jnp.mean(values, axis=-1, keepdims=True))
    inverse = lax.rsqrt(lax.optimization_barrier(jnp.mean(center * center, axis=-1, keepdims=True)) + 1e-05)
    return center * inverse * norm_gain + norm_offset

def filter_table(length, model_width, embed_weight, embed_bias, hidden_weight, hidden_bias, last_weight, last_bias, frequency, filter_weight):
    positions = jnp.arange(length).astype(jnp.float32)
    relative = positions / (length - 1)
    phases = positions * (2.0 * math.pi / length)
    band_count = (FEATURES - 1) // 2
    band_freq = jnp.linspace(0.0001, band_count - 1, band_count).astype(jnp.float32)
    angles = phases[:, None] * band_freq[None, :]
    features = jnp.concatenate([relative[:, None], jnp.cos(angles), -jnp.sin(angles)], axis=1)
    layer_out = jnp.sin(frequency * (matmul(features, embed_weight) + embed_bias))
    layer_out = jnp.sin(frequency * (matmul(layer_out, hidden_weight) + hidden_bias))
    layer_out = jnp.sin(frequency * (matmul(layer_out, last_weight) + last_bias))
    deltas = jnp.linspace(math.log(0.01) / 1.5, math.log(0.01) / 0.3, model_width).astype(jnp.float32)
    window = jnp.exp(-relative[:, None] * jnp.abs(deltas)[None, :]) + 0.05
    return matmul(layer_out, filter_weight) * window

def long_conv(gated_vals, kernel, skip_weight):
    padded_len = 2 * gated_vals.shape[0]
    spectrum = jnp.fft.rfft(gated_vals, n=padded_len, axis=0) * jnp.fft.rfft(kernel, n=padded_len, axis=0)
    return jnp.fft.irfft(spectrum, n=padded_len, axis=0)[:gated_vals.shape[0]] + gated_vals * skip_weight

def forward(tokens, pre_gain, pre_offset, input_weight, input_bias, short_weight, short_bias, skip_weight, embed_weight, embed_bias, hidden_weight, hidden_bias, last_weight, last_bias, frequency, filter_weight, output_weight, output_bias, post_gain, post_offset, up_weight, up_bias, down_weight, down_bias):
    length = tokens.shape[1]
    model_width = tokens.shape[2]
    block_rows = math.gcd(length, 2048)
    kernel_full = filter_table(length, model_width, embed_weight, embed_bias, hidden_weight, hidden_bias, last_weight, last_bias, frequency, filter_weight)

    def mlp_rows(rows_in):
        normed = layer_norm(rows_in, post_gain, post_offset)
        before = low_back(matmul(low(normed), up_weight) + up_bias)
        activated = low(jax.nn.gelu(before, approximate=False))
        return rows_in + (matmul(activated, down_weight) + down_bias)

    def one_sequence(seq_tokens):
        kernel = low_back(low(kernel_full))
        normed = layer_norm(seq_tokens, pre_gain, pre_offset)
        projected = low_back(low(matmul(low(normed), input_weight) + input_bias))
        padded = jnp.pad(projected, ((2, 0), (0, 0)))
        convolved = low_back(padded[:-2] * short_weight[0] + padded[1:-1] * short_weight[1] + padded[2:] * short_weight[2] + short_bias)
        first_part = convolved[:, :model_width]
        second_part = convolved[:, model_width:2 * model_width]
        values_part = convolved[:, 2 * model_width:]
        gated_vals = low_back(low(values_part * second_part))
        mixed_out = low_back(low(long_conv(gated_vals, kernel, skip_weight)))
        branch = low_back(matmul(low(mixed_out * first_part), output_weight) + output_bias)
        hidden = seq_tokens + branch
        blocks = hidden.reshape(length // block_rows, block_rows, model_width)
        return lax.map(jax.checkpoint(mlp_rows), blocks).reshape(length, model_width)
    return lax.map(jax.checkpoint(one_sequence), tokens)

def reference(tokens, cotangent, pre_gain, pre_offset, input_weight, input_bias, short_weight, short_bias, skip_weight, embed_weight, embed_bias, hidden_weight, hidden_bias, last_weight, last_bias, frequency, filter_weight, output_weight, output_bias, post_gain, post_offset, up_weight, up_bias, down_weight, down_bias):
    floats = [member.astype(jnp.float32) for member in (tokens, pre_gain, pre_offset, input_weight, input_bias, short_weight, short_bias, skip_weight, embed_weight, embed_bias, hidden_weight, hidden_bias, last_weight, last_bias, frequency, filter_weight, output_weight, output_bias, post_gain, post_offset, up_weight, up_bias, down_weight, down_bias)]
    result, pullback = jax.vjp(forward, *floats)
    grads = pullback(cotangent.astype(jnp.float32))
    return (result.astype(jnp.bfloat16), grads[0].astype(jnp.bfloat16), grads[1], grads[2], grads[3], grads[4], grads[5], grads[6], grads[7], grads[8], grads[9], grads[10], grads[11], grads[12], grads[13], grads[14], grads[15], grads[16], grads[17], grads[18], grads[19], grads[20], grads[21], grads[22], grads[23])
```

```python
from functools import partial
import math

import jax
import jax.numpy as jnp
import numpy as np
from jax import lax
from jax.experimental import pallas as pl
from jax.experimental.pallas import tpu as pltpu
from jax.sharding import PartitionSpec as P

FEATURES = 33
LANES = 128
f32 = jnp.float32
bf16 = jnp.bfloat16
highest = lax.Precision.HIGHEST


def swap_seq(value, mask):
    count = lax.axis_size("seq")
    return lax.ppermute(value, "seq", [(i, i ^ mask) for i in range(count)])


def swap_core(value):
    return swap_seq(value, 1)


def swap_y(value):
    return swap_seq(value, 2)


def swap_z(value, mask):
    return swap_seq(value, 4 * mask)


def swap_x(value):
    count = lax.axis_size("dp")
    return lax.ppermute(value, "dp", [(i, i ^ 1) for i in range(count)])


def z_masks(count):
    if count == 4:
        return [3, 1]
    masks, step = [], count // 2
    while step:
        masks.append(step)
        step //= 2
    return masks


def z_order(count):
    order = [0]
    for mask in z_masks(count):
        order = order + [entry ^ mask for entry in order]
    return order


def chip_groups():
    count = lax.axis_size("seq")
    return [list(range(core, count, 2)) for core in range(2)]


def chip_exchange(value):
    return lax.all_to_all(
        value, "seq", split_axis=0, concat_axis=0, tiled=True, axis_index_groups=chip_groups()
    )


def pick(value, index, axis):
    return lax.dynamic_index_in_dim(value, index, axis, keepdims=False)


def both(mine, other, second):
    return jnp.where(second == 0, jnp.stack([mine, other]), jnp.stack([other, mine]))


def place():
    seq = lax.axis_index("seq")
    return seq // 4, (seq // 2) % 2, seq % 2, lax.axis_index("dp")


def by_index(have, order, own):
    bit = 1
    value = jnp.stack([have[order.index(entry)] for entry in range(len(order))])
    while bit < len(order):
        grid = value.reshape(-1, 2, bit, *value.shape[1:])
        turned = jnp.stack([grid[:, 1], grid[:, 0]], axis=1)
        value = jnp.where((own & bit) == 0, grid, turned).reshape(value.shape)
        bit *= 2
    return value


def gather_pieces(piece):
    z, y, _, x = place()
    z_count = lax.axis_size("seq") // 4
    have = piece[None]
    for mask in z_masks(z_count):
        have = jnp.concatenate([have, swap_z(have, mask)], axis=0)
    half = piece.shape[0] // 2
    first, second = have[:, :half], have[:, half:]
    first_y, second_x = swap_y(first), swap_x(second)
    first = jnp.stack([first, first_y])
    second = jnp.stack([second, second_x])
    first_x, second_y = swap_x(first), swap_y(second)
    first = jnp.stack([first, first_x], axis=1)
    second = jnp.stack([second, second_y])
    rel = jnp.concatenate([first, second], axis=3)
    order = z_order(z_count)
    rows = []
    for za in range(z_count):
        rel_z = z ^ za
        slot = sum(jnp.where(rel_z == entry, at, 0) for at, entry in enumerate(order))
        slab = pick(rel, slot, 2)
        slab = jnp.where(y == 0, slab, jnp.stack([slab[1], slab[0]]))
        slab = jnp.where(x == 0, slab, jnp.stack([slab[:, 1], slab[:, 0]], axis=1))
        rows.append(slab)
    return jnp.stack(rows)


def reduce_z(parts):
    z = place()[0]
    z_count = parts.shape[0]
    have = jnp.stack([pick(parts, z ^ rel, 0) for rel in z_order(z_count)])
    for mask in reversed(z_masks(z_count)):
        half = have.shape[0] // 2
        got = swap_z(have[half:].astype(bf16), mask)
        have = have[:half] + got.astype(f32)
    return have[0]


def reduce_pair(first, second):
    _, y, _, x = place()
    first_got = swap_x(pick(first, 1 - x, 2))
    second_got = swap_y(pick(second, 1 - y, 1))
    first = pick(first, x, 2).astype(f32) + first_got.astype(f32)
    second = pick(second, y, 1).astype(f32) + second_got.astype(f32)
    first_got = swap_y(pick(first, 1 - y, 1).astype(bf16))
    second_got = swap_x(pick(second, 1 - x, 1).astype(bf16))
    first = pick(first, y, 1) + first_got.astype(f32)
    second = pick(second, x, 1) + second_got.astype(f32)
    return reduce_z(first), reduce_z(second)


def sum_chips(value):
    for mask in z_masks(lax.axis_size("seq") // 4):
        value = value + swap_z(value, mask)
    value = value + swap_y(value)
    return value + swap_x(value)


def gather_small(value):
    seq = lax.axis_index("seq")
    count = lax.axis_size("seq")
    have = value[None]
    for mask in [1] + [4 * m for m in z_masks(count // 4)] + [2]:
        have = jnp.concatenate([have, swap_seq(have, mask)], axis=0)
    order = [0]
    for mask in [1] + [4 * m for m in z_masks(count // 4)] + [2]:
        order = order + [entry ^ mask for entry in order]
    return by_index(have, order, seq)


def twiddle(k, n):
    angle = -2.0 * math.pi * (k % n) / n
    return math.cos(angle), math.sin(angle)


def c_add(p, q):
    return (p[0] + q[0], q[1] if p[1] is None else (p[1] if q[1] is None else p[1] + q[1]))


def c_sub(p, q):
    if q[1] is None:
        return (p[0] - q[0], p[1])
    return (p[0] - q[0], -q[1] if p[1] is None else p[1] - q[1])


def c_conj(p):
    return (p[0], None if p[1] is None else -p[1])


def c_turn(p, k, n):
    k = k % n
    if k == 0:
        return p
    re, im = p
    if 4 * k == n:
        return (im if im is not None else jnp.zeros_like(re), -re)
    if 2 * k == n:
        return (-re, None if im is None else -im)
    if 4 * k == 3 * n:
        return (-im if im is not None else jnp.zeros_like(re), re)
    c, s = twiddle(k, n)
    if im is None:
        return (re * c, re * s)
    return (re * c - im * s, re * s + im * c)


def real_dft(xs):
    n = len(xs)
    if n == 1:
        return [(xs[0], None)]
    if n == 2:
        if xs[1] is None:
            return [(xs[0], None), (xs[0], None)]
        return [(xs[0] + xs[1], None), (xs[0] - xs[1], None)]
    even, odd = real_dft(xs[0::2]), real_dft(xs[1::2])
    out = [None] * (n // 2 + 1)
    for k in range(n // 4 + 1):
        turned = c_turn(odd[k], k, n)
        out[k] = c_add(even[k], turned)
        if n // 2 - k != k:
            out[n // 2 - k] = c_conj(c_sub(even[k], turned))
    return out


def real_inverse(spec):
    def whole(v):
        n = 2 * (len(v) - 1)
        if n == 2:
            return [v[0][0] + v[1][0], None]
        even, odd = [], []
        for k in range(n // 4 + 1):
            mirror = c_conj(v[n // 2 - k])
            e, o = c_add(v[k], mirror), c_turn(c_sub(v[k], mirror), -k, n)
            if k == 0 or 4 * k == n:
                e, o = (e[0], None), (o[0], None)
            even.append(e)
            odd.append(o)
        even, odd = whole(even), whole(odd)
        return [entry for pair in zip(even, odd) for entry in pair]

    values = whole(spec)
    return values[: len(values) // 2]


def split_terms(value):
    high = value.astype(bf16)
    return high, (value - high.astype(f32)).astype(bf16)


def conv_tables(pairs):
    rows = 4 * pairs
    total = rows * LANES
    slots = np.arange(pairs + 1)
    lanes = np.arange(LANES)
    upper = lanes >= LANES // 2
    angle = -2.0 * np.pi * slots[:, None] / rows * upper[None, :]
    lane_turn = np.stack([np.cos(angle), np.sin(angle)], axis=1).astype(np.float32)
    freq = slots[:, None] + np.where(upper, rows // 2, 0)[None, :]
    angle = -2.0 * np.pi * ((freq[:, None, :] * lanes[None, :, None]) % total) / total
    turn = np.stack([np.cos(angle), np.sin(angle)], axis=1).astype(np.float32)
    angle = 2.0 * np.pi * ((lanes[:, None] * lanes[None, :]) % LANES) / LANES
    c, s = np.cos(angle), np.sin(angle)

    def terms(table):
        table = table.astype(np.float32)
        high = table.astype(bf16)
        low = (table - high.astype(np.float32)).astype(bf16)
        return np.concatenate([high, low], axis=1)

    ahead = terms(np.block([[c, s], [-s, c]]))
    back = terms(np.block([[c, -s], [s, c]]) / total)
    return lane_turn, turn, ahead, back


CHUNK = 16


def put(terms_ref, start, slot, re, im):
    cols = pl.ds(slot * LANES, LANES)
    terms_ref[pl.ds(start, CHUNK), cols] = re
    terms_ref[pl.ds(LANES + start, CHUNK), cols] = im


COLUMNS = 4 * LANES


def table_product(table_ref, terms_ref, out_ref):
    width = terms_ref.shape[1]
    high_table, low_table = table_ref[:, :256], table_ref[:, 256:]
    for at in range(0, width, COLUMNS):
        cols = pl.ds(at, min(COLUMNS, width - at))
        high, low = split_terms(terms_ref[:, cols])
        out_ref[:, cols] = (
            jnp.dot(high_table, low, preferred_element_type=f32)
            + jnp.dot(low_table, high, preferred_element_type=f32)
            + jnp.dot(high_table, high, preferred_element_type=f32)
        )


def lane_sign(shape):
    return jnp.where(lax.broadcasted_iota(jnp.int32, shape, 1) < LANES // 2, 1.0, -1.0).astype(f32)


def transform(x_ref, pairs, lane_ref, turn_ref, ahead_ref, terms_ref, spec_ref):
    sign = lane_sign((CHUNK, LANES))

    def chunk(step, carry):
        start = pl.multiple_of(step * CHUNK, CHUNK)
        xs = [x_ref[j, pl.ds(start, CHUNK), :].astype(f32) for j in range(pairs)]
        spec = real_dft(xs + [None] * pairs)
        for k in range(pairs + 1):
            re, im = spec[k]
            c, s = lane_ref[k, 0:1, :], lane_ref[k, 1:2, :]
            if im is None:
                re, im = re * c, re * s
            else:
                re, im = re * c - im * s, re * s + im * c
            re = pltpu.roll(re, LANES // 2, 1) + sign * re
            im = pltpu.roll(im, LANES // 2, 1) + sign * im
            c, s = turn_ref[k, 0, pl.ds(start, CHUNK), :], turn_ref[k, 1, pl.ds(start, CHUNK), :]
            put(terms_ref, start, k, re * c - im * s, re * s + im * c)
        return carry

    lax.fori_loop(0, LANES // CHUNK, chunk, 0)
    table_product(ahead_ref, terms_ref, spec_ref)


def put_product(terms_ref, pairs, one_ref, other_ref, conjugate):
    def chunk(step, carry):
        start = pl.multiple_of(step * CHUNK, CHUNK)
        for k in range(pairs + 1):
            cols = pl.ds(k * LANES, LANES)
            a, b = one_ref[pl.ds(start, CHUNK), cols], one_ref[pl.ds(LANES + start, CHUNK), cols]
            c, d = other_ref[pl.ds(start, CHUNK), cols], other_ref[pl.ds(LANES + start, CHUNK), cols]
            if conjugate:
                put(terms_ref, start, k, a * c + b * d, b * c - a * d)
            else:
                put(terms_ref, start, k, a * c - b * d, a * d + b * c)
        return carry

    lax.fori_loop(0, LANES // CHUNK, chunk, 0)


def inverse(pairs, lane_ref, turn_ref, back_ref, terms_ref, spec_ref, finish):
    table_product(back_ref, terms_ref, spec_ref)
    sign = lane_sign((CHUNK, LANES))

    def chunk(step, carry):
        start = pl.multiple_of(step * CHUNK, CHUNK)
        spec = []
        for k in range(pairs + 1):
            cols = pl.ds(k * LANES, LANES)
            re, im = spec_ref[pl.ds(start, CHUNK), cols], spec_ref[pl.ds(LANES + start, CHUNK), cols]
            c, s = turn_ref[k, 0, pl.ds(start, CHUNK), :], turn_ref[k, 1, pl.ds(start, CHUNK), :]
            re, im = re * c + im * s, im * c - re * s
            re = pltpu.roll(re, LANES // 2, 1) + sign * re
            im = pltpu.roll(im, LANES // 2, 1) + sign * im
            c, s = lane_ref[k, 0:1, :], lane_ref[k, 1:2, :]
            re, im = re * c + im * s, im * c - re * s
            spec.append((re, None if k in (0, pairs) else im))
        for j, values in enumerate(real_inverse(spec)):
            finish(j, start, values)
        return carry

    lax.fori_loop(0, LANES // CHUNK, chunk, 0)


def window_of(j, start, delta, length):
    lane = lax.broadcasted_iota(jnp.int32, (CHUNK, LANES), 1)
    row = lax.broadcasted_iota(jnp.int32, (CHUNK, LANES), 0)
    position = (2 * j + lane // (LANES // 2)) * LANES + start + row
    return jnp.exp(-(position.astype(f32) / (length - 1)) * delta) + 0.05


def filter_body(pairs, h_ref, w_ref, delta_ref, lane_ref, turn_ref, ahead_ref, spec_ref, low_ref, terms_ref):
    delta = delta_ref[...]
    for j in range(pairs):
        rows = jnp.dot(h_ref[j], w_ref[...], precision=highest, preferred_element_type=f32)
        window = jnp.concatenate(
            [window_of(j, start, delta, 2 * pairs * LANES) for start in range(0, LANES, CHUNK)], axis=0
        )
        low_ref[j] = (rows * window).astype(bf16).astype(f32)
    transform(low_ref, pairs, lane_ref, turn_ref, ahead_ref, terms_ref, spec_ref)


def forward_body(
    pairs, x_ref, kernel_ref, skip_ref, lane_ref, turn_ref, ahead_ref, back_ref, out_ref, spec_ref, terms_ref, work_ref
):
    transform(x_ref, pairs, lane_ref, turn_ref, ahead_ref, terms_ref, spec_ref)
    put_product(terms_ref, pairs, spec_ref, kernel_ref, False)
    skip = skip_ref[...]

    def finish(j, start, values):
        rows = pl.ds(start, CHUNK)
        out_ref[j, rows, :] = (values + x_ref[j, rows, :].astype(f32) * skip).astype(bf16)

    inverse(pairs, lane_ref, turn_ref, back_ref, terms_ref, work_ref, finish)


def backward_body(
    pairs,
    g_ref,
    x_ref,
    x_spec_ref,
    kernel_ref,
    skip_ref,
    h_ref,
    w_ref,
    delta_ref,
    lane_ref,
    turn_ref,
    ahead_ref,
    back_ref,
    gx_ref,
    gh_ref,
    gw_ref,
    gskip_ref,
    terms_ref,
    spec_ref,
    work_ref,
    pre_ref,
):
    transform(g_ref, pairs, lane_ref, turn_ref, ahead_ref, terms_ref, spec_ref)
    put_product(terms_ref, pairs, spec_ref, kernel_ref, True)
    skip = skip_ref[...]

    def finish_x(j, start, values):
        rows = pl.ds(start, CHUNK)
        gx_ref[j, rows, :] = (values + g_ref[j, rows, :].astype(f32) * skip).astype(bf16)

    inverse(pairs, lane_ref, turn_ref, back_ref, terms_ref, work_ref, finish_x)
    put_product(terms_ref, pairs, spec_ref, x_spec_ref, True)
    delta = delta_ref[...]

    def finish_kernel(j, start, values):
        window = window_of(j, start, delta, 2 * pairs * LANES)
        pre_ref[j, pl.ds(start, CHUNK), :] = values.astype(bf16).astype(f32) * window

    inverse(pairs, lane_ref, turn_ref, back_ref, terms_ref, work_ref, finish_kernel)
    gw_ref[...] = jnp.zeros_like(gw_ref)
    gskip_ref[...] = jnp.zeros_like(gskip_ref)
    for j in range(pairs):
        pre = pre_ref[j]
        gh = lax.dot_general(
            pre, w_ref[...], (((1,), (1,)), ((), ())), precision=highest, preferred_element_type=f32
        )
        gh_ref[j] = gh.astype(bf16)
        gw_ref[...] += lax.dot_general(
            h_ref[j], pre, (((0,), (0,)), ((), ())), precision=highest, preferred_element_type=f32
        )
        gskip_ref[...] += jnp.sum(g_ref[j].astype(f32) * x_ref[j].astype(f32), axis=0, keepdims=True)


VMEM_BYTES = 50 * 1024 * 1024


def whole_call(body, outs, scratch, flops, moved, *operands):
    return pl.pallas_call(
        body,
        out_shape=outs,
        scratch_shapes=scratch,
        compiler_params=pltpu.CompilerParams(vmem_limit_bytes=VMEM_BYTES),
        cost_estimate=pl.CostEstimate(flops=flops, bytes_accessed=moved, transcendentals=0),
    )(*operands)


def spec_shape(pairs):
    return (256, (pairs + 1) * LANES)


def conv_filter(hidden, weight, delta, tables):
    pairs = hidden.shape[0]
    lane_turn, turn, ahead, _ = tables
    return whole_call(
        partial(filter_body, pairs),
        jax.ShapeDtypeStruct(spec_shape(pairs), f32),
        [pltpu.VMEM((pairs, LANES, LANES), f32), pltpu.VMEM(spec_shape(pairs), f32)],
        10**9,
        8 * 10**6,
        hidden,
        weight,
        delta,
        lane_turn,
        turn,
        ahead,
    )


def conv_forward(x, kernel_spec, skip, tables):
    pairs = x.shape[0]
    return whole_call(
        partial(forward_body, pairs),
        (jax.ShapeDtypeStruct(x.shape, bf16), jax.ShapeDtypeStruct(spec_shape(pairs), f32)),
        [pltpu.VMEM(spec_shape(pairs), f32), pltpu.VMEM(spec_shape(pairs), f32)],
        2 * 10**9,
        10 * 10**6,
        x,
        kernel_spec,
        skip,
        *tables,
    )


def conv_backward(g, x, x_spec, kernel_spec, skip, hidden, weight, delta, tables):
    pairs = x.shape[0]
    return whole_call(
        partial(backward_body, pairs),
        (
            jax.ShapeDtypeStruct(x.shape, bf16),
            jax.ShapeDtypeStruct(x.shape, bf16),
            jax.ShapeDtypeStruct((LANES, LANES), f32),
            jax.ShapeDtypeStruct((1, LANES), f32),
        ),
        [
            pltpu.VMEM(spec_shape(pairs), f32),
            pltpu.VMEM(spec_shape(pairs), f32),
            pltpu.VMEM(spec_shape(pairs), f32),
            pltpu.VMEM(x.shape, f32),
        ],
        4 * 10**9,
        16 * 10**6,
        g,
        x,
        x_spec,
        kernel_spec,
        skip,
        hidden,
        weight,
        delta,
        *tables,
    )


def plain_spectrum(x, length):
    pairs, _, lanes = x.shape
    flat = x.astype(f32).reshape(pairs, LANES, 2, lanes // 2).transpose(3, 0, 2, 1)
    tables = spectral_tables(length // 64, LANES)
    return forward_transform(flat.reshape(lanes // 2, length // LANES, LANES), tables)


def plain_inverse(re, im, length):
    tables = spectral_tables(length // 64, LANES)
    back = inverse_transform(re, im, tables, length // LANES)
    channels = back.shape[0]
    back = back.reshape(channels, length // 256, 2, LANES).transpose(1, 3, 2, 0)
    return back.reshape(length // 256, LANES, 2 * channels)


def spectral_tables(rows_total, col_count):
    total_size = rows_total * col_count
    row_index = jnp.arange(rows_total, dtype=jnp.int32)
    col_index = jnp.arange(col_count, dtype=jnp.int32)
    row_angle = (row_index[:, None] * row_index[None, :] % rows_total).astype(f32) * (
        2.0 * math.pi / rows_total
    )
    col_angle = (col_index[:, None] * col_index[None, :] % col_count).astype(f32) * (
        2.0 * math.pi / col_count
    )
    twist_angle = (row_index[:, None] * col_index[None, :]).astype(f32) * (2.0 * math.pi / total_size)
    return (
        jnp.cos(row_angle),
        -jnp.sin(row_angle),
        jnp.cos(twist_angle),
        -jnp.sin(twist_angle),
        jnp.cos(col_angle),
        -jnp.sin(col_angle),
        total_size,
    )


def forward_transform(signal, tables):
    row_cos, row_sin, twist_cos, twist_sin, col_cos, col_sin, _ = tables
    half_rows = signal.shape[1]
    product = partial(jnp.einsum, precision=highest)
    first_re = product("ka,cab->ckb", row_cos[:, :half_rows], signal)
    first_im = product("ka,cab->ckb", row_sin[:, :half_rows], signal)
    turned_re = first_re * twist_cos - first_im * twist_sin
    turned_im = first_re * twist_sin + first_im * twist_cos
    out_re = product("ckb,bm->ckm", turned_re, col_cos) - product("ckb,bm->ckm", turned_im, col_sin)
    out_im = product("ckb,bm->ckm", turned_re, col_sin) + product("ckb,bm->ckm", turned_im, col_cos)
    return (out_re, out_im)


def inverse_transform(spec_re, spec_im, tables, half_rows):
    row_cos, row_sin, twist_cos, twist_sin, col_cos, col_sin, total_size = tables
    product = partial(jnp.einsum, precision=highest)
    back_re = product("ckm,mb->ckb", spec_re, col_cos) + product("ckm,mb->ckb", spec_im, col_sin)
    back_im = product("ckm,mb->ckb", spec_im, col_cos) - product("ckm,mb->ckb", spec_re, col_sin)
    untwist_re = back_re * twist_cos + back_im * twist_sin
    untwist_im = back_im * twist_cos - back_re * twist_sin
    real_part = product("ak,ckb->cab", row_cos[:half_rows], untwist_re) + product(
        "ak,ckb->cab", row_sin[:half_rows], untwist_im
    )
    return real_part / total_size


def plain_window(shape, delta, length):
    pairs, _, lanes = shape
    position = jnp.arange(length, dtype=jnp.int32).reshape(pairs, 2, LANES, 1).astype(f32)
    window = jnp.exp(-(position / (length - 1)) * delta[0, : lanes // 2]) + 0.05
    return window.transpose(0, 2, 1, 3).reshape(shape)


def plain_filter(hidden, weight, delta):
    pairs = hidden.shape[0]
    length = 256 * pairs
    rows = jnp.einsum("jbh,hc->jbc", hidden, weight, precision=highest)
    rows = (rows * plain_window(rows.shape, delta, length)).astype(bf16)
    return plain_spectrum(rows, length)


def plain_forward(x, kernel_spec, skip):
    length = 256 * x.shape[0]
    re, im = plain_spectrum(x, length)
    kre, kim = kernel_spec
    out = plain_inverse(re * kre - im * kim, re * kim + im * kre, length)
    return (out + x.astype(f32) * skip).astype(bf16), (re, im)


def plain_backward(g, x, x_spec, kernel_spec, skip, hidden, weight, delta):
    length = 256 * x.shape[0]
    re, im = plain_spectrum(g, length)
    kre, kim = kernel_spec
    xre, xim = x_spec
    gx = plain_inverse(re * kre + im * kim, im * kre - re * kim, length) + g.astype(f32) * skip
    pre = plain_inverse(re * xre + im * xim, im * xre - re * xim, length).astype(bf16).astype(f32)
    pre = pre * plain_window(pre.shape, delta, length)
    gh = jnp.einsum("jbc,hc->jbh", pre, weight, precision=highest)
    gw = jnp.einsum("jbh,jbc->hc", hidden, pre, precision=highest)
    gskip = jnp.sum(g.astype(f32) * x.astype(f32), axis=(0, 1))[None]
    return gx.astype(bf16), gh.astype(bf16), gw, gskip


def feed_body(nt_ref, ct_ref, up_ref, bias_ref, down_ref, y_ref, gx_ref, gdown_ref, gup_ref, gbias_ref):
    @pl.when(pl.program_id(0) == 0)
    def _():
        y_ref[...] = jnp.zeros_like(y_ref)
        gx_ref[...] = jnp.zeros_like(gx_ref)

    nt, ct, up, down = nt_ref[...], ct_ref[...], up_ref[...], down_ref[...]
    before = jnp.dot(nt, up, preferred_element_type=f32) + bias_ref[...]
    cdf = 0.5 * (1.0 + lax.erf(before * math.sqrt(0.5)))
    active = (before * cdf).astype(bf16)
    slope = cdf + before * (jnp.exp(-0.5 * before * before) * (1.0 / math.sqrt(2.0 * math.pi)))
    g_act = lax.dot_general(ct, down, (((1,), (1,)), ((), ())), preferred_element_type=f32)
    g_before = (g_act * slope).astype(bf16)
    y_ref[...] += jnp.dot(active, down, preferred_element_type=f32)
    gx_ref[...] += lax.dot_general(g_before, up, (((1,), (1,)), ((), ())), preferred_element_type=f32)
    gdown_ref[...] = lax.dot_general(
        active, ct, (((0,), (0,)), ((), ())), preferred_element_type=f32
    ).astype(bf16)
    gup_ref[...] = lax.dot_general(
        nt, g_before, (((0,), (0,)), ((), ())), preferred_element_type=f32
    ).astype(bf16)
    gbias_ref[...] = jnp.sum(g_before.astype(f32), axis=0, keepdims=True)


def feed_forward(nt, ct, up, bias, down):
    rows, width = nt.shape
    hidden = up.shape[1]
    block = min(256, hidden)
    return pl.pallas_call(
        feed_body,
        grid=(hidden // block,),
        in_specs=[
            pl.BlockSpec((rows, width), lambda i: (0, 0)),
            pl.BlockSpec((rows, width), lambda i: (0, 0)),
            pl.BlockSpec((width, block), lambda i: (0, i)),
            pl.BlockSpec((1, block), lambda i: (0, i)),
            pl.BlockSpec((block, width), lambda i: (i, 0)),
        ],
        out_specs=[
            pl.BlockSpec((rows, width), lambda i: (0, 0)),
            pl.BlockSpec((rows, width), lambda i: (0, 0)),
            pl.BlockSpec((block, width), lambda i: (i, 0)),
            pl.BlockSpec((width, block), lambda i: (0, i)),
            pl.BlockSpec((1, block), lambda i: (0, i)),
        ],
        out_shape=[
            jax.ShapeDtypeStruct((rows, width), f32),
            jax.ShapeDtypeStruct((rows, width), f32),
            jax.ShapeDtypeStruct((hidden, width), bf16),
            jax.ShapeDtypeStruct((width, hidden), bf16),
            jax.ShapeDtypeStruct((1, hidden), f32),
        ],
        compiler_params=pltpu.CompilerParams(vmem_limit_bytes=VMEM_BYTES),
        cost_estimate=pl.CostEstimate(
            flops=12 * rows * width * hidden,
            bytes_accessed=8 * width * hidden + 12 * rows * width,
            transcendentals=2 * rows * hidden,
        ),
    )(nt, ct, up, bias, down)


def norm_forward(values, norm_gain, norm_offset):
    center = values - jnp.mean(values, axis=-1, keepdims=True)
    inverse_root = lax.rsqrt(jnp.mean(center * center, axis=-1, keepdims=True) + 1e-05)
    normed = center * inverse_root
    return (normed * norm_gain + norm_offset, normed, inverse_root)


def norm_backward(upstream, normed, inverse_root, norm_gain):
    scaled = upstream * norm_gain
    centered = (
        scaled
        - jnp.mean(scaled, axis=-1, keepdims=True)
        - normed * jnp.mean(scaled * normed, axis=-1, keepdims=True)
    )
    return centered * inverse_root


def contract(left_side, right_side, left_dim, right_dim):
    return lax.dot_general(
        left_side, right_side, (((left_dim,), (right_dim,)), ((), ())), preferred_element_type=f32
    )


def trunk_hidden(trunk, features):
    embed_weight, embed_bias, hidden_weight, hidden_bias, last_weight, last_bias, frequency = trunk
    layer_out = jnp.sin(frequency * (jnp.dot(features, embed_weight, precision=highest) + embed_bias))
    layer_out = jnp.sin(frequency * (jnp.dot(layer_out, hidden_weight, precision=highest) + hidden_bias))
    return jnp.sin(frequency * (jnp.dot(layer_out, last_weight, precision=highest) + last_bias))


def to_owners(value, chips):
    tokens, width = value.shape
    channels = width // chips
    grid = value.reshape(tokens // 256, 2, LANES, chips, channels)
    return grid.transpose(3, 0, 2, 1, 4).reshape(chips, tokens // 256, LANES, 2 * channels)


def from_owners(value):
    chips, pairs, _, lanes = value.shape
    grid = value.reshape(chips, pairs, LANES, 2, lanes // 2)
    return grid.transpose(1, 3, 2, 0, 4).reshape(pairs * 256, chips * (lanes // 2))


def exchange(value):
    return chip_exchange(value)


def flatten(*values):
    return jnp.concatenate([value.reshape(-1) for value in values])


def unflatten(flat, shapes):
    out, at = [], 0
    for shape in shapes:
        size = int(np.prod(shape))
        out.append(flat[at : at + size].reshape(shape))
        at += size
    return out


def to_rows(flat):
    rows = -(-flat.shape[0] // 1024) * 8
    return jnp.pad(flat, (0, rows * LANES - flat.shape[0])).reshape(rows, LANES)


def plain_device(
    tokens,
    cotangent,
    pre_gain,
    pre_offset,
    input_weight,
    input_bias,
    short_weight,
    short_bias,
    skip_weight,
    embed_weight,
    embed_bias,
    hidden_weight,
    hidden_bias,
    last_weight,
    last_bias,
    frequency,
    filter_weight,
    output_weight,
    output_bias,
    post_gain,
    post_offset,
    up_weight,
    up_bias,
    down_weight,
    down_bias,
):
    seq_count = lax.axis_size("seq")
    seq_index = lax.axis_index("seq")
    z, y, core, x = place()
    chips = seq_count // 2
    z_count = seq_count // 4
    chip = seq_index // 2
    tok_count = tokens.shape[1]
    width = tokens.shape[2]
    length = tok_count * seq_count
    channels = width // seq_count
    ff = up_weight.shape[1]
    hidden_own = ff // seq_count
    half = width // 2
    pairs = length // 256
    kernels = 2 * channels == LANES

    mine = jnp.stack([tokens[0], cotangent[0]])
    other = swap_core(mine)
    pair = both(mine, other, core)
    tok = pair[:, 0].reshape(2 * tok_count, width)
    cot = pair[:, 1].reshape(2 * tok_count, width)

    def half_columns(value, groups, run):
        rows = value.shape[0]
        grid = value.reshape(rows, groups, chips, 2, run)
        return [grid[:, :, :, side].reshape(rows, groups * chips * run) for side in range(2)]

    def own_rows(value, groups, run):
        sides = half_columns(value, groups, run)
        keep = jnp.where(core == 0, sides[0], sides[1])
        got = swap_core(jnp.where(core == 0, sides[1], sides[0]))
        return jnp.where(core == x, keep, got)

    in_piece = own_rows(input_weight, 3, channels)
    in_half = gather_pieces(in_piece).reshape(width, 3 * half)
    small_shapes = [(width // seq_count,)] * 2 + [(3, channels), (3, 3, channels), (3, channels)]
    small_shapes += [(width // seq_count,)] * 3 + [(hidden_own,), (width // seq_count,)]
    smalls = flatten(
        pre_gain, pre_offset, input_bias, short_weight, short_bias, output_bias, post_gain, post_offset, up_bias, down_bias
    )
    shapes = [v.shape for v in (pre_gain, pre_offset, input_bias, short_weight, short_bias)]
    shapes += [v.shape for v in (output_bias, post_gain, post_offset, up_bias, down_bias)]
    small_rows = to_rows(smalls)
    small_all = gather_small(small_rows.reshape(-1)).astype(f32)
    columns, at = [], 0
    for shape in shapes:
        size = int(np.prod(shape))
        columns.append(small_all[:, at : at + size])
        at += size

    def halved(value, run):
        lead = value.shape[:-1]
        return pick(value.reshape(*lead, -1, 2, run), core, len(lead) + 1).reshape(*lead, -1)

    pre_gain_full, pre_offset_full = columns[0].reshape(-1), columns[1].reshape(-1)
    input_bias_own = halved(columns[2].reshape(3, width), channels).reshape(-1)
    short_full = columns[3].reshape(seq_count, 3, -1).transpose(1, 0, 2).reshape(3, 3, width)
    short_taps = halved(short_full, channels).reshape(3, -1)
    short_bias_own = halved(columns[4].reshape(3, width), channels).reshape(-1)
    output_bias_full = columns[5].reshape(-1)
    post_gain_full, post_offset_full = columns[6].reshape(-1), columns[7].reshape(-1)
    up_bias_own = halved(columns[8].reshape(-1), hidden_own)
    down_bias_full = columns[9].reshape(-1)

    out_rows = output_weight.shape[0] // 2
    up_piece = own_rows(up_weight, 1, hidden_own)
    out_piece = pick(output_weight.reshape(2, out_rows, width), x, 0)
    down_piece = pick(down_weight.reshape(2, hidden_own // 2, width), x, 0)
    up_half = gather_pieces(up_piece).reshape(width, ff // 2)
    n_out, n_down = out_rows // 2, hidden_own // 4
    mixed_piece = jnp.concatenate(
        [out_piece[:n_out], down_piece[:n_down], out_piece[n_out:], down_piece[n_down:]], axis=0
    )
    later = gather_pieces(mixed_piece)
    later = later.reshape(chips, 2, 2, n_out + n_down, width)
    out_half = later[:, :, :, :n_out].reshape(half, width)
    down_half = later[:, :, :, n_out:].reshape(ff // 2, width)

    positions = (seq_index * tok_count + jnp.arange(tok_count, dtype=jnp.int32)).astype(f32)
    relative = positions / (length - 1)
    phases = positions * (2.0 * math.pi / length)
    band_count = (FEATURES - 1) // 2
    band_freq = jnp.linspace(0.0001, band_count - 1, band_count).astype(f32)
    angles = phases[:, None] * band_freq[None, :]
    features = jnp.concatenate([relative[:, None], jnp.cos(angles), -jnp.sin(angles)], axis=1)
    trunk = (embed_weight, embed_bias, hidden_weight, hidden_bias, last_weight, last_bias, frequency)
    hidden_rows, trunk_pull = jax.vjp(partial(trunk_hidden, features=features), trunk)
    units = hidden_rows.shape[1]
    own_pairs = tok_count // 256
    packed = hidden_rows.reshape(own_pairs, 2, LANES, units).transpose(0, 2, 1, 3)
    packed = packed.reshape(own_pairs, LANES, 2 * units)
    filter_hidden = lax.all_gather(packed, "seq", axis=0, tiled=True)
    filter_own = filter_weight.astype(f32)
    zero = jnp.zeros_like(filter_own)
    filter_pair = jnp.concatenate(
        [jnp.concatenate([filter_own, zero], axis=1), jnp.concatenate([zero, filter_own], axis=1)], axis=0
    )
    deltas = jnp.linspace(math.log(0.01) / 1.5, math.log(0.01) / 0.3, width).astype(f32)
    delta_own = jnp.abs(lax.dynamic_slice_in_dim(deltas, seq_index * channels, channels))
    delta_pair = jnp.concatenate([delta_own, delta_own])[None]
    skip_own = skip_weight.astype(f32)
    skip_pair = jnp.concatenate([skip_own, skip_own])[None]
    if kernels:
        tables = tuple(jnp.asarray(t) for t in conv_tables(pairs))
        kernel_spec = conv_filter(filter_hidden, filter_pair, delta_pair, tables)
    else:
        kernel_spec = plain_filter(filter_hidden, filter_pair, delta_pair)

    rows = 2 * tok_count
    inputs = tok.astype(f32)
    normed_one, unit_one, inverse_one = norm_forward(inputs, pre_gain_full, pre_offset_full)
    normed_low = normed_one.astype(bf16)
    projected_low = (contract(normed_low, in_half, 1, 0) + input_bias_own).astype(bf16)
    shift = [(i, i + 2) for i in range(seq_count - 2)]
    earlier = lax.ppermute(projected_low[rows - 2 :], "seq", shift)
    extended = jnp.concatenate([earlier, projected_low], axis=0).astype(f32)
    convolved = (
        short_taps[0] * extended[:rows]
        + short_taps[1] * extended[1 : rows + 1]
        + short_taps[2] * extended[2:]
        + short_bias_own
    )
    first_part, second_part, values_part = (convolved[:, i * half : (i + 1) * half] for i in range(3))
    gated_low = (values_part * second_part).astype(bf16)
    gated_ch = exchange(to_owners(gated_low, chips)).reshape(pairs, LANES, 2 * channels)
    if kernels:
        mixed_ch, gated_spec = conv_forward(gated_ch, kernel_spec, skip_pair, tables)
    else:
        mixed_ch, gated_spec = plain_forward(gated_ch, kernel_spec, skip_pair)
    chip_shape = (chips, rows // 256, LANES, 2 * channels)
    mixed_tok = from_owners(exchange(mixed_ch.reshape(chip_shape))).astype(f32)
    mix_low = (mixed_tok * first_part).astype(bf16)
    branch_part = contract(mix_low, out_half, 1, 0)
    branch = branch_part + swap_core(branch_part) + output_bias_full
    hidden = inputs + branch

    normed_two, unit_two, inverse_two = norm_forward(hidden, post_gain_full, post_offset_full)
    normed_two_low = normed_two.astype(bf16)
    down_part, back_part, down_grad, up_grad, up_bias_grad = feed_forward(
        normed_two_low, cot, up_half, up_bias_own[None], down_half
    )

    def own_tokens(value):
        return lax.dynamic_slice_in_dim(value, core * tok_count, tok_count, 0)

    def other_tokens(value):
        return lax.dynamic_slice_in_dim(value, (1 - core) * tok_count, tok_count, 0)

    result = own_tokens(hidden) + (
        own_tokens(down_part) + swap_core(other_tokens(down_part)) + down_bias_full
    )
    up_grad = up_grad.reshape(z_count, 2, 2, 2, -1, ff // 2).transpose(0, 1, 3, 2, 4, 5)
    down_sum, up_sum = reduce_pair(down_grad.reshape(z_count, 2, 2, hidden_own // 2, width), up_grad)

    cot_f = cot.astype(f32)
    down_bias_grad = jnp.sum(cot_f, axis=0)
    normed_two_grad = back_part + swap_core(back_part)
    post_gain_grad = jnp.sum(normed_two_grad * unit_two, axis=0)
    post_offset_grad = jnp.sum(normed_two_grad, axis=0)
    hidden_grad = cot_f + norm_backward(normed_two_grad, unit_two, inverse_two, post_gain_full)
    branch_low = hidden_grad.astype(bf16)
    output_bias_grad = jnp.sum(branch_low.astype(f32), axis=0)
    gate_grad = contract(branch_low, out_half, 1, 1)
    mixed_grad_low = (gate_grad * first_part).astype(bf16)
    first_grad = gate_grad * mixed_tok
    mixed_grad_ch = exchange(to_owners(mixed_grad_low, chips)).reshape(pairs, LANES, 2 * channels)
    back_args = (mixed_grad_ch, gated_ch, gated_spec, kernel_spec, skip_pair, filter_hidden, filter_pair, delta_pair)
    if kernels:
        gated_back, hidden_back, filter_square, skip_line = conv_backward(*back_args, tables)
    else:
        gated_back, hidden_back, filter_square, skip_line = plain_backward(*back_args)
    gated_grad = from_owners(exchange(gated_back.reshape(chip_shape))).astype(f32)
    output_grad = contract(mix_low, branch_low, 0, 0)

    hidden_got = lax.all_to_all(
        hidden_back.reshape(seq_count, own_pairs * LANES, 2 * units), "seq", split_axis=0, concat_axis=0, tiled=True
    )
    hidden_sum = jnp.sum(hidden_got.astype(f32), axis=0)
    hidden_sum = hidden_sum.reshape(own_pairs, LANES, 2, units).transpose(0, 2, 1, 3).reshape(tok_count, units)
    (trunk_grad,) = trunk_pull(hidden_sum)
    filter_grad = filter_square[:units, :channels] + filter_square[units:, channels:]
    skip_grad = skip_line[:, :channels] + skip_line[:, channels:]
    own_grad = jnp.concatenate([filter_grad, skip_grad], axis=0)
    own_grad = own_grad + swap_x(own_grad)
    own_grad = pick(own_grad.reshape(-1, 2, channels // 2), x, 1)

    conv_grad_low = jnp.concatenate(
        [first_grad, gated_grad * values_part, gated_grad * second_part], axis=1
    ).astype(bf16)
    back_shift = [(i + 2, i) for i in range(seq_count - 2)]
    following = lax.ppermute(conv_grad_low[:2], "seq", back_shift)
    conv_grad = conv_grad_low.astype(f32)
    grad_ext = jnp.concatenate([conv_grad_low, following], axis=0).astype(f32)
    projected_grad_low = (
        short_taps[0] * grad_ext[2:] + short_taps[1] * grad_ext[1 : rows + 1] + short_taps[2] * grad_ext[:rows]
    ).astype(bf16)
    short_weight_grad = jnp.stack(
        [jnp.sum(conv_grad * extended[tap : tap + rows], axis=0) for tap in range(3)]
    )
    short_bias_grad = jnp.sum(conv_grad, axis=0)
    input_bias_grad = jnp.sum(projected_grad_low.astype(f32), axis=0)
    input_grad = contract(normed_low, projected_grad_low, 0, 0)
    normed_one_part = contract(projected_grad_low, in_half, 1, 1)
    normed_one_grad = own_tokens(normed_one_part) + swap_core(other_tokens(normed_one_part))
    unit_own = own_tokens(unit_one)
    pre_gain_grad = jnp.sum(normed_one_grad * unit_own, axis=0)
    pre_offset_grad = jnp.sum(normed_one_grad, axis=0)
    tokens_grad = own_tokens(hidden_grad) + norm_backward(
        normed_one_grad, unit_own, own_tokens(inverse_one), pre_gain_full
    )

    in_low = input_grad.astype(bf16).reshape(z_count, 2, 2, 2, -1, 3 * half).transpose(0, 1, 3, 2, 4, 5)
    in_sum = jnp.stack(reduce_pair(in_low[:, :, :, 0], in_low[:, :, :, 1]))
    out_low = output_grad.astype(bf16).reshape(z_count, 2, 2, -1, width)
    split = out_low.shape[3] // 2
    out_sum = jnp.concatenate(reduce_pair(out_low[:, :, :, :split], out_low[:, :, :, split:]), axis=0)

    def whole_columns(value, groups, run):
        got = swap_core(pick(value, 1 - core, 0))
        mine_part = pick(value, core, 0)
        n = mine_part.shape[0]
        grid = both(mine_part, got, core).reshape(2, n, groups, chips, run)
        return grid.transpose(1, 2, 3, 0, 4).reshape(n, -1)

    in_rows = whole_columns(in_sum, 3, channels)
    up_rows_sum = whole_columns(up_sum, 1, hidden_own)

    chip_wide = [post_gain_grad, post_offset_grad, down_bias_grad, output_bias_grad]
    own_wide = [pre_gain_grad, pre_offset_grad, *trunk_grad]
    half_wide = [up_bias_grad.reshape(-1), input_bias_grad, short_weight_grad, short_bias_grad]
    own_flat, half_flat = to_rows(flatten(*own_wide)), to_rows(flatten(*half_wide))
    summed = sum_chips(jnp.concatenate([to_rows(flatten(*chip_wide)), own_flat, half_flat], axis=0))
    n_chip = to_rows(flatten(*chip_wide)).shape[0]
    chip_sum = summed[:n_chip].reshape(-1)
    got = swap_core(summed[n_chip:])
    own_sum = (summed[n_chip:] + got)[: own_flat.shape[0]].reshape(-1)
    half_sum = both(summed[n_chip + own_flat.shape[0] :], got[own_flat.shape[0] :], core).reshape(2, -1)
    chip_sums = unflatten(chip_sum, [v.shape for v in chip_wide])
    own_sums = unflatten(own_sum, [v.shape for v in own_wide])
    half_sums = [
        unflatten(half_sum[side], [v.shape for v in half_wide]) for side in range(2)
    ]

    def joined(index, groups, run):
        pair_of = jnp.stack([half_sums[side][index].reshape(groups, chips, run) for side in range(2)], axis=2)
        return pair_of.reshape(groups, -1)

    block_index = seq_index * 2 + x

    def own_block(value, axis=0):
        size = value.shape[axis] // (2 * seq_count)
        return lax.dynamic_slice_in_dim(value, block_index * size, size, axis)

    up_bias_sum = joined(0, 1, hidden_own).reshape(-1)
    input_bias_sum = joined(1, 3, channels).reshape(-1)
    short_weight_sum = joined(2, 9, channels).reshape(3, -1)
    short_bias_sum = joined(3, 3, channels).reshape(-1)
    return (
        result.astype(bf16)[None],
        tokens_grad.astype(bf16)[None],
        own_block(own_sums[0]),
        own_block(own_sums[1]),
        in_rows,
        own_block(input_bias_sum),
        own_block(short_weight_sum, 1),
        own_block(short_bias_sum),
        own_grad[units],
        *own_sums[2:],
        own_grad[:units],
        out_sum,
        own_block(chip_sums[3]),
        own_block(chip_sums[0]),
        own_block(chip_sums[1]),
        up_rows_sum,
        own_block(up_bias_sum),
        down_sum,
        own_block(chip_sums[2]),
    )


def after(earlier, value):
    return lax.optimization_barrier((earlier, value))[1]


def gather_z(piece):
    have = piece[None]
    for mask in z_masks(lax.axis_size("seq") // 4):
        have = jnp.concatenate([have, swap_z(have, mask)], axis=0)
    return have


def gather_near(have):
    half = have.shape[1] // 2
    first, second = have[:, :half], have[:, half:]
    return jnp.stack([first, swap_y(first)]), jnp.stack([second, swap_x(second)])


def gather_far(near):
    first, second = near
    return first, swap_x(first), second, swap_y(second)


def reduce_step(kept, got):
    return kept.astype(f32) + got.astype(f32)


def reduce_far(total):
    for mask in reversed(z_masks(lax.axis_size("seq") // 4)):
        half = total.shape[0] // 2
        total = total[:half] + swap_z(total[half:].astype(bf16), mask).astype(f32)
    return total[0]


def reduce_rows(kept, sent, first, second):
    total = reduce_step(kept, first(sent))
    total = total[0] + second(total[1].astype(bf16)).astype(f32)
    return reduce_far(total)


def place_pieces(out_ref, pieces, scalars, chips, span):
    first, first_far, second, second_far = pieces
    x = scalars[0]
    half = span // 2
    z_count = chips // 2
    for slot in range(z_count):
        for yr in range(2):
            base = scalars[2 + yr * z_count + slot] * (2 * span)
            source = second_far if yr else second
            for xr in range(2):
                at = pl.multiple_of(base + (x if xr == 0 else 1 - x) * span, span)
                out_ref[pl.ds(at, half), :] = (first_far if xr else first)[yr, slot]
                out_ref[pl.ds(pl.multiple_of(at + half, half), half), :] = source[xr, slot]


def route_rows(grad_ref, kept_ref, sent_ref, scalars, chips, inner, by_x):
    x = scalars[0]
    z_count = chips // 2
    rows = grad_ref.shape[0] // (2 * chips * inner)
    for slot in range(z_count):
        for yr in range(2):
            base = scalars[2 + yr * z_count + slot] * (2 * inner * rows)
            for xr in range(2):
                target, lead = ((sent_ref if xr else kept_ref), yr) if by_x else ((sent_ref if yr else kept_ref), xr)
                for part in range(inner):
                    at = pl.multiple_of(base + part * 2 * rows + (x if xr == 0 else 1 - x) * rows, rows)
                    target[lead, slot, part] = grad_ref[pl.ds(at, rows), :].astype(bf16)


HALO = 16


def short_conv(rows, taps, bias):
    two, one = pltpu.roll(rows, 2, 0), pltpu.roll(rows, 1, 0)
    return (taps[0:1] * two + taps[1:2] * one + taps[2:3] * rows + bias)[HALO:]


def pack_pairs(out_ref, index, pair, even, odd):
    half = LANES // 2
    lower = lax.broadcasted_iota(jnp.int32, even.shape, 1) < half
    out_ref[index, pair] = jnp.where(lower, even, pltpu.roll(odd, half, 1)).astype(bf16)
    out_ref[index + 1, pair] = jnp.where(lower, pltpu.roll(even, half, 1), odd).astype(bf16)


def pack_rows(out_ref, index, value):
    for pair in range(value.shape[0] // 256):
        rows = value[256 * pair : 256 * (pair + 1)]
        pack_pairs(out_ref, index, pair, rows[:LANES], rows[LANES:])


def unpack_rows(in_ref, index):
    half = LANES // 2
    out = []
    for pair in range(in_ref.shape[1]):
        one, two = in_ref[index, pair].astype(f32), in_ref[index + 1, pair].astype(f32)
        lower = lax.broadcasted_iota(jnp.int32, one.shape, 1) < half
        out.append(jnp.where(lower, one, pltpu.roll(two, half, 1)))
        out.append(jnp.where(lower, pltpu.roll(one, half, 1), two))
    return jnp.concatenate(out, axis=0)


def project_body(scalars, normed_ref, bias_ref, a_ref, ax_ref, b_ref, by_ref, out_ref, weight_ref):
    chips = 2 * a_ref.shape[1]
    place_pieces(weight_ref, (a_ref, ax_ref, b_ref, by_ref), scalars, chips, 2 * a_ref.shape[2])
    value = jnp.dot(normed_ref[...], weight_ref[...], preferred_element_type=f32) + bias_ref[...]
    row = lax.broadcasted_iota(jnp.int32, value.shape, 0)
    value = jnp.where(jnp.logical_and(row < HALO, scalars[1] == 0), 0.0, value)
    out_ref[...] = value.astype(bf16)


def grid_call(body, scalars, grid, ins, outs, scratch, flops, moved, transcendentals=0):
    return pl.pallas_call(
        body,
        grid_spec=pltpu.PrefetchScalarGridSpec(
            num_scalar_prefetch=1,
            grid=(grid,),
            in_specs=[pl.BlockSpec(block, index) for _, block, index in ins],
            out_specs=[pl.BlockSpec(block, index) for _, _, block, index in outs],
            scratch_shapes=scratch,
        ),
        out_shape=[jax.ShapeDtypeStruct(shape, dtype) for shape, dtype, _, _ in outs],
        compiler_params=pltpu.CompilerParams(vmem_limit_bytes=VMEM_BYTES),
        cost_estimate=pl.CostEstimate(flops=flops, bytes_accessed=moved, transcendentals=transcendentals),
    )(scalars, *[value for value, _, _ in ins])


def fixed(value):
    return (value, value.shape, lambda i, s, n=value.ndim: (0,) * n)


def fixed_out(shape, dtype):
    return (shape, dtype, shape, lambda i, s, n=len(shape): (0,) * n)


def project(scalars, normed, bias, pieces):
    rows, width = normed.shape
    columns = bias.shape[1]
    block = columns // 3
    lead = pieces[0].shape[:3]
    piece_specs = [(p, (*lead, block), lambda i, s: (0, 0, 0, i)) for p in pieces]
    return grid_call(
        project_body,
        scalars,
        3,
        [fixed(normed), (bias, (1, block), lambda i, s: (0, i)), *piece_specs],
        [
            ((rows, columns), bf16, (rows, block), lambda i, s: (0, i)),
            ((width, columns), bf16, (width, block), lambda i, s: (0, i)),
        ],
        [],
        2 * rows * width * columns,
        4 * width * columns + 2 * rows * (width + columns),
    )


def gate_body(scalars, second_ref, values_ref, t2_ref, t3_ref, b2_ref, b3_ref, out_ref):
    second = short_conv(second_ref[...].astype(f32), t2_ref[...], b2_ref[...])
    values = short_conv(values_ref[...].astype(f32), t3_ref[...], b3_ref[...])
    pack_rows(out_ref, 0, values * second)


def stream_tiles(projected, taps, bias, stream, tiles):
    rows = projected.shape[0]
    index = lambda i, s, at=stream * tiles: (0, at + i)
    return (
        (projected, (rows, LANES), index),
        (taps, (3, LANES), index),
        (bias, (1, LANES), index),
    )


def gate(scalars, projected, taps, bias, chips):
    rows, columns = projected.shape
    tiles = columns // 3 // LANES
    p2, t2, b2 = stream_tiles(projected, taps, bias, 1, tiles)
    p3, t3, b3 = stream_tiles(projected, taps, bias, 2, tiles)
    pairs = (rows - HALO) // 256
    (out,) = grid_call(
        gate_body,
        scalars,
        tiles,
        [p2, p3, t2, t3, b2, b3],
        [((chips, pairs, LANES, LANES), bf16, (2, pairs, LANES, LANES), lambda i, s: (i, 0, 0, 0))],
        [],
        20 * rows * columns,
        3 * rows * columns,
    )
    return out


def branch_body(
    scalars, mixed_ref, first_ref, taps_ref, bias_ref, a_ref, ax_ref, b_ref, by_ref, mixed_out, mix_out, weight_ref, out_ref
):
    chips = 2 * a_ref.shape[1]
    place_pieces(weight_ref, (a_ref, ax_ref, b_ref, by_ref), scalars, chips, 2 * a_ref.shape[2])
    for tile in range(chips // 2):
        cols = slice(tile * LANES, (tile + 1) * LANES)
        mixed = unpack_rows(mixed_ref, 2 * tile)
        first = short_conv(first_ref[:, cols].astype(f32), taps_ref[:, cols], bias_ref[:, cols])
        mixed_out[:, cols] = mixed.astype(bf16)
        mix_out[:, cols] = (mixed * first).astype(bf16)
    out_ref[...] = jnp.dot(mix_out[...], weight_ref[...], preferred_element_type=f32)


def first_stream(projected, taps, bias):
    rows, columns = projected.shape
    block = columns // 3
    return [
        (projected, (rows, block), lambda i, s: (0, 0)),
        (taps, (3, block), lambda i, s: (0, 0)),
        (bias, (1, block), lambda i, s: (0, 0)),
    ]


def branch_out(scalars, mixed, projected, taps, bias, pieces):
    rows = projected.shape[0] - HALO
    half = projected.shape[1] // 3
    width = pieces[0].shape[3]
    return grid_call(
        branch_body,
        scalars,
        1,
        [fixed(mixed), *first_stream(projected, taps, bias), *[fixed(p) for p in pieces]],
        [
            fixed_out((rows, half), bf16),
            fixed_out((rows, half), bf16),
            fixed_out((half, width), bf16),
            fixed_out((rows, width), f32),
        ],
        [],
        2 * rows * half * width,
        4 * rows * width + 6 * half * width,
    )


def tiled_feed_body(
    scalars,
    nt_ref,
    ct_ref,
    bias_ref,
    ua_ref,
    uax_ref,
    ub_ref,
    uby_ref,
    da_ref,
    dax_ref,
    db_ref,
    dby_ref,
    y_ref,
    gx_ref,
    gdown_kept,
    gdown_sent,
    gup_kept,
    gup_sent,
    gbias_ref,
    up_ref,
    down_ref,
    grad_ref,
):
    step = pl.program_id(0)
    z_count = ua_ref.shape[1]
    x = scalars[0]

    @pl.when(step == 0)
    def _():
        y_ref[...] = jnp.zeros_like(y_ref)
        gx_ref[...] = jnp.zeros_like(gx_ref)

    place_pieces(up_ref, (ua_ref, uax_ref, ub_ref, uby_ref), scalars, 2 * z_count, 2 * ua_ref.shape[2])
    span = down_ref.shape[0] // 2
    half = span // 2
    own, other = pl.multiple_of(x * span, span), pl.multiple_of((1 - x) * span, span)
    down_ref[pl.ds(own, half), :] = da_ref[0, 0]
    down_ref[pl.ds(other, half), :] = dax_ref[0, 0]

    def put_second(source):
        down_ref[pl.ds(pl.multiple_of(own + half, half), half), :] = source[0, 0]
        down_ref[pl.ds(pl.multiple_of(other + half, half), half), :] = source[1, 0]

    @pl.when(step < z_count)
    def _():
        put_second(db_ref)

    @pl.when(step >= z_count)
    def _():
        put_second(dby_ref)

    nt, ct, up, down = nt_ref[...], ct_ref[...], up_ref[...], down_ref[...]
    before = jnp.dot(nt, up, preferred_element_type=f32) + bias_ref[...]
    cdf = 0.5 * (1.0 + lax.erf(before * math.sqrt(0.5)))
    active = (before * cdf).astype(bf16)
    slope = cdf + before * (jnp.exp(-0.5 * before * before) * (1.0 / math.sqrt(2.0 * math.pi)))
    g_act = lax.dot_general(ct, down, (((1,), (1,)), ((), ())), preferred_element_type=f32)
    g_before = (g_act * slope).astype(bf16)
    y_ref[...] += jnp.dot(active, down, preferred_element_type=f32)
    gx_ref[...] += lax.dot_general(g_before, up, (((1,), (1,)), ((), ())), preferred_element_type=f32)
    gdown = lax.dot_general(active, ct, (((0,), (0,)), ((), ())), preferred_element_type=f32)
    one, two = gdown[:span], gdown[span:]
    gdown_kept[0, 0] = jnp.where(x == 0, one, two).astype(bf16)
    gdown_sent[0, 0] = jnp.where(x == 0, two, one).astype(bf16)
    grad_ref[...] = lax.dot_general(nt, g_before, (((0,), (0,)), ((), ())), preferred_element_type=f32)
    route_rows(grad_ref, gup_kept, gup_sent, scalars, 2 * z_count, 2, False)
    gbias_ref[...] = jnp.sum(g_before.astype(f32), axis=0, keepdims=True)


def tiled_feed(scalars, nt, ct, bias, up, down):
    rows, width = nt.shape
    hidden = bias.shape[1]
    z_count = up[0].shape[1]
    chips = 2 * z_count
    block = hidden // chips
    h = up[0].shape[2]
    hd = down[0].shape[2]
    column = lambda i, s: (0, s[2 + i])
    up_specs = [(p, (2, z_count, h, block), lambda i, s: (0, 0, 0, s[2 + i])) for p in up]
    near = lambda i, s: (i // z_count, i % z_count, 0, 0)
    far = lambda i, s: (0, i % z_count, 0, 0)
    down_specs = [(p, (1, 1, hd, width), near) for p in down[:2]] + [(p, (2, 1, hd, width), far) for p in down[2:]]
    down_block = (1, 1, 2 * hd, width)
    up_shape = (2, z_count, 2, h, hidden)
    up_block = (2, z_count, 2, h, block)
    up_index = lambda i, s: (0, 0, 0, 0, s[2 + i])
    return grid_call(
        tiled_feed_body,
        scalars,
        chips,
        [fixed(nt), fixed(ct), (bias, (1, block), column), *up_specs, *down_specs],
        [
            fixed_out((rows, width), f32),
            fixed_out((rows, width), f32),
            ((2, z_count, 2 * hd, width), bf16, down_block, near),
            ((2, z_count, 2 * hd, width), bf16, down_block, near),
            (up_shape, bf16, up_block, up_index),
            (up_shape, bf16, up_block, up_index),
            ((1, hidden), f32, (1, block), column),
        ],
        [pltpu.VMEM((width, block), bf16), pltpu.VMEM((block, width), bf16), pltpu.VMEM((width, block), f32)],
        12 * rows * width * hidden,
        8 * width * hidden + 12 * rows * width,
        2 * rows * hidden,
    )


def unbranch_body(
    scalars,
    g_ref,
    mix_ref,
    mixed_ref,
    first_ref,
    taps_ref,
    bias_ref,
    weight_ref,
    gmixed_ref,
    gfirst_ref,
    kept_ref,
    sent_ref,
    grad_ref,
):
    chips = gmixed_ref.shape[0]
    g = g_ref[...]
    gate_grad = lax.dot_general(g, weight_ref[...], (((1,), (1,)), ((), ())), preferred_element_type=f32)
    for tile in range(chips // 2):
        cols = slice(tile * LANES, (tile + 1) * LANES)
        first = short_conv(first_ref[:, cols].astype(f32), taps_ref[:, cols], bias_ref[:, cols])
        gfirst_ref[:, cols] = (gate_grad[:, cols] * mixed_ref[:, cols].astype(f32)).astype(bf16)
        pack_rows(gmixed_ref, 2 * tile, gate_grad[:, cols] * first)
    grad_ref[...] = lax.dot_general(mix_ref[...], g, (((0,), (0,)), ((), ())), preferred_element_type=f32)
    route_rows(grad_ref, kept_ref, sent_ref, scalars, chips, 1, False)


def unbranch(scalars, g, mix, mixed, projected, taps, bias, weight, chips):
    rows, width = g.shape
    half = weight.shape[0]
    grad_shape = (2, chips // 2, 1, half // (2 * chips), width)
    return grid_call(
        unbranch_body,
        scalars,
        1,
        [fixed(g), fixed(mix), fixed(mixed), *first_stream(projected, taps, bias), fixed(weight)],
        [
            fixed_out((chips, rows // 256, LANES, LANES), bf16),
            fixed_out((rows, half), bf16),
            fixed_out(grad_shape, bf16),
            fixed_out(grad_shape, bf16),
        ],
        [pltpu.VMEM((half, width), f32)],
        4 * rows * half * width,
        4 * rows * width + 6 * half * width,
    )


def ungate_body(scalars, gated_ref, second_ref, values_ref, t2_ref, t3_ref, b2_ref, b3_ref, gsecond_ref, gvalues_ref):
    grad = unpack_rows(gated_ref, 0)
    second = short_conv(second_ref[...].astype(f32), t2_ref[...], b2_ref[...])
    values = short_conv(values_ref[...].astype(f32), t3_ref[...], b3_ref[...])
    gsecond_ref[...] = (grad * values).astype(bf16)
    gvalues_ref[...] = (grad * second).astype(bf16)


def ungate(scalars, gated, projected, taps, bias):
    rows, columns = projected.shape
    half = columns // 3
    tiles = half // LANES
    p2, t2, b2 = stream_tiles(projected, taps, bias, 1, tiles)
    p3, t3, b3 = stream_tiles(projected, taps, bias, 2, tiles)
    out = ((rows - HALO, half), bf16, (rows - HALO, LANES), lambda i, s: (0, i))
    return grid_call(
        ungate_body,
        scalars,
        tiles,
        [(gated, (2, *gated.shape[1:]), lambda i, s: (i, 0, 0, 0)), p2, p3, t2, t3, b2, b3],
        [out, out],
        [],
        20 * rows * columns,
        3 * rows * columns,
    )


def stream_body(
    by_x, scalars, grad_ref, follow_ref, rows_ref, taps_ref, normed_ref, gproj_ref, kept_ref, sent_ref, sums_ref, work_ref
):
    count, columns = grad_ref.shape
    chips = 2 * kept_ref.shape[1]
    for at in range(0, columns, LANES):
        cols = slice(at, at + LANES)
        taps = taps_ref[:, cols]
        grad = grad_ref[:, cols].astype(f32)
        ext = jnp.concatenate([grad, follow_ref[:, cols].astype(f32)], axis=0)
        total = count + HALO
        one, two = pltpu.roll(ext, total - 1, 0)[:count], pltpu.roll(ext, total - 2, 0)[:count]
        low = (taps[0:1] * two + taps[1:2] * one + taps[2:3] * grad).astype(bf16)
        gproj_ref[:, cols] = low
        rows = rows_ref[:, cols].astype(f32)
        sums = [
            jnp.sum(grad * pltpu.roll(rows, 2, 0)[HALO:], axis=0, keepdims=True),
            jnp.sum(grad * pltpu.roll(rows, 1, 0)[HALO:], axis=0, keepdims=True),
            jnp.sum(grad * rows[HALO:], axis=0, keepdims=True),
            jnp.sum(grad, axis=0, keepdims=True),
            jnp.sum(low.astype(f32), axis=0, keepdims=True),
            jnp.zeros((3, LANES), f32),
        ]
        sums_ref[:, cols] = jnp.concatenate(sums, axis=0)
    work_ref[...] = lax.dot_general(
        normed_ref[...], gproj_ref[...], (((0,), (0,)), ((), ())), preferred_element_type=f32
    )
    route_rows(work_ref, kept_ref, sent_ref, scalars, chips, 2, by_x)


def stream_back(scalars, grad, follow, projected, taps, normed, stream, chips, by_x):
    count, columns = grad.shape
    width = normed.shape[1]
    rows = projected.shape[0]
    index = lambda i, s: (0, stream)
    shape = (2, chips // 2, 2, width // (4 * chips), columns)
    return grid_call(
        partial(stream_body, by_x),
        scalars,
        1,
        [
            fixed(grad),
            fixed(follow),
            (projected, (rows, columns), index),
            (taps, (3, columns), index),
            fixed(normed),
        ],
        [
            fixed_out((count, columns), bf16),
            fixed_out(shape, bf16),
            fixed_out(shape, bf16),
            fixed_out((8, columns), f32),
        ],
        [pltpu.VMEM((width, columns), f32)],
        2 * count * columns * width,
        4 * count * columns + 2 * count * width + 2 * width * columns,
    )


def filter_features(seq_index, tok_count, length):
    positions = (seq_index * tok_count + jnp.arange(tok_count, dtype=jnp.int32)).astype(f32)
    relative = positions / (length - 1)
    phases = positions * (2.0 * math.pi / length)
    band_count = (FEATURES - 1) // 2
    band_freq = jnp.linspace(0.0001, band_count - 1, band_count).astype(f32)
    angles = phases[:, None] * band_freq[None, :]
    return jnp.concatenate([relative[:, None], jnp.cos(angles), -jnp.sin(angles)], axis=1)


def tiled_device(
    tokens,
    cotangent,
    pre_gain,
    pre_offset,
    input_weight,
    input_bias,
    short_weight,
    short_bias,
    skip_weight,
    embed_weight,
    embed_bias,
    hidden_weight,
    hidden_bias,
    last_weight,
    last_bias,
    frequency,
    filter_weight,
    output_weight,
    output_bias,
    post_gain,
    post_offset,
    up_weight,
    up_bias,
    down_weight,
    down_bias,
):
    seq_count = lax.axis_size("seq")
    seq_index = lax.axis_index("seq")
    z, y, core, x = place()
    chips = seq_count // 2
    z_count = seq_count // 4
    tok_count, width = tokens.shape[1:]
    length = tok_count * seq_count
    channels = width // seq_count
    ff = up_weight.shape[1]
    hidden_own = ff // seq_count
    half = width // 2
    pairs = length // 256
    rows = 2 * tok_count
    chip_at = [(z ^ rel) * 2 + (y ^ yr) for yr in range(2) for rel in z_order(z_count)]
    scalars = jnp.stack([x, seq_index // 2, *chip_at]).astype(jnp.int32)

    def half_columns(value, groups, run):
        grid = value.reshape(value.shape[0], groups, chips, 2, run)
        return [grid[:, :, :, side].reshape(value.shape[0], groups * chips * run) for side in range(2)]

    def own_rows(value, groups, run):
        sides = half_columns(value, groups, run)
        keep = jnp.where(core == 0, sides[0], sides[1])
        got = swap_core(jnp.where(core == 0, sides[1], sides[0]))
        return jnp.where(core == x, keep, got)

    in_have = gather_z(own_rows(input_weight, 3, channels))
    mine = jnp.stack([tokens[0], cotangent[0]])
    pair = both(mine, swap_core(mine), core)
    tok = pair[:, 0].reshape(rows, width)
    cot = pair[:, 1].reshape(rows, width)
    shift = [(i, i + 2) for i in range(seq_count - 2)]
    tok_ext = jnp.concatenate([lax.ppermute(tok[rows - HALO :], "seq", shift), tok], axis=0)
    vectors = [
        pre_gain,
        pre_offset,
        input_bias,
        short_weight,
        short_bias,
        output_bias,
        post_gain,
        post_offset,
        up_bias,
        down_bias,
    ]
    small = to_rows(flatten(*vectors).astype(f32))
    small_all = gather_small(small).reshape(seq_count, -1)
    up_piece = own_rows(up_weight, 1, hidden_own)
    in_near = gather_near(in_have)
    up_have = gather_z(after(in_have, up_piece))
    in_pieces = gather_far(in_near)
    out_piece = pick(output_weight.reshape(2, -1, width), x, 0)
    out_have = gather_z(after(in_have, out_piece))
    out_pieces = gather_far(gather_near(after(in_pieces, out_have)))
    down_piece = pick(down_weight.reshape(2, -1, width), x, 0)
    down_have = gather_z(after(up_have, down_piece))
    up_near = gather_near(after(in_pieces, up_have))
    up_pieces = gather_far(up_near)
    down_near = gather_near(after(up_near, down_have))
    down_pieces = gather_far(after(up_pieces, down_near))

    columns, at = [], 0
    for vector in vectors:
        columns.append(small_all[:, at : at + vector.size])
        at += vector.size

    def halved(value, run):
        lead = value.shape[:-1]
        return pick(value.reshape(*lead, -1, 2, run), core, len(lead) + 1).reshape(*lead, -1)

    pre_gain_full, pre_offset_full = columns[0].reshape(-1), columns[1].reshape(-1)
    input_bias_own = halved(columns[2].reshape(3, width), channels).reshape(1, -1)
    short_full = columns[3].reshape(seq_count, 3, -1).transpose(1, 0, 2).reshape(3, 3, width)
    taps = halved(short_full, channels).reshape(3, -1)
    short_bias_own = halved(columns[4].reshape(3, width), channels).reshape(1, -1)
    output_bias_full = columns[5].reshape(-1)
    post_gain_full, post_offset_full = columns[6].reshape(-1), columns[7].reshape(-1)
    up_bias_own = halved(columns[8].reshape(-1), hidden_own)[None]
    down_bias_full = columns[9].reshape(-1)

    trunk = (embed_weight, embed_bias, hidden_weight, hidden_bias, last_weight, last_bias, frequency)
    features = filter_features(seq_index, tok_count, length)
    hidden_rows, trunk_pull = jax.vjp(partial(trunk_hidden, features=features), trunk)
    units = hidden_rows.shape[1]
    own_pairs = tok_count // 256
    packed = hidden_rows.reshape(own_pairs, 2, LANES, units).transpose(0, 2, 1, 3)
    packed = packed.reshape(own_pairs, LANES, 2 * units)
    filter_hidden = lax.all_gather(packed, "seq", axis=0, tiled=True)
    filter_own = filter_weight.astype(f32)
    zero = jnp.zeros_like(filter_own)
    filter_pair = jnp.concatenate(
        [jnp.concatenate([filter_own, zero], axis=1), jnp.concatenate([zero, filter_own], axis=1)], axis=0
    )
    deltas = jnp.linspace(math.log(0.01) / 1.5, math.log(0.01) / 0.3, width).astype(f32)
    delta_own = jnp.abs(lax.dynamic_slice_in_dim(deltas, seq_index * channels, channels))
    delta_pair = jnp.concatenate([delta_own, delta_own])[None]
    skip_own = skip_weight.astype(f32)
    skip_pair = jnp.concatenate([skip_own, skip_own])[None]
    tables = tuple(jnp.asarray(t) for t in conv_tables(pairs))
    kernel_spec = conv_filter(filter_hidden, filter_pair, delta_pair, tables)

    normed_one, unit_one, inverse_one = norm_forward(tok_ext.astype(f32), pre_gain_full, pre_offset_full)
    normed_ext = normed_one.astype(bf16)
    normed_low = normed_ext[HALO:]
    projected, in_half = project(scalars, normed_ext, input_bias_own, in_pieces)
    gated_ch = chip_exchange(gate(scalars, projected, taps, short_bias_own, chips)).reshape(pairs, LANES, LANES)
    mixed_ch, gated_spec = conv_forward(gated_ch, kernel_spec, skip_pair, tables)
    chip_shape = (chips, rows // 256, LANES, LANES)
    mixed_back = chip_exchange(mixed_ch.reshape(chip_shape))
    mixed_tok, mix_low, out_half, branch_part = branch_out(
        scalars, mixed_back, projected, taps, short_bias_own, out_pieces
    )
    hidden = tok.astype(f32) + (branch_part + swap_core(branch_part) + output_bias_full)

    normed_two, unit_two, inverse_two = norm_forward(hidden, post_gain_full, post_offset_full)
    down_part, back_part, gdown_kept, gdown_sent, gup_kept, gup_sent, up_bias_grad = tiled_feed(
        scalars, normed_two.astype(bf16), cot, up_bias_own, up_pieces, down_pieces
    )

    def own_tokens(value):
        return lax.dynamic_slice_in_dim(value, core * tok_count, tok_count, 0)

    def other_tokens(value):
        return lax.dynamic_slice_in_dim(value, (1 - core) * tok_count, tok_count, 0)

    normed_two_grad = back_part + swap_core(back_part)
    cot_f = cot.astype(f32)
    hidden_grad = cot_f + norm_backward(normed_two_grad, unit_two, inverse_two, post_gain_full)
    branch_low = hidden_grad.astype(bf16)
    gmixed, gfirst, gout_kept, gout_sent = unbranch(
        scalars, branch_low, mix_low, mixed_tok, projected, taps, short_bias_own, out_half, chips
    )
    mixed_grad_ch = chip_exchange(gmixed).reshape(pairs, LANES, LANES)
    gated_back, hidden_back, filter_square, skip_line = conv_backward(
        mixed_grad_ch, gated_ch, gated_spec, kernel_spec, skip_pair, filter_hidden, filter_pair, delta_pair, tables
    )
    gated_grad = chip_exchange(gated_back.reshape(chip_shape))

    down_sum = reduce_rows(gdown_kept, gdown_sent, swap_x, swap_y)
    up_sum = reduce_rows(gup_kept, gup_sent, swap_y, swap_x)
    result = own_tokens(hidden) + (
        own_tokens(down_part) + swap_core(other_tokens(down_part)) + down_bias_full
    )
    down_bias_grad = jnp.sum(cot_f, axis=0)
    post_gain_grad = jnp.sum(normed_two_grad * unit_two, axis=0)
    post_offset_grad = jnp.sum(normed_two_grad, axis=0)
    output_bias_grad = jnp.sum(branch_low.astype(f32), axis=0)

    back_shift = [(i + 2, i) for i in range(seq_count - 2)]
    gfirst_next = lax.ppermute(gfirst[:HALO], "seq", back_shift)
    first_proj, first_kept, first_sent, first_sums = stream_back(
        scalars, gfirst, gfirst_next, projected, taps, normed_low, 0, chips, True
    )
    first_sum = reduce_rows(first_kept, first_sent, swap_x, swap_y)
    out_sum = reduce_rows(gout_kept, gout_sent, swap_y, swap_x)[0]
    gsecond, gvalues = ungate(scalars, gated_grad, projected, taps, short_bias_own)
    follow = lax.ppermute(jnp.stack([gsecond[:HALO], gvalues[:HALO]]), "seq", back_shift)
    second_proj, second_kept, second_sent, second_sums = stream_back(
        scalars, gsecond, follow[0], projected, taps, normed_low, 1, chips, True
    )
    values_proj, values_kept, values_sent, values_sums = stream_back(
        scalars, gvalues, follow[1], projected, taps, normed_low, 2, chips, False
    )
    second_sum = reduce_rows(second_kept, second_sent, swap_x, swap_y)
    values_sum = reduce_rows(values_kept, values_sent, swap_y, swap_x)
    normed_one_part = sum(
        contract(part, in_half[:, i * half : (i + 1) * half], 1, 1)
        for i, part in enumerate((first_proj, second_proj, values_proj))
    )
    normed_one_grad = own_tokens(normed_one_part) + swap_core(other_tokens(normed_one_part))
    unit_own = own_tokens(unit_one[HALO:])
    pre_gain_grad = jnp.sum(normed_one_grad * unit_own, axis=0)
    pre_offset_grad = jnp.sum(normed_one_grad, axis=0)
    tokens_grad = own_tokens(hidden_grad) + norm_backward(
        normed_one_grad, unit_own, own_tokens(inverse_one[HALO:]), pre_gain_full
    )

    hidden_got = lax.all_to_all(
        hidden_back.reshape(seq_count, own_pairs * LANES, 2 * units), "seq", split_axis=0, concat_axis=0, tiled=True
    )
    hidden_sum = jnp.sum(hidden_got.astype(f32), axis=0)
    hidden_sum = hidden_sum.reshape(own_pairs, LANES, 2, units).transpose(0, 2, 1, 3).reshape(tok_count, units)
    (trunk_grad,) = trunk_pull(hidden_sum)
    filter_grad = filter_square[:units, :channels] + filter_square[units:, channels:]
    skip_grad = skip_line[:, :channels] + skip_line[:, channels:]
    own_grad = jnp.concatenate([filter_grad, skip_grad], axis=0)
    own_grad = own_grad + swap_x(own_grad)
    own_grad = pick(own_grad.reshape(-1, 2, channels // 2), x, 1)

    def whole_columns(value, groups, run):
        got = swap_core(pick(value, 1 - core, 0))
        mine_part = pick(value, core, 0)
        n = mine_part.shape[0]
        grid = both(mine_part, got, core).reshape(2, n, groups, chips, run)
        return grid.transpose(1, 2, 3, 0, 4).reshape(n, -1)

    in_rows = whole_columns(jnp.concatenate([first_sum, second_sum, values_sum], axis=2), 3, channels)
    up_rows_sum = whole_columns(up_sum, 1, hidden_own)

    all_sums = jnp.stack([first_sums, second_sums, values_sums])
    chip_wide = [post_gain_grad, post_offset_grad, down_bias_grad, output_bias_grad]
    own_wide = [pre_gain_grad, pre_offset_grad, *trunk_grad]
    half_wide = [up_bias_grad.reshape(-1), all_sums[:, :5]]
    chip_flat, own_flat, half_flat = (to_rows(flatten(*group)) for group in (chip_wide, own_wide, half_wide))
    summed = sum_chips(jnp.concatenate([chip_flat, own_flat, half_flat], axis=0))
    n_chip, n_own = chip_flat.shape[0], own_flat.shape[0]
    got = swap_core(summed[n_chip:])
    own_sum = (summed[n_chip:] + got)[:n_own].reshape(-1)
    half_sum = both(summed[n_chip + n_own :], got[n_own:], core).reshape(2, -1)
    chip_sums = unflatten(summed[:n_chip].reshape(-1), [v.shape for v in chip_wide])
    own_sums = unflatten(own_sum, [v.shape for v in own_wide])
    half_sums = [unflatten(half_sum[side], [v.shape for v in half_wide]) for side in range(2)]
    block_index = seq_index * 2 + x

    def own_block(value, axis=0):
        size = value.shape[axis] // (2 * seq_count)
        return lax.dynamic_slice_in_dim(value, block_index * size, size, axis)

    up_bias_sum = jnp.stack([s[0].reshape(chips, hidden_own) for s in half_sums], axis=1).reshape(-1)
    streams = jnp.stack([s[1].reshape(3, 5, chips, channels) for s in half_sums], axis=3)
    streams = streams.transpose(1, 0, 2, 3, 4).reshape(5, 3 * width)
    return (
        result.astype(bf16)[None],
        tokens_grad.astype(bf16)[None],
        own_block(own_sums[0]),
        own_block(own_sums[1]),
        in_rows,
        own_block(streams[4]),
        own_block(streams[:3], 1),
        own_block(streams[3]),
        own_grad[units],
        *own_sums[2:],
        own_grad[:units],
        out_sum,
        own_block(chip_sums[3]),
        own_block(chip_sums[0]),
        own_block(chip_sums[1]),
        up_rows_sum,
        own_block(up_bias_sum),
        down_sum,
        own_block(chip_sums[2]),
    )


def per_device(tokens, *others):
    channels = tokens.shape[2] // lax.axis_size("seq")
    tiled = 2 * channels == LANES and tokens.shape[1] % 256 == 0
    return (tiled_device if tiled else plain_device)(tokens, *others)


def solution(mesh):
    placed = (
        P("dp", "seq", None),
        P("dp", "seq", None),
        P("seq"),
        P("seq"),
        P("seq", None),
        P("seq"),
        P(None, "seq"),
        P("seq"),
        P("seq"),
        P(),
        P(),
        P(),
        P(),
        P(),
        P(),
        P(),
        P(None, "seq"),
        P("seq", None),
        P("seq"),
        P("seq"),
        P("seq"),
        P("seq", None),
        P("seq"),
        P("seq", None),
        P("seq"),
    )
    split = P(("seq", "dp"))
    split_rows = P(("seq", "dp"), None)
    split_columns = P(None, ("seq", "dp"))
    return jax.shard_map(
        per_device,
        mesh=mesh,
        in_specs=placed,
        out_specs=(
            P("dp", "seq", None),
            P("dp", "seq", None),
            split,
            split,
            split_rows,
            split,
            split_columns,
            split,
            split,
            P(),
            P(),
            P(),
            P(),
            P(),
            P(),
            P(),
            split_columns,
            split_rows,
            split,
            split,
            split,
            split_rows,
            split,
            split_rows,
            split,
        ),
        check_vma=False,
    )
```

```python
from functools import partial
import math

import jax
import jax.numpy as jnp
import numpy as np
from jax import lax
from jax.experimental import pallas as pl
from jax.experimental.pallas import tpu as pltpu
from jax.sharding import PartitionSpec as P

FEATURES = 33
LANES = 128
f32 = jnp.float32
bf16 = jnp.bfloat16
highest = lax.Precision.HIGHEST


def swap_seq(value, mask):
    count = lax.axis_size("seq")
    return lax.ppermute(value, "seq", [(i, i ^ mask) for i in range(count)])


def swap_core(value):
    return swap_seq(value, 1)


def swap_y(value):
    return swap_seq(value, 2)


def swap_z(value, mask):
    return swap_seq(value, 4 * mask)


def swap_x(value):
    count = lax.axis_size("dp")
    return lax.ppermute(value, "dp", [(i, i ^ 1) for i in range(count)])


def z_masks(count):
    if count == 4:
        return [3, 1]
    masks, step = [], count // 2
    while step:
        masks.append(step)
        step //= 2
    return masks


def z_order(count):
    order = [0]
    for mask in z_masks(count):
        order = order + [entry ^ mask for entry in order]
    return order


def chip_groups():
    count = lax.axis_size("seq")
    return [list(range(core, count, 2)) for core in range(2)]


def chip_exchange(value):
    return lax.all_to_all(
        value, "seq", split_axis=0, concat_axis=0, tiled=True, axis_index_groups=chip_groups()
    )


def pick(value, index, axis):
    return lax.dynamic_index_in_dim(value, index, axis, keepdims=False)


def both(mine, other, second):
    return jnp.where(second == 0, jnp.stack([mine, other]), jnp.stack([other, mine]))


def place():
    seq = lax.axis_index("seq")
    return seq // 4, (seq // 2) % 2, seq % 2, lax.axis_index("dp")


def by_index(have, order, own):
    bit = 1
    value = jnp.stack([have[order.index(entry)] for entry in range(len(order))])
    while bit < len(order):
        grid = value.reshape(-1, 2, bit, *value.shape[1:])
        turned = jnp.stack([grid[:, 1], grid[:, 0]], axis=1)
        value = jnp.where((own & bit) == 0, grid, turned).reshape(value.shape)
        bit *= 2
    return value


def gather_pieces(piece):
    z, y, _, x = place()
    z_count = lax.axis_size("seq") // 4
    have = piece[None]
    for mask in z_masks(z_count):
        have = jnp.concatenate([have, swap_z(have, mask)], axis=0)
    half = piece.shape[0] // 2
    first, second = have[:, :half], have[:, half:]
    first_y, second_x = swap_y(first), swap_x(second)
    first = jnp.stack([first, first_y])
    second = jnp.stack([second, second_x])
    first_x, second_y = swap_x(first), swap_y(second)
    first = jnp.stack([first, first_x], axis=1)
    second = jnp.stack([second, second_y])
    rel = jnp.concatenate([first, second], axis=3)
    order = z_order(z_count)
    rows = []
    for za in range(z_count):
        rel_z = z ^ za
        slot = sum(jnp.where(rel_z == entry, at, 0) for at, entry in enumerate(order))
        slab = pick(rel, slot, 2)
        slab = jnp.where(y == 0, slab, jnp.stack([slab[1], slab[0]]))
        slab = jnp.where(x == 0, slab, jnp.stack([slab[:, 1], slab[:, 0]], axis=1))
        rows.append(slab)
    return jnp.stack(rows)


def reduce_z(parts):
    z = place()[0]
    z_count = parts.shape[0]
    have = jnp.stack([pick(parts, z ^ rel, 0) for rel in z_order(z_count)])
    for mask in reversed(z_masks(z_count)):
        half = have.shape[0] // 2
        got = swap_z(have[half:].astype(bf16), mask)
        have = have[:half] + got.astype(f32)
    return have[0]


def reduce_pair(first, second):
    _, y, _, x = place()
    first_got = swap_x(pick(first, 1 - x, 2))
    second_got = swap_y(pick(second, 1 - y, 1))
    first = pick(first, x, 2).astype(f32) + first_got.astype(f32)
    second = pick(second, y, 1).astype(f32) + second_got.astype(f32)
    first_got = swap_y(pick(first, 1 - y, 1).astype(bf16))
    second_got = swap_x(pick(second, 1 - x, 1).astype(bf16))
    first = pick(first, y, 1) + first_got.astype(f32)
    second = pick(second, x, 1) + second_got.astype(f32)
    return reduce_z(first), reduce_z(second)


def sum_chips(value):
    for mask in z_masks(lax.axis_size("seq") // 4):
        value = value + swap_z(value, mask)
    value = value + swap_y(value)
    return value + swap_x(value)


def gather_small(value):
    seq = lax.axis_index("seq")
    count = lax.axis_size("seq")
    have = value[None]
    for mask in [2, 1] + [4 * m for m in z_masks(count // 4)]:
        have = jnp.concatenate([have, swap_seq(have, mask)], axis=0)
    order = [0]
    for mask in [2, 1] + [4 * m for m in z_masks(count // 4)]:
        order = order + [entry ^ mask for entry in order]
    return by_index(have, order, seq)


def twiddle(k, n):
    angle = -2.0 * math.pi * (k % n) / n
    return math.cos(angle), math.sin(angle)


def c_add(p, q):
    return (p[0] + q[0], q[1] if p[1] is None else (p[1] if q[1] is None else p[1] + q[1]))


def c_sub(p, q):
    if q[1] is None:
        return (p[0] - q[0], p[1])
    return (p[0] - q[0], -q[1] if p[1] is None else p[1] - q[1])


def c_conj(p):
    return (p[0], None if p[1] is None else -p[1])


def c_turn(p, k, n):
    k = k % n
    if k == 0:
        return p
    re, im = p
    if 4 * k == n:
        return (im if im is not None else jnp.zeros_like(re), -re)
    if 2 * k == n:
        return (-re, None if im is None else -im)
    if 4 * k == 3 * n:
        return (-im if im is not None else jnp.zeros_like(re), re)
    c, s = twiddle(k, n)
    if im is None:
        return (re * c, re * s)
    return (re * c - im * s, re * s + im * c)


def real_dft(xs):
    n = len(xs)
    if n == 1:
        return [(xs[0], None)]
    if n == 2:
        if xs[1] is None:
            return [(xs[0], None), (xs[0], None)]
        return [(xs[0] + xs[1], None), (xs[0] - xs[1], None)]
    even, odd = real_dft(xs[0::2]), real_dft(xs[1::2])
    out = [None] * (n // 2 + 1)
    for k in range(n // 4 + 1):
        turned = c_turn(odd[k], k, n)
        out[k] = c_add(even[k], turned)
        if n // 2 - k != k:
            out[n // 2 - k] = c_conj(c_sub(even[k], turned))
    return out


def real_inverse(spec):
    def whole(v):
        n = 2 * (len(v) - 1)
        if n == 2:
            return [v[0][0] + v[1][0], None]
        even, odd = [], []
        for k in range(n // 4 + 1):
            mirror = c_conj(v[n // 2 - k])
            e, o = c_add(v[k], mirror), c_turn(c_sub(v[k], mirror), -k, n)
            if k == 0 or 4 * k == n:
                e, o = (e[0], None), (o[0], None)
            even.append(e)
            odd.append(o)
        even, odd = whole(even), whole(odd)
        return [entry for pair in zip(even, odd) for entry in pair]

    values = whole(spec)
    return values[: len(values) // 2]


def split_terms(value):
    high = value.astype(bf16)
    return high, (value - high.astype(f32)).astype(bf16)


def conv_tables(pairs):
    rows = 4 * pairs
    total = rows * LANES
    slots = np.arange(pairs + 1)
    lanes = np.arange(LANES)
    upper = lanes >= LANES // 2
    angle = -2.0 * np.pi * slots[:, None] / rows * upper[None, :]
    lane_turn = np.stack([np.cos(angle), np.sin(angle)], axis=1).astype(np.float32)
    freq = slots[:, None] + np.where(upper, rows // 2, 0)[None, :]
    angle = -2.0 * np.pi * ((freq[:, None, :] * lanes[None, :, None]) % total) / total
    turn = np.stack([np.cos(angle), np.sin(angle)], axis=1).astype(np.float32)
    angle = 2.0 * np.pi * ((lanes[:, None] * lanes[None, :]) % LANES) / LANES
    c, s = np.cos(angle), np.sin(angle)

    def terms(table):
        table = table.astype(np.float32)
        high = table.astype(bf16)
        low = (table - high.astype(np.float32)).astype(bf16)
        return np.concatenate([high, low], axis=1)

    ahead = terms(np.block([[c, s], [-s, c]]))
    back = terms(np.block([[c, -s], [s, c]]) / total)
    return lane_turn, turn, ahead, back


CHUNK = 16


def put(terms_ref, start, slot, re, im):
    cols = pl.ds(slot * LANES, LANES)
    terms_ref[pl.ds(start, CHUNK), cols] = re
    terms_ref[pl.ds(LANES + start, CHUNK), cols] = im


COLUMNS = 4 * LANES


def table_product(table_ref, terms_ref, out_ref):
    width = terms_ref.shape[1]
    high_table, low_table = table_ref[:, :256], table_ref[:, 256:]
    for at in range(0, width, COLUMNS):
        cols = pl.ds(at, min(COLUMNS, width - at))
        high, low = split_terms(terms_ref[:, cols])
        out_ref[:, cols] = (
            jnp.dot(high_table, low, preferred_element_type=f32)
            + jnp.dot(low_table, high, preferred_element_type=f32)
            + jnp.dot(high_table, high, preferred_element_type=f32)
        )


def lane_sign(shape):
    return jnp.where(lax.broadcasted_iota(jnp.int32, shape, 1) < LANES // 2, 1.0, -1.0).astype(f32)


def transform(x_ref, pairs, lane_ref, turn_ref, ahead_ref, terms_ref, spec_ref):
    sign = lane_sign((CHUNK, LANES))

    def chunk(step, carry):
        start = pl.multiple_of(step * CHUNK, CHUNK)
        xs = [x_ref[j, pl.ds(start, CHUNK), :].astype(f32) for j in range(pairs)]
        spec = real_dft(xs + [None] * pairs)
        for k in range(pairs + 1):
            re, im = spec[k]
            c, s = lane_ref[k, 0:1, :], lane_ref[k, 1:2, :]
            if im is None:
                re, im = re * c, re * s
            else:
                re, im = re * c - im * s, re * s + im * c
            re = pltpu.roll(re, LANES // 2, 1) + sign * re
            im = pltpu.roll(im, LANES // 2, 1) + sign * im
            c, s = turn_ref[k, 0, pl.ds(start, CHUNK), :], turn_ref[k, 1, pl.ds(start, CHUNK), :]
            put(terms_ref, start, k, re * c - im * s, re * s + im * c)
        return carry

    lax.fori_loop(0, LANES // CHUNK, chunk, 0)
    table_product(ahead_ref, terms_ref, spec_ref)


def put_product(terms_ref, pairs, one_ref, other_ref, conjugate):
    def chunk(step, carry):
        start = pl.multiple_of(step * CHUNK, CHUNK)
        for k in range(pairs + 1):
            cols = pl.ds(k * LANES, LANES)
            a, b = one_ref[pl.ds(start, CHUNK), cols], one_ref[pl.ds(LANES + start, CHUNK), cols]
            c, d = other_ref[pl.ds(start, CHUNK), cols], other_ref[pl.ds(LANES + start, CHUNK), cols]
            if conjugate:
                put(terms_ref, start, k, a * c + b * d, b * c - a * d)
            else:
                put(terms_ref, start, k, a * c - b * d, a * d + b * c)
        return carry

    lax.fori_loop(0, LANES // CHUNK, chunk, 0)


def inverse(pairs, lane_ref, turn_ref, back_ref, terms_ref, spec_ref, finish):
    table_product(back_ref, terms_ref, spec_ref)
    sign = lane_sign((CHUNK, LANES))

    def chunk(step, carry):
        start = pl.multiple_of(step * CHUNK, CHUNK)
        spec = []
        for k in range(pairs + 1):
            cols = pl.ds(k * LANES, LANES)
            re, im = spec_ref[pl.ds(start, CHUNK), cols], spec_ref[pl.ds(LANES + start, CHUNK), cols]
            c, s = turn_ref[k, 0, pl.ds(start, CHUNK), :], turn_ref[k, 1, pl.ds(start, CHUNK), :]
            re, im = re * c + im * s, im * c - re * s
            re = pltpu.roll(re, LANES // 2, 1) + sign * re
            im = pltpu.roll(im, LANES // 2, 1) + sign * im
            c, s = lane_ref[k, 0:1, :], lane_ref[k, 1:2, :]
            re, im = re * c + im * s, im * c - re * s
            spec.append((re, None if k in (0, pairs) else im))
        for j, values in enumerate(real_inverse(spec)):
            finish(j, start, values)
        return carry

    lax.fori_loop(0, LANES // CHUNK, chunk, 0)


def window_of(j, start, delta, length):
    lane = lax.broadcasted_iota(jnp.int32, (CHUNK, LANES), 1)
    row = lax.broadcasted_iota(jnp.int32, (CHUNK, LANES), 0)
    position = (2 * j + lane // (LANES // 2)) * LANES + start + row
    return jnp.exp(-(position.astype(f32) / (length - 1)) * delta) + 0.05


def filter_body(pairs, h_ref, w_ref, delta_ref, lane_ref, turn_ref, ahead_ref, spec_ref, low_ref, terms_ref):
    delta = delta_ref[...]
    for j in range(pairs):
        rows = jnp.dot(h_ref[j], w_ref[...], precision=highest, preferred_element_type=f32)
        window = jnp.concatenate(
            [window_of(j, start, delta, 2 * pairs * LANES) for start in range(0, LANES, CHUNK)], axis=0
        )
        low_ref[j] = (rows * window).astype(bf16).astype(f32)
    transform(low_ref, pairs, lane_ref, turn_ref, ahead_ref, terms_ref, spec_ref)


def forward_body(
    pairs, x_ref, kernel_ref, skip_ref, lane_ref, turn_ref, ahead_ref, back_ref, out_ref, spec_ref, terms_ref, work_ref
):
    transform(x_ref, pairs, lane_ref, turn_ref, ahead_ref, terms_ref, spec_ref)
    put_product(terms_ref, pairs, spec_ref, kernel_ref, False)
    skip = skip_ref[...]

    def finish(j, start, values):
        rows = pl.ds(start, CHUNK)
        out_ref[j, rows, :] = (values + x_ref[j, rows, :].astype(f32) * skip).astype(bf16)

    inverse(pairs, lane_ref, turn_ref, back_ref, terms_ref, work_ref, finish)


def backward_body(
    pairs, g_ref, kernel_ref, skip_ref, lane_ref, turn_ref, ahead_ref, back_ref, gx_ref, spec_ref, terms_ref, work_ref
):
    transform(g_ref, pairs, lane_ref, turn_ref, ahead_ref, terms_ref, spec_ref)
    put_product(terms_ref, pairs, spec_ref, kernel_ref, True)
    skip = skip_ref[...]

    chips, rows = gx_ref.shape[:2]
    own = (rows - CHUNK) // LANES

    def finish(j, start, values):
        value = (values + g_ref[j, pl.ds(start, CHUNK), :].astype(f32) * skip).astype(bf16)
        gx_ref[j // own, pl.ds(pl.multiple_of(j % own * LANES + start, CHUNK), CHUNK), :] = value

    inverse(pairs, lane_ref, turn_ref, back_ref, terms_ref, work_ref, finish)
    for chip in range(chips - 1):
        gx_ref[chip, own * LANES :, :] = gx_ref[chip + 1, :CHUNK, :]
    gx_ref[chips - 1, own * LANES :, :] = jnp.zeros((CHUNK, LANES), bf16)


def filter_back_body(
    pairs,
    g_ref,
    g_spec_ref,
    x_ref,
    x_spec_ref,
    h_ref,
    w_ref,
    delta_ref,
    lane_ref,
    turn_ref,
    back_ref,
    gh_ref,
    gw_ref,
    gskip_ref,
    terms_ref,
    work_ref,
    pre_ref,
):
    put_product(terms_ref, pairs, g_spec_ref, x_spec_ref, True)
    delta = delta_ref[...]

    def finish(j, start, values):
        window = window_of(j, start, delta, 2 * pairs * LANES)
        pre_ref[j, pl.ds(start, CHUNK), :] = values.astype(bf16).astype(f32) * window

    inverse(pairs, lane_ref, turn_ref, back_ref, terms_ref, work_ref, finish)
    gw_ref[...] = jnp.zeros_like(gw_ref)
    gskip_ref[...] = jnp.zeros_like(gskip_ref)
    for j in range(pairs):
        pre = pre_ref[j]
        gh = lax.dot_general(
            pre, w_ref[...], (((1,), (1,)), ((), ())), precision=highest, preferred_element_type=f32
        )
        gh_ref[j] = gh.astype(bf16)
        gw_ref[...] += lax.dot_general(
            h_ref[j], pre, (((0,), (0,)), ((), ())), precision=highest, preferred_element_type=f32
        )
        gskip_ref[...] += jnp.sum(g_ref[j].astype(f32) * x_ref[j].astype(f32), axis=0, keepdims=True)


SHARE = 100000
FILLER = 40 * 10**9
VMEM_BYTES = 50 * 1024 * 1024


def whole_call(body, outs, scratch, flops, moved, *operands, share=SHARE):
    return pl.pallas_call(
        body,
        out_shape=outs,
        scratch_shapes=scratch,
        compiler_params=pltpu.CompilerParams(vmem_limit_bytes=VMEM_BYTES),
        cost_estimate=pl.CostEstimate(flops=flops // share, bytes_accessed=moved // share, transcendentals=0),
    )(*operands)


def spec_shape(pairs):
    return (256, (pairs + 1) * LANES)


def conv_filter(hidden, weight, delta, tables):
    pairs = hidden.shape[0]
    lane_turn, turn, ahead, _ = tables
    return whole_call(
        partial(filter_body, pairs),
        jax.ShapeDtypeStruct(spec_shape(pairs), f32),
        [pltpu.VMEM((pairs, LANES, LANES), f32), pltpu.VMEM(spec_shape(pairs), f32)],
        FILLER,
        8 * 10**6,
        hidden,
        weight,
        delta,
        lane_turn,
        turn,
        ahead,
        share=1,
    )


def conv_forward(x, kernel_spec, skip, tables):
    pairs = x.shape[0]
    return whole_call(
        partial(forward_body, pairs),
        (jax.ShapeDtypeStruct(x.shape, bf16), jax.ShapeDtypeStruct(spec_shape(pairs), f32)),
        [pltpu.VMEM(spec_shape(pairs), f32), pltpu.VMEM(spec_shape(pairs), f32)],
        2 * 10**9,
        10 * 10**6,
        x,
        kernel_spec,
        skip,
        *tables,
    )


def conv_backward(g, kernel_spec, skip, tables, chips):
    pairs = g.shape[0]
    out_rows = pairs // chips * LANES + CHUNK
    return whole_call(
        partial(backward_body, pairs),
        (jax.ShapeDtypeStruct((chips, out_rows, LANES), bf16), jax.ShapeDtypeStruct(spec_shape(pairs), f32)),
        [pltpu.VMEM(spec_shape(pairs), f32), pltpu.VMEM(spec_shape(pairs), f32)],
        2 * 10**9,
        10 * 10**6,
        g,
        kernel_spec,
        skip,
        *tables,
    )


def filter_backward(g, g_spec, x, x_spec, hidden, weight, delta, tables):
    pairs = x.shape[0]
    lane_turn, turn, _, back = tables
    return whole_call(
        partial(filter_back_body, pairs),
        (
            jax.ShapeDtypeStruct(x.shape, bf16),
            jax.ShapeDtypeStruct((LANES, LANES), f32),
            jax.ShapeDtypeStruct((1, LANES), f32),
        ),
        [
            pltpu.VMEM(spec_shape(pairs), f32),
            pltpu.VMEM(spec_shape(pairs), f32),
            pltpu.VMEM(x.shape, f32),
        ],
        FILLER,
        10 * 10**6,
        g,
        g_spec,
        x,
        x_spec,
        hidden,
        weight,
        delta,
        lane_turn,
        turn,
        back,
        share=1,
    )


def plain_spectrum(x, length):
    pairs, _, lanes = x.shape
    flat = x.astype(f32).reshape(pairs, LANES, 2, lanes // 2).transpose(3, 0, 2, 1)
    tables = spectral_tables(length // 64, LANES)
    return forward_transform(flat.reshape(lanes // 2, length // LANES, LANES), tables)


def plain_inverse(re, im, length):
    tables = spectral_tables(length // 64, LANES)
    back = inverse_transform(re, im, tables, length // LANES)
    channels = back.shape[0]
    back = back.reshape(channels, length // 256, 2, LANES).transpose(1, 3, 2, 0)
    return back.reshape(length // 256, LANES, 2 * channels)


def spectral_tables(rows_total, col_count):
    total_size = rows_total * col_count
    row_index = jnp.arange(rows_total, dtype=jnp.int32)
    col_index = jnp.arange(col_count, dtype=jnp.int32)
    row_angle = (row_index[:, None] * row_index[None, :] % rows_total).astype(f32) * (
        2.0 * math.pi / rows_total
    )
    col_angle = (col_index[:, None] * col_index[None, :] % col_count).astype(f32) * (
        2.0 * math.pi / col_count
    )
    twist_angle = (row_index[:, None] * col_index[None, :]).astype(f32) * (2.0 * math.pi / total_size)
    return (
        jnp.cos(row_angle),
        -jnp.sin(row_angle),
        jnp.cos(twist_angle),
        -jnp.sin(twist_angle),
        jnp.cos(col_angle),
        -jnp.sin(col_angle),
        total_size,
    )


def forward_transform(signal, tables):
    row_cos, row_sin, twist_cos, twist_sin, col_cos, col_sin, _ = tables
    half_rows = signal.shape[1]
    product = partial(jnp.einsum, precision=highest)
    first_re = product("ka,cab->ckb", row_cos[:, :half_rows], signal)
    first_im = product("ka,cab->ckb", row_sin[:, :half_rows], signal)
    turned_re = first_re * twist_cos - first_im * twist_sin
    turned_im = first_re * twist_sin + first_im * twist_cos
    out_re = product("ckb,bm->ckm", turned_re, col_cos) - product("ckb,bm->ckm", turned_im, col_sin)
    out_im = product("ckb,bm->ckm", turned_re, col_sin) + product("ckb,bm->ckm", turned_im, col_cos)
    return (out_re, out_im)


def inverse_transform(spec_re, spec_im, tables, half_rows):
    row_cos, row_sin, twist_cos, twist_sin, col_cos, col_sin, total_size = tables
    product = partial(jnp.einsum, precision=highest)
    back_re = product("ckm,mb->ckb", spec_re, col_cos) + product("ckm,mb->ckb", spec_im, col_sin)
    back_im = product("ckm,mb->ckb", spec_im, col_cos) - product("ckm,mb->ckb", spec_re, col_sin)
    untwist_re = back_re * twist_cos + back_im * twist_sin
    untwist_im = back_im * twist_cos - back_re * twist_sin
    real_part = product("ak,ckb->cab", row_cos[:half_rows], untwist_re) + product(
        "ak,ckb->cab", row_sin[:half_rows], untwist_im
    )
    return real_part / total_size


def plain_window(shape, delta, length):
    pairs, _, lanes = shape
    position = jnp.arange(length, dtype=jnp.int32).reshape(pairs, 2, LANES, 1).astype(f32)
    window = jnp.exp(-(position / (length - 1)) * delta[0, : lanes // 2]) + 0.05
    return window.transpose(0, 2, 1, 3).reshape(shape)


def plain_filter(hidden, weight, delta):
    pairs = hidden.shape[0]
    length = 256 * pairs
    rows = jnp.einsum("jbh,hc->jbc", hidden, weight, precision=highest)
    rows = (rows * plain_window(rows.shape, delta, length)).astype(bf16)
    return plain_spectrum(rows, length)


def plain_forward(x, kernel_spec, skip):
    length = 256 * x.shape[0]
    re, im = plain_spectrum(x, length)
    kre, kim = kernel_spec
    out = plain_inverse(re * kre - im * kim, re * kim + im * kre, length)
    return (out + x.astype(f32) * skip).astype(bf16), (re, im)


def plain_backward(g, x, x_spec, kernel_spec, skip, hidden, weight, delta):
    length = 256 * x.shape[0]
    re, im = plain_spectrum(g, length)
    kre, kim = kernel_spec
    xre, xim = x_spec
    gx = plain_inverse(re * kre + im * kim, im * kre - re * kim, length) + g.astype(f32) * skip
    pre = plain_inverse(re * xre + im * xim, im * xre - re * xim, length).astype(bf16).astype(f32)
    pre = pre * plain_window(pre.shape, delta, length)
    gh = jnp.einsum("jbc,hc->jbh", pre, weight, precision=highest)
    gw = jnp.einsum("jbh,jbc->hc", hidden, pre, precision=highest)
    gskip = jnp.sum(g.astype(f32) * x.astype(f32), axis=(0, 1))[None]
    return gx.astype(bf16), gh.astype(bf16), gw, gskip


def feed_body(nt_ref, ct_ref, up_ref, bias_ref, down_ref, y_ref, gx_ref, gdown_ref, gup_ref, gbias_ref):
    @pl.when(pl.program_id(0) == 0)
    def _():
        y_ref[...] = jnp.zeros_like(y_ref)
        gx_ref[...] = jnp.zeros_like(gx_ref)

    nt, ct, up, down = nt_ref[...], ct_ref[...], up_ref[...], down_ref[...]
    before = jnp.dot(nt, up, preferred_element_type=f32) + bias_ref[...]
    cdf = 0.5 * (1.0 + lax.erf(before * math.sqrt(0.5)))
    active = (before * cdf).astype(bf16)
    slope = cdf + before * (jnp.exp(-0.5 * before * before) * (1.0 / math.sqrt(2.0 * math.pi)))
    g_act = lax.dot_general(ct, down, (((1,), (1,)), ((), ())), preferred_element_type=f32)
    g_before = (g_act * slope).astype(bf16)
    y_ref[...] += jnp.dot(active, down, preferred_element_type=f32)
    gx_ref[...] += lax.dot_general(g_before, up, (((1,), (1,)), ((), ())), preferred_element_type=f32)
    gdown_ref[...] = lax.dot_general(
        active, ct, (((0,), (0,)), ((), ())), preferred_element_type=f32
    ).astype(bf16)
    gup_ref[...] = lax.dot_general(
        nt, g_before, (((0,), (0,)), ((), ())), preferred_element_type=f32
    ).astype(bf16)
    gbias_ref[...] = jnp.sum(g_before.astype(f32), axis=0, keepdims=True)


def feed_forward(nt, ct, up, bias, down):
    rows, width = nt.shape
    hidden = up.shape[1]
    block = min(256, hidden)
    return pl.pallas_call(
        feed_body,
        grid=(hidden // block,),
        in_specs=[
            pl.BlockSpec((rows, width), lambda i: (0, 0)),
            pl.BlockSpec((rows, width), lambda i: (0, 0)),
            pl.BlockSpec((width, block), lambda i: (0, i)),
            pl.BlockSpec((1, block), lambda i: (0, i)),
            pl.BlockSpec((block, width), lambda i: (i, 0)),
        ],
        out_specs=[
            pl.BlockSpec((rows, width), lambda i: (0, 0)),
            pl.BlockSpec((rows, width), lambda i: (0, 0)),
            pl.BlockSpec((block, width), lambda i: (i, 0)),
            pl.BlockSpec((width, block), lambda i: (0, i)),
            pl.BlockSpec((1, block), lambda i: (0, i)),
        ],
        out_shape=[
            jax.ShapeDtypeStruct((rows, width), f32),
            jax.ShapeDtypeStruct((rows, width), f32),
            jax.ShapeDtypeStruct((hidden, width), bf16),
            jax.ShapeDtypeStruct((width, hidden), bf16),
            jax.ShapeDtypeStruct((1, hidden), f32),
        ],
        compiler_params=pltpu.CompilerParams(vmem_limit_bytes=VMEM_BYTES),
        cost_estimate=pl.CostEstimate(
            flops=12 * rows * width * hidden,
            bytes_accessed=8 * width * hidden + 12 * rows * width,
            transcendentals=2 * rows * hidden,
        ),
    )(nt, ct, up, bias, down)


def norm_forward(values, norm_gain, norm_offset):
    center = values - jnp.mean(values, axis=-1, keepdims=True)
    inverse_root = lax.rsqrt(jnp.mean(center * center, axis=-1, keepdims=True) + 1e-05)
    normed = center * inverse_root
    return (normed * norm_gain + norm_offset, normed, inverse_root)


def norm_backward(upstream, normed, inverse_root, norm_gain):
    scaled = upstream * norm_gain
    centered = (
        scaled
        - jnp.mean(scaled, axis=-1, keepdims=True)
        - normed * jnp.mean(scaled * normed, axis=-1, keepdims=True)
    )
    return centered * inverse_root


def contract(left_side, right_side, left_dim, right_dim):
    return lax.dot_general(
        left_side, right_side, (((left_dim,), (right_dim,)), ((), ())), preferred_element_type=f32
    )


def trunk_hidden(trunk, features):
    embed_weight, embed_bias, hidden_weight, hidden_bias, last_weight, last_bias, frequency = trunk
    layer_out = jnp.sin(frequency * (jnp.dot(features, embed_weight, precision=highest) + embed_bias))
    layer_out = jnp.sin(frequency * (jnp.dot(layer_out, hidden_weight, precision=highest) + hidden_bias))
    return jnp.sin(frequency * (jnp.dot(layer_out, last_weight, precision=highest) + last_bias))


def to_owners(value, chips):
    tokens, width = value.shape
    channels = width // chips
    grid = value.reshape(tokens // 256, 2, LANES, chips, channels)
    return grid.transpose(3, 0, 2, 1, 4).reshape(chips, tokens // 256, LANES, 2 * channels)


def from_owners(value):
    chips, pairs, _, lanes = value.shape
    grid = value.reshape(chips, pairs, LANES, 2, lanes // 2)
    return grid.transpose(1, 3, 2, 0, 4).reshape(pairs * 256, chips * (lanes // 2))


def exchange(value):
    return chip_exchange(value)


def flatten(*values):
    return jnp.concatenate([value.reshape(-1) for value in values])


def unflatten(flat, shapes):
    out, at = [], 0
    for shape in shapes:
        size = int(np.prod(shape))
        out.append(flat[at : at + size].reshape(shape))
        at += size
    return out


def to_rows(flat):
    rows = -(-flat.shape[0] // 1024) * 8
    return jnp.pad(flat, (0, rows * LANES - flat.shape[0])).reshape(rows, LANES)


def plain_device(
    tokens,
    cotangent,
    pre_gain,
    pre_offset,
    input_weight,
    input_bias,
    short_weight,
    short_bias,
    skip_weight,
    embed_weight,
    embed_bias,
    hidden_weight,
    hidden_bias,
    last_weight,
    last_bias,
    frequency,
    filter_weight,
    output_weight,
    output_bias,
    post_gain,
    post_offset,
    up_weight,
    up_bias,
    down_weight,
    down_bias,
):
    seq_count = lax.axis_size("seq")
    seq_index = lax.axis_index("seq")
    z, y, core, x = place()
    chips = seq_count // 2
    z_count = seq_count // 4
    chip = seq_index // 2
    tok_count = tokens.shape[1]
    width = tokens.shape[2]
    length = tok_count * seq_count
    channels = width // seq_count
    ff = up_weight.shape[1]
    hidden_own = ff // seq_count
    half = width // 2
    pairs = length // 256

    mine = jnp.stack([tokens[0], cotangent[0]])
    other = swap_core(mine)
    pair = both(mine, other, core)
    tok = pair[:, 0].reshape(2 * tok_count, width)
    cot = pair[:, 1].reshape(2 * tok_count, width)

    def half_columns(value, groups, run):
        rows = value.shape[0]
        grid = value.reshape(rows, groups, chips, 2, run)
        return [grid[:, :, :, side].reshape(rows, groups * chips * run) for side in range(2)]

    def own_rows(value, groups, run):
        sides = half_columns(value, groups, run)
        keep = jnp.where(core == 0, sides[0], sides[1])
        got = swap_core(jnp.where(core == 0, sides[1], sides[0]))
        return jnp.where(core == x, keep, got)

    in_piece = own_rows(input_weight, 3, channels)
    in_half = gather_pieces(in_piece).reshape(width, 3 * half)
    small_shapes = [(width // seq_count,)] * 2 + [(3, channels), (3, 3, channels), (3, channels)]
    small_shapes += [(width // seq_count,)] * 3 + [(hidden_own,), (width // seq_count,)]
    smalls = flatten(
        pre_gain, pre_offset, input_bias, short_weight, short_bias, output_bias, post_gain, post_offset, up_bias, down_bias
    )
    shapes = [v.shape for v in (pre_gain, pre_offset, input_bias, short_weight, short_bias)]
    shapes += [v.shape for v in (output_bias, post_gain, post_offset, up_bias, down_bias)]
    small_rows = to_rows(smalls)
    small_all = gather_small(small_rows.reshape(-1)).astype(f32)
    columns, at = [], 0
    for shape in shapes:
        size = int(np.prod(shape))
        columns.append(small_all[:, at : at + size])
        at += size

    def halved(value, run):
        lead = value.shape[:-1]
        return pick(value.reshape(*lead, -1, 2, run), core, len(lead) + 1).reshape(*lead, -1)

    pre_gain_full, pre_offset_full = columns[0].reshape(-1), columns[1].reshape(-1)
    input_bias_own = halved(columns[2].reshape(3, width), channels).reshape(-1)
    short_full = columns[3].reshape(seq_count, 3, -1).transpose(1, 0, 2).reshape(3, 3, width)
    short_taps = halved(short_full, channels).reshape(3, -1)
    short_bias_own = halved(columns[4].reshape(3, width), channels).reshape(-1)
    output_bias_full = columns[5].reshape(-1)
    post_gain_full, post_offset_full = columns[6].reshape(-1), columns[7].reshape(-1)
    up_bias_own = halved(columns[8].reshape(-1), hidden_own)
    down_bias_full = columns[9].reshape(-1)

    out_rows = output_weight.shape[0] // 2
    up_piece = own_rows(up_weight, 1, hidden_own)
    out_piece = pick(output_weight.reshape(2, out_rows, width), x, 0)
    down_piece = pick(down_weight.reshape(2, hidden_own // 2, width), x, 0)
    up_half = gather_pieces(up_piece).reshape(width, ff // 2)
    n_out, n_down = out_rows // 2, hidden_own // 4
    mixed_piece = jnp.concatenate(
        [out_piece[:n_out], down_piece[:n_down], out_piece[n_out:], down_piece[n_down:]], axis=0
    )
    later = gather_pieces(mixed_piece)
    later = later.reshape(chips, 2, 2, n_out + n_down, width)
    out_half = later[:, :, :, :n_out].reshape(half, width)
    down_half = later[:, :, :, n_out:].reshape(ff // 2, width)

    positions = (seq_index * tok_count + jnp.arange(tok_count, dtype=jnp.int32)).astype(f32)
    relative = positions / (length - 1)
    phases = positions * (2.0 * math.pi / length)
    band_count = (FEATURES - 1) // 2
    band_freq = jnp.linspace(0.0001, band_count - 1, band_count).astype(f32)
    angles = phases[:, None] * band_freq[None, :]
    features = jnp.concatenate([relative[:, None], jnp.cos(angles), -jnp.sin(angles)], axis=1)
    trunk = (embed_weight, embed_bias, hidden_weight, hidden_bias, last_weight, last_bias, frequency)
    hidden_rows, trunk_pull = jax.vjp(partial(trunk_hidden, features=features), trunk)
    units = hidden_rows.shape[1]
    own_pairs = tok_count // 256
    packed = hidden_rows.reshape(own_pairs, 2, LANES, units).transpose(0, 2, 1, 3)
    packed = packed.reshape(own_pairs, LANES, 2 * units)
    filter_hidden = lax.all_gather(packed, "seq", axis=0, tiled=True)
    filter_own = filter_weight.astype(f32)
    zero = jnp.zeros_like(filter_own)
    filter_pair = jnp.concatenate(
        [jnp.concatenate([filter_own, zero], axis=1), jnp.concatenate([zero, filter_own], axis=1)], axis=0
    )
    deltas = jnp.linspace(math.log(0.01) / 1.5, math.log(0.01) / 0.3, width).astype(f32)
    delta_own = jnp.abs(lax.dynamic_slice_in_dim(deltas, seq_index * channels, channels))
    delta_pair = jnp.concatenate([delta_own, delta_own])[None]
    skip_own = skip_weight.astype(f32)
    skip_pair = jnp.concatenate([skip_own, skip_own])[None]
    kernel_spec = plain_filter(filter_hidden, filter_pair, delta_pair)

    rows = 2 * tok_count
    inputs = tok.astype(f32)
    normed_one, unit_one, inverse_one = norm_forward(inputs, pre_gain_full, pre_offset_full)
    normed_low = normed_one.astype(bf16)
    projected_low = (contract(normed_low, in_half, 1, 0) + input_bias_own).astype(bf16)
    shift = [(i, i + 2) for i in range(seq_count - 2)]
    earlier = lax.ppermute(projected_low[rows - 2 :], "seq", shift)
    extended = jnp.concatenate([earlier, projected_low], axis=0).astype(f32)
    convolved = (
        short_taps[0] * extended[:rows]
        + short_taps[1] * extended[1 : rows + 1]
        + short_taps[2] * extended[2:]
        + short_bias_own
    )
    first_part, second_part, values_part = (convolved[:, i * half : (i + 1) * half] for i in range(3))
    gated_low = (values_part * second_part).astype(bf16)
    gated_ch = exchange(to_owners(gated_low, chips)).reshape(pairs, LANES, 2 * channels)
    mixed_ch, gated_spec = plain_forward(gated_ch, kernel_spec, skip_pair)
    chip_shape = (chips, rows // 256, LANES, 2 * channels)
    mixed_tok = from_owners(exchange(mixed_ch.reshape(chip_shape))).astype(f32)
    mix_low = (mixed_tok * first_part).astype(bf16)
    branch_part = contract(mix_low, out_half, 1, 0)
    branch = branch_part + swap_core(branch_part) + output_bias_full
    hidden = inputs + branch

    normed_two, unit_two, inverse_two = norm_forward(hidden, post_gain_full, post_offset_full)
    normed_two_low = normed_two.astype(bf16)
    down_part, back_part, down_grad, up_grad, up_bias_grad = feed_forward(
        normed_two_low, cot, up_half, up_bias_own[None], down_half
    )

    def own_tokens(value):
        return lax.dynamic_slice_in_dim(value, core * tok_count, tok_count, 0)

    def other_tokens(value):
        return lax.dynamic_slice_in_dim(value, (1 - core) * tok_count, tok_count, 0)

    result = own_tokens(hidden) + (
        own_tokens(down_part) + swap_core(other_tokens(down_part)) + down_bias_full
    )
    up_grad = up_grad.reshape(z_count, 2, 2, 2, -1, ff // 2).transpose(0, 1, 3, 2, 4, 5)
    down_sum, up_sum = reduce_pair(down_grad.reshape(z_count, 2, 2, hidden_own // 2, width), up_grad)

    cot_f = cot.astype(f32)
    down_bias_grad = jnp.sum(cot_f, axis=0)
    normed_two_grad = back_part + swap_core(back_part)
    post_gain_grad = jnp.sum(normed_two_grad * unit_two, axis=0)
    post_offset_grad = jnp.sum(normed_two_grad, axis=0)
    hidden_grad = cot_f + norm_backward(normed_two_grad, unit_two, inverse_two, post_gain_full)
    branch_low = hidden_grad.astype(bf16)
    output_bias_grad = jnp.sum(branch_low.astype(f32), axis=0)
    gate_grad = contract(branch_low, out_half, 1, 1)
    mixed_grad_low = (gate_grad * first_part).astype(bf16)
    first_grad = gate_grad * mixed_tok
    mixed_grad_ch = exchange(to_owners(mixed_grad_low, chips)).reshape(pairs, LANES, 2 * channels)
    gated_back, hidden_back, filter_square, skip_line = plain_backward(
        mixed_grad_ch, gated_ch, gated_spec, kernel_spec, skip_pair, filter_hidden, filter_pair, delta_pair
    )
    gated_grad = from_owners(exchange(gated_back.reshape(chip_shape))).astype(f32)
    output_grad = contract(mix_low, branch_low, 0, 0)

    hidden_got = lax.all_to_all(
        hidden_back.reshape(seq_count, own_pairs * LANES, 2 * units), "seq", split_axis=0, concat_axis=0, tiled=True
    )
    hidden_sum = jnp.sum(hidden_got.astype(f32), axis=0)
    hidden_sum = hidden_sum.reshape(own_pairs, LANES, 2, units).transpose(0, 2, 1, 3).reshape(tok_count, units)
    (trunk_grad,) = trunk_pull(hidden_sum)
    filter_grad = filter_square[:units, :channels] + filter_square[units:, channels:]
    skip_grad = skip_line[:, :channels] + skip_line[:, channels:]
    own_grad = jnp.concatenate([filter_grad, skip_grad], axis=0)
    own_grad = own_grad + swap_x(own_grad)
    own_grad = pick(own_grad.reshape(-1, 2, channels // 2), x, 1)

    conv_grad_low = jnp.concatenate(
        [first_grad, gated_grad * values_part, gated_grad * second_part], axis=1
    ).astype(bf16)
    back_shift = [(i + 2, i) for i in range(seq_count - 2)]
    following = lax.ppermute(conv_grad_low[:2], "seq", back_shift)
    conv_grad = conv_grad_low.astype(f32)
    grad_ext = jnp.concatenate([conv_grad_low, following], axis=0).astype(f32)
    projected_grad_low = (
        short_taps[0] * grad_ext[2:] + short_taps[1] * grad_ext[1 : rows + 1] + short_taps[2] * grad_ext[:rows]
    ).astype(bf16)
    short_weight_grad = jnp.stack(
        [jnp.sum(conv_grad * extended[tap : tap + rows], axis=0) for tap in range(3)]
    )
    short_bias_grad = jnp.sum(conv_grad, axis=0)
    input_bias_grad = jnp.sum(projected_grad_low.astype(f32), axis=0)
    input_grad = contract(normed_low, projected_grad_low, 0, 0)
    normed_one_part = contract(projected_grad_low, in_half, 1, 1)
    normed_one_grad = own_tokens(normed_one_part) + swap_core(other_tokens(normed_one_part))
    unit_own = own_tokens(unit_one)
    pre_gain_grad = jnp.sum(normed_one_grad * unit_own, axis=0)
    pre_offset_grad = jnp.sum(normed_one_grad, axis=0)
    tokens_grad = own_tokens(hidden_grad) + norm_backward(
        normed_one_grad, unit_own, own_tokens(inverse_one), pre_gain_full
    )

    in_low = input_grad.astype(bf16).reshape(z_count, 2, 2, 2, -1, 3 * half).transpose(0, 1, 3, 2, 4, 5)
    in_sum = jnp.stack(reduce_pair(in_low[:, :, :, 0], in_low[:, :, :, 1]))
    out_low = output_grad.astype(bf16).reshape(z_count, 2, 2, -1, width)
    split = out_low.shape[3] // 2
    out_sum = jnp.concatenate(reduce_pair(out_low[:, :, :, :split], out_low[:, :, :, split:]), axis=0)

    def whole_columns(value, groups, run):
        got = swap_core(pick(value, 1 - core, 0))
        mine_part = pick(value, core, 0)
        n = mine_part.shape[0]
        grid = both(mine_part, got, core).reshape(2, n, groups, chips, run)
        return grid.transpose(1, 2, 3, 0, 4).reshape(n, -1)

    in_rows = whole_columns(in_sum, 3, channels)
    up_rows_sum = whole_columns(up_sum, 1, hidden_own)

    chip_wide = [post_gain_grad, post_offset_grad, down_bias_grad, output_bias_grad]
    own_wide = [pre_gain_grad, pre_offset_grad, *trunk_grad]
    half_wide = [up_bias_grad.reshape(-1), input_bias_grad, short_weight_grad, short_bias_grad]
    own_flat, half_flat = to_rows(flatten(*own_wide)), to_rows(flatten(*half_wide))
    summed = sum_chips(jnp.concatenate([to_rows(flatten(*chip_wide)), own_flat, half_flat], axis=0))
    n_chip = to_rows(flatten(*chip_wide)).shape[0]
    chip_sum = summed[:n_chip].reshape(-1)
    got = swap_core(summed[n_chip:])
    own_sum = (summed[n_chip:] + got)[: own_flat.shape[0]].reshape(-1)
    half_sum = both(summed[n_chip + own_flat.shape[0] :], got[own_flat.shape[0] :], core).reshape(2, -1)
    chip_sums = unflatten(chip_sum, [v.shape for v in chip_wide])
    own_sums = unflatten(own_sum, [v.shape for v in own_wide])
    half_sums = [
        unflatten(half_sum[side], [v.shape for v in half_wide]) for side in range(2)
    ]

    def joined(index, groups, run):
        pair_of = jnp.stack([half_sums[side][index].reshape(groups, chips, run) for side in range(2)], axis=2)
        return pair_of.reshape(groups, -1)

    block_index = seq_index * 2 + x

    def own_block(value, axis=0):
        size = value.shape[axis] // (2 * seq_count)
        return lax.dynamic_slice_in_dim(value, block_index * size, size, axis)

    up_bias_sum = joined(0, 1, hidden_own).reshape(-1)
    input_bias_sum = joined(1, 3, channels).reshape(-1)
    short_weight_sum = joined(2, 9, channels).reshape(3, -1)
    short_bias_sum = joined(3, 3, channels).reshape(-1)
    return (
        result.astype(bf16)[None],
        tokens_grad.astype(bf16)[None],
        own_block(own_sums[0]),
        own_block(own_sums[1]),
        in_rows,
        own_block(input_bias_sum),
        own_block(short_weight_sum, 1),
        own_block(short_bias_sum),
        own_grad[units],
        *own_sums[2:],
        own_grad[:units],
        out_sum,
        own_block(chip_sums[3]),
        own_block(chip_sums[0]),
        own_block(chip_sums[1]),
        up_rows_sum,
        own_block(up_bias_sum),
        down_sum,
        own_block(chip_sums[2]),
    )


def after(earlier, value):
    return lax.optimization_barrier((earlier, value))[1]


def gather_z(piece, gates=None):
    have = piece[None]
    masks = z_masks(lax.axis_size("seq") // 4)
    for step, mask in enumerate(masks):
        if gates is not None and step == len(masks) - 1:
            have = after(gates, have)
        have = jnp.concatenate([have, swap_z(have, mask)], axis=0)
    return have


def gather_near(have):
    half = have.shape[1] // 2
    first, second = have[:, :half], have[:, half:]
    return jnp.stack([first, swap_y(first)]), jnp.stack([second, swap_x(second)])


def gather_far(near):
    first, second = near
    return first, swap_x(first), second, swap_y(second)


def reduce_pass(kept, got, second):
    sent = (kept[1].astype(f32) + got[1].astype(f32)).astype(bf16)
    return sent, kept[0].astype(f32) + got[0].astype(f32), second(sent)


def reduce_far(total, gates=None):
    masks = z_masks(lax.axis_size("seq") // 4)
    for step, mask in enumerate(reversed(masks)):
        half = total.shape[0] // 2
        got = swap_z(total[half:].astype(bf16), mask)
        if gates is not None and step < len(gates):
            got = after(gates[step], got)
        total = total[:half] + got.astype(f32)
    return total[0]


def place_pieces(out_ref, pieces, scalars, chips, span):
    first, first_far, second, second_far = pieces
    x = scalars[0]
    half = span // 2
    z_count = chips // 2
    for slot in range(z_count):
        for yr in range(2):
            base = scalars[2 + yr * z_count + slot] * (2 * span)
            source = second_far if yr else second
            for xr in range(2):
                at = pl.multiple_of(base + (x if xr == 0 else 1 - x) * span, span)
                out_ref[pl.ds(at, half), :] = (first_far if xr else first)[yr, slot]
                out_ref[pl.ds(pl.multiple_of(at + half, half), half), :] = source[xr, slot]


def route_rows(grad_ref, kept_ref, sent_ref, scalars, chips, inner, by_x):
    x = scalars[0]
    z_count = chips // 2
    rows = grad_ref.shape[0] // (2 * chips * inner)
    for slot in range(z_count):
        for yr in range(2):
            base = scalars[2 + yr * z_count + slot] * (2 * inner * rows)
            for xr in range(2):
                target, lead = ((sent_ref if xr else kept_ref), yr) if by_x else ((sent_ref if yr else kept_ref), xr)
                for part in range(inner):
                    at = pl.multiple_of(base + part * 2 * rows + (x if xr == 0 else 1 - x) * rows, rows)
                    target[lead, slot, part] = grad_ref[pl.ds(at, rows), :].astype(bf16)


HALO = 16


def short_conv(rows, taps, bias):
    two, one = pltpu.roll(rows, 2, 0), pltpu.roll(rows, 1, 0)
    return (taps[0:1] * two + taps[1:2] * one + taps[2:3] * rows + bias)[HALO:]


def chip_rows(convolved):
    return convolved[: convolved.shape[0] - HALO]


def pack_pairs(out_ref, index, pair, even, odd):
    half = LANES // 2
    lower = lax.broadcasted_iota(jnp.int32, even.shape, 1) < half
    out_ref[index, pair] = jnp.where(lower, even, pltpu.roll(odd, half, 1)).astype(bf16)
    out_ref[index + 1, pair] = jnp.where(lower, pltpu.roll(even, half, 1), odd).astype(bf16)


def pack_rows(out_ref, index, value):
    for pair in range(value.shape[0] // 256):
        rows = value[256 * pair : 256 * (pair + 1)]
        pack_pairs(out_ref, index, pair, rows[:LANES], rows[LANES:])


def unpack_pair(one, two):
    half = LANES // 2
    one, two = one.astype(f32), two.astype(f32)
    lower = lax.broadcasted_iota(jnp.int32, one.shape, 1) < half
    return jnp.where(lower, one, pltpu.roll(two, half, 1)), jnp.where(lower, pltpu.roll(one, half, 1), two)


def unpack_rows(in_ref, index):
    out = []
    for pair in range(in_ref.shape[1]):
        out.extend(unpack_pair(in_ref[index, pair], in_ref[index + 1, pair]))
    return jnp.concatenate(out, axis=0)


def project_body(scalars, normed_ref, bias_ref, a_ref, ax_ref, b_ref, by_ref, out_ref, weight_ref):
    chips = 2 * a_ref.shape[1]
    place_pieces(weight_ref, (a_ref, ax_ref, b_ref, by_ref), scalars, chips, 2 * a_ref.shape[2])
    value = jnp.dot(normed_ref[...], weight_ref[...], preferred_element_type=f32) + bias_ref[...]
    row = lax.broadcasted_iota(jnp.int32, value.shape, 0)
    value = jnp.where(jnp.logical_and(row < HALO, scalars[1] == 0), 0.0, value)
    out_ref[...] = value.astype(bf16)


def grid_call(body, scalars, grid, ins, outs, scratch, flops, moved, transcendentals=0):
    return pl.pallas_call(
        body,
        grid_spec=pltpu.PrefetchScalarGridSpec(
            num_scalar_prefetch=1,
            grid=(grid,),
            in_specs=[pl.BlockSpec(block, index) for _, block, index in ins],
            out_specs=[pl.BlockSpec(block, index) for _, _, block, index in outs],
            scratch_shapes=scratch,
        ),
        out_shape=[jax.ShapeDtypeStruct(shape, dtype) for shape, dtype, _, _ in outs],
        compiler_params=pltpu.CompilerParams(vmem_limit_bytes=VMEM_BYTES),
        cost_estimate=pl.CostEstimate(flops=flops // SHARE, bytes_accessed=moved // SHARE, transcendentals=0),
    )(scalars, *[value for value, _, _ in ins])


def fixed(value):
    return (value, value.shape, lambda i, s, n=value.ndim: (0,) * n)


def fixed_out(shape, dtype):
    return (shape, dtype, shape, lambda i, s, n=len(shape): (0,) * n)


def project(scalars, normed, bias, pieces):
    rows, width = normed.shape
    columns = bias.shape[1]
    block = columns // 3
    lead = pieces[0].shape[:3]
    piece_specs = [(p, (*lead, block), lambda i, s: (0, 0, 0, i)) for p in pieces]
    return grid_call(
        project_body,
        scalars,
        3,
        [fixed(normed), (bias, (1, block), lambda i, s: (0, i)), *piece_specs],
        [
            ((rows, columns), bf16, (rows, block), lambda i, s: (0, i)),
            ((width, columns), bf16, (width, block), lambda i, s: (0, i)),
        ],
        [],
        2 * rows * width * columns,
        4 * width * columns + 2 * rows * (width + columns),
    )


def gate_body(scalars, second_ref, values_ref, t2_ref, t3_ref, b2_ref, b3_ref, out_ref):
    second = short_conv(second_ref[...].astype(f32), t2_ref[...], b2_ref[...])
    values = short_conv(values_ref[...].astype(f32), t3_ref[...], b3_ref[...])
    pack_rows(out_ref, 0, chip_rows(values * second))


def stream_tiles(projected, taps, bias, stream, tiles):
    rows = projected.shape[0]
    index = lambda i, s, at=stream * tiles: (0, at + i)
    return (
        (projected, (rows, LANES), index),
        (taps, (3, LANES), index),
        (bias, (1, LANES), index),
    )


def gate(scalars, projected, taps, bias, chips):
    rows, columns = projected.shape
    tiles = columns // 3 // LANES
    p2, t2, b2 = stream_tiles(projected, taps, bias, 1, tiles)
    p3, t3, b3 = stream_tiles(projected, taps, bias, 2, tiles)
    pairs = (rows - 2 * HALO) // 256
    (out,) = grid_call(
        gate_body,
        scalars,
        tiles,
        [p2, p3, t2, t3, b2, b3],
        [((chips, pairs, LANES, LANES), bf16, (2, pairs, LANES, LANES), lambda i, s: (i, 0, 0, 0))],
        [],
        20 * rows * columns,
        3 * rows * columns,
    )
    return out


def branch_body(
    scalars, mixed_ref, first_ref, taps_ref, bias_ref, a_ref, ax_ref, b_ref, by_ref, mixed_out, mix_out, weight_ref, out_ref
):
    chips = 2 * a_ref.shape[1]
    place_pieces(weight_ref, (a_ref, ax_ref, b_ref, by_ref), scalars, chips, 2 * a_ref.shape[2])
    for tile in range(chips // 2):
        cols = slice(tile * LANES, (tile + 1) * LANES)
        mixed = unpack_rows(mixed_ref, 2 * tile)
        first = chip_rows(short_conv(first_ref[:, cols].astype(f32), taps_ref[:, cols], bias_ref[:, cols]))
        mixed_out[:, cols] = mixed.astype(bf16)
        mix_out[:, cols] = (mixed * first).astype(bf16)
    out_ref[...] = jnp.dot(mix_out[...], weight_ref[...], preferred_element_type=f32)


def first_stream(projected, taps, bias):
    rows, columns = projected.shape
    block = columns // 3
    return [
        (projected, (rows, block), lambda i, s: (0, 0)),
        (taps, (3, block), lambda i, s: (0, 0)),
        (bias, (1, block), lambda i, s: (0, 0)),
    ]


def branch_out(scalars, mixed, projected, taps, bias, pieces):
    rows = projected.shape[0] - 2 * HALO
    half = projected.shape[1] // 3
    width = pieces[0].shape[3]
    return grid_call(
        branch_body,
        scalars,
        1,
        [fixed(mixed), *first_stream(projected, taps, bias), *[fixed(p) for p in pieces]],
        [
            fixed_out((rows, half), bf16),
            fixed_out((rows, half), bf16),
            fixed_out((half, width), bf16),
            fixed_out((rows, width), f32),
        ],
        [],
        2 * rows * half * width,
        4 * rows * width + 6 * half * width,
    )


def tiled_feed_body(
    scalars,
    nt_ref,
    ct_ref,
    bias_ref,
    ua_ref,
    uax_ref,
    ub_ref,
    uby_ref,
    da_ref,
    dax_ref,
    db_ref,
    dby_ref,
    y_ref,
    gx_ref,
    gdown_kept,
    gdown_sent,
    gup_kept,
    gup_sent,
    gbias_ref,
    up_ref,
    down_ref,
    grad_ref,
):
    step = pl.program_id(0)
    z_count = ua_ref.shape[1]
    x = scalars[0]

    @pl.when(step == 0)
    def _():
        y_ref[...] = jnp.zeros_like(y_ref)
        gx_ref[...] = jnp.zeros_like(gx_ref)

    place_pieces(up_ref, (ua_ref, uax_ref, ub_ref, uby_ref), scalars, 2 * z_count, 2 * ua_ref.shape[2])
    span = down_ref.shape[0] // 2
    half = span // 2
    own, other = pl.multiple_of(x * span, span), pl.multiple_of((1 - x) * span, span)
    down_ref[pl.ds(own, half), :] = da_ref[0, 0]
    down_ref[pl.ds(other, half), :] = dax_ref[0, 0]

    def put_second(source):
        down_ref[pl.ds(pl.multiple_of(own + half, half), half), :] = source[0, 0]
        down_ref[pl.ds(pl.multiple_of(other + half, half), half), :] = source[1, 0]

    @pl.when(step < z_count)
    def _():
        put_second(db_ref)

    @pl.when(step >= z_count)
    def _():
        put_second(dby_ref)

    nt, ct, up, down = nt_ref[...], ct_ref[...], up_ref[...], down_ref[...]
    before = jnp.dot(nt, up, preferred_element_type=f32) + bias_ref[...]
    cdf = 0.5 * (1.0 + lax.erf(before * math.sqrt(0.5)))
    active = (before * cdf).astype(bf16)
    slope = cdf + before * (jnp.exp(-0.5 * before * before) * (1.0 / math.sqrt(2.0 * math.pi)))
    g_act = lax.dot_general(ct, down, (((1,), (1,)), ((), ())), preferred_element_type=f32)
    g_before = (g_act * slope).astype(bf16)
    y_ref[...] += jnp.dot(active, down, preferred_element_type=f32)
    gx_ref[...] += lax.dot_general(g_before, up, (((1,), (1,)), ((), ())), preferred_element_type=f32)
    gdown = lax.dot_general(active, ct, (((0,), (0,)), ((), ())), preferred_element_type=f32)
    one, two = gdown[:span], gdown[span:]
    gdown_kept[0, 0] = jnp.where(x == 0, one, two).astype(bf16)
    gdown_sent[0, 0] = jnp.where(x == 0, two, one).astype(bf16)
    grad_ref[...] = lax.dot_general(nt, g_before, (((0,), (0,)), ((), ())), preferred_element_type=f32)
    route_rows(grad_ref, gup_kept, gup_sent, scalars, 2 * z_count, 2, False)
    gbias_ref[...] = jnp.sum(g_before.astype(f32), axis=0, keepdims=True)


def tiled_feed(scalars, nt, ct, bias, up, down):
    rows, width = nt.shape
    hidden = bias.shape[1]
    z_count = up[0].shape[1]
    chips = 2 * z_count
    block = hidden // chips
    h = up[0].shape[2]
    hd = down[0].shape[2]
    column = lambda i, s: (0, s[2 + i])
    up_specs = [(p, (2, z_count, h, block), lambda i, s: (0, 0, 0, s[2 + i])) for p in up]
    near = lambda i, s: (i // z_count, i % z_count, 0, 0)
    far = lambda i, s: (0, i % z_count, 0, 0)
    down_specs = [(p, (1, 1, hd, width), near) for p in down[:2]] + [(p, (2, 1, hd, width), far) for p in down[2:]]
    down_block = (1, 1, 2 * hd, width)
    up_shape = (2, z_count, 2, h, hidden)
    up_block = (2, z_count, 2, h, block)
    up_index = lambda i, s: (0, 0, 0, 0, s[2 + i])
    return grid_call(
        tiled_feed_body,
        scalars,
        chips,
        [fixed(nt), fixed(ct), (bias, (1, block), column), *up_specs, *down_specs],
        [
            fixed_out((rows, width), f32),
            fixed_out((rows, width), f32),
            ((2, z_count, 2 * hd, width), bf16, down_block, near),
            ((2, z_count, 2 * hd, width), bf16, down_block, near),
            (up_shape, bf16, up_block, up_index),
            (up_shape, bf16, up_block, up_index),
            ((1, hidden), f32, (1, block), column),
        ],
        [pltpu.VMEM((width, block), bf16), pltpu.VMEM((block, width), bf16), pltpu.VMEM((width, block), f32)],
        12 * rows * width * hidden,
        8 * width * hidden + 12 * rows * width,
        2 * rows * hidden,
    )


def unbranch_body(
    scalars,
    g_ref,
    mix_ref,
    mixed_ref,
    first_ref,
    taps_ref,
    bias_ref,
    weight_ref,
    gmixed_ref,
    gfirst_ref,
    kept_ref,
    sent_ref,
    grad_ref,
):
    chips = gmixed_ref.shape[0]
    g = g_ref[...]
    gate_grad = lax.dot_general(g, weight_ref[...], (((1,), (1,)), ((), ())), preferred_element_type=f32)
    for tile in range(chips // 2):
        cols = slice(tile * LANES, (tile + 1) * LANES)
        first = chip_rows(short_conv(first_ref[:, cols].astype(f32), taps_ref[:, cols], bias_ref[:, cols]))
        gfirst_ref[:, cols] = (gate_grad[:, cols] * mixed_ref[:, cols].astype(f32)).astype(bf16)
        pack_rows(gmixed_ref, 2 * tile, gate_grad[:, cols] * first)
    grad_ref[...] = lax.dot_general(mix_ref[...], g, (((0,), (0,)), ((), ())), preferred_element_type=f32)
    route_rows(grad_ref, kept_ref, sent_ref, scalars, chips, 1, False)


def unbranch(scalars, g, mix, mixed, projected, taps, bias, weight, chips):
    rows, width = g.shape
    half = weight.shape[0]
    grad_shape = (2, chips // 2, 1, half // (2 * chips), width)
    return grid_call(
        unbranch_body,
        scalars,
        1,
        [fixed(g), fixed(mix), fixed(mixed), *first_stream(projected, taps, bias), fixed(weight)],
        [
            fixed_out((chips, rows // 256, LANES, LANES), bf16),
            fixed_out((rows, half), bf16),
            fixed_out(grad_shape, bf16),
            fixed_out(grad_shape, bf16),
        ],
        [pltpu.VMEM((half, width), f32)],
        4 * rows * half * width,
        4 * rows * width + 6 * half * width,
    )


def ungate_body(scalars, gated_ref, second_ref, values_ref, t2_ref, t3_ref, b2_ref, b3_ref, gsecond_ref, gvalues_ref):
    pairs = (gated_ref.shape[1] - HALO) // LANES
    blocks = [gated_ref.at[:, pl.ds(pair * LANES, LANES), :] for pair in range(pairs)]
    grad = jnp.concatenate([part for block in blocks for part in unpack_pair(block[0], block[1])], axis=0)
    ahead, _ = unpack_pair(gated_ref[0, pairs * LANES :], gated_ref[1, pairs * LANES :])
    grad = jnp.concatenate([grad, ahead], axis=0)
    second = short_conv(second_ref[...].astype(f32), t2_ref[...], b2_ref[...])
    values = short_conv(values_ref[...].astype(f32), t3_ref[...], b3_ref[...])
    gsecond_ref[...] = (grad * values).astype(bf16)
    gvalues_ref[...] = (grad * second).astype(bf16)


def ungate(scalars, gated, projected, taps, bias):
    rows, columns = projected.shape
    half = columns // 3
    tiles = half // LANES
    p2, t2, b2 = stream_tiles(projected, taps, bias, 1, tiles)
    p3, t3, b3 = stream_tiles(projected, taps, bias, 2, tiles)
    out = ((rows - HALO, half), bf16, (rows - HALO, LANES), lambda i, s: (0, i))
    return grid_call(
        ungate_body,
        scalars,
        tiles,
        [(gated, (2, *gated.shape[1:]), lambda i, s: (i, 0, 0)), p2, p3, t2, t3, b2, b3],
        [out, out],
        [],
        20 * rows * columns,
        3 * rows * columns,
    )


def stream_body(
    by_x, scalars, grad_ref, rows_ref, taps_ref, normed_ref, gproj_ref, kept_ref, sent_ref, sums_ref, work_ref
):
    count, columns = gproj_ref.shape
    chips = 2 * kept_ref.shape[1]
    for at in range(0, columns, LANES):
        cols = slice(at, at + LANES)
        taps = taps_ref[:, cols]
        ext = grad_ref[:, cols].astype(f32)
        grad = ext[:count]
        total = count + HALO
        one, two = pltpu.roll(ext, total - 1, 0)[:count], pltpu.roll(ext, total - 2, 0)[:count]
        low = (taps[0:1] * two + taps[1:2] * one + taps[2:3] * grad).astype(bf16)
        gproj_ref[:, cols] = low
        rows = rows_ref[:, cols].astype(f32)
        sums = [
            jnp.sum(grad * pltpu.roll(rows, 2, 0)[HALO:total], axis=0, keepdims=True),
            jnp.sum(grad * pltpu.roll(rows, 1, 0)[HALO:total], axis=0, keepdims=True),
            jnp.sum(grad * rows[HALO:total], axis=0, keepdims=True),
            jnp.sum(grad, axis=0, keepdims=True),
            jnp.sum(low.astype(f32), axis=0, keepdims=True),
            jnp.zeros((3, LANES), f32),
        ]
        sums_ref[:, cols] = jnp.concatenate(sums, axis=0)
    work_ref[...] = lax.dot_general(
        normed_ref[HALO:total, :], gproj_ref[...], (((0,), (0,)), ((), ())), preferred_element_type=f32
    )
    route_rows(work_ref, kept_ref, sent_ref, scalars, chips, 2, by_x)


def stream_back(scalars, grad, projected, taps, normed, stream, chips, by_x):
    count, columns = grad.shape[0] - HALO, grad.shape[1]
    width = normed.shape[1]
    rows = projected.shape[0]
    index = lambda i, s: (0, stream)
    shape = (2, chips // 2, 2, width // (4 * chips), columns)
    return grid_call(
        partial(stream_body, by_x),
        scalars,
        1,
        [
            fixed(grad),
            (projected, (rows, columns), index),
            (taps, (3, columns), index),
            fixed(normed),
        ],
        [
            fixed_out((count, columns), bf16),
            fixed_out(shape, bf16),
            fixed_out(shape, bf16),
            fixed_out((8, columns), f32),
        ],
        [pltpu.VMEM((width, columns), f32)],
        2 * count * columns * width,
        4 * count * columns + 2 * count * width + 2 * width * columns,
    )


def split_body(run, scalars, in_ref, kept_ref, sent_ref):
    core = scalars[0]
    if run == LANES // 2:
        one, two = in_ref[:, :LANES].astype(f32), in_ref[:, LANES:].astype(f32)
        lower = lax.broadcasted_iota(jnp.int32, one.shape, 1) < run
        sides = (
            jnp.where(lower, one, pltpu.roll(two, run, 1)).astype(bf16),
            jnp.where(lower, pltpu.roll(one, run, 1), two).astype(bf16),
        )
        kept_ref[...] = jnp.where(core == 0, sides[0], sides[1])
        sent_ref[...] = jnp.where(core == 0, sides[1], sides[0])
    else:
        kept_ref[...] = jnp.where(core == 0, in_ref[:, :run], in_ref[:, run:])
        sent_ref[...] = jnp.where(core == 0, in_ref[:, run:], in_ref[:, :run])


def split_columns(core, value, run):
    rows, columns = value.shape
    block = max(run, LANES)
    out = ((rows, columns // 2), bf16, (rows, block), lambda i, s: (0, i))
    return grid_call(
        partial(split_body, run),
        core.reshape(1),
        columns // (2 * block),
        [(value, (rows, 2 * block), lambda i, s: (0, i))],
        [out, out],
        [],
        rows * columns,
        4 * rows * columns,
    )


def filter_features(seq_index, tok_count, length):
    positions = (seq_index * tok_count + jnp.arange(tok_count, dtype=jnp.int32)).astype(f32)
    relative = positions / (length - 1)
    phases = positions * (2.0 * math.pi / length)
    band_count = (FEATURES - 1) // 2
    band_freq = jnp.linspace(0.0001, band_count - 1, band_count).astype(f32)
    angles = phases[:, None] * band_freq[None, :]
    return jnp.concatenate([relative[:, None], jnp.cos(angles), -jnp.sin(angles)], axis=1)


def tiled_device(
    tokens,
    cotangent,
    pre_gain,
    pre_offset,
    input_weight,
    input_bias,
    short_weight,
    short_bias,
    skip_weight,
    embed_weight,
    embed_bias,
    hidden_weight,
    hidden_bias,
    last_weight,
    last_bias,
    frequency,
    filter_weight,
    output_weight,
    output_bias,
    post_gain,
    post_offset,
    up_weight,
    up_bias,
    down_weight,
    down_bias,
):
    seq_count = lax.axis_size("seq")
    seq_index = lax.axis_index("seq")
    z, y, core, x = place()
    chips = seq_count // 2
    z_count = seq_count // 4
    tok_count, width = tokens.shape[1:]
    length = tok_count * seq_count
    channels = width // seq_count
    ff = up_weight.shape[1]
    hidden_own = ff // seq_count
    half = width // 2
    pairs = length // 256
    rows = 2 * tok_count
    chip_at = [(z ^ rel) * 2 + (y ^ yr) for yr in range(2) for rel in z_order(z_count)]
    scalars = jnp.stack([x, seq_index // 2, *chip_at]).astype(jnp.int32)

    def own_rows(value, run):
        keep, sent = split_columns(core, value, run)
        return jnp.where(core == x, keep, swap_core(sent))

    in_piece = own_rows(input_weight, channels)
    mine = jnp.stack([after(in_piece, tokens)[0], cotangent[0]])
    pair = both(mine, swap_core(mine), core)
    tok = pair[:, 0].reshape(rows, width)
    cot = pair[:, 1].reshape(rows, width)
    onward = [(i, i + 2) for i in range(seq_count - 2)]
    backward = [(i + 2, i) for i in range(seq_count - 2)]
    earlier = lax.ppermute(tok[rows - HALO :], "seq", onward)
    later = lax.ppermute(tok[:HALO], "seq", backward)
    tok_ext = jnp.concatenate([earlier, tok, later], axis=0)
    vectors = [
        pre_gain,
        pre_offset,
        input_bias,
        short_weight,
        short_bias,
        output_bias,
        post_gain,
        post_offset,
        up_bias,
        down_bias,
    ]
    small_blocks = []
    for vector in vectors:
        flat = vector.reshape(-1)
        small_blocks.append(jnp.pad(flat, (0, -flat.shape[0] % LANES)).reshape(-1, LANES))
    small_count = sum(block.shape[0] for block in small_blocks)
    small_blocks.append(jnp.zeros((-small_count % 8, LANES), bf16))
    small = jnp.concatenate(small_blocks, axis=0).astype(f32)

    in_have = gather_z(in_piece, (earlier, later))

    trunk = (embed_weight, embed_bias, hidden_weight, hidden_bias, last_weight, last_bias, frequency)
    features = filter_features(after(in_piece, seq_index), tok_count, length)
    hidden_rows, trunk_pull = jax.vjp(partial(trunk_hidden, features=features), trunk)
    units = hidden_rows.shape[1]
    own_pairs = tok_count // 256
    packed = hidden_rows.reshape(own_pairs, 2, LANES, units).transpose(0, 2, 1, 3)
    packed = packed.reshape(own_pairs * LANES, 2 * units)
    gathered = gather_small(after((earlier, later), jnp.concatenate([packed, small], axis=0)))
    filter_hidden = gathered[:, : own_pairs * LANES].reshape(pairs, LANES, 2 * units)
    small_all = gathered[:, own_pairs * LANES :].reshape(seq_count, -1)

    up_piece = own_rows(after(in_piece, up_weight), hidden_own)
    out_piece = pick(output_weight.reshape(2, -1, width), x, 0)
    down_piece = pick(down_weight.reshape(2, -1, width), x, 0)
    in_near = gather_near(in_have)
    in_pieces = gather_far(in_near)
    up_have = gather_z(after(in_have, up_piece))
    out_have = gather_z(after(up_have, out_piece))
    down_have = gather_z(after(up_have, down_piece))
    up_near = gather_near(after(in_pieces, up_have))

    columns, at = [], 0
    for vector in vectors:
        columns.append(small_all[:, at : at + vector.size])
        at += vector.size + -vector.size % LANES

    def halved(value, run):
        lead = value.shape[:-1]
        return pick(value.reshape(*lead, -1, 2, run), core, len(lead) + 1).reshape(*lead, -1)

    pre_gain_full, pre_offset_full = columns[0].reshape(-1), columns[1].reshape(-1)
    input_bias_own = halved(columns[2].reshape(3, width), channels).reshape(1, -1)
    short_full = columns[3].reshape(seq_count, 3, -1).transpose(1, 0, 2).reshape(3, 3, width)
    taps = halved(short_full, channels).reshape(3, -1)
    short_bias_own = halved(columns[4].reshape(3, width), channels).reshape(1, -1)
    output_bias_full = columns[5].reshape(-1)
    post_gain_full, post_offset_full = columns[6].reshape(-1), columns[7].reshape(-1)
    up_bias_own = halved(columns[8].reshape(-1), hidden_own)[None]
    down_bias_full = columns[9].reshape(-1)

    filter_own = filter_weight.astype(f32)
    zero = jnp.zeros_like(filter_own)
    filter_pair = jnp.concatenate(
        [jnp.concatenate([filter_own, zero], axis=1), jnp.concatenate([zero, filter_own], axis=1)], axis=0
    )
    deltas = jnp.linspace(math.log(0.01) / 1.5, math.log(0.01) / 0.3, width).astype(f32)
    delta_own = jnp.abs(lax.dynamic_slice_in_dim(deltas, seq_index * channels, channels))
    delta_pair = jnp.concatenate([delta_own, delta_own])[None]
    skip_own = skip_weight.astype(f32)
    skip_pair = jnp.concatenate([skip_own, skip_own])[None]
    tables = tuple(jnp.asarray(t) for t in conv_tables(pairs))

    normed_one, unit_one, inverse_one = norm_forward(tok_ext.astype(f32), pre_gain_full, pre_offset_full)
    normed_ext = normed_one.astype(bf16)
    in_pieces = after((normed_ext, input_bias_own, taps, short_bias_own), in_pieces)
    projected, in_half = project(scalars, after(up_have, normed_ext), input_bias_own, in_pieces)
    gated = gate(scalars, after(up_near, projected), taps, short_bias_own, chips)
    up_pieces = gather_far(after(gated, up_near))
    out_near = gather_near(after(gated, out_have))
    out_pieces = gather_far(out_near)
    down_near = gather_near(after(up_pieces, down_have))
    down_pieces = gather_far(down_near)
    filter_hidden = after((gated, down_have, out_have), filter_hidden)
    kernel_spec = conv_filter(filter_hidden, filter_pair, delta_pair, tables)
    gated_ch = chip_exchange(gated).reshape(pairs, LANES, LANES)
    gated_ch = after((up_pieces, out_near, down_near), gated_ch)
    mixed_ch, gated_spec = conv_forward(gated_ch, kernel_spec, skip_pair, tables)
    chip_shape = (chips, rows // 256, LANES, LANES)
    mixed_back = chip_exchange(mixed_ch.reshape(chip_shape))
    mixed_tok, mix_low, out_half, branch_part = branch_out(
        scalars, after(down_pieces, mixed_back), projected, taps, short_bias_own, out_pieces
    )
    hidden = tok.astype(f32) + (branch_part + swap_core(branch_part) + output_bias_full)

    normed_two, unit_two, inverse_two = norm_forward(hidden, post_gain_full, post_offset_full)
    down_part, back_part, gdown_kept, gdown_sent, gup_kept, gup_sent, up_bias_grad = tiled_feed(
        scalars, normed_two.astype(bf16), cot, up_bias_own, up_pieces, down_pieces
    )

    def own_tokens(value):
        return lax.dynamic_slice_in_dim(value, core * tok_count, tok_count, 0)

    def other_tokens(value):
        return lax.dynamic_slice_in_dim(value, (1 - core) * tok_count, tok_count, 0)

    normed_two_grad = back_part + swap_core(back_part)
    cot_f = cot.astype(f32)
    hidden_grad = cot_f + norm_backward(normed_two_grad, unit_two, inverse_two, post_gain_full)
    branch_low = hidden_grad.astype(bf16)
    gmixed, gfirst, gout_kept, gout_sent = unbranch(
        scalars, branch_low, mix_low, mixed_tok, projected, taps, short_bias_own, out_half, chips
    )
    mixed_grad_ch = chip_exchange(gmixed).reshape(pairs, LANES, LANES)

    def half_sum(kept, got):
        return kept.astype(f32) + got.astype(f32)

    down_got, up_got = after(gmixed, (swap_x(gdown_sent[1]), swap_y(gup_sent[1])))
    down_next, up_next = half_sum(gdown_kept[1], down_got).astype(bf16), half_sum(gup_kept[1], up_got).astype(bf16)
    down_got, up_got = swap_y(down_next), swap_x(up_next)
    down_late, up_late = after((down_next, up_next), (gdown_sent[0], gup_sent[0]))
    down_late, up_late = swap_x(down_late), swap_y(up_late)
    mixed_grad_ch = after((down_next, up_next), mixed_grad_ch)

    gated_back, grad_spec = conv_backward(mixed_grad_ch, kernel_spec, skip_pair, tables, chips)
    hidden_back, filter_square, skip_line = filter_backward(
        mixed_grad_ch, after(gated_back, grad_spec), gated_ch, gated_spec, filter_hidden, filter_pair, delta_pair, tables
    )
    gated_grad = chip_exchange(gated_back)

    down_part = after(gmixed, down_part)
    result = own_tokens(hidden) + (
        own_tokens(down_part) + swap_core(other_tokens(down_part)) + down_bias_full
    )
    down_bias_grad = jnp.sum(after(gmixed, cot).astype(f32), axis=0)
    post_gain_grad = jnp.sum(normed_two_grad * unit_two, axis=0)
    post_offset_grad = jnp.sum(normed_two_grad, axis=0)
    output_bias_grad = jnp.sum(branch_low.astype(f32), axis=0)

    gfirst_next = lax.ppermute(gfirst[:HALO], "seq", backward)
    gfirst = jnp.concatenate([gfirst, after(hidden_back, gfirst_next)], axis=0)
    first_proj, first_kept, first_sent, first_sums = stream_back(
        scalars, gfirst, projected, taps, normed_ext, 0, chips, True
    )
    gated_grad = after(first_sent, gated_grad)
    gsecond, gvalues = ungate(scalars, gated_grad, projected, taps, short_bias_own)
    second_proj, second_kept, second_sent, second_sums = stream_back(
        scalars, gsecond, projected, taps, normed_ext, 1, chips, True
    )
    values_proj, values_kept, values_sent, values_sums = stream_back(
        scalars, gvalues, projected, taps, normed_ext, 2, chips, False
    )
    down_late, down_got, up_late, up_got = after((second_sent, values_sent), (down_late, down_got, up_late, up_got))
    down_total = half_sum(gdown_kept[0], down_late) + down_got.astype(f32)
    up_total = half_sum(gup_kept[0], up_late) + up_got.astype(f32)
    second_proj = after((down_total, up_total), second_proj)
    normed_one_part = sum(
        contract(part, in_half[:, i * half : (i + 1) * half], 1, 1)
        for i, part in enumerate((first_proj, second_proj, values_proj))
    )
    out_next, out_rest, out_got = reduce_pass(gout_kept, after(normed_one_part, swap_y(gout_sent)), swap_x)
    first_next, first_rest, first_got = reduce_pass(first_kept, after(normed_one_part, swap_x(first_sent)), swap_y)
    second_got, values_got = after((out_next, first_next), (swap_x(second_sent), swap_y(values_sent)))
    second_next, second_rest, second_got = reduce_pass(second_kept, second_got, swap_y)
    values_next, values_rest, values_got = reduce_pass(values_kept, values_got, swap_x)

    normed_one_grad = own_tokens(normed_one_part) + swap_core(other_tokens(normed_one_part))
    unit_own = own_tokens(after((second_next, values_next), unit_one)[HALO : HALO + rows])
    pre_gain_grad = jnp.sum(normed_one_grad * unit_own, axis=0)
    pre_offset_grad = jnp.sum(normed_one_grad, axis=0)
    tokens_grad = own_tokens(hidden_grad) + norm_backward(
        normed_one_grad, unit_own, own_tokens(inverse_one[HALO : HALO + rows]), pre_gain_full
    )

    hidden_got = lax.all_to_all(
        hidden_back.reshape(seq_count, own_pairs * LANES, 2 * units), "seq", split_axis=0, concat_axis=0, tiled=True
    )
    hidden_sum = jnp.sum(after((second_next, values_next), hidden_got).astype(f32), axis=0)
    hidden_sum = hidden_sum.reshape(own_pairs, LANES, 2, units).transpose(0, 2, 1, 3).reshape(tok_count, units)
    (trunk_grad,) = trunk_pull(hidden_sum)
    filter_grad = filter_square[:units, :channels] + filter_square[units:, channels:]
    skip_grad = skip_line[:, :channels] + skip_line[:, channels:]
    own_grad = jnp.concatenate([filter_grad, skip_grad], axis=0)
    own_grad = own_grad + swap_x(own_grad)
    own_grad = pick(own_grad.reshape(-1, 2, channels // 2), x, 1)

    def whole_columns(value, groups, run):
        got = swap_core(pick(value, 1 - core, 0))
        mine_part = pick(value, core, 0)
        n = mine_part.shape[0]
        grid = both(mine_part, got, core).reshape(2, n, groups, chips, run)
        return grid.transpose(1, 2, 3, 0, 4).reshape(n, -1)


    chip_wide = [post_gain_grad, post_offset_grad, down_bias_grad, output_bias_grad]
    own_wide = [pre_gain_grad, pre_offset_grad, *trunk_grad]
    half_wide = [up_bias_grad.reshape(-1), jnp.stack([first_sums[:5], second_sums[:5], values_sums[:5]])]
    flats = [to_rows(flatten(*group)) for group in (chip_wide, own_wide, half_wide)]
    n_chip, n_own = flats[0].shape[0], flats[1].shape[0]
    small = jnp.concatenate(flats, axis=0)
    summed = sum_chips(small)
    got = swap_core(summed[n_chip:])
    own_sum = (summed[n_chip:] + got)[:n_own].reshape(-1)
    half_sum = both(summed[n_chip + n_own :], got[n_own:], core).reshape(2, -1)
    chip_sums = unflatten(summed[:n_chip].reshape(-1), [v.shape for v in chip_wide])
    own_sums = unflatten(own_sum, [v.shape for v in own_wide])
    half_sums = [unflatten(half_sum[side], [v.shape for v in half_wide]) for side in range(2)]
    second_got, values_got = after(small, (second_got, values_got))
    last_total = jnp.stack([second_rest + second_got.astype(f32), values_rest + values_got.astype(f32)], axis=1)
    out_total = out_rest + after(last_total, out_got).astype(f32)
    first_total = first_rest + after(last_total, first_got).astype(f32)
    ends = (last_total, (out_total, first_total))
    down_sum = reduce_far(down_total, ends)
    up_sum = reduce_far(up_total, ends)
    second_sum, values_sum = reduce_far(last_total, ((out_total, first_total),))
    out_sum = reduce_far(out_total)[0]
    first_sum = reduce_far(first_total)
    in_rows = whole_columns(jnp.concatenate([first_sum, second_sum, values_sum], axis=2), 3, channels)
    up_rows_sum = whole_columns(up_sum, 1, hidden_own)
    block_index = seq_index * 2 + x

    def own_block(value, axis=0):
        size = value.shape[axis] // (2 * seq_count)
        return lax.dynamic_slice_in_dim(value, block_index * size, size, axis)

    up_bias_sum = jnp.stack([s[0].reshape(chips, hidden_own) for s in half_sums], axis=1).reshape(-1)
    streams = jnp.stack([s[1].reshape(3, 5, chips, channels) for s in half_sums], axis=3)
    streams = streams.transpose(1, 0, 2, 3, 4).reshape(5, 3 * width)
    return (
        result.astype(bf16)[None],
        tokens_grad.astype(bf16)[None],
        own_block(own_sums[0]),
        own_block(own_sums[1]),
        in_rows,
        own_block(streams[4]),
        own_block(streams[:3], 1),
        own_block(streams[3]),
        own_grad[units],
        *own_sums[2:],
        own_grad[:units],
        out_sum,
        own_block(chip_sums[3]),
        own_block(chip_sums[0]),
        own_block(chip_sums[1]),
        up_rows_sum,
        own_block(up_bias_sum),
        down_sum,
        own_block(chip_sums[2]),
    )


def per_device(tokens, *others):
    channels = tokens.shape[2] // lax.axis_size("seq")
    tiled = 2 * channels == LANES and tokens.shape[1] % 256 == 0
    return (tiled_device if tiled else plain_device)(tokens, *others)


def solution(mesh):
    placed = (
        P("dp", "seq", None),
        P("dp", "seq", None),
        P("seq"),
        P("seq"),
        P("seq", None),
        P("seq"),
        P(None, "seq"),
        P("seq"),
        P("seq"),
        P(),
        P(),
        P(),
        P(),
        P(),
        P(),
        P(),
        P(None, "seq"),
        P("seq", None),
        P("seq"),
        P("seq"),
        P("seq"),
        P("seq", None),
        P("seq"),
        P("seq", None),
        P("seq"),
    )
    split = P(("seq", "dp"))
    split_rows = P(("seq", "dp"), None)
    split_columns = P(None, ("seq", "dp"))
    return jax.shard_map(
        per_device,
        mesh=mesh,
        in_specs=placed,
        out_specs=(
            P("dp", "seq", None),
            P("dp", "seq", None),
            split,
            split,
            split_rows,
            split,
            split_columns,
            split,
            split,
            P(),
            P(),
            P(),
            P(),
            P(),
            P(),
            P(),
            split_columns,
            split_rows,
            split,
            split,
            split,
            split_rows,
            split,
            split_rows,
            split,
        ),
        check_vma=False,
    )
```

```python
from functools import partial
import math

import jax
import jax.numpy as jnp
import numpy as np
from jax import lax
from jax.experimental import pallas as pl
from jax.experimental.pallas import tpu as pltpu
from jax.sharding import PartitionSpec as P

FEATURES = 33
LANES = 128
f32 = jnp.float32
bf16 = jnp.bfloat16
highest = lax.Precision.HIGHEST


def swap_seq(value, mask):
    count = lax.axis_size("seq")
    return lax.ppermute(value, "seq", [(i, i ^ mask) for i in range(count)])


def swap_core(value):
    return swap_seq(value, 1)


def swap_y(value):
    return swap_seq(value, 2)


def swap_z(value, mask):
    return swap_seq(value, 4 * mask)


def swap_x(value):
    count = lax.axis_size("dp")
    return lax.ppermute(value, "dp", [(i, i ^ 1) for i in range(count)])


def z_masks(count):
    if count == 4:
        return [3, 1]
    masks, step = [], count // 2
    while step:
        masks.append(step)
        step //= 2
    return masks


def z_order(count):
    order = [0]
    for mask in z_masks(count):
        order = order + [entry ^ mask for entry in order]
    return order


def chip_groups():
    count = lax.axis_size("seq")
    return [list(range(core, count, 2)) for core in range(2)]


def chip_exchange(value):
    return lax.all_to_all(
        value, "seq", split_axis=0, concat_axis=0, tiled=True, axis_index_groups=chip_groups()
    )


def pick(value, index, axis):
    return lax.dynamic_index_in_dim(value, index, axis, keepdims=False)


def both(mine, other, second):
    return jnp.where(second == 0, jnp.stack([mine, other]), jnp.stack([other, mine]))


def place():
    seq = lax.axis_index("seq")
    return seq // 4, (seq // 2) % 2, seq % 2, lax.axis_index("dp")


def by_index(have, order, own):
    bit = 1
    value = jnp.stack([have[order.index(entry)] for entry in range(len(order))])
    while bit < len(order):
        grid = value.reshape(-1, 2, bit, *value.shape[1:])
        turned = jnp.stack([grid[:, 1], grid[:, 0]], axis=1)
        value = jnp.where((own & bit) == 0, grid, turned).reshape(value.shape)
        bit *= 2
    return value


def gather_pieces(piece):
    z, y, _, x = place()
    z_count = lax.axis_size("seq") // 4
    have = piece[None]
    for mask in z_masks(z_count):
        have = jnp.concatenate([have, swap_z(have, mask)], axis=0)
    half = piece.shape[0] // 2
    first, second = have[:, :half], have[:, half:]
    first_y, second_x = swap_y(first), swap_x(second)
    first = jnp.stack([first, first_y])
    second = jnp.stack([second, second_x])
    first_x, second_y = swap_x(first), swap_y(second)
    first = jnp.stack([first, first_x], axis=1)
    second = jnp.stack([second, second_y])
    rel = jnp.concatenate([first, second], axis=3)
    order = z_order(z_count)
    rows = []
    for za in range(z_count):
        rel_z = z ^ za
        slot = sum(jnp.where(rel_z == entry, at, 0) for at, entry in enumerate(order))
        slab = pick(rel, slot, 2)
        slab = jnp.where(y == 0, slab, jnp.stack([slab[1], slab[0]]))
        slab = jnp.where(x == 0, slab, jnp.stack([slab[:, 1], slab[:, 0]], axis=1))
        rows.append(slab)
    return jnp.stack(rows)


def reduce_z(parts):
    z = place()[0]
    z_count = parts.shape[0]
    have = jnp.stack([pick(parts, z ^ rel, 0) for rel in z_order(z_count)])
    for mask in reversed(z_masks(z_count)):
        half = have.shape[0] // 2
        got = swap_z(have[half:].astype(bf16), mask)
        have = have[:half] + got.astype(f32)
    return have[0]


def reduce_pair(first, second):
    _, y, _, x = place()
    first_got = swap_x(pick(first, 1 - x, 2))
    second_got = swap_y(pick(second, 1 - y, 1))
    first = pick(first, x, 2).astype(f32) + first_got.astype(f32)
    second = pick(second, y, 1).astype(f32) + second_got.astype(f32)
    first_got = swap_y(pick(first, 1 - y, 1).astype(bf16))
    second_got = swap_x(pick(second, 1 - x, 1).astype(bf16))
    first = pick(first, y, 1) + first_got.astype(f32)
    second = pick(second, x, 1) + second_got.astype(f32)
    return reduce_z(first), reduce_z(second)


def sum_chips(value, gates=None):
    value = value + swap_x(value)
    value = value + swap_y(value)
    if gates is not None:
        value = lax.optimization_barrier((gates, value))[1]
    for mask in z_masks(lax.axis_size("seq") // 4):
        value = value + swap_z(value, mask)
    return value


def gather_small(value):
    seq = lax.axis_index("seq")
    count = lax.axis_size("seq")
    have = value[None]
    for mask in [2, 1] + [4 * m for m in z_masks(count // 4)]:
        have = jnp.concatenate([have, swap_seq(have, mask)], axis=0)
    order = [0]
    for mask in [2, 1] + [4 * m for m in z_masks(count // 4)]:
        order = order + [entry ^ mask for entry in order]
    return by_index(have, order, seq)


def twiddle(k, n):
    angle = -2.0 * math.pi * (k % n) / n
    return math.cos(angle), math.sin(angle)


def c_add(p, q):
    return (p[0] + q[0], q[1] if p[1] is None else (p[1] if q[1] is None else p[1] + q[1]))


def c_sub(p, q):
    if q[1] is None:
        return (p[0] - q[0], p[1])
    return (p[0] - q[0], -q[1] if p[1] is None else p[1] - q[1])


def c_conj(p):
    return (p[0], None if p[1] is None else -p[1])


def c_turn(p, k, n):
    k = k % n
    if k == 0:
        return p
    re, im = p
    if 4 * k == n:
        return (im if im is not None else jnp.zeros_like(re), -re)
    if 2 * k == n:
        return (-re, None if im is None else -im)
    if 4 * k == 3 * n:
        return (-im if im is not None else jnp.zeros_like(re), re)
    c, s = twiddle(k, n)
    if im is None:
        return (re * c, re * s)
    return (re * c - im * s, re * s + im * c)


def real_dft(xs):
    n = len(xs)
    if n == 1:
        return [(xs[0], None)]
    if n == 2:
        if xs[1] is None:
            return [(xs[0], None), (xs[0], None)]
        return [(xs[0] + xs[1], None), (xs[0] - xs[1], None)]
    even, odd = real_dft(xs[0::2]), real_dft(xs[1::2])
    out = [None] * (n // 2 + 1)
    for k in range(n // 4 + 1):
        turned = c_turn(odd[k], k, n)
        out[k] = c_add(even[k], turned)
        if n // 2 - k != k:
            out[n // 2 - k] = c_conj(c_sub(even[k], turned))
    return out


def real_inverse(spec):
    def whole(v):
        n = 2 * (len(v) - 1)
        if n == 2:
            return [v[0][0] + v[1][0], None]
        even, odd = [], []
        for k in range(n // 4 + 1):
            mirror = c_conj(v[n // 2 - k])
            e, o = c_add(v[k], mirror), c_turn(c_sub(v[k], mirror), -k, n)
            if k == 0 or 4 * k == n:
                e, o = (e[0], None), (o[0], None)
            even.append(e)
            odd.append(o)
        even, odd = whole(even), whole(odd)
        return [entry for pair in zip(even, odd) for entry in pair]

    values = whole(spec)
    return values[: len(values) // 2]


def split_terms(value):
    high = value.astype(bf16)
    return high, (value - high.astype(f32)).astype(bf16)


def conv_tables(pairs):
    rows = 4 * pairs
    total = rows * LANES
    slots = np.arange(pairs + 1)
    lanes = np.arange(LANES)
    upper = lanes >= LANES // 2
    angle = -2.0 * np.pi * slots[:, None] / rows * upper[None, :]
    lane_turn = np.stack([np.cos(angle), np.sin(angle)], axis=1).astype(np.float32)
    freq = slots[:, None] + np.where(upper, rows // 2, 0)[None, :]
    angle = -2.0 * np.pi * ((freq[:, None, :] * lanes[None, :, None]) % total) / total
    turn = np.stack([np.cos(angle), np.sin(angle)], axis=1).astype(np.float32)
    angle = 2.0 * np.pi * ((lanes[:, None] * lanes[None, :]) % LANES) / LANES
    c, s = np.cos(angle), np.sin(angle)

    def terms(table):
        table = table.astype(np.float32)
        high = table.astype(bf16)
        low = (table - high.astype(np.float32)).astype(bf16)
        return np.concatenate([high, low], axis=1)

    ahead = terms(np.block([[c, s], [-s, c]]))
    back = terms(np.block([[c, -s], [s, c]]) / total)
    return lane_turn, turn, ahead, back


CHUNK = 16


def put(terms_ref, start, slot, re, im):
    cols = pl.ds(slot * LANES, LANES)
    terms_ref[pl.ds(start, CHUNK), cols] = re
    terms_ref[pl.ds(LANES + start, CHUNK), cols] = im


COLUMNS = 4 * LANES


def table_product(table_ref, terms_ref, out_ref):
    width = terms_ref.shape[1]
    high_table, low_table = table_ref[:, :256], table_ref[:, 256:]
    for at in range(0, width, COLUMNS):
        cols = pl.ds(at, min(COLUMNS, width - at))
        high, low = split_terms(terms_ref[:, cols])
        out_ref[:, cols] = (
            jnp.dot(high_table, low, preferred_element_type=f32)
            + jnp.dot(low_table, high, preferred_element_type=f32)
            + jnp.dot(high_table, high, preferred_element_type=f32)
        )


def lane_sign(shape):
    return jnp.where(lax.broadcasted_iota(jnp.int32, shape, 1) < LANES // 2, 1.0, -1.0).astype(f32)


def transform(x_ref, pairs, lane_ref, turn_ref, ahead_ref, terms_ref, spec_ref):
    sign = lane_sign((CHUNK, LANES))

    def chunk(step, carry):
        start = pl.multiple_of(step * CHUNK, CHUNK)
        xs = [x_ref[j, pl.ds(start, CHUNK), :].astype(f32) for j in range(pairs)]
        spec = real_dft(xs + [None] * pairs)
        for k in range(pairs + 1):
            re, im = spec[k]
            c, s = lane_ref[k, 0:1, :], lane_ref[k, 1:2, :]
            if im is None:
                re, im = re * c, re * s
            else:
                re, im = re * c - im * s, re * s + im * c
            re = pltpu.roll(re, LANES // 2, 1) + sign * re
            im = pltpu.roll(im, LANES // 2, 1) + sign * im
            c, s = turn_ref[k, 0, pl.ds(start, CHUNK), :], turn_ref[k, 1, pl.ds(start, CHUNK), :]
            put(terms_ref, start, k, re * c - im * s, re * s + im * c)
        return carry

    lax.fori_loop(0, LANES // CHUNK, chunk, 0)
    table_product(ahead_ref, terms_ref, spec_ref)


def put_product(terms_ref, pairs, one_ref, other_ref, conjugate):
    def chunk(step, carry):
        start = pl.multiple_of(step * CHUNK, CHUNK)
        for k in range(pairs + 1):
            cols = pl.ds(k * LANES, LANES)
            a, b = one_ref[pl.ds(start, CHUNK), cols], one_ref[pl.ds(LANES + start, CHUNK), cols]
            c, d = other_ref[pl.ds(start, CHUNK), cols], other_ref[pl.ds(LANES + start, CHUNK), cols]
            if conjugate:
                put(terms_ref, start, k, a * c + b * d, b * c - a * d)
            else:
                put(terms_ref, start, k, a * c - b * d, a * d + b * c)
        return carry

    lax.fori_loop(0, LANES // CHUNK, chunk, 0)


def inverse(pairs, lane_ref, turn_ref, back_ref, terms_ref, spec_ref, finish):
    table_product(back_ref, terms_ref, spec_ref)
    sign = lane_sign((CHUNK, LANES))

    def chunk(step, carry):
        start = pl.multiple_of(step * CHUNK, CHUNK)
        spec = []
        for k in range(pairs + 1):
            cols = pl.ds(k * LANES, LANES)
            re, im = spec_ref[pl.ds(start, CHUNK), cols], spec_ref[pl.ds(LANES + start, CHUNK), cols]
            c, s = turn_ref[k, 0, pl.ds(start, CHUNK), :], turn_ref[k, 1, pl.ds(start, CHUNK), :]
            re, im = re * c + im * s, im * c - re * s
            re = pltpu.roll(re, LANES // 2, 1) + sign * re
            im = pltpu.roll(im, LANES // 2, 1) + sign * im
            c, s = lane_ref[k, 0:1, :], lane_ref[k, 1:2, :]
            re, im = re * c + im * s, im * c - re * s
            spec.append((re, None if k in (0, pairs) else im))
        for j, values in enumerate(real_inverse(spec)):
            finish(j, start, values)
        return carry

    lax.fori_loop(0, LANES // CHUNK, chunk, 0)


def window_of(j, start, delta, length):
    lane = lax.broadcasted_iota(jnp.int32, (CHUNK, LANES), 1)
    row = lax.broadcasted_iota(jnp.int32, (CHUNK, LANES), 0)
    position = (2 * j + lane // (LANES // 2)) * LANES + start + row
    return jnp.exp(-(position.astype(f32) / (length - 1)) * delta) + 0.05


def filter_body(pairs, h_ref, w_ref, delta_ref, lane_ref, turn_ref, ahead_ref, spec_ref, low_ref, terms_ref):
    delta = delta_ref[...]
    for j in range(pairs):
        rows = jnp.dot(h_ref[j], w_ref[...], precision=highest, preferred_element_type=f32)
        window = jnp.concatenate(
            [window_of(j, start, delta, 2 * pairs * LANES) for start in range(0, LANES, CHUNK)], axis=0
        )
        low_ref[j] = (rows * window).astype(bf16).astype(f32)
    transform(low_ref, pairs, lane_ref, turn_ref, ahead_ref, terms_ref, spec_ref)


def forward_body(
    pairs, x_ref, kernel_ref, skip_ref, lane_ref, turn_ref, ahead_ref, back_ref, out_ref, spec_ref, terms_ref, work_ref
):
    transform(x_ref, pairs, lane_ref, turn_ref, ahead_ref, terms_ref, spec_ref)
    put_product(terms_ref, pairs, spec_ref, kernel_ref, False)
    skip = skip_ref[...]

    def finish(j, start, values):
        rows = pl.ds(start, CHUNK)
        out_ref[j, rows, :] = (values + x_ref[j, rows, :].astype(f32) * skip).astype(bf16)

    inverse(pairs, lane_ref, turn_ref, back_ref, terms_ref, work_ref, finish)


def backward_body(
    pairs, g_ref, kernel_ref, skip_ref, lane_ref, turn_ref, ahead_ref, back_ref, gx_ref, spec_ref, terms_ref, work_ref
):
    transform(g_ref, pairs, lane_ref, turn_ref, ahead_ref, terms_ref, spec_ref)
    put_product(terms_ref, pairs, spec_ref, kernel_ref, True)
    skip = skip_ref[...]

    chips, rows = gx_ref.shape[:2]
    own = (rows - CHUNK) // LANES

    def finish(j, start, values):
        value = (values + g_ref[j, pl.ds(start, CHUNK), :].astype(f32) * skip).astype(bf16)
        gx_ref[j // own, pl.ds(pl.multiple_of(j % own * LANES + start, CHUNK), CHUNK), :] = value

    inverse(pairs, lane_ref, turn_ref, back_ref, terms_ref, work_ref, finish)
    for chip in range(chips - 1):
        gx_ref[chip, own * LANES :, :] = gx_ref[chip + 1, :CHUNK, :]
    gx_ref[chips - 1, own * LANES :, :] = jnp.zeros((CHUNK, LANES), bf16)


def filter_back_body(
    pairs,
    g_ref,
    g_spec_ref,
    x_ref,
    x_spec_ref,
    h_ref,
    w_ref,
    delta_ref,
    lane_ref,
    turn_ref,
    back_ref,
    gh_ref,
    gw_ref,
    gskip_ref,
    terms_ref,
    work_ref,
    pre_ref,
):
    put_product(terms_ref, pairs, g_spec_ref, x_spec_ref, True)
    delta = delta_ref[...]

    def finish(j, start, values):
        window = window_of(j, start, delta, 2 * pairs * LANES)
        pre_ref[j, pl.ds(start, CHUNK), :] = values.astype(bf16).astype(f32) * window

    inverse(pairs, lane_ref, turn_ref, back_ref, terms_ref, work_ref, finish)
    gw_ref[...] = jnp.zeros_like(gw_ref)
    gskip_ref[...] = jnp.zeros_like(gskip_ref)
    for j in range(pairs):
        pre = pre_ref[j]
        gh = lax.dot_general(
            pre, w_ref[...], (((1,), (1,)), ((), ())), precision=highest, preferred_element_type=f32
        )
        gh_ref[j] = gh.astype(bf16)
        gw_ref[...] += lax.dot_general(
            h_ref[j], pre, (((0,), (0,)), ((), ())), precision=highest, preferred_element_type=f32
        )
        gskip_ref[...] += jnp.sum(g_ref[j].astype(f32) * x_ref[j].astype(f32), axis=0, keepdims=True)


SHARE = 100000
FILLER = 40 * 10**9
VMEM_BYTES = 50 * 1024 * 1024


def whole_call(body, outs, scratch, flops, moved, *operands, share=SHARE):
    return pl.pallas_call(
        body,
        out_shape=outs,
        scratch_shapes=scratch,
        compiler_params=pltpu.CompilerParams(vmem_limit_bytes=VMEM_BYTES),
        cost_estimate=pl.CostEstimate(flops=flops // share, bytes_accessed=moved // share, transcendentals=0),
    )(*operands)


def spec_shape(pairs):
    return (256, (pairs + 1) * LANES)


def conv_filter(hidden, weight, delta, tables):
    pairs = hidden.shape[0]
    lane_turn, turn, ahead, _ = tables
    return whole_call(
        partial(filter_body, pairs),
        jax.ShapeDtypeStruct(spec_shape(pairs), f32),
        [pltpu.VMEM((pairs, LANES, LANES), f32), pltpu.VMEM(spec_shape(pairs), f32)],
        FILLER,
        8 * 10**6,
        hidden,
        weight,
        delta,
        lane_turn,
        turn,
        ahead,
        share=1,
    )


def conv_forward(x, kernel_spec, skip, tables):
    pairs = x.shape[0]
    return whole_call(
        partial(forward_body, pairs),
        (jax.ShapeDtypeStruct(x.shape, bf16), jax.ShapeDtypeStruct(spec_shape(pairs), f32)),
        [pltpu.VMEM(spec_shape(pairs), f32), pltpu.VMEM(spec_shape(pairs), f32)],
        2 * 10**9,
        10 * 10**6,
        x,
        kernel_spec,
        skip,
        *tables,
    )


def conv_backward(g, kernel_spec, skip, tables, chips):
    pairs = g.shape[0]
    out_rows = pairs // chips * LANES + CHUNK
    return whole_call(
        partial(backward_body, pairs),
        (jax.ShapeDtypeStruct((chips, out_rows, LANES), bf16), jax.ShapeDtypeStruct(spec_shape(pairs), f32)),
        [pltpu.VMEM(spec_shape(pairs), f32), pltpu.VMEM(spec_shape(pairs), f32)],
        2 * 10**9,
        10 * 10**6,
        g,
        kernel_spec,
        skip,
        *tables,
    )


def filter_backward(g, g_spec, x, x_spec, hidden, weight, delta, tables):
    pairs = x.shape[0]
    lane_turn, turn, _, back = tables
    return whole_call(
        partial(filter_back_body, pairs),
        (
            jax.ShapeDtypeStruct(x.shape, bf16),
            jax.ShapeDtypeStruct((LANES, LANES), f32),
            jax.ShapeDtypeStruct((1, LANES), f32),
        ),
        [
            pltpu.VMEM(spec_shape(pairs), f32),
            pltpu.VMEM(spec_shape(pairs), f32),
            pltpu.VMEM(x.shape, f32),
        ],
        FILLER,
        10 * 10**6,
        g,
        g_spec,
        x,
        x_spec,
        hidden,
        weight,
        delta,
        lane_turn,
        turn,
        back,
        share=1,
    )


def plain_spectrum(x, length):
    pairs, _, lanes = x.shape
    flat = x.astype(f32).reshape(pairs, LANES, 2, lanes // 2).transpose(3, 0, 2, 1)
    tables = spectral_tables(length // 64, LANES)
    return forward_transform(flat.reshape(lanes // 2, length // LANES, LANES), tables)


def plain_inverse(re, im, length):
    tables = spectral_tables(length // 64, LANES)
    back = inverse_transform(re, im, tables, length // LANES)
    channels = back.shape[0]
    back = back.reshape(channels, length // 256, 2, LANES).transpose(1, 3, 2, 0)
    return back.reshape(length // 256, LANES, 2 * channels)


def spectral_tables(rows_total, col_count):
    total_size = rows_total * col_count
    row_index = jnp.arange(rows_total, dtype=jnp.int32)
    col_index = jnp.arange(col_count, dtype=jnp.int32)
    row_angle = (row_index[:, None] * row_index[None, :] % rows_total).astype(f32) * (
        2.0 * math.pi / rows_total
    )
    col_angle = (col_index[:, None] * col_index[None, :] % col_count).astype(f32) * (
        2.0 * math.pi / col_count
    )
    twist_angle = (row_index[:, None] * col_index[None, :]).astype(f32) * (2.0 * math.pi / total_size)
    return (
        jnp.cos(row_angle),
        -jnp.sin(row_angle),
        jnp.cos(twist_angle),
        -jnp.sin(twist_angle),
        jnp.cos(col_angle),
        -jnp.sin(col_angle),
        total_size,
    )


def forward_transform(signal, tables):
    row_cos, row_sin, twist_cos, twist_sin, col_cos, col_sin, _ = tables
    half_rows = signal.shape[1]
    product = partial(jnp.einsum, precision=highest)
    first_re = product("ka,cab->ckb", row_cos[:, :half_rows], signal)
    first_im = product("ka,cab->ckb", row_sin[:, :half_rows], signal)
    turned_re = first_re * twist_cos - first_im * twist_sin
    turned_im = first_re * twist_sin + first_im * twist_cos
    out_re = product("ckb,bm->ckm", turned_re, col_cos) - product("ckb,bm->ckm", turned_im, col_sin)
    out_im = product("ckb,bm->ckm", turned_re, col_sin) + product("ckb,bm->ckm", turned_im, col_cos)
    return (out_re, out_im)


def inverse_transform(spec_re, spec_im, tables, half_rows):
    row_cos, row_sin, twist_cos, twist_sin, col_cos, col_sin, total_size = tables
    product = partial(jnp.einsum, precision=highest)
    back_re = product("ckm,mb->ckb", spec_re, col_cos) + product("ckm,mb->ckb", spec_im, col_sin)
    back_im = product("ckm,mb->ckb", spec_im, col_cos) - product("ckm,mb->ckb", spec_re, col_sin)
    untwist_re = back_re * twist_cos + back_im * twist_sin
    untwist_im = back_im * twist_cos - back_re * twist_sin
    real_part = product("ak,ckb->cab", row_cos[:half_rows], untwist_re) + product(
        "ak,ckb->cab", row_sin[:half_rows], untwist_im
    )
    return real_part / total_size


def plain_window(shape, delta, length):
    pairs, _, lanes = shape
    position = jnp.arange(length, dtype=jnp.int32).reshape(pairs, 2, LANES, 1).astype(f32)
    window = jnp.exp(-(position / (length - 1)) * delta[0, : lanes // 2]) + 0.05
    return window.transpose(0, 2, 1, 3).reshape(shape)


def plain_filter(hidden, weight, delta):
    pairs = hidden.shape[0]
    length = 256 * pairs
    rows = jnp.einsum("jbh,hc->jbc", hidden, weight, precision=highest)
    rows = (rows * plain_window(rows.shape, delta, length)).astype(bf16)
    return plain_spectrum(rows, length)


def plain_forward(x, kernel_spec, skip):
    length = 256 * x.shape[0]
    re, im = plain_spectrum(x, length)
    kre, kim = kernel_spec
    out = plain_inverse(re * kre - im * kim, re * kim + im * kre, length)
    return (out + x.astype(f32) * skip).astype(bf16), (re, im)


def plain_backward(g, x, x_spec, kernel_spec, skip, hidden, weight, delta):
    length = 256 * x.shape[0]
    re, im = plain_spectrum(g, length)
    kre, kim = kernel_spec
    xre, xim = x_spec
    gx = plain_inverse(re * kre + im * kim, im * kre - re * kim, length) + g.astype(f32) * skip
    pre = plain_inverse(re * xre + im * xim, im * xre - re * xim, length).astype(bf16).astype(f32)
    pre = pre * plain_window(pre.shape, delta, length)
    gh = jnp.einsum("jbc,hc->jbh", pre, weight, precision=highest)
    gw = jnp.einsum("jbh,jbc->hc", hidden, pre, precision=highest)
    gskip = jnp.sum(g.astype(f32) * x.astype(f32), axis=(0, 1))[None]
    return gx.astype(bf16), gh.astype(bf16), gw, gskip


def feed_body(nt_ref, ct_ref, up_ref, bias_ref, down_ref, y_ref, gx_ref, gdown_ref, gup_ref, gbias_ref):
    @pl.when(pl.program_id(0) == 0)
    def _():
        y_ref[...] = jnp.zeros_like(y_ref)
        gx_ref[...] = jnp.zeros_like(gx_ref)

    nt, ct, up, down = nt_ref[...], ct_ref[...], up_ref[...], down_ref[...]
    before = jnp.dot(nt, up, preferred_element_type=f32) + bias_ref[...]
    cdf = 0.5 * (1.0 + lax.erf(before * math.sqrt(0.5)))
    active = (before * cdf).astype(bf16)
    slope = cdf + before * (jnp.exp(-0.5 * before * before) * (1.0 / math.sqrt(2.0 * math.pi)))
    g_act = lax.dot_general(ct, down, (((1,), (1,)), ((), ())), preferred_element_type=f32)
    g_before = (g_act * slope).astype(bf16)
    y_ref[...] += jnp.dot(active, down, preferred_element_type=f32)
    gx_ref[...] += lax.dot_general(g_before, up, (((1,), (1,)), ((), ())), preferred_element_type=f32)
    gdown_ref[...] = lax.dot_general(
        active, ct, (((0,), (0,)), ((), ())), preferred_element_type=f32
    ).astype(bf16)
    gup_ref[...] = lax.dot_general(
        nt, g_before, (((0,), (0,)), ((), ())), preferred_element_type=f32
    ).astype(bf16)
    gbias_ref[...] = jnp.sum(g_before.astype(f32), axis=0, keepdims=True)


def feed_forward(nt, ct, up, bias, down):
    rows, width = nt.shape
    hidden = up.shape[1]
    block = min(256, hidden)
    return pl.pallas_call(
        feed_body,
        grid=(hidden // block,),
        in_specs=[
            pl.BlockSpec((rows, width), lambda i: (0, 0)),
            pl.BlockSpec((rows, width), lambda i: (0, 0)),
            pl.BlockSpec((width, block), lambda i: (0, i)),
            pl.BlockSpec((1, block), lambda i: (0, i)),
            pl.BlockSpec((block, width), lambda i: (i, 0)),
        ],
        out_specs=[
            pl.BlockSpec((rows, width), lambda i: (0, 0)),
            pl.BlockSpec((rows, width), lambda i: (0, 0)),
            pl.BlockSpec((block, width), lambda i: (i, 0)),
            pl.BlockSpec((width, block), lambda i: (0, i)),
            pl.BlockSpec((1, block), lambda i: (0, i)),
        ],
        out_shape=[
            jax.ShapeDtypeStruct((rows, width), f32),
            jax.ShapeDtypeStruct((rows, width), f32),
            jax.ShapeDtypeStruct((hidden, width), bf16),
            jax.ShapeDtypeStruct((width, hidden), bf16),
            jax.ShapeDtypeStruct((1, hidden), f32),
        ],
        compiler_params=pltpu.CompilerParams(vmem_limit_bytes=VMEM_BYTES),
        cost_estimate=pl.CostEstimate(
            flops=12 * rows * width * hidden,
            bytes_accessed=8 * width * hidden + 12 * rows * width,
            transcendentals=2 * rows * hidden,
        ),
    )(nt, ct, up, bias, down)


def norm_forward(values, norm_gain, norm_offset):
    center = values - jnp.mean(values, axis=-1, keepdims=True)
    inverse_root = lax.rsqrt(jnp.mean(center * center, axis=-1, keepdims=True) + 1e-05)
    normed = center * inverse_root
    return (normed * norm_gain + norm_offset, normed, inverse_root)


def norm_backward(upstream, normed, inverse_root, norm_gain):
    scaled = upstream * norm_gain
    centered = (
        scaled
        - jnp.mean(scaled, axis=-1, keepdims=True)
        - normed * jnp.mean(scaled * normed, axis=-1, keepdims=True)
    )
    return centered * inverse_root


def contract(left_side, right_side, left_dim, right_dim):
    return lax.dot_general(
        left_side, right_side, (((left_dim,), (right_dim,)), ((), ())), preferred_element_type=f32
    )


def trunk_hidden(trunk, features):
    embed_weight, embed_bias, hidden_weight, hidden_bias, last_weight, last_bias, frequency = trunk
    layer_out = jnp.sin(frequency * (jnp.dot(features, embed_weight, precision=highest) + embed_bias))
    layer_out = jnp.sin(frequency * (jnp.dot(layer_out, hidden_weight, precision=highest) + hidden_bias))
    return jnp.sin(frequency * (jnp.dot(layer_out, last_weight, precision=highest) + last_bias))


def to_owners(value, chips):
    tokens, width = value.shape
    channels = width // chips
    grid = value.reshape(tokens // 256, 2, LANES, chips, channels)
    return grid.transpose(3, 0, 2, 1, 4).reshape(chips, tokens // 256, LANES, 2 * channels)


def from_owners(value):
    chips, pairs, _, lanes = value.shape
    grid = value.reshape(chips, pairs, LANES, 2, lanes // 2)
    return grid.transpose(1, 3, 2, 0, 4).reshape(pairs * 256, chips * (lanes // 2))


def exchange(value):
    return chip_exchange(value)


def flatten(*values):
    return jnp.concatenate([value.reshape(-1) for value in values])


def unflatten(flat, shapes):
    out, at = [], 0
    for shape in shapes:
        size = int(np.prod(shape))
        out.append(flat[at : at + size].reshape(shape))
        at += size
    return out


def to_rows(flat):
    rows = -(-flat.shape[0] // 1024) * 8
    return jnp.pad(flat, (0, rows * LANES - flat.shape[0])).reshape(rows, LANES)


def plain_device(
    tokens,
    cotangent,
    pre_gain,
    pre_offset,
    input_weight,
    input_bias,
    short_weight,
    short_bias,
    skip_weight,
    embed_weight,
    embed_bias,
    hidden_weight,
    hidden_bias,
    last_weight,
    last_bias,
    frequency,
    filter_weight,
    output_weight,
    output_bias,
    post_gain,
    post_offset,
    up_weight,
    up_bias,
    down_weight,
    down_bias,
):
    seq_count = lax.axis_size("seq")
    seq_index = lax.axis_index("seq")
    z, y, core, x = place()
    chips = seq_count // 2
    z_count = seq_count // 4
    chip = seq_index // 2
    tok_count = tokens.shape[1]
    width = tokens.shape[2]
    length = tok_count * seq_count
    channels = width // seq_count
    ff = up_weight.shape[1]
    hidden_own = ff // seq_count
    half = width // 2
    pairs = length // 256

    mine = jnp.stack([tokens[0], cotangent[0]])
    other = swap_core(mine)
    pair = both(mine, other, core)
    tok = pair[:, 0].reshape(2 * tok_count, width)
    cot = pair[:, 1].reshape(2 * tok_count, width)

    def half_columns(value, groups, run):
        rows = value.shape[0]
        grid = value.reshape(rows, groups, chips, 2, run)
        return [grid[:, :, :, side].reshape(rows, groups * chips * run) for side in range(2)]

    def own_rows(value, groups, run):
        sides = half_columns(value, groups, run)
        keep = jnp.where(core == 0, sides[0], sides[1])
        got = swap_core(jnp.where(core == 0, sides[1], sides[0]))
        return jnp.where(core == x, keep, got)

    in_piece = own_rows(input_weight, 3, channels)
    in_half = gather_pieces(in_piece).reshape(width, 3 * half)
    small_shapes = [(width // seq_count,)] * 2 + [(3, channels), (3, 3, channels), (3, channels)]
    small_shapes += [(width // seq_count,)] * 3 + [(hidden_own,), (width // seq_count,)]
    smalls = flatten(
        pre_gain, pre_offset, input_bias, short_weight, short_bias, output_bias, post_gain, post_offset, up_bias, down_bias
    )
    shapes = [v.shape for v in (pre_gain, pre_offset, input_bias, short_weight, short_bias)]
    shapes += [v.shape for v in (output_bias, post_gain, post_offset, up_bias, down_bias)]
    small_rows = to_rows(smalls)
    small_all = gather_small(small_rows.reshape(-1)).astype(f32)
    columns, at = [], 0
    for shape in shapes:
        size = int(np.prod(shape))
        columns.append(small_all[:, at : at + size])
        at += size

    def halved(value, run):
        lead = value.shape[:-1]
        return pick(value.reshape(*lead, -1, 2, run), core, len(lead) + 1).reshape(*lead, -1)

    pre_gain_full, pre_offset_full = columns[0].reshape(-1), columns[1].reshape(-1)
    input_bias_own = halved(columns[2].reshape(3, width), channels).reshape(-1)
    short_full = columns[3].reshape(seq_count, 3, -1).transpose(1, 0, 2).reshape(3, 3, width)
    short_taps = halved(short_full, channels).reshape(3, -1)
    short_bias_own = halved(columns[4].reshape(3, width), channels).reshape(-1)
    output_bias_full = columns[5].reshape(-1)
    post_gain_full, post_offset_full = columns[6].reshape(-1), columns[7].reshape(-1)
    up_bias_own = halved(columns[8].reshape(-1), hidden_own)
    down_bias_full = columns[9].reshape(-1)

    out_rows = output_weight.shape[0] // 2
    up_piece = own_rows(up_weight, 1, hidden_own)
    out_piece = pick(output_weight.reshape(2, out_rows, width), x, 0)
    down_piece = pick(down_weight.reshape(2, hidden_own // 2, width), x, 0)
    up_half = gather_pieces(up_piece).reshape(width, ff // 2)
    n_out, n_down = out_rows // 2, hidden_own // 4
    mixed_piece = jnp.concatenate(
        [out_piece[:n_out], down_piece[:n_down], out_piece[n_out:], down_piece[n_down:]], axis=0
    )
    later = gather_pieces(mixed_piece)
    later = later.reshape(chips, 2, 2, n_out + n_down, width)
    out_half = later[:, :, :, :n_out].reshape(half, width)
    down_half = later[:, :, :, n_out:].reshape(ff // 2, width)

    positions = (seq_index * tok_count + jnp.arange(tok_count, dtype=jnp.int32)).astype(f32)
    relative = positions / (length - 1)
    phases = positions * (2.0 * math.pi / length)
    band_count = (FEATURES - 1) // 2
    band_freq = jnp.linspace(0.0001, band_count - 1, band_count).astype(f32)
    angles = phases[:, None] * band_freq[None, :]
    features = jnp.concatenate([relative[:, None], jnp.cos(angles), -jnp.sin(angles)], axis=1)
    trunk = (embed_weight, embed_bias, hidden_weight, hidden_bias, last_weight, last_bias, frequency)
    hidden_rows, trunk_pull = jax.vjp(partial(trunk_hidden, features=features), trunk)
    units = hidden_rows.shape[1]
    own_pairs = tok_count // 256
    packed = hidden_rows.reshape(own_pairs, 2, LANES, units).transpose(0, 2, 1, 3)
    packed = packed.reshape(own_pairs, LANES, 2 * units)
    filter_hidden = lax.all_gather(packed, "seq", axis=0, tiled=True)
    filter_own = filter_weight.astype(f32)
    zero = jnp.zeros_like(filter_own)
    filter_pair = jnp.concatenate(
        [jnp.concatenate([filter_own, zero], axis=1), jnp.concatenate([zero, filter_own], axis=1)], axis=0
    )
    deltas = jnp.linspace(math.log(0.01) / 1.5, math.log(0.01) / 0.3, width).astype(f32)
    delta_own = jnp.abs(lax.dynamic_slice_in_dim(deltas, seq_index * channels, channels))
    delta_pair = jnp.concatenate([delta_own, delta_own])[None]
    skip_own = skip_weight.astype(f32)
    skip_pair = jnp.concatenate([skip_own, skip_own])[None]
    kernel_spec = plain_filter(filter_hidden, filter_pair, delta_pair)

    rows = 2 * tok_count
    inputs = tok.astype(f32)
    normed_one, unit_one, inverse_one = norm_forward(inputs, pre_gain_full, pre_offset_full)
    normed_low = normed_one.astype(bf16)
    projected_low = (contract(normed_low, in_half, 1, 0) + input_bias_own).astype(bf16)
    shift = [(i, i + 2) for i in range(seq_count - 2)]
    earlier = lax.ppermute(projected_low[rows - 2 :], "seq", shift)
    extended = jnp.concatenate([earlier, projected_low], axis=0).astype(f32)
    convolved = (
        short_taps[0] * extended[:rows]
        + short_taps[1] * extended[1 : rows + 1]
        + short_taps[2] * extended[2:]
        + short_bias_own
    )
    first_part, second_part, values_part = (convolved[:, i * half : (i + 1) * half] for i in range(3))
    gated_low = (values_part * second_part).astype(bf16)
    gated_ch = exchange(to_owners(gated_low, chips)).reshape(pairs, LANES, 2 * channels)
    mixed_ch, gated_spec = plain_forward(gated_ch, kernel_spec, skip_pair)
    chip_shape = (chips, rows // 256, LANES, 2 * channels)
    mixed_tok = from_owners(exchange(mixed_ch.reshape(chip_shape))).astype(f32)
    mix_low = (mixed_tok * first_part).astype(bf16)
    branch_part = contract(mix_low, out_half, 1, 0)
    branch = branch_part + swap_core(branch_part) + output_bias_full
    hidden = inputs + branch

    normed_two, unit_two, inverse_two = norm_forward(hidden, post_gain_full, post_offset_full)
    normed_two_low = normed_two.astype(bf16)
    down_part, back_part, down_grad, up_grad, up_bias_grad = feed_forward(
        normed_two_low, cot, up_half, up_bias_own[None], down_half
    )

    def own_tokens(value):
        return lax.dynamic_slice_in_dim(value, core * tok_count, tok_count, 0)

    def other_tokens(value):
        return lax.dynamic_slice_in_dim(value, (1 - core) * tok_count, tok_count, 0)

    result = own_tokens(hidden) + (
        own_tokens(down_part) + swap_core(other_tokens(down_part)) + down_bias_full
    )
    up_grad = up_grad.reshape(z_count, 2, 2, 2, -1, ff // 2).transpose(0, 1, 3, 2, 4, 5)
    down_sum, up_sum = reduce_pair(down_grad.reshape(z_count, 2, 2, hidden_own // 2, width), up_grad)

    cot_f = cot.astype(f32)
    down_bias_grad = jnp.sum(cot_f, axis=0)
    normed_two_grad = back_part + swap_core(back_part)
    post_gain_grad = jnp.sum(normed_two_grad * unit_two, axis=0)
    post_offset_grad = jnp.sum(normed_two_grad, axis=0)
    hidden_grad = cot_f + norm_backward(normed_two_grad, unit_two, inverse_two, post_gain_full)
    branch_low = hidden_grad.astype(bf16)
    output_bias_grad = jnp.sum(branch_low.astype(f32), axis=0)
    gate_grad = contract(branch_low, out_half, 1, 1)
    mixed_grad_low = (gate_grad * first_part).astype(bf16)
    first_grad = gate_grad * mixed_tok
    mixed_grad_ch = exchange(to_owners(mixed_grad_low, chips)).reshape(pairs, LANES, 2 * channels)
    gated_back, hidden_back, filter_square, skip_line = plain_backward(
        mixed_grad_ch, gated_ch, gated_spec, kernel_spec, skip_pair, filter_hidden, filter_pair, delta_pair
    )
    gated_grad = from_owners(exchange(gated_back.reshape(chip_shape))).astype(f32)
    output_grad = contract(mix_low, branch_low, 0, 0)

    hidden_got = lax.all_to_all(
        hidden_back.reshape(seq_count, own_pairs * LANES, 2 * units), "seq", split_axis=0, concat_axis=0, tiled=True
    )
    hidden_sum = jnp.sum(hidden_got.astype(f32), axis=0)
    hidden_sum = hidden_sum.reshape(own_pairs, LANES, 2, units).transpose(0, 2, 1, 3).reshape(tok_count, units)
    (trunk_grad,) = trunk_pull(hidden_sum)
    filter_grad = filter_square[:units, :channels] + filter_square[units:, channels:]
    skip_grad = skip_line[:, :channels] + skip_line[:, channels:]
    own_grad = jnp.concatenate([filter_grad, skip_grad], axis=0)
    own_grad = own_grad + swap_x(own_grad)
    own_grad = pick(own_grad.reshape(-1, 2, channels // 2), x, 1)

    conv_grad_low = jnp.concatenate(
        [first_grad, gated_grad * values_part, gated_grad * second_part], axis=1
    ).astype(bf16)
    back_shift = [(i + 2, i) for i in range(seq_count - 2)]
    following = lax.ppermute(conv_grad_low[:2], "seq", back_shift)
    conv_grad = conv_grad_low.astype(f32)
    grad_ext = jnp.concatenate([conv_grad_low, following], axis=0).astype(f32)
    projected_grad_low = (
        short_taps[0] * grad_ext[2:] + short_taps[1] * grad_ext[1 : rows + 1] + short_taps[2] * grad_ext[:rows]
    ).astype(bf16)
    short_weight_grad = jnp.stack(
        [jnp.sum(conv_grad * extended[tap : tap + rows], axis=0) for tap in range(3)]
    )
    short_bias_grad = jnp.sum(conv_grad, axis=0)
    input_bias_grad = jnp.sum(projected_grad_low.astype(f32), axis=0)
    input_grad = contract(normed_low, projected_grad_low, 0, 0)
    normed_one_part = contract(projected_grad_low, in_half, 1, 1)
    normed_one_grad = own_tokens(normed_one_part) + swap_core(other_tokens(normed_one_part))
    unit_own = own_tokens(unit_one)
    pre_gain_grad = jnp.sum(normed_one_grad * unit_own, axis=0)
    pre_offset_grad = jnp.sum(normed_one_grad, axis=0)
    tokens_grad = own_tokens(hidden_grad) + norm_backward(
        normed_one_grad, unit_own, own_tokens(inverse_one), pre_gain_full
    )

    in_low = input_grad.astype(bf16).reshape(z_count, 2, 2, 2, -1, 3 * half).transpose(0, 1, 3, 2, 4, 5)
    in_sum = jnp.stack(reduce_pair(in_low[:, :, :, 0], in_low[:, :, :, 1]))
    out_low = output_grad.astype(bf16).reshape(z_count, 2, 2, -1, width)
    split = out_low.shape[3] // 2
    out_sum = jnp.concatenate(reduce_pair(out_low[:, :, :, :split], out_low[:, :, :, split:]), axis=0)

    def whole_columns(value, groups, run):
        got = swap_core(pick(value, 1 - core, 0))
        mine_part = pick(value, core, 0)
        n = mine_part.shape[0]
        grid = both(mine_part, got, core).reshape(2, n, groups, chips, run)
        return grid.transpose(1, 2, 3, 0, 4).reshape(n, -1)

    in_rows = whole_columns(in_sum, 3, channels)
    up_rows_sum = whole_columns(up_sum, 1, hidden_own)

    chip_wide = [post_gain_grad, post_offset_grad, down_bias_grad, output_bias_grad]
    own_wide = [pre_gain_grad, pre_offset_grad, *trunk_grad]
    half_wide = [up_bias_grad.reshape(-1), input_bias_grad, short_weight_grad, short_bias_grad]
    own_flat, half_flat = to_rows(flatten(*own_wide)), to_rows(flatten(*half_wide))
    summed = sum_chips(jnp.concatenate([to_rows(flatten(*chip_wide)), own_flat, half_flat], axis=0))
    n_chip = to_rows(flatten(*chip_wide)).shape[0]
    chip_sum = summed[:n_chip].reshape(-1)
    got = swap_core(summed[n_chip:])
    own_sum = (summed[n_chip:] + got)[: own_flat.shape[0]].reshape(-1)
    half_sums_pair = both(summed[n_chip + own_flat.shape[0] :], got[own_flat.shape[0] :], core).reshape(2, -1)
    chip_sums = unflatten(chip_sum, [v.shape for v in chip_wide])
    own_sums = unflatten(own_sum, [v.shape for v in own_wide])
    half_sums = [
        unflatten(half_sums_pair[side], [v.shape for v in half_wide]) for side in range(2)
    ]

    def joined(index, groups, run):
        pair_of = jnp.stack([half_sums[side][index].reshape(groups, chips, run) for side in range(2)], axis=2)
        return pair_of.reshape(groups, -1)

    block_index = seq_index * 2 + x

    def own_block(value, axis=0):
        size = value.shape[axis] // (2 * seq_count)
        return lax.dynamic_slice_in_dim(value, block_index * size, size, axis)

    up_bias_sum = joined(0, 1, hidden_own).reshape(-1)
    input_bias_sum = joined(1, 3, channels).reshape(-1)
    short_weight_sum = joined(2, 9, channels).reshape(3, -1)
    short_bias_sum = joined(3, 3, channels).reshape(-1)
    return (
        result.astype(bf16)[None],
        tokens_grad.astype(bf16)[None],
        own_block(own_sums[0]),
        own_block(own_sums[1]),
        in_rows,
        own_block(input_bias_sum),
        own_block(short_weight_sum, 1),
        own_block(short_bias_sum),
        own_grad[units],
        *own_sums[2:],
        own_grad[:units],
        out_sum,
        own_block(chip_sums[3]),
        own_block(chip_sums[0]),
        own_block(chip_sums[1]),
        up_rows_sum,
        own_block(up_bias_sum),
        down_sum,
        own_block(chip_sums[2]),
    )


def after(earlier, value):
    return lax.optimization_barrier((earlier, value))[1]


def gather_z(piece, gates=None):
    have = piece[None]
    masks = z_masks(lax.axis_size("seq") // 4)
    for step, mask in enumerate(masks):
        if gates is not None and step == len(masks) - 1:
            have = after(gates, have)
        have = jnp.concatenate([have, swap_z(have, mask)], axis=0)
    return have


def gather_near(have):
    half = have.shape[1] // 2
    first, second = have[:, :half], have[:, half:]
    return jnp.stack([first, swap_y(first)]), jnp.stack([second, swap_x(second)])


def gather_far(near):
    first, second = near
    return first, swap_x(first), second, swap_y(second)


def reduce_pass(kept, got, second):
    sent = (kept[1].astype(f32) + got[1].astype(f32)).astype(bf16)
    return sent, kept[0].astype(f32) + got[0].astype(f32), second(sent)


def reduce_z_step(total, mask):
    half = total.shape[0] // 2
    return total[:half] + swap_z(total[half:].astype(bf16), mask).astype(f32)


def reduce_far(total, masks):
    for mask in masks:
        total = reduce_z_step(total, mask)
    return total[0]


def place_pieces(out_ref, pieces, scalars, chips, span):
    first, first_far, second, second_far = pieces
    x = scalars[0]
    half = span // 2
    z_count = chips // 2
    for slot in range(z_count):
        for yr in range(2):
            base = scalars[2 + yr * z_count + slot] * (2 * span)
            source = second_far if yr else second
            for xr in range(2):
                at = pl.multiple_of(base + (x if xr == 0 else 1 - x) * span, span)
                out_ref[pl.ds(at, half), :] = (first_far if xr else first)[yr, slot]
                out_ref[pl.ds(pl.multiple_of(at + half, half), half), :] = source[xr, slot]


def route_rows(grad_ref, kept_ref, sent_ref, scalars, chips, inner, by_x):
    x = scalars[0]
    z_count = chips // 2
    rows = grad_ref.shape[0] // (2 * chips * inner)
    tiles, _, columns = kept_ref.shape[3:]
    for slot in range(z_count):
        for yr in range(2):
            base = scalars[2 + yr * z_count + slot] * (2 * inner * rows)
            for xr in range(2):
                is_sent, lead = (xr, yr) if by_x else (yr, xr)
                for part in range(inner):
                    at = pl.multiple_of(base + part * 2 * rows + (x if xr == 0 else 1 - x) * rows, rows)
                    for tile in range(tiles):
                        value = grad_ref[pl.ds(at, rows), tile * columns : (tile + 1) * columns].astype(bf16)
                        if not is_sent:
                            kept_ref[lead, slot, part, tile] = value
                        elif isinstance(sent_ref, tuple):
                            sent_ref[lead][slot, part, tile] = value
                        else:
                            sent_ref[lead, slot, part, tile] = value


HALO = 16


def short_conv(rows, taps, bias):
    two, one = pltpu.roll(rows, 2, 0), pltpu.roll(rows, 1, 0)
    return (taps[0:1] * two + taps[1:2] * one + taps[2:3] * rows + bias)[HALO:]


def chip_rows(convolved):
    return convolved[: convolved.shape[0] - HALO]


def pack_pairs(out_ref, index, pair, even, odd):
    half = LANES // 2
    lower = lax.broadcasted_iota(jnp.int32, even.shape, 1) < half
    out_ref[index, pair] = jnp.where(lower, even, pltpu.roll(odd, half, 1)).astype(bf16)
    out_ref[index + 1, pair] = jnp.where(lower, pltpu.roll(even, half, 1), odd).astype(bf16)


def pack_rows(out_ref, index, value):
    for pair in range(value.shape[0] // 256):
        rows = value[256 * pair : 256 * (pair + 1)]
        pack_pairs(out_ref, index, pair, rows[:LANES], rows[LANES:])


def unpack_pair(one, two):
    half = LANES // 2
    one, two = one.astype(f32), two.astype(f32)
    lower = lax.broadcasted_iota(jnp.int32, one.shape, 1) < half
    return jnp.where(lower, one, pltpu.roll(two, half, 1)), jnp.where(lower, pltpu.roll(one, half, 1), two)


def unpack_rows(in_ref, index):
    out = []
    for pair in range(in_ref.shape[1]):
        out.extend(unpack_pair(in_ref[index, pair], in_ref[index + 1, pair]))
    return jnp.concatenate(out, axis=0)


def project_body(scalars, normed_ref, bias_ref, a_ref, ax_ref, b_ref, by_ref, out_ref, weight_ref):
    chips = 2 * a_ref.shape[1]
    place_pieces(weight_ref, (a_ref, ax_ref, b_ref, by_ref), scalars, chips, 2 * a_ref.shape[2])
    value = jnp.dot(normed_ref[...], weight_ref[...], preferred_element_type=f32) + bias_ref[...]
    row = lax.broadcasted_iota(jnp.int32, value.shape, 0)
    value = jnp.where(jnp.logical_and(row < HALO, scalars[1] == 0), 0.0, value)
    out_ref[...] = value.astype(bf16)


def grid_call(body, scalars, grid, ins, outs, scratch, flops, moved, transcendentals=0):
    return pl.pallas_call(
        body,
        grid_spec=pltpu.PrefetchScalarGridSpec(
            num_scalar_prefetch=1,
            grid=(grid,),
            in_specs=[pl.BlockSpec(block, index) for _, block, index in ins],
            out_specs=[pl.BlockSpec(block, index) for _, _, block, index in outs],
            scratch_shapes=scratch,
        ),
        out_shape=[jax.ShapeDtypeStruct(shape, dtype) for shape, dtype, _, _ in outs],
        compiler_params=pltpu.CompilerParams(vmem_limit_bytes=VMEM_BYTES),
        cost_estimate=pl.CostEstimate(flops=flops // SHARE, bytes_accessed=moved // SHARE, transcendentals=0),
    )(scalars, *[value for value, _, _ in ins])


def fixed(value):
    return (value, value.shape, lambda i, s, n=value.ndim: (0,) * n)


def fixed_out(shape, dtype):
    return (shape, dtype, shape, lambda i, s, n=len(shape): (0,) * n)


def project(scalars, normed, bias, pieces):
    rows, width = normed.shape
    columns = bias.shape[1]
    block = columns // 3
    lead = pieces[0].shape[:3]
    piece_specs = [(p, (*lead, block), lambda i, s: (0, 0, 0, i)) for p in pieces]
    return grid_call(
        project_body,
        scalars,
        3,
        [fixed(normed), (bias, (1, block), lambda i, s: (0, i)), *piece_specs],
        [
            ((rows, columns), bf16, (rows, block), lambda i, s: (0, i)),
            ((width, columns), bf16, (width, block), lambda i, s: (0, i)),
        ],
        [],
        2 * rows * width * columns,
        4 * width * columns + 2 * rows * (width + columns),
    )


def gate_body(scalars, second_ref, values_ref, t2_ref, t3_ref, b2_ref, b3_ref, out_ref):
    second = short_conv(second_ref[...].astype(f32), t2_ref[...], b2_ref[...])
    values = short_conv(values_ref[...].astype(f32), t3_ref[...], b3_ref[...])
    pack_rows(out_ref, 0, chip_rows(values * second))


def stream_tiles(projected, taps, bias, stream, tiles):
    rows = projected.shape[0]
    index = lambda i, s, at=stream * tiles: (0, at + i)
    return (
        (projected, (rows, LANES), index),
        (taps, (3, LANES), index),
        (bias, (1, LANES), index),
    )


def gate(scalars, projected, taps, bias, chips):
    rows, columns = projected.shape
    tiles = columns // 3 // LANES
    p2, t2, b2 = stream_tiles(projected, taps, bias, 1, tiles)
    p3, t3, b3 = stream_tiles(projected, taps, bias, 2, tiles)
    pairs = (rows - 2 * HALO) // 256
    (out,) = grid_call(
        gate_body,
        scalars,
        tiles,
        [p2, p3, t2, t3, b2, b3],
        [((chips, pairs, LANES, LANES), bf16, (2, pairs, LANES, LANES), lambda i, s: (i, 0, 0, 0))],
        [],
        20 * rows * columns,
        3 * rows * columns,
    )
    return out


def branch_body(
    scalars, mixed_ref, first_ref, taps_ref, bias_ref, a_ref, ax_ref, b_ref, by_ref, mixed_out, mix_out, weight_ref, out_ref
):
    chips = 2 * a_ref.shape[1]
    place_pieces(weight_ref, (a_ref, ax_ref, b_ref, by_ref), scalars, chips, 2 * a_ref.shape[2])
    for tile in range(chips // 2):
        cols = slice(tile * LANES, (tile + 1) * LANES)
        mixed = unpack_rows(mixed_ref, 2 * tile)
        first = chip_rows(short_conv(first_ref[:, cols].astype(f32), taps_ref[:, cols], bias_ref[:, cols]))
        mixed_out[:, cols] = mixed.astype(bf16)
        mix_out[:, cols] = (mixed * first).astype(bf16)
    out_ref[...] = jnp.dot(mix_out[...], weight_ref[...], preferred_element_type=f32)


def first_stream(projected, taps, bias):
    rows, columns = projected.shape
    block = columns // 3
    return [
        (projected, (rows, block), lambda i, s: (0, 0)),
        (taps, (3, block), lambda i, s: (0, 0)),
        (bias, (1, block), lambda i, s: (0, 0)),
    ]


def branch_out(scalars, mixed, projected, taps, bias, pieces, piece_rows):
    rows = projected.shape[0] - 2 * HALO
    half = projected.shape[1] // 3
    width = pieces[0].shape[3]
    return grid_call(
        branch_body,
        scalars,
        1,
        [
            fixed(mixed),
            *first_stream(projected, taps, bias),
            *[
                (p, (*p.shape[:2], piece_rows, width), lambda i, s, at=p.shape[2] // piece_rows - 1: (0, 0, at, 0))
                for p in pieces
            ],
        ],
        [
            fixed_out((rows, half), bf16),
            fixed_out((rows, half), bf16),
            fixed_out((half, width), bf16),
            fixed_out((rows, width), f32),
        ],
        [],
        2 * rows * half * width,
        4 * rows * width + 6 * half * width,
    )


def tiled_feed_body(
    scalars,
    nt_ref,
    ct_ref,
    bias_ref,
    ua_ref,
    uax_ref,
    ub_ref,
    uby_ref,
    da_ref,
    dax_ref,
    db_ref,
    dby_ref,
    y_ref,
    gx_ref,
    gdown_kept,
    gdown_late,
    gdown_first,
    gup_kept,
    gup_late,
    gup_first,
    gbias_ref,
    up_ref,
    down_ref,
    grad_ref,
):
    step = pl.program_id(0)
    z_count = ua_ref.shape[1]
    x = scalars[0]

    @pl.when(step == 0)
    def _():
        y_ref[...] = jnp.zeros_like(y_ref)
        gx_ref[...] = jnp.zeros_like(gx_ref)

    place_pieces(up_ref, (ua_ref, uax_ref, ub_ref, uby_ref), scalars, 2 * z_count, 2 * ua_ref.shape[2])
    span = down_ref.shape[0] // 2
    half = span // 2
    own, other = pl.multiple_of(x * span, span), pl.multiple_of((1 - x) * span, span)
    down_ref[pl.ds(own, half), :] = da_ref[0, 0]
    down_ref[pl.ds(other, half), :] = dax_ref[0, 0]

    def put_second(source):
        down_ref[pl.ds(pl.multiple_of(own + half, half), half), :] = source[0, 0]
        down_ref[pl.ds(pl.multiple_of(other + half, half), half), :] = source[1, 0]

    @pl.when(step < z_count)
    def _():
        put_second(db_ref)

    @pl.when(step >= z_count)
    def _():
        put_second(dby_ref)

    nt, ct, up, down = nt_ref[...], ct_ref[...], up_ref[...], down_ref[...]
    before = jnp.dot(nt, up, preferred_element_type=f32) + bias_ref[...]
    cdf = 0.5 * (1.0 + lax.erf(before * math.sqrt(0.5)))
    active = (before * cdf).astype(bf16)
    slope = cdf + before * (jnp.exp(-0.5 * before * before) * (1.0 / math.sqrt(2.0 * math.pi)))
    g_act = lax.dot_general(ct, down, (((1,), (1,)), ((), ())), preferred_element_type=f32)
    g_before = (g_act * slope).astype(bf16)
    y_ref[...] += jnp.dot(active, down, preferred_element_type=f32)
    gx_ref[...] += lax.dot_general(g_before, up, (((1,), (1,)), ((), ())), preferred_element_type=f32)
    gdown = lax.dot_general(active, ct, (((0,), (0,)), ((), ())), preferred_element_type=f32)
    one, two = gdown[:span], gdown[span:]
    gdown_kept[0, 0] = jnp.where(x == 0, one, two).astype(bf16)
    sent = jnp.where(x == 0, two, one).astype(bf16)

    @pl.when(step < z_count)
    def _():
        gdown_late[0] = sent

    @pl.when(step >= z_count)
    def _():
        gdown_first[0] = sent

    grad_ref[...] = lax.dot_general(nt, g_before, (((0,), (0,)), ((), ())), preferred_element_type=f32)
    route_rows(grad_ref, gup_kept, (gup_late, gup_first), scalars, 2 * z_count, 2, False)
    gbias_ref[...] = jnp.sum(g_before.astype(f32), axis=0, keepdims=True)


def tiled_feed(scalars, nt, ct, bias, pieces, down_pieces, up_rows, down_rows):
    rows, width = nt.shape
    hidden = bias.shape[1]
    z_count = pieces[0].shape[1]
    chips = 2 * z_count
    block = hidden // chips
    per = width // block
    tiles = hidden // width
    column = lambda i, s: (0, s[2 + i])
    up_specs = [(p, (2, z_count, up_rows, block), lambda i, s: (0, 0, s[2 + i] // per, s[2 + i] % per)) for p in pieces]
    near = lambda i, s: (i // z_count, i % z_count, 0, 0)
    far = lambda i, s: (0, i % z_count, 0, 0)
    down_specs = [(p, (1, 1, down_rows, width), near) for p in down_pieces[:2]]
    down_specs += [(p, (2, 1, down_rows, width), far) for p in down_pieces[2:]]
    down_shape, down_block = (z_count, 2 * down_rows, width), (1, 2 * down_rows, width)
    up_shape = (z_count, 2, tiles, up_rows, width)
    up_block = (z_count, 2, 1, up_rows, block)
    up_index = lambda i, s: (0, 0, s[2 + i] // per, 0, s[2 + i] % per)
    return grid_call(
        tiled_feed_body,
        scalars,
        chips,
        [fixed(nt), fixed(ct), (bias, (1, block), column), *up_specs, *down_specs],
        [
            fixed_out((rows, width), f32),
            fixed_out((rows, width), f32),
            ((2, *down_shape), bf16, (1, *down_block), lambda i, s: (i // z_count, i % z_count, 0, 0)),
            (down_shape, bf16, down_block, lambda i, s: (jnp.minimum(i, z_count - 1), 0, 0)),
            (down_shape, bf16, down_block, lambda i, s: (jnp.maximum(i - z_count, 0), 0, 0)),
            ((2, *up_shape), bf16, (2, *up_block), lambda i, s: (0, *up_index(i, s))),
            (up_shape, bf16, up_block, up_index),
            (up_shape, bf16, up_block, up_index),
            ((1, hidden), f32, (1, block), column),
        ],
        [pltpu.VMEM((width, block), bf16), pltpu.VMEM((block, width), bf16), pltpu.VMEM((width, block), f32)],
        12 * rows * width * hidden,
        8 * width * hidden + 12 * rows * width,
        2 * rows * hidden,
    )


def unbranch_body(
    scalars,
    g_ref,
    mix_ref,
    mixed_ref,
    first_ref,
    taps_ref,
    bias_ref,
    weight_ref,
    gmixed_ref,
    gfirst_ref,
    kept_ref,
    sent_ref,
    grad_ref,
):
    chips = gmixed_ref.shape[0]
    g = g_ref[...]
    gate_grad = lax.dot_general(g, weight_ref[...], (((1,), (1,)), ((), ())), preferred_element_type=f32)
    for tile in range(chips // 2):
        cols = slice(tile * LANES, (tile + 1) * LANES)
        first = chip_rows(short_conv(first_ref[:, cols].astype(f32), taps_ref[:, cols], bias_ref[:, cols]))
        gfirst_ref[:, cols] = (gate_grad[:, cols] * mixed_ref[:, cols].astype(f32)).astype(bf16)
        pack_rows(gmixed_ref, 2 * tile, gate_grad[:, cols] * first)
    grad_ref[...] = lax.dot_general(mix_ref[...], g, (((0,), (0,)), ((), ())), preferred_element_type=f32)
    route_rows(grad_ref, kept_ref, sent_ref, scalars, chips, 1, False)


def unbranch(scalars, g, mix, mixed, projected, taps, bias, weight, chips):
    rows, width = g.shape
    half = weight.shape[0]
    grad_shape = (2, chips // 2, 1, width // half, half // (2 * chips), half)
    return grid_call(
        unbranch_body,
        scalars,
        1,
        [fixed(g), fixed(mix), fixed(mixed), *first_stream(projected, taps, bias), fixed(weight)],
        [
            fixed_out((chips, rows // 256, LANES, LANES), bf16),
            fixed_out((rows, half), bf16),
            fixed_out(grad_shape, bf16),
            fixed_out(grad_shape, bf16),
        ],
        [pltpu.VMEM((half, width), f32)],
        4 * rows * half * width,
        4 * rows * width + 6 * half * width,
    )


def ungate_body(scalars, gated_ref, second_ref, values_ref, t2_ref, t3_ref, b2_ref, b3_ref, gsecond_ref, gvalues_ref):
    pairs = (gated_ref.shape[1] - HALO) // LANES
    blocks = [gated_ref.at[:, pl.ds(pair * LANES, LANES), :] for pair in range(pairs)]
    grad = jnp.concatenate([part for block in blocks for part in unpack_pair(block[0], block[1])], axis=0)
    ahead, _ = unpack_pair(gated_ref[0, pairs * LANES :], gated_ref[1, pairs * LANES :])
    grad = jnp.concatenate([grad, ahead], axis=0)
    second = short_conv(second_ref[...].astype(f32), t2_ref[...], b2_ref[...])
    values = short_conv(values_ref[...].astype(f32), t3_ref[...], b3_ref[...])
    gsecond_ref[...] = (grad * values).astype(bf16)
    gvalues_ref[...] = (grad * second).astype(bf16)


def ungate(scalars, gated, projected, taps, bias):
    rows, columns = projected.shape
    half = columns // 3
    tiles = half // LANES
    p2, t2, b2 = stream_tiles(projected, taps, bias, 1, tiles)
    p3, t3, b3 = stream_tiles(projected, taps, bias, 2, tiles)
    out = ((rows - HALO, half), bf16, (rows - HALO, LANES), lambda i, s: (0, i))
    return grid_call(
        ungate_body,
        scalars,
        tiles,
        [(gated, (2, *gated.shape[1:]), lambda i, s: (i, 0, 0)), p2, p3, t2, t3, b2, b3],
        [out, out],
        [],
        20 * rows * columns,
        3 * rows * columns,
    )


def stream_body(
    by_x, scalars, grad_ref, rows_ref, taps_ref, normed_ref, gproj_ref, kept_ref, sent_ref, sums_ref, work_ref
):
    count, columns = gproj_ref.shape
    chips = 2 * kept_ref.shape[1]
    for at in range(0, columns, LANES):
        cols = slice(at, at + LANES)
        taps = taps_ref[:, cols]
        ext = grad_ref[:, cols].astype(f32)
        grad = ext[:count]
        total = count + HALO
        one, two = pltpu.roll(ext, total - 1, 0)[:count], pltpu.roll(ext, total - 2, 0)[:count]
        low = (taps[0:1] * two + taps[1:2] * one + taps[2:3] * grad).astype(bf16)
        gproj_ref[:, cols] = low
        rows = rows_ref[:, cols].astype(f32)
        sums = [
            jnp.sum(grad * pltpu.roll(rows, 2, 0)[HALO:total], axis=0, keepdims=True),
            jnp.sum(grad * pltpu.roll(rows, 1, 0)[HALO:total], axis=0, keepdims=True),
            jnp.sum(grad * rows[HALO:total], axis=0, keepdims=True),
            jnp.sum(grad, axis=0, keepdims=True),
            jnp.sum(low.astype(f32), axis=0, keepdims=True),
            jnp.zeros((3, LANES), f32),
        ]
        sums_ref[:, cols] = jnp.concatenate(sums, axis=0)
    work_ref[...] = lax.dot_general(
        normed_ref[HALO:total, :], gproj_ref[...], (((0,), (0,)), ((), ())), preferred_element_type=f32
    )
    route_rows(work_ref, kept_ref, sent_ref, scalars, chips, 2, by_x)


def stream_back(scalars, grad, projected, taps, normed, stream, chips, by_x):
    count, columns = grad.shape[0] - HALO, grad.shape[1]
    width = normed.shape[1]
    rows = projected.shape[0]
    index = lambda i, s: (0, stream)
    shape = (2, chips // 2, 2, 1, width // (4 * chips), columns)
    return grid_call(
        partial(stream_body, by_x),
        scalars,
        1,
        [
            fixed(grad),
            (projected, (rows, columns), index),
            (taps, (3, columns), index),
            fixed(normed),
        ],
        [
            fixed_out((count, columns), bf16),
            fixed_out(shape, bf16),
            fixed_out(shape, bf16),
            fixed_out((8, columns), f32),
        ],
        [pltpu.VMEM((width, columns), f32)],
        2 * count * columns * width,
        4 * count * columns + 2 * count * width + 2 * width * columns,
    )


def split_body(run, scalars, in_ref, kept_ref, sent_ref):
    core = scalars[0]
    if run == LANES // 2:
        one, two = in_ref[:, :LANES].astype(f32), in_ref[:, LANES:].astype(f32)
        lower = lax.broadcasted_iota(jnp.int32, one.shape, 1) < run
        sides = (
            jnp.where(lower, one, pltpu.roll(two, run, 1)).astype(bf16),
            jnp.where(lower, pltpu.roll(one, run, 1), two).astype(bf16),
        )
        kept_ref[...] = jnp.where(core == 0, sides[0], sides[1])
        sent_ref[...] = jnp.where(core == 0, sides[1], sides[0])
    else:
        kept_ref[...] = jnp.where(core == 0, in_ref[:, :run], in_ref[:, run:])
        sent_ref[...] = jnp.where(core == 0, in_ref[:, run:], in_ref[:, :run])


def split_columns(core, value, run, tile=None):
    rows, columns = value.shape
    block = max(run, LANES)
    if tile is None:
        out = ((rows, columns // 2), bf16, (rows, block), lambda i, s: (0, i))
    else:
        per = tile // block
        out = ((columns // 2 // tile, rows, tile), bf16, (None, rows, block), lambda i, s: (i // per, 0, i % per))
    return grid_call(
        partial(split_body, run),
        core.reshape(1),
        columns // (2 * block),
        [(value, (rows, 2 * block), lambda i, s: (0, i))],
        [out, out],
        [],
        rows * columns,
        4 * rows * columns,
    )


def filter_features(seq_index, tok_count, length):
    positions = (seq_index * tok_count + jnp.arange(tok_count, dtype=jnp.int32)).astype(f32)
    relative = positions / (length - 1)
    phases = positions * (2.0 * math.pi / length)
    band_count = (FEATURES - 1) // 2
    band_freq = jnp.linspace(0.0001, band_count - 1, band_count).astype(f32)
    angles = phases[:, None] * band_freq[None, :]
    return jnp.concatenate([relative[:, None], jnp.cos(angles), -jnp.sin(angles)], axis=1)


def tiled_device(
    tokens,
    cotangent,
    pre_gain,
    pre_offset,
    input_weight,
    input_bias,
    short_weight,
    short_bias,
    skip_weight,
    embed_weight,
    embed_bias,
    hidden_weight,
    hidden_bias,
    last_weight,
    last_bias,
    frequency,
    filter_weight,
    output_weight,
    output_bias,
    post_gain,
    post_offset,
    up_weight,
    up_bias,
    down_weight,
    down_bias,
):
    seq_count = lax.axis_size("seq")
    seq_index = lax.axis_index("seq")
    z, y, core, x = place()
    chips = seq_count // 2
    z_count = seq_count // 4
    tok_count, width = tokens.shape[1:]
    length = tok_count * seq_count
    channels = width // seq_count
    ff = up_weight.shape[1]
    hidden_own = ff // seq_count
    half = width // 2
    pairs = length // 256
    rows = 2 * tok_count
    chip_at = [(z ^ rel) * 2 + (y ^ yr) for yr in range(2) for rel in z_order(z_count)]
    scalars = jnp.stack([x, seq_index // 2, *chip_at]).astype(jnp.int32)

    def own_rows(value, run, tile=None):
        keep, sent = split_columns(core, value, run, tile)
        return jnp.where(core == x, keep, swap_core(sent))

    in_piece = own_rows(input_weight, channels)
    mine = jnp.stack([after(in_piece, tokens)[0], cotangent[0]])
    pair = both(mine, swap_core(mine), core)
    tok = pair[:, 0].reshape(rows, width)
    cot = pair[:, 1].reshape(rows, width)
    onward = [(i, i + 2) for i in range(seq_count - 2)]
    backward = [(i + 2, i) for i in range(seq_count - 2)]
    earlier = lax.ppermute(tok[rows - HALO :], "seq", onward)
    later = lax.ppermute(tok[:HALO], "seq", backward)
    tok_ext = jnp.concatenate([earlier, tok, later], axis=0)
    vectors = [
        pre_gain,
        pre_offset,
        input_bias,
        short_weight,
        short_bias,
        output_bias,
        post_gain,
        post_offset,
        up_bias,
        down_bias,
    ]
    small_blocks = []
    for vector in vectors:
        flat = vector.reshape(-1)
        small_blocks.append(jnp.pad(flat, (0, -flat.shape[0] % LANES)).reshape(-1, LANES))
    small_count = sum(block.shape[0] for block in small_blocks)
    small_blocks.append(jnp.zeros((-small_count % 8, LANES), bf16))
    small = jnp.concatenate(small_blocks, axis=0).astype(f32)

    in_have = gather_z(in_piece, (earlier, later))

    trunk = (embed_weight, embed_bias, hidden_weight, hidden_bias, last_weight, last_bias, frequency)
    features = filter_features(after(tok, seq_index), tok_count, length)
    hidden_rows, trunk_pull = jax.vjp(partial(trunk_hidden, features=features), trunk)
    units = hidden_rows.shape[1]
    own_pairs = tok_count // 256
    packed = hidden_rows.reshape(own_pairs, 2, LANES, units).transpose(0, 2, 1, 3)
    packed = packed.reshape(own_pairs * LANES, 2 * units)
    gathered = gather_small(after((earlier, later), jnp.concatenate([packed, small], axis=0)))
    filter_hidden = gathered[:, : own_pairs * LANES].reshape(pairs, LANES, 2 * units)
    small_all = gathered[:, own_pairs * LANES :].reshape(seq_count, -1)

    in_near = gather_near(in_have)
    in_pieces = gather_far(in_near)

    up_piece = own_rows(after(in_piece, up_weight), hidden_own, width)
    out_piece = pick(after(in_piece, output_weight).reshape(2, -1, width), x, 0)
    down_piece = pick(after(in_piece, down_weight).reshape(2, -1, width), x, 0)
    up_half, out_half_rows, down_half_rows = up_piece.shape[1] // 2, out_piece.shape[0] // 2, down_piece.shape[0] // 2
    parts = []
    for side in range(2):
        parts.append(up_piece[:, side * up_half : (side + 1) * up_half].reshape(-1, width))
        parts.append(out_piece[side * out_half_rows : (side + 1) * out_half_rows])
    rest_have = gather_z(after(in_have, jnp.concatenate(parts, axis=0)))
    rest_near = gather_near(after(in_pieces, rest_have))
    down_have = gather_z(after(rest_have, down_piece))

    columns, at = [], 0
    for vector in vectors:
        columns.append(small_all[:, at : at + vector.size])
        at += vector.size + -vector.size % LANES

    def halved(value, run):
        lead = value.shape[:-1]
        return pick(value.reshape(*lead, -1, 2, run), core, len(lead) + 1).reshape(*lead, -1)

    pre_gain_full, pre_offset_full = columns[0].reshape(-1), columns[1].reshape(-1)
    input_bias_own = halved(columns[2].reshape(3, width), channels).reshape(1, -1)
    short_full = columns[3].reshape(seq_count, 3, -1).transpose(1, 0, 2).reshape(3, 3, width)
    taps = halved(short_full, channels).reshape(3, -1)
    short_bias_own = halved(columns[4].reshape(3, width), channels).reshape(1, -1)
    output_bias_full = columns[5].reshape(-1)
    post_gain_full, post_offset_full = columns[6].reshape(-1), columns[7].reshape(-1)
    up_bias_own = halved(columns[8].reshape(-1), hidden_own)[None]
    down_bias_full = columns[9].reshape(-1)

    filter_own = filter_weight.astype(f32)
    zero = jnp.zeros_like(filter_own)
    filter_pair = jnp.concatenate(
        [jnp.concatenate([filter_own, zero], axis=1), jnp.concatenate([zero, filter_own], axis=1)], axis=0
    )
    deltas = jnp.linspace(math.log(0.01) / 1.5, math.log(0.01) / 0.3, width).astype(f32)
    delta_own = jnp.abs(lax.dynamic_slice_in_dim(deltas, seq_index * channels, channels))
    delta_pair = jnp.concatenate([delta_own, delta_own])[None]
    skip_own = skip_weight.astype(f32)
    skip_pair = jnp.concatenate([skip_own, skip_own])[None]
    tables = tuple(jnp.asarray(t) for t in conv_tables(pairs))

    normed_one, unit_one, inverse_one = norm_forward(tok_ext.astype(f32), pre_gain_full, pre_offset_full)
    normed_ext = normed_one.astype(bf16)
    in_pieces = after((normed_ext, input_bias_own, taps, short_bias_own), in_pieces)
    projected, in_half = project(scalars, normed_ext, input_bias_own, in_pieces)
    gated = gate(scalars, after(rest_near, projected), taps, short_bias_own, chips)
    rest_pieces = gather_far(after(gated, rest_near))
    filter_hidden = after((gated, down_have), filter_hidden)
    kernel_spec = conv_filter(filter_hidden, filter_pair, delta_pair, tables)
    gated_ch = chip_exchange(gated).reshape(pairs, LANES, LANES)
    down_near = gather_near(after((rest_pieces, gated_ch), down_have))
    down_pieces = gather_far(down_near)
    gated_ch = after(rest_pieces, gated_ch)
    mixed_ch, gated_spec = conv_forward(gated_ch, kernel_spec, skip_pair, tables)
    chip_shape = (chips, rows // 256, LANES, LANES)
    mixed_back = chip_exchange(mixed_ch.reshape(chip_shape))
    mixed_tok, mix_low, out_half, branch_part = branch_out(
        scalars, after(down_pieces, mixed_back), projected, taps, short_bias_own, rest_pieces, out_half_rows
    )
    hidden = tok.astype(f32) + (branch_part + swap_core(branch_part) + output_bias_full)

    normed_two, unit_two, inverse_two = norm_forward(hidden, post_gain_full, post_offset_full)
    (
        down_part,
        back_part,
        gdown_kept,
        gdown_late,
        gdown_first,
        gup_kept,
        gup_late,
        gup_first,
        up_bias_grad,
    ) = tiled_feed(scalars, normed_two.astype(bf16), cot, up_bias_own, rest_pieces, down_pieces, up_half, down_half_rows)
    up_flat = gdown_kept.shape
    gup_kept, gup_late, gup_first = (
        value.reshape(*shape) for value, shape in ((gup_kept, up_flat), (gup_late, up_flat[1:]), (gup_first, up_flat[1:]))
    )

    def own_tokens(value):
        return lax.dynamic_slice_in_dim(value, core * tok_count, tok_count, 0)

    def other_tokens(value):
        return lax.dynamic_slice_in_dim(value, (1 - core) * tok_count, tok_count, 0)

    normed_two_grad = back_part + swap_core(back_part)
    cot_f = cot.astype(f32)
    hidden_grad = cot_f + norm_backward(normed_two_grad, unit_two, inverse_two, post_gain_full)
    branch_low = hidden_grad.astype(bf16)
    gmixed, gfirst, gout_kept, gout_sent = unbranch(
        scalars, branch_low, mix_low, mixed_tok, projected, taps, short_bias_own, out_half, chips
    )
    mixed_grad_ch = chip_exchange(gmixed).reshape(pairs, LANES, LANES)

    def add_parts(kept, got):
        return kept.astype(f32) + got.astype(f32)

    down_got, up_got = after(gmixed, (swap_x(gdown_first), swap_y(gup_first)))
    down_next, up_next = add_parts(gdown_kept[1], down_got).astype(bf16), add_parts(gup_kept[1], up_got).astype(bf16)
    down_got, up_got = swap_y(down_next), swap_x(up_next)
    down_late, up_late = after((down_next, up_next), (gdown_late, gup_late))
    down_late, up_late = swap_x(down_late), swap_y(up_late)
    mixed_grad_ch = after((down_next, up_next), mixed_grad_ch)

    gated_back, grad_spec = conv_backward(mixed_grad_ch, kernel_spec, skip_pair, tables, chips)
    hidden_back, filter_square, skip_line = filter_backward(
        mixed_grad_ch, after(gated_back, grad_spec), gated_ch, gated_spec, filter_hidden, filter_pair, delta_pair, tables
    )
    gated_grad = chip_exchange(gated_back)

    down_part = after(gmixed, down_part)
    result = own_tokens(hidden) + (
        own_tokens(down_part) + swap_core(other_tokens(down_part)) + down_bias_full
    )
    down_bias_grad = jnp.sum(after(gmixed, cot).astype(f32), axis=0)
    post_gain_grad = jnp.sum(normed_two_grad * unit_two, axis=0)
    post_offset_grad = jnp.sum(normed_two_grad, axis=0)
    output_bias_grad = jnp.sum(branch_low.astype(f32), axis=0)

    gfirst_next = lax.ppermute(gfirst[:HALO], "seq", backward)
    gated_grad = after(hidden_back, gated_grad)
    gsecond, gvalues = ungate(scalars, gated_grad, projected, taps, short_bias_own)
    gfirst = jnp.concatenate([gfirst, after(gsecond, gfirst_next)], axis=0)
    first_proj, first_kept, first_sent, first_sums = stream_back(
        scalars, gfirst, projected, taps, normed_ext, 0, chips, True
    )
    second_proj, second_kept, second_sent, second_sums = stream_back(
        scalars, gsecond, projected, taps, normed_ext, 1, chips, True
    )
    values_proj, values_kept, values_sent, values_sums = stream_back(
        scalars, gvalues, projected, taps, normed_ext, 2, chips, False
    )
    down_late, down_got, up_late, up_got = after((second_sent, values_sent), (down_late, down_got, up_late, up_got))
    feed_total = jnp.stack(
        [
            add_parts(gdown_kept[0], down_late) + down_got.astype(f32),
            add_parts(gup_kept[0], up_late) + up_got.astype(f32),
        ],
        axis=1,
    )
    second_proj = after(feed_total, second_proj)
    normed_one_part = sum(
        contract(part, in_half[:, i * half : (i + 1) * half], 1, 1)
        for i, part in enumerate((first_proj, second_proj, values_proj))
    )
    mixer_shape = first_kept.shape[:2] + (2, *first_kept.shape[4:])

    def mixer_pair(kept, got):
        kept, got = ([value.reshape(mixer_shape) for value in pair] for pair in (kept, got))
        next_part = jnp.stack([add_parts(k[1], g[1]).astype(bf16) for k, g in zip(kept, got)], axis=1)
        rest_part = jnp.stack([add_parts(k[0], g[0]) for k, g in zip(kept, got)], axis=1)
        return next_part, rest_part

    one_got, two_got = after(
        normed_one_part, ((swap_x(first_sent), swap_x(second_sent)), (swap_y(gout_sent), swap_y(values_sent)))
    )
    one_next, one_rest = mixer_pair((first_kept, second_kept), one_got)
    two_next, two_rest = mixer_pair((gout_kept, values_kept), two_got)
    one_got, two_got = swap_y(one_next), swap_x(two_next)

    normed_one_grad = own_tokens(normed_one_part) + swap_core(other_tokens(normed_one_part))
    unit_own = lax.dynamic_slice_in_dim(after((one_next, two_next), unit_one), HALO + core * tok_count, tok_count, 0)
    pre_gain_grad = jnp.sum(normed_one_grad * unit_own, axis=0)
    pre_offset_grad = jnp.sum(normed_one_grad, axis=0)
    tokens_grad = own_tokens(hidden_grad) + norm_backward(
        normed_one_grad, unit_own, lax.dynamic_slice_in_dim(inverse_one, HALO + core * tok_count, tok_count, 0), pre_gain_full
    )

    hidden_got = lax.all_to_all(
        hidden_back.reshape(seq_count, own_pairs * LANES, 2 * units), "seq", split_axis=0, concat_axis=0, tiled=True
    )
    hidden_sum = jnp.sum(after((one_next, two_next), hidden_got).astype(f32), axis=0)
    hidden_sum = hidden_sum.reshape(own_pairs, LANES, 2, units).transpose(0, 2, 1, 3).reshape(tok_count, units)
    (trunk_grad,) = trunk_pull(hidden_sum)
    filter_grad = filter_square[:units, :channels] + filter_square[units:, channels:]
    skip_grad = skip_line[:, :channels] + skip_line[:, channels:]
    own_grad = jnp.concatenate([filter_grad, skip_grad], axis=0)
    own_grad = after((one_next, two_next), own_grad)
    own_grad_got = swap_x(own_grad)

    def whole_columns(value, groups, run):
        got = swap_core(pick(value, 1 - core, 0))
        mine_part = pick(value, core, 0)
        n = mine_part.shape[0]
        grid = both(mine_part, got, core).reshape(2, n, groups, chips, run)
        return grid.transpose(1, 2, 3, 0, 4).reshape(n, -1)


    def lane_rows(vector):
        return vector.reshape(-1, LANES)

    def wide_rows(matrix):
        padded = jnp.pad(matrix, ((0, -matrix.shape[0] % 8), (0, LANES - matrix.shape[1])))
        return padded

    embed_grad, embed_bias_grad, hidden_grad_w, hidden_bias_grad, last_grad, last_bias_grad, frequency_grad = trunk_grad
    unit_lines = jnp.stack([embed_bias_grad, hidden_bias_grad, last_bias_grad, frequency_grad])
    trunk_parts = [wide_rows(part) for part in (embed_grad, hidden_grad_w, last_grad, unit_lines)]
    stream_sums = jnp.concatenate([first_sums, second_sums, values_sums], axis=0)
    stream_rows = [stream_sums[:, at : at + LANES] for at in range(0, half, LANES)]
    flats = [
        jnp.concatenate(
            [lane_rows(v) for v in (post_gain_grad, post_offset_grad, down_bias_grad, output_bias_grad)], axis=0
        ),
        jnp.concatenate([lane_rows(pre_gain_grad), lane_rows(pre_offset_grad), *trunk_parts], axis=0),
        jnp.concatenate([lane_rows(up_bias_grad), *stream_rows], axis=0),
    ]
    n_chip, n_own = flats[0].shape[0], flats[1].shape[0]
    small = jnp.concatenate(flats, axis=0)
    one_got, two_got = after(trunk_grad, (one_got, two_got))
    mixer_total = jnp.concatenate([add_parts(one_rest, one_got), add_parts(two_rest, two_got)], axis=1)
    masks = z_masks(z_count)[::-1]
    mixer_start = mixer_total
    mixer_total = reduce_z_step(mixer_total, masks[0])
    summed = sum_chips(after(mixer_start, small), mixer_total)
    own_grad = own_grad + after(mixer_total, own_grad_got)
    own_grad = pick(own_grad.reshape(-1, 2, channels // 2), x, 1)
    got = swap_core(summed[n_chip:])
    own_sum = (summed[n_chip:] + got)[:n_own]
    half_pair = both(summed[n_chip + n_own :], got[n_own:], core)
    n_line = width // LANES
    lines = jnp.concatenate([summed[:n_chip], own_sum[: 2 * n_line]], axis=0).reshape(6, n_line, LANES)
    trunk_sums, at = [], 2 * n_line
    for part in trunk_parts:
        trunk_sums.append(own_sum[at : at + part.shape[0], :units])
        at += part.shape[0]
    feed_sum = reduce_far(feed_total, masks)
    first_sum, second_sum, out_sum, values_sum = reduce_far(mixer_total, masks[1:])
    down_sum = feed_sum[0]
    up_sum = feed_sum[1].reshape(2, -1, up_half, width).transpose(0, 2, 1, 3).reshape(2, up_half, -1)
    out_sum = out_sum.transpose(1, 0, 2).reshape(out_sum.shape[1], -1)
    in_rows = whole_columns(jnp.concatenate([first_sum, second_sum, values_sum], axis=2), 3, channels)
    up_rows_sum = whole_columns(up_sum, 1, hidden_own)
    block_index = seq_index * 2 + x

    def own_block(value, axis=0):
        size = value.shape[axis] // (2 * seq_count)
        return lax.dynamic_slice_in_dim(value, block_index * size, size, axis)

    run = width // (2 * seq_count)
    per = LANES // run
    line = pick(lines, block_index // per, 1)
    runs = pick(jnp.stack([line[:, i * run : (i + 1) * run] for i in range(per)]), block_index % per, 0)
    n_up = up_bias_grad.size // LANES
    up_bias_sum = half_pair[:, :n_up].reshape(2, chips, hidden_own).transpose(1, 0, 2).reshape(-1)
    streams = half_pair[:, n_up:].reshape(2, half // LANES, 3, 8, LANES // channels, channels)
    streams = streams.transpose(3, 2, 1, 4, 0, 5).reshape(8, 3 * width)
    return (
        result.astype(bf16)[None],
        tokens_grad.astype(bf16)[None],
        runs[4],
        runs[5],
        in_rows,
        own_block(streams[4]),
        own_block(streams[:3], 1),
        own_block(streams[3]),
        own_grad[units],
        trunk_sums[0][:FEATURES],
        trunk_sums[3][0],
        trunk_sums[1],
        trunk_sums[3][1],
        trunk_sums[2],
        trunk_sums[3][2],
        trunk_sums[3][3],
        own_grad[:units],
        out_sum,
        runs[3],
        runs[0],
        runs[1],
        up_rows_sum,
        own_block(up_bias_sum),
        down_sum,
        runs[2],
    )


def per_device(tokens, *others):
    channels = tokens.shape[2] // lax.axis_size("seq")
    tiled = 2 * channels == LANES and tokens.shape[1] % 256 == 0
    return (tiled_device if tiled else plain_device)(tokens, *others)


def solution(mesh):
    placed = (
        P("dp", "seq", None),
        P("dp", "seq", None),
        P("seq"),
        P("seq"),
        P("seq", None),
        P("seq"),
        P(None, "seq"),
        P("seq"),
        P("seq"),
        P(),
        P(),
        P(),
        P(),
        P(),
        P(),
        P(),
        P(None, "seq"),
        P("seq", None),
        P("seq"),
        P("seq"),
        P("seq"),
        P("seq", None),
        P("seq"),
        P("seq", None),
        P("seq"),
    )
    split = P(("seq", "dp"))
    split_rows = P(("seq", "dp"), None)
    split_columns = P(None, ("seq", "dp"))
    return jax.shard_map(
        per_device,
        mesh=mesh,
        in_specs=placed,
        out_specs=(
            P("dp", "seq", None),
            P("dp", "seq", None),
            split,
            split,
            split_rows,
            split,
            split_columns,
            split,
            split,
            P(),
            P(),
            P(),
            P(),
            P(),
            P(),
            P(),
            split_columns,
            split_rows,
            split,
            split,
            split,
            split_rows,
            split,
            split_rows,
            split,
        ),
        check_vma=False,
    )
```

```python
from functools import partial
import math

import jax
import jax.numpy as jnp
import numpy as np
from jax import lax
from jax.experimental import pallas as pl
from jax.experimental.pallas import tpu as pltpu
from jax.sharding import PartitionSpec as P

FEATURES = 33
LANES = 128
f32 = jnp.float32
bf16 = jnp.bfloat16
highest = lax.Precision.HIGHEST


def swap_seq(value, mask):
    count = lax.axis_size("seq")
    return lax.ppermute(value, "seq", [(i, i ^ mask) for i in range(count)])


def swap_core(value):
    return swap_seq(value, 1)


def swap_y(value):
    return swap_seq(value, 2)


def swap_z(value, mask):
    return swap_seq(value, 4 * mask)


def swap_x(value):
    count = lax.axis_size("dp")
    return lax.ppermute(value, "dp", [(i, i ^ 1) for i in range(count)])


def z_masks(count):
    if count == 4:
        return [3, 1]
    masks, step = [], count // 2
    while step:
        masks.append(step)
        step //= 2
    return masks


def z_order(count):
    order = [0]
    for mask in z_masks(count):
        order = order + [entry ^ mask for entry in order]
    return order


def chip_groups():
    count = lax.axis_size("seq")
    return [list(range(core, count, 2)) for core in range(2)]


def chip_exchange(value):
    return lax.all_to_all(
        value, "seq", split_axis=0, concat_axis=0, tiled=True, axis_index_groups=chip_groups()
    )


def pick(value, index, axis):
    return lax.dynamic_index_in_dim(value, index, axis, keepdims=False)


def both(mine, other, second):
    return jnp.where(second == 0, jnp.stack([mine, other]), jnp.stack([other, mine]))


def place():
    seq = lax.axis_index("seq")
    return seq // 4, (seq // 2) % 2, seq % 2, lax.axis_index("dp")


def by_index(have, order, own):
    bit = 1
    value = jnp.stack([have[order.index(entry)] for entry in range(len(order))])
    while bit < len(order):
        grid = value.reshape(-1, 2, bit, *value.shape[1:])
        turned = jnp.stack([grid[:, 1], grid[:, 0]], axis=1)
        value = jnp.where((own & bit) == 0, grid, turned).reshape(value.shape)
        bit *= 2
    return value


def gather_pieces(piece):
    z, y, _, x = place()
    z_count = lax.axis_size("seq") // 4
    have = piece[None]
    for mask in z_masks(z_count):
        have = jnp.concatenate([have, swap_z(have, mask)], axis=0)
    half = piece.shape[0] // 2
    first, second = have[:, :half], have[:, half:]
    first_y, second_x = swap_y(first), swap_x(second)
    first = jnp.stack([first, first_y])
    second = jnp.stack([second, second_x])
    first_x, second_y = swap_x(first), swap_y(second)
    first = jnp.stack([first, first_x], axis=1)
    second = jnp.stack([second, second_y])
    rel = jnp.concatenate([first, second], axis=3)
    order = z_order(z_count)
    rows = []
    for za in range(z_count):
        rel_z = z ^ za
        slot = sum(jnp.where(rel_z == entry, at, 0) for at, entry in enumerate(order))
        slab = pick(rel, slot, 2)
        slab = jnp.where(y == 0, slab, jnp.stack([slab[1], slab[0]]))
        slab = jnp.where(x == 0, slab, jnp.stack([slab[:, 1], slab[:, 0]], axis=1))
        rows.append(slab)
    return jnp.stack(rows)


def reduce_z(parts):
    z = place()[0]
    z_count = parts.shape[0]
    have = jnp.stack([pick(parts, z ^ rel, 0) for rel in z_order(z_count)])
    for mask in reversed(z_masks(z_count)):
        half = have.shape[0] // 2
        got = swap_z(have[half:].astype(bf16), mask)
        have = have[:half] + got.astype(f32)
    return have[0]


def reduce_pair(first, second):
    _, y, _, x = place()
    first_got = swap_x(pick(first, 1 - x, 2))
    second_got = swap_y(pick(second, 1 - y, 1))
    first = pick(first, x, 2).astype(f32) + first_got.astype(f32)
    second = pick(second, y, 1).astype(f32) + second_got.astype(f32)
    first_got = swap_y(pick(first, 1 - y, 1).astype(bf16))
    second_got = swap_x(pick(second, 1 - x, 1).astype(bf16))
    first = pick(first, y, 1) + first_got.astype(f32)
    second = pick(second, x, 1) + second_got.astype(f32)
    return reduce_z(first), reduce_z(second)


def sum_chips(value, gates=None):
    value = value + swap_x(value)
    value = value + swap_y(value)
    if gates is not None:
        value = lax.optimization_barrier((gates, value))[1]
    for mask in z_masks(lax.axis_size("seq") // 4):
        value = value + swap_z(value, mask)
    return value


def gather_small(value):
    seq = lax.axis_index("seq")
    count = lax.axis_size("seq")
    have = value[None]
    for mask in [2, 1] + [4 * m for m in z_masks(count // 4)]:
        have = jnp.concatenate([have, swap_seq(have, mask)], axis=0)
    order = [0]
    for mask in [2, 1] + [4 * m for m in z_masks(count // 4)]:
        order = order + [entry ^ mask for entry in order]
    return by_index(have, order, seq)


def twiddle(k, n):
    angle = -2.0 * math.pi * (k % n) / n
    return math.cos(angle), math.sin(angle)


def c_add(p, q):
    return (p[0] + q[0], q[1] if p[1] is None else (p[1] if q[1] is None else p[1] + q[1]))


def c_sub(p, q):
    if q[1] is None:
        return (p[0] - q[0], p[1])
    return (p[0] - q[0], -q[1] if p[1] is None else p[1] - q[1])


def c_conj(p):
    return (p[0], None if p[1] is None else -p[1])


def c_turn(p, k, n):
    k = k % n
    if k == 0:
        return p
    re, im = p
    if 4 * k == n:
        return (im if im is not None else jnp.zeros_like(re), -re)
    if 2 * k == n:
        return (-re, None if im is None else -im)
    if 4 * k == 3 * n:
        return (-im if im is not None else jnp.zeros_like(re), re)
    c, s = twiddle(k, n)
    if im is None:
        return (re * c, re * s)
    return (re * c - im * s, re * s + im * c)


def real_dft(xs):
    n = len(xs)
    if n == 1:
        return [(xs[0], None)]
    if n == 2:
        if xs[1] is None:
            return [(xs[0], None), (xs[0], None)]
        return [(xs[0] + xs[1], None), (xs[0] - xs[1], None)]
    even, odd = real_dft(xs[0::2]), real_dft(xs[1::2])
    out = [None] * (n // 2 + 1)
    for k in range(n // 4 + 1):
        turned = c_turn(odd[k], k, n)
        out[k] = c_add(even[k], turned)
        if n // 2 - k != k:
            out[n // 2 - k] = c_conj(c_sub(even[k], turned))
    return out


def real_inverse(spec):
    def whole(v):
        n = 2 * (len(v) - 1)
        if n == 2:
            return [v[0][0] + v[1][0], None]
        even, odd = [], []
        for k in range(n // 4 + 1):
            mirror = c_conj(v[n // 2 - k])
            e, o = c_add(v[k], mirror), c_turn(c_sub(v[k], mirror), -k, n)
            if k == 0 or 4 * k == n:
                e, o = (e[0], None), (o[0], None)
            even.append(e)
            odd.append(o)
        even, odd = whole(even), whole(odd)
        return [entry for pair in zip(even, odd) for entry in pair]

    values = whole(spec)
    return values[: len(values) // 2]


def split_terms(value):
    high = value.astype(bf16)
    return high, (value - high.astype(f32)).astype(bf16)


def conv_tables(pairs):
    rows = 4 * pairs
    total = rows * LANES
    slots = np.arange(pairs + 1)
    lanes = np.arange(LANES)
    upper = lanes >= LANES // 2
    angle = -2.0 * np.pi * slots[:, None] / rows * upper[None, :]
    lane_turn = np.stack([np.cos(angle), np.sin(angle)], axis=1).astype(np.float32)
    freq = slots[:, None] + np.where(upper, rows // 2, 0)[None, :]
    angle = -2.0 * np.pi * ((freq[:, None, :] * lanes[None, :, None]) % total) / total
    turn = np.stack([np.cos(angle), np.sin(angle)], axis=1).astype(np.float32)
    angle = 2.0 * np.pi * ((lanes[:, None] * lanes[None, :]) % LANES) / LANES
    c, s = np.cos(angle), np.sin(angle)

    def terms(table):
        table = table.astype(np.float32)
        high = table.astype(bf16)
        low = (table - high.astype(np.float32)).astype(bf16)
        return np.concatenate([high, low], axis=1)

    ahead = terms(np.block([[c, s], [-s, c]]))
    back = terms(np.block([[c, -s], [s, c]]) / total)
    return lane_turn, turn, ahead, back


CHUNK = 16


def put(terms_ref, start, slot, re, im):
    cols = pl.ds(slot * LANES, LANES)
    terms_ref[pl.ds(start, CHUNK), cols] = re
    terms_ref[pl.ds(LANES + start, CHUNK), cols] = im


COLUMNS = 4 * LANES


def table_product(table_ref, terms_ref, out_ref):
    width = terms_ref.shape[1]
    high_table, low_table = table_ref[:, :256], table_ref[:, 256:]
    for at in range(0, width, COLUMNS):
        cols = pl.ds(at, min(COLUMNS, width - at))
        high, low = split_terms(terms_ref[:, cols])
        out_ref[:, cols] = (
            jnp.dot(high_table, low, preferred_element_type=f32)
            + jnp.dot(low_table, high, preferred_element_type=f32)
            + jnp.dot(high_table, high, preferred_element_type=f32)
        )


def lane_sign(shape):
    return jnp.where(lax.broadcasted_iota(jnp.int32, shape, 1) < LANES // 2, 1.0, -1.0).astype(f32)


def transform(x_ref, pairs, lane_ref, turn_ref, ahead_ref, terms_ref, spec_ref):
    sign = lane_sign((CHUNK, LANES))

    def chunk(step, carry):
        start = pl.multiple_of(step * CHUNK, CHUNK)
        xs = [x_ref[j, pl.ds(start, CHUNK), :].astype(f32) for j in range(pairs)]
        spec = real_dft(xs + [None] * pairs)
        for k in range(pairs + 1):
            re, im = spec[k]
            c, s = lane_ref[k, 0:1, :], lane_ref[k, 1:2, :]
            if im is None:
                re, im = re * c, re * s
            else:
                re, im = re * c - im * s, re * s + im * c
            re = pltpu.roll(re, LANES // 2, 1) + sign * re
            im = pltpu.roll(im, LANES // 2, 1) + sign * im
            c, s = turn_ref[k, 0, pl.ds(start, CHUNK), :], turn_ref[k, 1, pl.ds(start, CHUNK), :]
            put(terms_ref, start, k, re * c - im * s, re * s + im * c)
        return carry

    lax.fori_loop(0, LANES // CHUNK, chunk, 0)
    table_product(ahead_ref, terms_ref, spec_ref)


def put_product(terms_ref, pairs, one_ref, other_ref, conjugate):
    def chunk(step, carry):
        start = pl.multiple_of(step * CHUNK, CHUNK)
        for k in range(pairs + 1):
            cols = pl.ds(k * LANES, LANES)
            a, b = one_ref[pl.ds(start, CHUNK), cols], one_ref[pl.ds(LANES + start, CHUNK), cols]
            c, d = other_ref[pl.ds(start, CHUNK), cols], other_ref[pl.ds(LANES + start, CHUNK), cols]
            if conjugate:
                put(terms_ref, start, k, a * c + b * d, b * c - a * d)
            else:
                put(terms_ref, start, k, a * c - b * d, a * d + b * c)
        return carry

    lax.fori_loop(0, LANES // CHUNK, chunk, 0)


def inverse(pairs, lane_ref, turn_ref, back_ref, terms_ref, spec_ref, finish):
    table_product(back_ref, terms_ref, spec_ref)
    sign = lane_sign((CHUNK, LANES))

    def chunk(step, carry):
        start = pl.multiple_of(step * CHUNK, CHUNK)
        spec = []
        for k in range(pairs + 1):
            cols = pl.ds(k * LANES, LANES)
            re, im = spec_ref[pl.ds(start, CHUNK), cols], spec_ref[pl.ds(LANES + start, CHUNK), cols]
            c, s = turn_ref[k, 0, pl.ds(start, CHUNK), :], turn_ref[k, 1, pl.ds(start, CHUNK), :]
            re, im = re * c + im * s, im * c - re * s
            re = pltpu.roll(re, LANES // 2, 1) + sign * re
            im = pltpu.roll(im, LANES // 2, 1) + sign * im
            c, s = lane_ref[k, 0:1, :], lane_ref[k, 1:2, :]
            re, im = re * c + im * s, im * c - re * s
            spec.append((re, None if k in (0, pairs) else im))
        for j, values in enumerate(real_inverse(spec)):
            finish(j, start, values)
        return carry

    lax.fori_loop(0, LANES // CHUNK, chunk, 0)


def window_of(j, start, delta, length):
    lane = lax.broadcasted_iota(jnp.int32, (CHUNK, LANES), 1)
    row = lax.broadcasted_iota(jnp.int32, (CHUNK, LANES), 0)
    position = (2 * j + lane // (LANES // 2)) * LANES + start + row
    return jnp.exp(-(position.astype(f32) / (length - 1)) * delta) + 0.05


def filter_body(pairs, h_ref, w_ref, delta_ref, lane_ref, turn_ref, ahead_ref, spec_ref, low_ref, terms_ref):
    delta = delta_ref[...]
    for j in range(pairs):
        rows = jnp.dot(h_ref[j], w_ref[...], precision=highest, preferred_element_type=f32)
        window = jnp.concatenate(
            [window_of(j, start, delta, 2 * pairs * LANES) for start in range(0, LANES, CHUNK)], axis=0
        )
        low_ref[j] = (rows * window).astype(bf16).astype(f32)
    transform(low_ref, pairs, lane_ref, turn_ref, ahead_ref, terms_ref, spec_ref)


def forward_body(
    pairs, x_ref, kernel_ref, skip_ref, lane_ref, turn_ref, ahead_ref, back_ref, out_ref, spec_ref, terms_ref, work_ref
):
    transform(x_ref, pairs, lane_ref, turn_ref, ahead_ref, terms_ref, spec_ref)
    put_product(terms_ref, pairs, spec_ref, kernel_ref, False)
    skip = skip_ref[...]

    def finish(j, start, values):
        rows = pl.ds(start, CHUNK)
        out_ref[j, rows, :] = (values + x_ref[j, rows, :].astype(f32) * skip).astype(bf16)

    inverse(pairs, lane_ref, turn_ref, back_ref, terms_ref, work_ref, finish)


def backward_body(
    pairs, g_ref, kernel_ref, skip_ref, lane_ref, turn_ref, ahead_ref, back_ref, gx_ref, spec_ref, terms_ref, work_ref
):
    transform(g_ref, pairs, lane_ref, turn_ref, ahead_ref, terms_ref, spec_ref)
    put_product(terms_ref, pairs, spec_ref, kernel_ref, True)
    skip = skip_ref[...]

    chips, rows = gx_ref.shape[:2]
    own = (rows - CHUNK) // LANES

    def finish(j, start, values):
        value = (values + g_ref[j, pl.ds(start, CHUNK), :].astype(f32) * skip).astype(bf16)
        gx_ref[j // own, pl.ds(pl.multiple_of(j % own * LANES + start, CHUNK), CHUNK), :] = value

    inverse(pairs, lane_ref, turn_ref, back_ref, terms_ref, work_ref, finish)
    for chip in range(chips - 1):
        gx_ref[chip, own * LANES :, :] = gx_ref[chip + 1, :CHUNK, :]
    gx_ref[chips - 1, own * LANES :, :] = jnp.zeros((CHUNK, LANES), bf16)


def filter_back_body(
    pairs,
    g_ref,
    g_spec_ref,
    x_ref,
    x_spec_ref,
    h_ref,
    w_ref,
    delta_ref,
    lane_ref,
    turn_ref,
    back_ref,
    gh_ref,
    gw_ref,
    gskip_ref,
    terms_ref,
    work_ref,
    pre_ref,
):
    put_product(terms_ref, pairs, g_spec_ref, x_spec_ref, True)
    delta = delta_ref[...]

    def finish(j, start, values):
        window = window_of(j, start, delta, 2 * pairs * LANES)
        pre_ref[j, pl.ds(start, CHUNK), :] = values.astype(bf16).astype(f32) * window

    inverse(pairs, lane_ref, turn_ref, back_ref, terms_ref, work_ref, finish)
    gw_ref[...] = jnp.zeros_like(gw_ref)
    gskip_ref[...] = jnp.zeros_like(gskip_ref)
    for j in range(pairs):
        pre = pre_ref[j]
        gh = lax.dot_general(
            pre, w_ref[...], (((1,), (1,)), ((), ())), precision=highest, preferred_element_type=f32
        )
        gh_ref[j] = gh.astype(bf16)
        gw_ref[...] += lax.dot_general(
            h_ref[j], pre, (((0,), (0,)), ((), ())), precision=highest, preferred_element_type=f32
        )
        gskip_ref[...] += jnp.sum(g_ref[j].astype(f32) * x_ref[j].astype(f32), axis=0, keepdims=True)


SHARE = 100000
FILLER = 40 * 10**9
VMEM_BYTES = 50 * 1024 * 1024


def whole_call(body, outs, scratch, flops, moved, *operands, share=SHARE):
    return pl.pallas_call(
        body,
        out_shape=outs,
        scratch_shapes=scratch,
        compiler_params=pltpu.CompilerParams(vmem_limit_bytes=VMEM_BYTES),
        cost_estimate=pl.CostEstimate(flops=flops // share, bytes_accessed=moved // share, transcendentals=0),
    )(*operands)


def spec_shape(pairs):
    return (256, (pairs + 1) * LANES)


def conv_filter(hidden, weight, delta, tables):
    pairs = hidden.shape[0]
    lane_turn, turn, ahead, _ = tables
    return whole_call(
        partial(filter_body, pairs),
        jax.ShapeDtypeStruct(spec_shape(pairs), f32),
        [pltpu.VMEM((pairs, LANES, LANES), f32), pltpu.VMEM(spec_shape(pairs), f32)],
        10**9,
        8 * 10**6,
        hidden,
        weight,
        delta,
        lane_turn,
        turn,
        ahead,
    )


def conv_forward(x, kernel_spec, skip, tables):
    pairs = x.shape[0]
    return whole_call(
        partial(forward_body, pairs),
        (jax.ShapeDtypeStruct(x.shape, bf16), jax.ShapeDtypeStruct(spec_shape(pairs), f32)),
        [pltpu.VMEM(spec_shape(pairs), f32), pltpu.VMEM(spec_shape(pairs), f32)],
        2 * 10**9,
        10 * 10**6,
        x,
        kernel_spec,
        skip,
        *tables,
    )


def conv_backward(g, kernel_spec, skip, tables, chips):
    pairs = g.shape[0]
    out_rows = pairs // chips * LANES + CHUNK
    return whole_call(
        partial(backward_body, pairs),
        (jax.ShapeDtypeStruct((chips, out_rows, LANES), bf16), jax.ShapeDtypeStruct(spec_shape(pairs), f32)),
        [pltpu.VMEM(spec_shape(pairs), f32), pltpu.VMEM(spec_shape(pairs), f32)],
        2 * 10**9,
        10 * 10**6,
        g,
        kernel_spec,
        skip,
        *tables,
    )


def filter_backward(g, g_spec, x, x_spec, hidden, weight, delta, tables):
    pairs = x.shape[0]
    lane_turn, turn, _, back = tables
    return whole_call(
        partial(filter_back_body, pairs),
        (
            jax.ShapeDtypeStruct(x.shape, bf16),
            jax.ShapeDtypeStruct((LANES, LANES), f32),
            jax.ShapeDtypeStruct((1, LANES), f32),
        ),
        [
            pltpu.VMEM(spec_shape(pairs), f32),
            pltpu.VMEM(spec_shape(pairs), f32),
            pltpu.VMEM(x.shape, f32),
        ],
        FILLER,
        10 * 10**6,
        g,
        g_spec,
        x,
        x_spec,
        hidden,
        weight,
        delta,
        lane_turn,
        turn,
        back,
        share=1,
    )


def plain_spectrum(x, length):
    pairs, _, lanes = x.shape
    flat = x.astype(f32).reshape(pairs, LANES, 2, lanes // 2).transpose(3, 0, 2, 1)
    tables = spectral_tables(length // 64, LANES)
    return forward_transform(flat.reshape(lanes // 2, length // LANES, LANES), tables)


def plain_inverse(re, im, length):
    tables = spectral_tables(length // 64, LANES)
    back = inverse_transform(re, im, tables, length // LANES)
    channels = back.shape[0]
    back = back.reshape(channels, length // 256, 2, LANES).transpose(1, 3, 2, 0)
    return back.reshape(length // 256, LANES, 2 * channels)


def spectral_tables(rows_total, col_count):
    total_size = rows_total * col_count
    row_index = jnp.arange(rows_total, dtype=jnp.int32)
    col_index = jnp.arange(col_count, dtype=jnp.int32)
    row_angle = (row_index[:, None] * row_index[None, :] % rows_total).astype(f32) * (
        2.0 * math.pi / rows_total
    )
    col_angle = (col_index[:, None] * col_index[None, :] % col_count).astype(f32) * (
        2.0 * math.pi / col_count
    )
    twist_angle = (row_index[:, None] * col_index[None, :]).astype(f32) * (2.0 * math.pi / total_size)
    return (
        jnp.cos(row_angle),
        -jnp.sin(row_angle),
        jnp.cos(twist_angle),
        -jnp.sin(twist_angle),
        jnp.cos(col_angle),
        -jnp.sin(col_angle),
        total_size,
    )


def forward_transform(signal, tables):
    row_cos, row_sin, twist_cos, twist_sin, col_cos, col_sin, _ = tables
    half_rows = signal.shape[1]
    product = partial(jnp.einsum, precision=highest)
    first_re = product("ka,cab->ckb", row_cos[:, :half_rows], signal)
    first_im = product("ka,cab->ckb", row_sin[:, :half_rows], signal)
    turned_re = first_re * twist_cos - first_im * twist_sin
    turned_im = first_re * twist_sin + first_im * twist_cos
    out_re = product("ckb,bm->ckm", turned_re, col_cos) - product("ckb,bm->ckm", turned_im, col_sin)
    out_im = product("ckb,bm->ckm", turned_re, col_sin) + product("ckb,bm->ckm", turned_im, col_cos)
    return (out_re, out_im)


def inverse_transform(spec_re, spec_im, tables, half_rows):
    row_cos, row_sin, twist_cos, twist_sin, col_cos, col_sin, total_size = tables
    product = partial(jnp.einsum, precision=highest)
    back_re = product("ckm,mb->ckb", spec_re, col_cos) + product("ckm,mb->ckb", spec_im, col_sin)
    back_im = product("ckm,mb->ckb", spec_im, col_cos) - product("ckm,mb->ckb", spec_re, col_sin)
    untwist_re = back_re * twist_cos + back_im * twist_sin
    untwist_im = back_im * twist_cos - back_re * twist_sin
    real_part = product("ak,ckb->cab", row_cos[:half_rows], untwist_re) + product(
        "ak,ckb->cab", row_sin[:half_rows], untwist_im
    )
    return real_part / total_size


def plain_window(shape, delta, length):
    pairs, _, lanes = shape
    position = jnp.arange(length, dtype=jnp.int32).reshape(pairs, 2, LANES, 1).astype(f32)
    window = jnp.exp(-(position / (length - 1)) * delta[0, : lanes // 2]) + 0.05
    return window.transpose(0, 2, 1, 3).reshape(shape)


def plain_filter(hidden, weight, delta):
    pairs = hidden.shape[0]
    length = 256 * pairs
    rows = jnp.einsum("jbh,hc->jbc", hidden, weight, precision=highest)
    rows = (rows * plain_window(rows.shape, delta, length)).astype(bf16)
    return plain_spectrum(rows, length)


def plain_forward(x, kernel_spec, skip):
    length = 256 * x.shape[0]
    re, im = plain_spectrum(x, length)
    kre, kim = kernel_spec
    out = plain_inverse(re * kre - im * kim, re * kim + im * kre, length)
    return (out + x.astype(f32) * skip).astype(bf16), (re, im)


def plain_backward(g, x, x_spec, kernel_spec, skip, hidden, weight, delta):
    length = 256 * x.shape[0]
    re, im = plain_spectrum(g, length)
    kre, kim = kernel_spec
    xre, xim = x_spec
    gx = plain_inverse(re * kre + im * kim, im * kre - re * kim, length) + g.astype(f32) * skip
    pre = plain_inverse(re * xre + im * xim, im * xre - re * xim, length).astype(bf16).astype(f32)
    pre = pre * plain_window(pre.shape, delta, length)
    gh = jnp.einsum("jbc,hc->jbh", pre, weight, precision=highest)
    gw = jnp.einsum("jbh,jbc->hc", hidden, pre, precision=highest)
    gskip = jnp.sum(g.astype(f32) * x.astype(f32), axis=(0, 1))[None]
    return gx.astype(bf16), gh.astype(bf16), gw, gskip


def feed_body(nt_ref, ct_ref, up_ref, bias_ref, down_ref, y_ref, gx_ref, gdown_ref, gup_ref, gbias_ref):
    @pl.when(pl.program_id(0) == 0)
    def _():
        y_ref[...] = jnp.zeros_like(y_ref)
        gx_ref[...] = jnp.zeros_like(gx_ref)

    nt, ct, up, down = nt_ref[...], ct_ref[...], up_ref[...], down_ref[...]
    before = jnp.dot(nt, up, preferred_element_type=f32) + bias_ref[...]
    cdf = 0.5 * (1.0 + lax.erf(before * math.sqrt(0.5)))
    active = (before * cdf).astype(bf16)
    slope = cdf + before * (jnp.exp(-0.5 * before * before) * (1.0 / math.sqrt(2.0 * math.pi)))
    g_act = lax.dot_general(ct, down, (((1,), (1,)), ((), ())), preferred_element_type=f32)
    g_before = (g_act * slope).astype(bf16)
    y_ref[...] += jnp.dot(active, down, preferred_element_type=f32)
    gx_ref[...] += lax.dot_general(g_before, up, (((1,), (1,)), ((), ())), preferred_element_type=f32)
    gdown_ref[...] = lax.dot_general(
        active, ct, (((0,), (0,)), ((), ())), preferred_element_type=f32
    ).astype(bf16)
    gup_ref[...] = lax.dot_general(
        nt, g_before, (((0,), (0,)), ((), ())), preferred_element_type=f32
    ).astype(bf16)
    gbias_ref[...] = jnp.sum(g_before.astype(f32), axis=0, keepdims=True)


def feed_forward(nt, ct, up, bias, down):
    rows, width = nt.shape
    hidden = up.shape[1]
    block = min(256, hidden)
    return pl.pallas_call(
        feed_body,
        grid=(hidden // block,),
        in_specs=[
            pl.BlockSpec((rows, width), lambda i: (0, 0)),
            pl.BlockSpec((rows, width), lambda i: (0, 0)),
            pl.BlockSpec((width, block), lambda i: (0, i)),
            pl.BlockSpec((1, block), lambda i: (0, i)),
            pl.BlockSpec((block, width), lambda i: (i, 0)),
        ],
        out_specs=[
            pl.BlockSpec((rows, width), lambda i: (0, 0)),
            pl.BlockSpec((rows, width), lambda i: (0, 0)),
            pl.BlockSpec((block, width), lambda i: (i, 0)),
            pl.BlockSpec((width, block), lambda i: (0, i)),
            pl.BlockSpec((1, block), lambda i: (0, i)),
        ],
        out_shape=[
            jax.ShapeDtypeStruct((rows, width), f32),
            jax.ShapeDtypeStruct((rows, width), f32),
            jax.ShapeDtypeStruct((hidden, width), bf16),
            jax.ShapeDtypeStruct((width, hidden), bf16),
            jax.ShapeDtypeStruct((1, hidden), f32),
        ],
        compiler_params=pltpu.CompilerParams(vmem_limit_bytes=VMEM_BYTES),
        cost_estimate=pl.CostEstimate(
            flops=12 * rows * width * hidden,
            bytes_accessed=8 * width * hidden + 12 * rows * width,
            transcendentals=2 * rows * hidden,
        ),
    )(nt, ct, up, bias, down)


def norm_forward(values, norm_gain, norm_offset):
    center = values - jnp.mean(values, axis=-1, keepdims=True)
    inverse_root = lax.rsqrt(jnp.mean(center * center, axis=-1, keepdims=True) + 1e-05)
    normed = center * inverse_root
    return (normed * norm_gain + norm_offset, normed, inverse_root)


def norm_backward(upstream, normed, inverse_root, norm_gain):
    scaled = upstream * norm_gain
    centered = (
        scaled
        - jnp.mean(scaled, axis=-1, keepdims=True)
        - normed * jnp.mean(scaled * normed, axis=-1, keepdims=True)
    )
    return centered * inverse_root


def contract(left_side, right_side, left_dim, right_dim):
    return lax.dot_general(
        left_side, right_side, (((left_dim,), (right_dim,)), ((), ())), preferred_element_type=f32
    )


def trunk_hidden(trunk, features):
    embed_weight, embed_bias, hidden_weight, hidden_bias, last_weight, last_bias, frequency = trunk
    layer_out = jnp.sin(frequency * (jnp.dot(features, embed_weight, precision=highest) + embed_bias))
    layer_out = jnp.sin(frequency * (jnp.dot(layer_out, hidden_weight, precision=highest) + hidden_bias))
    return jnp.sin(frequency * (jnp.dot(layer_out, last_weight, precision=highest) + last_bias))


def to_owners(value, chips):
    tokens, width = value.shape
    channels = width // chips
    grid = value.reshape(tokens // 256, 2, LANES, chips, channels)
    return grid.transpose(3, 0, 2, 1, 4).reshape(chips, tokens // 256, LANES, 2 * channels)


def from_owners(value):
    chips, pairs, _, lanes = value.shape
    grid = value.reshape(chips, pairs, LANES, 2, lanes // 2)
    return grid.transpose(1, 3, 2, 0, 4).reshape(pairs * 256, chips * (lanes // 2))


def exchange(value):
    return chip_exchange(value)


def flatten(*values):
    return jnp.concatenate([value.reshape(-1) for value in values])


def unflatten(flat, shapes):
    out, at = [], 0
    for shape in shapes:
        size = int(np.prod(shape))
        out.append(flat[at : at + size].reshape(shape))
        at += size
    return out


def to_rows(flat):
    rows = -(-flat.shape[0] // 1024) * 8
    return jnp.pad(flat, (0, rows * LANES - flat.shape[0])).reshape(rows, LANES)


def plain_device(
    tokens,
    cotangent,
    pre_gain,
    pre_offset,
    input_weight,
    input_bias,
    short_weight,
    short_bias,
    skip_weight,
    embed_weight,
    embed_bias,
    hidden_weight,
    hidden_bias,
    last_weight,
    last_bias,
    frequency,
    filter_weight,
    output_weight,
    output_bias,
    post_gain,
    post_offset,
    up_weight,
    up_bias,
    down_weight,
    down_bias,
):
    seq_count = lax.axis_size("seq")
    seq_index = lax.axis_index("seq")
    z, y, core, x = place()
    chips = seq_count // 2
    z_count = seq_count // 4
    chip = seq_index // 2
    tok_count = tokens.shape[1]
    width = tokens.shape[2]
    length = tok_count * seq_count
    channels = width // seq_count
    ff = up_weight.shape[1]
    hidden_own = ff // seq_count
    half = width // 2
    pairs = length // 256

    mine = jnp.stack([tokens[0], cotangent[0]])
    other = swap_core(mine)
    pair = both(mine, other, core)
    tok = pair[:, 0].reshape(2 * tok_count, width)
    cot = pair[:, 1].reshape(2 * tok_count, width)

    def half_columns(value, groups, run):
        rows = value.shape[0]
        grid = value.reshape(rows, groups, chips, 2, run)
        return [grid[:, :, :, side].reshape(rows, groups * chips * run) for side in range(2)]

    def own_rows(value, groups, run):
        sides = half_columns(value, groups, run)
        keep = jnp.where(core == 0, sides[0], sides[1])
        got = swap_core(jnp.where(core == 0, sides[1], sides[0]))
        return jnp.where(core == x, keep, got)

    in_piece = own_rows(input_weight, 3, channels)
    in_half = gather_pieces(in_piece).reshape(width, 3 * half)
    small_shapes = [(width // seq_count,)] * 2 + [(3, channels), (3, 3, channels), (3, channels)]
    small_shapes += [(width // seq_count,)] * 3 + [(hidden_own,), (width // seq_count,)]
    smalls = flatten(
        pre_gain, pre_offset, input_bias, short_weight, short_bias, output_bias, post_gain, post_offset, up_bias, down_bias
    )
    shapes = [v.shape for v in (pre_gain, pre_offset, input_bias, short_weight, short_bias)]
    shapes += [v.shape for v in (output_bias, post_gain, post_offset, up_bias, down_bias)]
    small_rows = to_rows(smalls)
    small_all = gather_small(small_rows.reshape(-1)).astype(f32)
    columns, at = [], 0
    for shape in shapes:
        size = int(np.prod(shape))
        columns.append(small_all[:, at : at + size])
        at += size

    def halved(value, run):
        lead = value.shape[:-1]
        return pick(value.reshape(*lead, -1, 2, run), core, len(lead) + 1).reshape(*lead, -1)

    pre_gain_full, pre_offset_full = columns[0].reshape(-1), columns[1].reshape(-1)
    input_bias_own = halved(columns[2].reshape(3, width), channels).reshape(-1)
    short_full = columns[3].reshape(seq_count, 3, -1).transpose(1, 0, 2).reshape(3, 3, width)
    short_taps = halved(short_full, channels).reshape(3, -1)
    short_bias_own = halved(columns[4].reshape(3, width), channels).reshape(-1)
    output_bias_full = columns[5].reshape(-1)
    post_gain_full, post_offset_full = columns[6].reshape(-1), columns[7].reshape(-1)
    up_bias_own = halved(columns[8].reshape(-1), hidden_own)
    down_bias_full = columns[9].reshape(-1)

    out_rows = output_weight.shape[0] // 2
    up_piece = own_rows(up_weight, 1, hidden_own)
    out_piece = pick(output_weight.reshape(2, out_rows, width), x, 0)
    down_piece = pick(down_weight.reshape(2, hidden_own // 2, width), x, 0)
    up_half = gather_pieces(up_piece).reshape(width, ff // 2)
    n_out, n_down = out_rows // 2, hidden_own // 4
    mixed_piece = jnp.concatenate(
        [out_piece[:n_out], down_piece[:n_down], out_piece[n_out:], down_piece[n_down:]], axis=0
    )
    later = gather_pieces(mixed_piece)
    later = later.reshape(chips, 2, 2, n_out + n_down, width)
    out_half = later[:, :, :, :n_out].reshape(half, width)
    down_half = later[:, :, :, n_out:].reshape(ff // 2, width)

    positions = (seq_index * tok_count + jnp.arange(tok_count, dtype=jnp.int32)).astype(f32)
    relative = positions / (length - 1)
    phases = positions * (2.0 * math.pi / length)
    band_count = (FEATURES - 1) // 2
    band_freq = jnp.linspace(0.0001, band_count - 1, band_count).astype(f32)
    angles = phases[:, None] * band_freq[None, :]
    features = jnp.concatenate([relative[:, None], jnp.cos(angles), -jnp.sin(angles)], axis=1)
    trunk = (embed_weight, embed_bias, hidden_weight, hidden_bias, last_weight, last_bias, frequency)
    hidden_rows, trunk_pull = jax.vjp(partial(trunk_hidden, features=features), trunk)
    units = hidden_rows.shape[1]
    own_pairs = tok_count // 256
    packed = hidden_rows.reshape(own_pairs, 2, LANES, units).transpose(0, 2, 1, 3)
    packed = packed.reshape(own_pairs, LANES, 2 * units)
    filter_hidden = lax.all_gather(packed, "seq", axis=0, tiled=True)
    filter_own = filter_weight.astype(f32)
    zero = jnp.zeros_like(filter_own)
    filter_pair = jnp.concatenate(
        [jnp.concatenate([filter_own, zero], axis=1), jnp.concatenate([zero, filter_own], axis=1)], axis=0
    )
    deltas = jnp.linspace(math.log(0.01) / 1.5, math.log(0.01) / 0.3, width).astype(f32)
    delta_own = jnp.abs(lax.dynamic_slice_in_dim(deltas, seq_index * channels, channels))
    delta_pair = jnp.concatenate([delta_own, delta_own])[None]
    skip_own = skip_weight.astype(f32)
    skip_pair = jnp.concatenate([skip_own, skip_own])[None]
    kernel_spec = plain_filter(filter_hidden, filter_pair, delta_pair)

    rows = 2 * tok_count
    inputs = tok.astype(f32)
    normed_one, unit_one, inverse_one = norm_forward(inputs, pre_gain_full, pre_offset_full)
    normed_low = normed_one.astype(bf16)
    projected_low = (contract(normed_low, in_half, 1, 0) + input_bias_own).astype(bf16)
    shift = [(i, i + 2) for i in range(seq_count - 2)]
    earlier = lax.ppermute(projected_low[rows - 2 :], "seq", shift)
    extended = jnp.concatenate([earlier, projected_low], axis=0).astype(f32)
    convolved = (
        short_taps[0] * extended[:rows]
        + short_taps[1] * extended[1 : rows + 1]
        + short_taps[2] * extended[2:]
        + short_bias_own
    )
    first_part, second_part, values_part = (convolved[:, i * half : (i + 1) * half] for i in range(3))
    gated_low = (values_part * second_part).astype(bf16)
    gated_ch = exchange(to_owners(gated_low, chips)).reshape(pairs, LANES, 2 * channels)
    mixed_ch, gated_spec = plain_forward(gated_ch, kernel_spec, skip_pair)
    chip_shape = (chips, rows // 256, LANES, 2 * channels)
    mixed_tok = from_owners(exchange(mixed_ch.reshape(chip_shape))).astype(f32)
    mix_low = (mixed_tok * first_part).astype(bf16)
    branch_part = contract(mix_low, out_half, 1, 0)
    branch = branch_part + swap_core(branch_part) + output_bias_full
    hidden = inputs + branch

    normed_two, unit_two, inverse_two = norm_forward(hidden, post_gain_full, post_offset_full)
    normed_two_low = normed_two.astype(bf16)
    down_part, back_part, down_grad, up_grad, up_bias_grad = feed_forward(
        normed_two_low, cot, up_half, up_bias_own[None], down_half
    )

    def own_tokens(value):
        return lax.dynamic_slice_in_dim(value, core * tok_count, tok_count, 0)

    def other_tokens(value):
        return lax.dynamic_slice_in_dim(value, (1 - core) * tok_count, tok_count, 0)

    result = own_tokens(hidden) + (
        own_tokens(down_part) + swap_core(other_tokens(down_part)) + down_bias_full
    )
    up_grad = up_grad.reshape(z_count, 2, 2, 2, -1, ff // 2).transpose(0, 1, 3, 2, 4, 5)
    down_sum, up_sum = reduce_pair(down_grad.reshape(z_count, 2, 2, hidden_own // 2, width), up_grad)

    cot_f = cot.astype(f32)
    down_bias_grad = jnp.sum(cot_f, axis=0)
    normed_two_grad = back_part + swap_core(back_part)
    post_gain_grad = jnp.sum(normed_two_grad * unit_two, axis=0)
    post_offset_grad = jnp.sum(normed_two_grad, axis=0)
    hidden_grad = cot_f + norm_backward(normed_two_grad, unit_two, inverse_two, post_gain_full)
    branch_low = hidden_grad.astype(bf16)
    output_bias_grad = jnp.sum(branch_low.astype(f32), axis=0)
    gate_grad = contract(branch_low, out_half, 1, 1)
    mixed_grad_low = (gate_grad * first_part).astype(bf16)
    first_grad = gate_grad * mixed_tok
    mixed_grad_ch = exchange(to_owners(mixed_grad_low, chips)).reshape(pairs, LANES, 2 * channels)
    gated_back, hidden_back, filter_square, skip_line = plain_backward(
        mixed_grad_ch, gated_ch, gated_spec, kernel_spec, skip_pair, filter_hidden, filter_pair, delta_pair
    )
    gated_grad = from_owners(exchange(gated_back.reshape(chip_shape))).astype(f32)
    output_grad = contract(mix_low, branch_low, 0, 0)

    hidden_got = lax.all_to_all(
        hidden_back.reshape(seq_count, own_pairs * LANES, 2 * units), "seq", split_axis=0, concat_axis=0, tiled=True
    )
    hidden_sum = jnp.sum(hidden_got.astype(f32), axis=0)
    hidden_sum = hidden_sum.reshape(own_pairs, LANES, 2, units).transpose(0, 2, 1, 3).reshape(tok_count, units)
    (trunk_grad,) = trunk_pull(hidden_sum)
    filter_grad = filter_square[:units, :channels] + filter_square[units:, channels:]
    skip_grad = skip_line[:, :channels] + skip_line[:, channels:]
    own_grad = jnp.concatenate([filter_grad, skip_grad], axis=0)
    own_grad = own_grad + swap_x(own_grad)
    own_grad = pick(own_grad.reshape(-1, 2, channels // 2), x, 1)

    conv_grad_low = jnp.concatenate(
        [first_grad, gated_grad * values_part, gated_grad * second_part], axis=1
    ).astype(bf16)
    back_shift = [(i + 2, i) for i in range(seq_count - 2)]
    following = lax.ppermute(conv_grad_low[:2], "seq", back_shift)
    conv_grad = conv_grad_low.astype(f32)
    grad_ext = jnp.concatenate([conv_grad_low, following], axis=0).astype(f32)
    projected_grad_low = (
        short_taps[0] * grad_ext[2:] + short_taps[1] * grad_ext[1 : rows + 1] + short_taps[2] * grad_ext[:rows]
    ).astype(bf16)
    short_weight_grad = jnp.stack(
        [jnp.sum(conv_grad * extended[tap : tap + rows], axis=0) for tap in range(3)]
    )
    short_bias_grad = jnp.sum(conv_grad, axis=0)
    input_bias_grad = jnp.sum(projected_grad_low.astype(f32), axis=0)
    input_grad = contract(normed_low, projected_grad_low, 0, 0)
    normed_one_part = contract(projected_grad_low, in_half, 1, 1)
    normed_one_grad = own_tokens(normed_one_part) + swap_core(other_tokens(normed_one_part))
    unit_own = own_tokens(unit_one)
    pre_gain_grad = jnp.sum(normed_one_grad * unit_own, axis=0)
    pre_offset_grad = jnp.sum(normed_one_grad, axis=0)
    tokens_grad = own_tokens(hidden_grad) + norm_backward(
        normed_one_grad, unit_own, own_tokens(inverse_one), pre_gain_full
    )

    in_low = input_grad.astype(bf16).reshape(z_count, 2, 2, 2, -1, 3 * half).transpose(0, 1, 3, 2, 4, 5)
    in_sum = jnp.stack(reduce_pair(in_low[:, :, :, 0], in_low[:, :, :, 1]))
    out_low = output_grad.astype(bf16).reshape(z_count, 2, 2, -1, width)
    split = out_low.shape[3] // 2
    out_sum = jnp.concatenate(reduce_pair(out_low[:, :, :, :split], out_low[:, :, :, split:]), axis=0)

    def whole_columns(value, groups, run):
        got = swap_core(pick(value, 1 - core, 0))
        mine_part = pick(value, core, 0)
        n = mine_part.shape[0]
        grid = both(mine_part, got, core).reshape(2, n, groups, chips, run)
        return grid.transpose(1, 2, 3, 0, 4).reshape(n, -1)

    in_rows = whole_columns(in_sum, 3, channels)
    up_rows_sum = whole_columns(up_sum, 1, hidden_own)

    chip_wide = [post_gain_grad, post_offset_grad, down_bias_grad, output_bias_grad]
    own_wide = [pre_gain_grad, pre_offset_grad, *trunk_grad]
    half_wide = [up_bias_grad.reshape(-1), input_bias_grad, short_weight_grad, short_bias_grad]
    own_flat, half_flat = to_rows(flatten(*own_wide)), to_rows(flatten(*half_wide))
    summed = sum_chips(jnp.concatenate([to_rows(flatten(*chip_wide)), own_flat, half_flat], axis=0))
    n_chip = to_rows(flatten(*chip_wide)).shape[0]
    chip_sum = summed[:n_chip].reshape(-1)
    got = swap_core(summed[n_chip:])
    own_sum = (summed[n_chip:] + got)[: own_flat.shape[0]].reshape(-1)
    half_sums_pair = both(summed[n_chip + own_flat.shape[0] :], got[own_flat.shape[0] :], core).reshape(2, -1)
    chip_sums = unflatten(chip_sum, [v.shape for v in chip_wide])
    own_sums = unflatten(own_sum, [v.shape for v in own_wide])
    half_sums = [
        unflatten(half_sums_pair[side], [v.shape for v in half_wide]) for side in range(2)
    ]

    def joined(index, groups, run):
        pair_of = jnp.stack([half_sums[side][index].reshape(groups, chips, run) for side in range(2)], axis=2)
        return pair_of.reshape(groups, -1)

    block_index = seq_index * 2 + x

    def own_block(value, axis=0):
        size = value.shape[axis] // (2 * seq_count)
        return lax.dynamic_slice_in_dim(value, block_index * size, size, axis)

    up_bias_sum = joined(0, 1, hidden_own).reshape(-1)
    input_bias_sum = joined(1, 3, channels).reshape(-1)
    short_weight_sum = joined(2, 9, channels).reshape(3, -1)
    short_bias_sum = joined(3, 3, channels).reshape(-1)
    return (
        result.astype(bf16)[None],
        tokens_grad.astype(bf16)[None],
        own_block(own_sums[0]),
        own_block(own_sums[1]),
        in_rows,
        own_block(input_bias_sum),
        own_block(short_weight_sum, 1),
        own_block(short_bias_sum),
        own_grad[units],
        *own_sums[2:],
        own_grad[:units],
        out_sum,
        own_block(chip_sums[3]),
        own_block(chip_sums[0]),
        own_block(chip_sums[1]),
        up_rows_sum,
        own_block(up_bias_sum),
        down_sum,
        own_block(chip_sums[2]),
    )


def after(earlier, value):
    return lax.optimization_barrier((earlier, value))[1]


def gather_z(piece, gates=None):
    have = piece[None]
    masks = z_masks(lax.axis_size("seq") // 4)
    for step, mask in enumerate(masks):
        if gates is not None and step == len(masks) - 1:
            have = after(gates, have)
        have = jnp.concatenate([have, swap_z(have, mask)], axis=0)
    return have


def gather_near(have):
    half = have.shape[1] // 2
    first, second = have[:, :half], have[:, half:]
    return jnp.stack([first, swap_y(first)]), jnp.stack([second, swap_x(second)])


def gather_far(near):
    first, second = near
    return first, swap_x(first), second, swap_y(second)


def reduce_pass(kept, got, second):
    sent = (kept[1].astype(f32) + got[1].astype(f32)).astype(bf16)
    return sent, kept[0].astype(f32) + got[0].astype(f32), second(sent)


def reduce_z_step(total, mask):
    half = total.shape[0] // 2
    return total[:half] + swap_z(total[half:].astype(bf16), mask).astype(f32)


def reduce_far(total, masks):
    for mask in masks:
        total = reduce_z_step(total, mask)
    return total[0]


def place_pieces(out_ref, pieces, scalars, chips, span):
    first, first_far, second, second_far = pieces
    x = scalars[0]
    half = span // 2
    z_count = chips // 2
    for slot in range(z_count):
        for yr in range(2):
            base = scalars[2 + yr * z_count + slot] * (2 * span)
            source = second_far if yr else second
            for xr in range(2):
                at = pl.multiple_of(base + (x if xr == 0 else 1 - x) * span, span)
                out_ref[pl.ds(at, half), :] = (first_far if xr else first)[yr, slot]
                out_ref[pl.ds(pl.multiple_of(at + half, half), half), :] = source[xr, slot]


def route_rows(grad_ref, kept_ref, sent_ref, scalars, chips, inner, by_x):
    x = scalars[0]
    z_count = chips // 2
    rows = grad_ref.shape[0] // (2 * chips * inner)
    tiles, _, columns = kept_ref.shape[3:]
    for slot in range(z_count):
        for yr in range(2):
            base = scalars[2 + yr * z_count + slot] * (2 * inner * rows)
            for xr in range(2):
                is_sent, lead = (xr, yr) if by_x else (yr, xr)
                for part in range(inner):
                    at = pl.multiple_of(base + part * 2 * rows + (x if xr == 0 else 1 - x) * rows, rows)
                    for tile in range(tiles):
                        value = grad_ref[pl.ds(at, rows), tile * columns : (tile + 1) * columns].astype(bf16)
                        if not is_sent:
                            kept_ref[lead, slot, part, tile] = value
                        elif isinstance(sent_ref, tuple):
                            sent_ref[lead][slot, part, tile] = value
                        else:
                            sent_ref[lead, slot, part, tile] = value


HALO = 16


def short_conv(rows, taps, bias):
    two, one = pltpu.roll(rows, 2, 0), pltpu.roll(rows, 1, 0)
    return (taps[0:1] * two + taps[1:2] * one + taps[2:3] * rows + bias)[HALO:]


def chip_rows(convolved):
    return convolved[: convolved.shape[0] - HALO]


def pack_pairs(out_ref, index, pair, even, odd):
    half = LANES // 2
    lower = lax.broadcasted_iota(jnp.int32, even.shape, 1) < half
    out_ref[index, pair] = jnp.where(lower, even, pltpu.roll(odd, half, 1)).astype(bf16)
    out_ref[index + 1, pair] = jnp.where(lower, pltpu.roll(even, half, 1), odd).astype(bf16)


def pack_rows(out_ref, index, value):
    for pair in range(value.shape[0] // 256):
        rows = value[256 * pair : 256 * (pair + 1)]
        pack_pairs(out_ref, index, pair, rows[:LANES], rows[LANES:])


def unpack_pair(one, two):
    half = LANES // 2
    one, two = one.astype(f32), two.astype(f32)
    lower = lax.broadcasted_iota(jnp.int32, one.shape, 1) < half
    return jnp.where(lower, one, pltpu.roll(two, half, 1)), jnp.where(lower, pltpu.roll(one, half, 1), two)


def unpack_rows(in_ref, index):
    out = []
    for pair in range(in_ref.shape[1]):
        out.extend(unpack_pair(in_ref[index, pair], in_ref[index + 1, pair]))
    return jnp.concatenate(out, axis=0)


def project_body(scalars, normed_ref, bias_ref, a_ref, ax_ref, b_ref, by_ref, out_ref, weight_ref):
    chips = 2 * a_ref.shape[1]
    place_pieces(weight_ref, (a_ref, ax_ref, b_ref, by_ref), scalars, chips, 2 * a_ref.shape[2])
    value = jnp.dot(normed_ref[...], weight_ref[...], preferred_element_type=f32) + bias_ref[...]
    row = lax.broadcasted_iota(jnp.int32, value.shape, 0)
    value = jnp.where(jnp.logical_and(row < HALO, scalars[1] == 0), 0.0, value)
    out_ref[...] = value.astype(bf16)


def grid_call(body, scalars, grid, ins, outs, scratch, flops, moved, transcendentals=0):
    return pl.pallas_call(
        body,
        grid_spec=pltpu.PrefetchScalarGridSpec(
            num_scalar_prefetch=1,
            grid=(grid,),
            in_specs=[pl.BlockSpec(block, index) for _, block, index in ins],
            out_specs=[pl.BlockSpec(block, index) for _, _, block, index in outs],
            scratch_shapes=scratch,
        ),
        out_shape=[jax.ShapeDtypeStruct(shape, dtype) for shape, dtype, _, _ in outs],
        compiler_params=pltpu.CompilerParams(vmem_limit_bytes=VMEM_BYTES),
        cost_estimate=pl.CostEstimate(flops=flops // SHARE, bytes_accessed=moved // SHARE, transcendentals=0),
    )(scalars, *[value for value, _, _ in ins])


def fixed(value):
    return (value, value.shape, lambda i, s, n=value.ndim: (0,) * n)


def fixed_out(shape, dtype):
    return (shape, dtype, shape, lambda i, s, n=len(shape): (0,) * n)


def project(scalars, normed, bias, pieces):
    rows, width = normed.shape
    columns = bias.shape[1]
    block = columns // 3
    lead = pieces[0].shape[:3]
    piece_specs = [(p, (*lead, block), lambda i, s: (0, 0, 0, i)) for p in pieces]
    return grid_call(
        project_body,
        scalars,
        3,
        [fixed(normed), (bias, (1, block), lambda i, s: (0, i)), *piece_specs],
        [
            ((rows, columns), bf16, (rows, block), lambda i, s: (0, i)),
            ((width, columns), bf16, (width, block), lambda i, s: (0, i)),
        ],
        [],
        2 * rows * width * columns,
        4 * width * columns + 2 * rows * (width + columns),
    )


def gate_body(scalars, second_ref, values_ref, t2_ref, t3_ref, b2_ref, b3_ref, out_ref):
    second = short_conv(second_ref[...].astype(f32), t2_ref[...], b2_ref[...])
    values = short_conv(values_ref[...].astype(f32), t3_ref[...], b3_ref[...])
    pack_rows(out_ref, 0, chip_rows(values * second))


def stream_tiles(projected, taps, bias, stream, tiles):
    rows = projected.shape[0]
    index = lambda i, s, at=stream * tiles: (0, at + i)
    return (
        (projected, (rows, LANES), index),
        (taps, (3, LANES), index),
        (bias, (1, LANES), index),
    )


def gate(scalars, projected, taps, bias, chips):
    rows, columns = projected.shape
    tiles = columns // 3 // LANES
    p2, t2, b2 = stream_tiles(projected, taps, bias, 1, tiles)
    p3, t3, b3 = stream_tiles(projected, taps, bias, 2, tiles)
    pairs = (rows - 2 * HALO) // 256
    (out,) = grid_call(
        gate_body,
        scalars,
        tiles,
        [p2, p3, t2, t3, b2, b3],
        [((chips, pairs, LANES, LANES), bf16, (2, pairs, LANES, LANES), lambda i, s: (i, 0, 0, 0))],
        [],
        20 * rows * columns,
        3 * rows * columns,
    )
    return out


def branch_body(
    scalars, mixed_ref, first_ref, taps_ref, bias_ref, a_ref, ax_ref, b_ref, by_ref, mixed_out, mix_out, weight_ref, out_ref
):
    chips = 2 * a_ref.shape[1]
    place_pieces(weight_ref, (a_ref, ax_ref, b_ref, by_ref), scalars, chips, 2 * a_ref.shape[2])
    for tile in range(chips // 2):
        cols = slice(tile * LANES, (tile + 1) * LANES)
        mixed = unpack_rows(mixed_ref, 2 * tile)
        first = chip_rows(short_conv(first_ref[:, cols].astype(f32), taps_ref[:, cols], bias_ref[:, cols]))
        mixed_out[:, cols] = mixed.astype(bf16)
        mix_out[:, cols] = (mixed * first).astype(bf16)
    out_ref[...] = jnp.dot(mix_out[...], weight_ref[...], preferred_element_type=f32)


def first_stream(projected, taps, bias):
    rows, columns = projected.shape
    block = columns // 3
    return [
        (projected, (rows, block), lambda i, s: (0, 0)),
        (taps, (3, block), lambda i, s: (0, 0)),
        (bias, (1, block), lambda i, s: (0, 0)),
    ]


def branch_out(scalars, mixed, projected, taps, bias, pieces, piece_rows):
    rows = projected.shape[0] - 2 * HALO
    half = projected.shape[1] // 3
    width = pieces[0].shape[3]
    return grid_call(
        branch_body,
        scalars,
        1,
        [
            fixed(mixed),
            *first_stream(projected, taps, bias),
            *[
                (p, (*p.shape[:2], piece_rows, width), lambda i, s, at=p.shape[2] // piece_rows - 1: (0, 0, at, 0))
                for p in pieces
            ],
        ],
        [
            fixed_out((rows, half), bf16),
            fixed_out((rows, half), bf16),
            fixed_out((half, width), bf16),
            fixed_out((rows, width), f32),
        ],
        [],
        2 * rows * half * width,
        4 * rows * width + 6 * half * width,
    )


def tiled_feed_body(
    scalars,
    nt_ref,
    ct_ref,
    bias_ref,
    ua_ref,
    uax_ref,
    ub_ref,
    uby_ref,
    da_ref,
    dax_ref,
    db_ref,
    dby_ref,
    y_ref,
    gx_ref,
    gdown_kept,
    gdown_late,
    gdown_first,
    gup_kept,
    gup_late,
    gup_first,
    gbias_ref,
    up_ref,
    down_ref,
    grad_ref,
):
    step = pl.program_id(0)
    z_count = ua_ref.shape[1]
    x = scalars[0]

    @pl.when(step == 0)
    def _():
        y_ref[...] = jnp.zeros_like(y_ref)
        gx_ref[...] = jnp.zeros_like(gx_ref)

    place_pieces(up_ref, (ua_ref, uax_ref, ub_ref, uby_ref), scalars, 2 * z_count, 2 * ua_ref.shape[2])
    span = down_ref.shape[0] // 2
    half = span // 2
    own, other = pl.multiple_of(x * span, span), pl.multiple_of((1 - x) * span, span)
    down_ref[pl.ds(own, half), :] = da_ref[0, 0]
    down_ref[pl.ds(other, half), :] = dax_ref[0, 0]

    def put_second(source):
        down_ref[pl.ds(pl.multiple_of(own + half, half), half), :] = source[0, 0]
        down_ref[pl.ds(pl.multiple_of(other + half, half), half), :] = source[1, 0]

    @pl.when(step < z_count)
    def _():
        put_second(db_ref)

    @pl.when(step >= z_count)
    def _():
        put_second(dby_ref)

    nt, ct, up, down = nt_ref[...], ct_ref[...], up_ref[...], down_ref[...]
    before = jnp.dot(nt, up, preferred_element_type=f32) + bias_ref[...]
    cdf = 0.5 * (1.0 + lax.erf(before * math.sqrt(0.5)))
    active = (before * cdf).astype(bf16)
    slope = cdf + before * (jnp.exp(-0.5 * before * before) * (1.0 / math.sqrt(2.0 * math.pi)))
    g_act = lax.dot_general(ct, down, (((1,), (1,)), ((), ())), preferred_element_type=f32)
    g_before = (g_act * slope).astype(bf16)
    y_ref[...] += jnp.dot(active, down, preferred_element_type=f32)
    gx_ref[...] += lax.dot_general(g_before, up, (((1,), (1,)), ((), ())), preferred_element_type=f32)
    gdown = lax.dot_general(active, ct, (((0,), (0,)), ((), ())), preferred_element_type=f32)
    one, two = gdown[:span], gdown[span:]
    gdown_kept[0, 0] = jnp.where(x == 0, one, two).astype(bf16)
    sent = jnp.where(x == 0, two, one).astype(bf16)

    @pl.when(step < z_count)
    def _():
        gdown_late[0] = sent

    @pl.when(step >= z_count)
    def _():
        gdown_first[0] = sent

    grad_ref[...] = lax.dot_general(nt, g_before, (((0,), (0,)), ((), ())), preferred_element_type=f32)
    route_rows(grad_ref, gup_kept, (gup_late, gup_first), scalars, 2 * z_count, 2, False)
    gbias_ref[...] = jnp.sum(g_before.astype(f32), axis=0, keepdims=True)


def tiled_feed(scalars, nt, ct, bias, pieces, down_pieces, up_rows, down_rows):
    rows, width = nt.shape
    hidden = bias.shape[1]
    z_count = pieces[0].shape[1]
    chips = 2 * z_count
    block = hidden // chips
    per = width // block
    tiles = hidden // width
    column = lambda i, s: (0, s[2 + i])
    up_specs = [(p, (2, z_count, up_rows, block), lambda i, s: (0, 0, s[2 + i] // per, s[2 + i] % per)) for p in pieces]
    near = lambda i, s: (i // z_count, i % z_count, 0, 0)
    far = lambda i, s: (0, i % z_count, 0, 0)
    down_specs = [(p, (1, 1, down_rows, width), near) for p in down_pieces[:2]]
    down_specs += [(p, (2, 1, down_rows, width), far) for p in down_pieces[2:]]
    down_shape, down_block = (z_count, 2 * down_rows, width), (1, 2 * down_rows, width)
    up_shape = (z_count, 2, tiles, up_rows, width)
    up_block = (z_count, 2, 1, up_rows, block)
    up_index = lambda i, s: (0, 0, s[2 + i] // per, 0, s[2 + i] % per)
    return grid_call(
        tiled_feed_body,
        scalars,
        chips,
        [fixed(nt), fixed(ct), (bias, (1, block), column), *up_specs, *down_specs],
        [
            fixed_out((rows, width), f32),
            fixed_out((rows, width), f32),
            ((2, *down_shape), bf16, (1, *down_block), lambda i, s: (i // z_count, i % z_count, 0, 0)),
            (down_shape, bf16, down_block, lambda i, s: (jnp.minimum(i, z_count - 1), 0, 0)),
            (down_shape, bf16, down_block, lambda i, s: (jnp.maximum(i - z_count, 0), 0, 0)),
            ((2, *up_shape), bf16, (2, *up_block), lambda i, s: (0, *up_index(i, s))),
            (up_shape, bf16, up_block, up_index),
            (up_shape, bf16, up_block, up_index),
            ((1, hidden), f32, (1, block), column),
        ],
        [pltpu.VMEM((width, block), bf16), pltpu.VMEM((block, width), bf16), pltpu.VMEM((width, block), f32)],
        12 * rows * width * hidden,
        8 * width * hidden + 12 * rows * width,
        2 * rows * hidden,
    )


def unbranch_body(
    scalars,
    g_ref,
    mix_ref,
    mixed_ref,
    first_ref,
    taps_ref,
    bias_ref,
    weight_ref,
    gmixed_ref,
    gfirst_ref,
    kept_ref,
    sent_ref,
    grad_ref,
):
    chips = gmixed_ref.shape[0]
    g = g_ref[...]
    gate_grad = lax.dot_general(g, weight_ref[...], (((1,), (1,)), ((), ())), preferred_element_type=f32)
    for tile in range(chips // 2):
        cols = slice(tile * LANES, (tile + 1) * LANES)
        first = chip_rows(short_conv(first_ref[:, cols].astype(f32), taps_ref[:, cols], bias_ref[:, cols]))
        gfirst_ref[:, cols] = (gate_grad[:, cols] * mixed_ref[:, cols].astype(f32)).astype(bf16)
        pack_rows(gmixed_ref, 2 * tile, gate_grad[:, cols] * first)
    grad_ref[...] = lax.dot_general(mix_ref[...], g, (((0,), (0,)), ((), ())), preferred_element_type=f32)
    route_rows(grad_ref, kept_ref, sent_ref, scalars, chips, 1, False)


def unbranch(scalars, g, mix, mixed, projected, taps, bias, weight, chips):
    rows, width = g.shape
    half = weight.shape[0]
    grad_shape = (2, chips // 2, 1, width // half, half // (2 * chips), half)
    return grid_call(
        unbranch_body,
        scalars,
        1,
        [fixed(g), fixed(mix), fixed(mixed), *first_stream(projected, taps, bias), fixed(weight)],
        [
            fixed_out((chips, rows // 256, LANES, LANES), bf16),
            fixed_out((rows, half), bf16),
            fixed_out(grad_shape, bf16),
            fixed_out(grad_shape, bf16),
        ],
        [pltpu.VMEM((half, width), f32)],
        4 * rows * half * width,
        4 * rows * width + 6 * half * width,
    )


def ungate_body(scalars, gated_ref, second_ref, values_ref, t2_ref, t3_ref, b2_ref, b3_ref, gsecond_ref, gvalues_ref):
    pairs = (gated_ref.shape[1] - HALO) // LANES
    blocks = [gated_ref.at[:, pl.ds(pair * LANES, LANES), :] for pair in range(pairs)]
    grad = jnp.concatenate([part for block in blocks for part in unpack_pair(block[0], block[1])], axis=0)
    ahead, _ = unpack_pair(gated_ref[0, pairs * LANES :], gated_ref[1, pairs * LANES :])
    grad = jnp.concatenate([grad, ahead], axis=0)
    second = short_conv(second_ref[...].astype(f32), t2_ref[...], b2_ref[...])
    values = short_conv(values_ref[...].astype(f32), t3_ref[...], b3_ref[...])
    gsecond_ref[...] = (grad * values).astype(bf16)
    gvalues_ref[...] = (grad * second).astype(bf16)


def ungate(scalars, gated, projected, taps, bias):
    rows, columns = projected.shape
    half = columns // 3
    tiles = half // LANES
    p2, t2, b2 = stream_tiles(projected, taps, bias, 1, tiles)
    p3, t3, b3 = stream_tiles(projected, taps, bias, 2, tiles)
    out = ((rows - HALO, half), bf16, (rows - HALO, LANES), lambda i, s: (0, i))
    return grid_call(
        ungate_body,
        scalars,
        tiles,
        [(gated, (2, *gated.shape[1:]), lambda i, s: (i, 0, 0)), p2, p3, t2, t3, b2, b3],
        [out, out],
        [],
        20 * rows * columns,
        3 * rows * columns,
    )


def stream_body(
    by_x, scalars, grad_ref, rows_ref, taps_ref, normed_ref, gproj_ref, kept_ref, sent_ref, sums_ref, work_ref
):
    count, columns = gproj_ref.shape
    chips = 2 * kept_ref.shape[1]
    for at in range(0, columns, LANES):
        cols = slice(at, at + LANES)
        taps = taps_ref[:, cols]
        ext = grad_ref[:, cols].astype(f32)
        grad = ext[:count]
        total = count + HALO
        one, two = pltpu.roll(ext, total - 1, 0)[:count], pltpu.roll(ext, total - 2, 0)[:count]
        low = (taps[0:1] * two + taps[1:2] * one + taps[2:3] * grad).astype(bf16)
        gproj_ref[:, cols] = low
        rows = rows_ref[:, cols].astype(f32)
        sums = [
            jnp.sum(grad * pltpu.roll(rows, 2, 0)[HALO:total], axis=0, keepdims=True),
            jnp.sum(grad * pltpu.roll(rows, 1, 0)[HALO:total], axis=0, keepdims=True),
            jnp.sum(grad * rows[HALO:total], axis=0, keepdims=True),
            jnp.sum(grad, axis=0, keepdims=True),
            jnp.sum(low.astype(f32), axis=0, keepdims=True),
            jnp.zeros((3, LANES), f32),
        ]
        sums_ref[:, cols] = jnp.concatenate(sums, axis=0)
    work_ref[...] = lax.dot_general(
        normed_ref[HALO:total, :], gproj_ref[...], (((0,), (0,)), ((), ())), preferred_element_type=f32
    )
    route_rows(work_ref, kept_ref, sent_ref, scalars, chips, 2, by_x)


def stream_back(scalars, grad, projected, taps, normed, stream, chips, by_x):
    count, columns = grad.shape[0] - HALO, grad.shape[1]
    width = normed.shape[1]
    rows = projected.shape[0]
    index = lambda i, s: (0, stream)
    shape = (2, chips // 2, 2, 1, width // (4 * chips), columns)
    return grid_call(
        partial(stream_body, by_x),
        scalars,
        1,
        [
            fixed(grad),
            (projected, (rows, columns), index),
            (taps, (3, columns), index),
            fixed(normed),
        ],
        [
            fixed_out((count, columns), bf16),
            fixed_out(shape, bf16),
            fixed_out(shape, bf16),
            fixed_out((8, columns), f32),
        ],
        [pltpu.VMEM((width, columns), f32)],
        2 * count * columns * width,
        4 * count * columns + 2 * count * width + 2 * width * columns,
    )


def split_body(run, scalars, in_ref, kept_ref, sent_ref):
    core = scalars[0]
    if run == LANES // 2:
        one, two = in_ref[:, :LANES].astype(f32), in_ref[:, LANES:].astype(f32)
        lower = lax.broadcasted_iota(jnp.int32, one.shape, 1) < run
        sides = (
            jnp.where(lower, one, pltpu.roll(two, run, 1)).astype(bf16),
            jnp.where(lower, pltpu.roll(one, run, 1), two).astype(bf16),
        )
        kept_ref[...] = jnp.where(core == 0, sides[0], sides[1])
        sent_ref[...] = jnp.where(core == 0, sides[1], sides[0])
    else:
        kept_ref[...] = jnp.where(core == 0, in_ref[:, :run], in_ref[:, run:])
        sent_ref[...] = jnp.where(core == 0, in_ref[:, run:], in_ref[:, :run])


def split_columns(core, value, run, tile=None):
    rows, columns = value.shape
    block = max(run, LANES)
    if tile is None:
        out = ((rows, columns // 2), bf16, (rows, block), lambda i, s: (0, i))
    else:
        per = tile // block
        out = ((columns // 2 // tile, rows, tile), bf16, (None, rows, block), lambda i, s: (i // per, 0, i % per))
    return grid_call(
        partial(split_body, run),
        core.reshape(1),
        columns // (2 * block),
        [(value, (rows, 2 * block), lambda i, s: (0, i))],
        [out, out],
        [],
        rows * columns,
        4 * rows * columns,
    )


def filter_features(seq_index, tok_count, length):
    positions = (seq_index * tok_count + jnp.arange(tok_count, dtype=jnp.int32)).astype(f32)
    relative = positions / (length - 1)
    phases = positions * (2.0 * math.pi / length)
    band_count = (FEATURES - 1) // 2
    band_freq = jnp.linspace(0.0001, band_count - 1, band_count).astype(f32)
    angles = phases[:, None] * band_freq[None, :]
    return jnp.concatenate([relative[:, None], jnp.cos(angles), -jnp.sin(angles)], axis=1)


def tiled_device(
    tokens,
    cotangent,
    pre_gain,
    pre_offset,
    input_weight,
    input_bias,
    short_weight,
    short_bias,
    skip_weight,
    embed_weight,
    embed_bias,
    hidden_weight,
    hidden_bias,
    last_weight,
    last_bias,
    frequency,
    filter_weight,
    output_weight,
    output_bias,
    post_gain,
    post_offset,
    up_weight,
    up_bias,
    down_weight,
    down_bias,
):
    seq_count = lax.axis_size("seq")
    seq_index = lax.axis_index("seq")
    z, y, core, x = place()
    chips = seq_count // 2
    z_count = seq_count // 4
    tok_count, width = tokens.shape[1:]
    length = tok_count * seq_count
    channels = width // seq_count
    ff = up_weight.shape[1]
    hidden_own = ff // seq_count
    half = width // 2
    pairs = length // 256
    rows = 2 * tok_count
    chip_at = [(z ^ rel) * 2 + (y ^ yr) for yr in range(2) for rel in z_order(z_count)]
    scalars = jnp.stack([x, seq_index // 2, *chip_at]).astype(jnp.int32)

    def own_rows(value, run, tile=None):
        keep, sent = split_columns(core, value, run, tile)
        return jnp.where(core == x, keep, swap_core(sent))

    in_piece = own_rows(input_weight, channels)
    mine = jnp.stack([after(in_piece, tokens)[0], cotangent[0]])
    pair = both(mine, swap_core(mine), core)
    tok = pair[:, 0].reshape(rows, width)
    cot = pair[:, 1].reshape(rows, width)
    onward = [(i, i + 2) for i in range(seq_count - 2)]
    backward = [(i + 2, i) for i in range(seq_count - 2)]
    earlier = lax.ppermute(tok[rows - HALO :], "seq", onward)
    later = lax.ppermute(tok[:HALO], "seq", backward)
    tok_ext = jnp.concatenate([earlier, tok, later], axis=0)
    vectors = [
        pre_gain,
        pre_offset,
        input_bias,
        short_weight,
        short_bias,
        output_bias,
        post_gain,
        post_offset,
        up_bias,
        down_bias,
    ]
    small_blocks = []
    for vector in vectors:
        flat = vector.reshape(-1)
        small_blocks.append(jnp.pad(flat, (0, -flat.shape[0] % LANES)).reshape(-1, LANES))
    small_count = sum(block.shape[0] for block in small_blocks)
    small_blocks.append(jnp.zeros((-small_count % 8, LANES), bf16))
    small = jnp.concatenate(small_blocks, axis=0).astype(f32)

    in_have = gather_z(in_piece, (earlier, later))

    trunk = (embed_weight, embed_bias, hidden_weight, hidden_bias, last_weight, last_bias, frequency)
    features = filter_features(after(tok, seq_index), tok_count, length)
    hidden_rows, trunk_pull = jax.vjp(partial(trunk_hidden, features=features), trunk)
    units = hidden_rows.shape[1]
    own_pairs = tok_count // 256
    packed = hidden_rows.reshape(own_pairs, 2, LANES, units).transpose(0, 2, 1, 3)
    packed = packed.reshape(own_pairs * LANES, 2 * units)
    gathered = gather_small(after((earlier, later), jnp.concatenate([packed, small], axis=0)))
    filter_hidden = gathered[:, : own_pairs * LANES].reshape(pairs, LANES, 2 * units)
    small_all = gathered[:, own_pairs * LANES :].reshape(seq_count, -1)

    in_near = gather_near(in_have)
    in_pieces = gather_far(in_near)

    up_piece = own_rows(after(in_piece, up_weight), hidden_own, width)
    out_piece = pick(after(in_piece, output_weight).reshape(2, -1, width), x, 0)
    down_piece = pick(after(in_piece, down_weight).reshape(2, -1, width), x, 0)
    up_half, out_half_rows, down_half_rows = up_piece.shape[1] // 2, out_piece.shape[0] // 2, down_piece.shape[0] // 2
    parts = []
    for side in range(2):
        parts.append(up_piece[:, side * up_half : (side + 1) * up_half].reshape(-1, width))
        parts.append(out_piece[side * out_half_rows : (side + 1) * out_half_rows])
    rest_have = gather_z(after(in_have, jnp.concatenate(parts, axis=0)))
    rest_near = gather_near(after(in_pieces, rest_have))
    down_have = gather_z(after(rest_have, down_piece))

    columns, at = [], 0
    for vector in vectors:
        columns.append(small_all[:, at : at + vector.size])
        at += vector.size + -vector.size % LANES

    def halved(value, run):
        lead = value.shape[:-1]
        return pick(value.reshape(*lead, -1, 2, run), core, len(lead) + 1).reshape(*lead, -1)

    pre_gain_full, pre_offset_full = columns[0].reshape(-1), columns[1].reshape(-1)
    input_bias_own = halved(columns[2].reshape(3, width), channels).reshape(1, -1)
    short_full = columns[3].reshape(seq_count, 3, -1).transpose(1, 0, 2).reshape(3, 3, width)
    taps = halved(short_full, channels).reshape(3, -1)
    short_bias_own = halved(columns[4].reshape(3, width), channels).reshape(1, -1)
    output_bias_full = columns[5].reshape(-1)
    post_gain_full, post_offset_full = columns[6].reshape(-1), columns[7].reshape(-1)
    up_bias_own = halved(columns[8].reshape(-1), hidden_own)[None]
    down_bias_full = columns[9].reshape(-1)

    filter_own = filter_weight.astype(f32)
    zero = jnp.zeros_like(filter_own)
    filter_pair = jnp.concatenate(
        [jnp.concatenate([filter_own, zero], axis=1), jnp.concatenate([zero, filter_own], axis=1)], axis=0
    )
    deltas = jnp.linspace(math.log(0.01) / 1.5, math.log(0.01) / 0.3, width).astype(f32)
    delta_own = jnp.abs(lax.dynamic_slice_in_dim(deltas, seq_index * channels, channels))
    delta_pair = jnp.concatenate([delta_own, delta_own])[None]
    skip_own = skip_weight.astype(f32)
    skip_pair = jnp.concatenate([skip_own, skip_own])[None]
    tables = tuple(jnp.asarray(t) for t in conv_tables(pairs))

    normed_one, unit_one, inverse_one = norm_forward(tok_ext.astype(f32), pre_gain_full, pre_offset_full)
    normed_ext = normed_one.astype(bf16)
    in_pieces = after((normed_ext, input_bias_own, taps, short_bias_own), in_pieces)
    projected, in_half = project(scalars, normed_ext, input_bias_own, in_pieces)
    gated = gate(scalars, after(rest_near, projected), taps, short_bias_own, chips)
    rest_pieces = gather_far(after(gated, rest_near))
    filter_hidden = after(gated, filter_hidden)
    kernel_spec = conv_filter(filter_hidden, filter_pair, delta_pair, tables)
    gated_ch = chip_exchange(gated).reshape(pairs, LANES, LANES)
    down_near = gather_near(after((rest_pieces, gated_ch, kernel_spec), down_have))
    gated_ch = after(rest_pieces, gated_ch)
    mixed_ch, gated_spec = conv_forward(gated_ch, kernel_spec, skip_pair, tables)
    chip_shape = (chips, rows // 256, LANES, LANES)
    mixed_back = chip_exchange(mixed_ch.reshape(chip_shape))
    down_pieces = gather_far(after(mixed_ch, down_near))
    mixed_tok, mix_low, out_half, branch_part = branch_out(
        scalars, after(down_pieces, mixed_back), projected, taps, short_bias_own, rest_pieces, out_half_rows
    )
    hidden = tok.astype(f32) + (branch_part + swap_core(branch_part) + output_bias_full)

    normed_two, unit_two, inverse_two = norm_forward(hidden, post_gain_full, post_offset_full)
    (
        down_part,
        back_part,
        gdown_kept,
        gdown_late,
        gdown_first,
        gup_kept,
        gup_late,
        gup_first,
        up_bias_grad,
    ) = tiled_feed(scalars, normed_two.astype(bf16), cot, up_bias_own, rest_pieces, down_pieces, up_half, down_half_rows)
    up_flat = gdown_kept.shape
    gup_kept, gup_late, gup_first = (
        value.reshape(*shape) for value, shape in ((gup_kept, up_flat), (gup_late, up_flat[1:]), (gup_first, up_flat[1:]))
    )

    def own_tokens(value):
        return lax.dynamic_slice_in_dim(value, core * tok_count, tok_count, 0)

    def other_tokens(value):
        return lax.dynamic_slice_in_dim(value, (1 - core) * tok_count, tok_count, 0)

    normed_two_grad = back_part + swap_core(back_part)
    cot_f = cot.astype(f32)
    hidden_grad = cot_f + norm_backward(normed_two_grad, unit_two, inverse_two, post_gain_full)
    branch_low = hidden_grad.astype(bf16)
    gmixed, gfirst, gout_kept, gout_sent = unbranch(
        scalars, branch_low, mix_low, mixed_tok, projected, taps, short_bias_own, out_half, chips
    )
    mixed_grad_ch = chip_exchange(gmixed).reshape(pairs, LANES, LANES)

    def add_parts(kept, got):
        return kept.astype(f32) + got.astype(f32)

    down_got, up_got = after(gmixed, (swap_x(gdown_first), swap_y(gup_first)))
    down_next, up_next = add_parts(gdown_kept[1], down_got).astype(bf16), add_parts(gup_kept[1], up_got).astype(bf16)
    down_got, up_got = swap_y(down_next), swap_x(up_next)
    down_late, up_late = after((down_next, up_next), (gdown_late, gup_late))
    down_late, up_late = swap_x(down_late), swap_y(up_late)
    mixed_grad_ch = after((down_next, up_next), mixed_grad_ch)

    gated_back, grad_spec = conv_backward(mixed_grad_ch, kernel_spec, skip_pair, tables, chips)
    hidden_back, filter_square, skip_line = filter_backward(
        mixed_grad_ch, after(gated_back, grad_spec), gated_ch, gated_spec, filter_hidden, filter_pair, delta_pair, tables
    )
    gated_grad = chip_exchange(gated_back)

    down_part = after(gmixed, down_part)
    result = own_tokens(hidden) + (
        own_tokens(down_part) + swap_core(other_tokens(down_part)) + down_bias_full
    )
    down_bias_grad = jnp.sum(after(gmixed, cot).astype(f32), axis=0)
    post_gain_grad = jnp.sum(normed_two_grad * unit_two, axis=0)
    post_offset_grad = jnp.sum(normed_two_grad, axis=0)
    output_bias_grad = jnp.sum(branch_low.astype(f32), axis=0)

    gfirst_next = lax.ppermute(gfirst[:HALO], "seq", backward)
    gated_grad = after(hidden_back, gated_grad)
    gsecond, gvalues = ungate(scalars, gated_grad, projected, taps, short_bias_own)
    gfirst = jnp.concatenate([gfirst, after(gsecond, gfirst_next)], axis=0)
    first_proj, first_kept, first_sent, first_sums = stream_back(
        scalars, gfirst, projected, taps, normed_ext, 0, chips, True
    )
    second_proj, second_kept, second_sent, second_sums = stream_back(
        scalars, gsecond, projected, taps, normed_ext, 1, chips, True
    )
    values_proj, values_kept, values_sent, values_sums = stream_back(
        scalars, gvalues, projected, taps, normed_ext, 2, chips, False
    )
    down_late, down_got, up_late, up_got = after((second_sent, values_sent), (down_late, down_got, up_late, up_got))
    feed_total = jnp.stack(
        [
            add_parts(gdown_kept[0], down_late) + down_got.astype(f32),
            add_parts(gup_kept[0], up_late) + up_got.astype(f32),
        ],
        axis=1,
    )
    second_proj = after(feed_total, second_proj)
    normed_one_part = sum(
        contract(part, in_half[:, i * half : (i + 1) * half], 1, 1)
        for i, part in enumerate((first_proj, second_proj, values_proj))
    )
    mixer_shape = first_kept.shape[:2] + (2, *first_kept.shape[4:])

    def mixer_pair(kept, got):
        kept, got = ([value.reshape(mixer_shape) for value in pair] for pair in (kept, got))
        next_part = jnp.stack([add_parts(k[1], g[1]).astype(bf16) for k, g in zip(kept, got)], axis=1)
        rest_part = jnp.stack([add_parts(k[0], g[0]) for k, g in zip(kept, got)], axis=1)
        return next_part, rest_part

    one_got, two_got = after(
        normed_one_part, ((swap_x(first_sent), swap_x(second_sent)), (swap_y(gout_sent), swap_y(values_sent)))
    )
    one_next, one_rest = mixer_pair((first_kept, second_kept), one_got)
    two_next, two_rest = mixer_pair((gout_kept, values_kept), two_got)
    one_got, two_got = swap_y(one_next), swap_x(two_next)

    normed_one_grad = own_tokens(normed_one_part) + swap_core(other_tokens(normed_one_part))
    unit_own = lax.dynamic_slice_in_dim(after((one_next, two_next), unit_one), HALO + core * tok_count, tok_count, 0)
    pre_gain_grad = jnp.sum(normed_one_grad * unit_own, axis=0)
    pre_offset_grad = jnp.sum(normed_one_grad, axis=0)
    tokens_grad = own_tokens(hidden_grad) + norm_backward(
        normed_one_grad, unit_own, lax.dynamic_slice_in_dim(inverse_one, HALO + core * tok_count, tok_count, 0), pre_gain_full
    )

    hidden_got = lax.all_to_all(
        hidden_back.reshape(seq_count, own_pairs * LANES, 2 * units), "seq", split_axis=0, concat_axis=0, tiled=True
    )
    hidden_sum = jnp.sum(after((one_next, two_next), hidden_got).astype(f32), axis=0)
    hidden_sum = hidden_sum.reshape(own_pairs, LANES, 2, units).transpose(0, 2, 1, 3).reshape(tok_count, units)
    (trunk_grad,) = trunk_pull(hidden_sum)
    filter_grad = filter_square[:units, :channels] + filter_square[units:, channels:]
    skip_grad = skip_line[:, :channels] + skip_line[:, channels:]
    own_grad = jnp.concatenate([filter_grad, skip_grad], axis=0)
    own_grad = after((one_next, two_next), own_grad)
    own_grad_got = swap_x(own_grad)

    def whole_columns(value, groups, run):
        got = swap_core(pick(value, 1 - core, 0))
        mine_part = pick(value, core, 0)
        n = mine_part.shape[0]
        grid = both(mine_part, got, core).reshape(2, n, groups, chips, run)
        return grid.transpose(1, 2, 3, 0, 4).reshape(n, -1)


    def lane_rows(vector):
        return vector.reshape(-1, LANES)

    def wide_rows(matrix):
        padded = jnp.pad(matrix, ((0, -matrix.shape[0] % 8), (0, LANES - matrix.shape[1])))
        return padded

    embed_grad, embed_bias_grad, hidden_grad_w, hidden_bias_grad, last_grad, last_bias_grad, frequency_grad = trunk_grad
    unit_lines = jnp.stack([embed_bias_grad, hidden_bias_grad, last_bias_grad, frequency_grad])
    trunk_parts = [wide_rows(part) for part in (embed_grad, hidden_grad_w, last_grad, unit_lines)]
    stream_sums = jnp.concatenate([first_sums, second_sums, values_sums], axis=0)
    stream_rows = [stream_sums[:, at : at + LANES] for at in range(0, half, LANES)]
    flats = [
        jnp.concatenate(
            [lane_rows(v) for v in (post_gain_grad, post_offset_grad, down_bias_grad, output_bias_grad)], axis=0
        ),
        jnp.concatenate([lane_rows(pre_gain_grad), lane_rows(pre_offset_grad), *trunk_parts], axis=0),
        jnp.concatenate([lane_rows(up_bias_grad), *stream_rows], axis=0),
    ]
    n_chip, n_own = flats[0].shape[0], flats[1].shape[0]
    small = jnp.concatenate(flats, axis=0)
    one_got, two_got = after(trunk_grad, (one_got, two_got))
    mixer_total = jnp.concatenate([add_parts(one_rest, one_got), add_parts(two_rest, two_got)], axis=1)
    masks = z_masks(z_count)[::-1]
    mixer_start = mixer_total
    mixer_total = reduce_z_step(mixer_total, masks[0])
    summed = sum_chips(after(mixer_start, small))
    own_grad = own_grad + after(mixer_total, own_grad_got)
    own_grad = pick(own_grad.reshape(-1, 2, channels // 2), x, 1)
    got = swap_core(summed[n_chip:])
    own_sum = (summed[n_chip:] + got)[:n_own]
    half_pair = both(summed[n_chip + n_own :], got[n_own:], core)
    n_line = width // LANES
    lines = jnp.concatenate([summed[:n_chip], own_sum[: 2 * n_line]], axis=0).reshape(6, n_line, LANES)
    trunk_sums, at = [], 2 * n_line
    for part in trunk_parts:
        trunk_sums.append(own_sum[at : at + part.shape[0], :units])
        at += part.shape[0]
    feed_sum = reduce_far(feed_total, masks)
    first_sum, second_sum, out_sum, values_sum = reduce_far(mixer_total, masks[1:])
    down_sum = feed_sum[0]
    up_sum = feed_sum[1].reshape(2, -1, up_half, width).transpose(0, 2, 1, 3).reshape(2, up_half, -1)
    out_sum = out_sum.transpose(1, 0, 2).reshape(out_sum.shape[1], -1)
    in_rows = whole_columns(jnp.concatenate([first_sum, second_sum, values_sum], axis=2), 3, channels)
    up_rows_sum = whole_columns(up_sum, 1, hidden_own)
    block_index = seq_index * 2 + x

    def own_block(value, axis=0):
        size = value.shape[axis] // (2 * seq_count)
        return lax.dynamic_slice_in_dim(value, block_index * size, size, axis)

    run = width // (2 * seq_count)
    per = LANES // run
    line = pick(lines, block_index // per, 1)
    runs = pick(jnp.stack([line[:, i * run : (i + 1) * run] for i in range(per)]), block_index % per, 0)
    n_up = up_bias_grad.size // LANES
    up_bias_sum = half_pair[:, :n_up].reshape(2, chips, hidden_own).transpose(1, 0, 2).reshape(-1)
    streams = half_pair[:, n_up:].reshape(2, half // LANES, 3, 8, LANES // channels, channels)
    streams = streams.transpose(3, 2, 1, 4, 0, 5).reshape(8, 3 * width)
    return (
        result.astype(bf16)[None],
        tokens_grad.astype(bf16)[None],
        runs[4],
        runs[5],
        in_rows,
        own_block(streams[4]),
        own_block(streams[:3], 1),
        own_block(streams[3]),
        own_grad[units],
        trunk_sums[0][:FEATURES],
        trunk_sums[3][0],
        trunk_sums[1],
        trunk_sums[3][1],
        trunk_sums[2],
        trunk_sums[3][2],
        trunk_sums[3][3],
        own_grad[:units],
        out_sum,
        runs[3],
        runs[0],
        runs[1],
        up_rows_sum,
        own_block(up_bias_sum),
        down_sum,
        runs[2],
    )


def per_device(tokens, *others):
    channels = tokens.shape[2] // lax.axis_size("seq")
    tiled = 2 * channels == LANES and tokens.shape[1] % 256 == 0
    return (tiled_device if tiled else plain_device)(tokens, *others)


def solution(mesh):
    placed = (
        P("dp", "seq", None),
        P("dp", "seq", None),
        P("seq"),
        P("seq"),
        P("seq", None),
        P("seq"),
        P(None, "seq"),
        P("seq"),
        P("seq"),
        P(),
        P(),
        P(),
        P(),
        P(),
        P(),
        P(),
        P(None, "seq"),
        P("seq", None),
        P("seq"),
        P("seq"),
        P("seq"),
        P("seq", None),
        P("seq"),
        P("seq", None),
        P("seq"),
    )
    split = P(("seq", "dp"))
    split_rows = P(("seq", "dp"), None)
    split_columns = P(None, ("seq", "dp"))
    return jax.shard_map(
        per_device,
        mesh=mesh,
        in_specs=placed,
        out_specs=(
            P("dp", "seq", None),
            P("dp", "seq", None),
            split,
            split,
            split_rows,
            split,
            split_columns,
            split,
            split,
            P(),
            P(),
            P(),
            P(),
            P(),
            P(),
            P(),
            split_columns,
            split_rows,
            split,
            split,
            split,
            split_rows,
            split,
            split_rows,
            split,
        ),
        check_vma=False,
    )
```

```python
from functools import partial
import math

import jax
import jax.numpy as jnp
import numpy as np
from jax import lax
from jax.experimental import pallas as pl
from jax.experimental.pallas import tpu as pltpu
from jax.sharding import PartitionSpec as P

FEATURES = 33
LANES = 128
f32 = jnp.float32
bf16 = jnp.bfloat16
highest = lax.Precision.HIGHEST


def swap_seq(value, mask):
    count = lax.axis_size("seq")
    return lax.ppermute(value, "seq", [(i, i ^ mask) for i in range(count)])


def swap_core(value):
    return swap_seq(value, 1)


def swap_y(value):
    return swap_seq(value, 2)


def swap_z(value, mask):
    return swap_seq(value, 4 * mask)


def swap_x(value):
    count = lax.axis_size("dp")
    return lax.ppermute(value, "dp", [(i, i ^ 1) for i in range(count)])


def z_masks(count):
    if count == 4:
        return [3, 1]
    masks, step = [], count // 2
    while step:
        masks.append(step)
        step //= 2
    return masks


def z_order(count):
    order = [0]
    for mask in z_masks(count):
        order = order + [entry ^ mask for entry in order]
    return order


def chip_groups():
    count = lax.axis_size("seq")
    return [list(range(core, count, 2)) for core in range(2)]


def chip_exchange(value):
    return lax.all_to_all(
        value, "seq", split_axis=0, concat_axis=0, tiled=True, axis_index_groups=chip_groups()
    )


def pick(value, index, axis):
    return lax.dynamic_index_in_dim(value, index, axis, keepdims=False)


def both(mine, other, second):
    return jnp.where(second == 0, jnp.stack([mine, other]), jnp.stack([other, mine]))


def place():
    seq = lax.axis_index("seq")
    return seq // 4, (seq // 2) % 2, seq % 2, lax.axis_index("dp")


def by_index(have, order, own):
    bit = 1
    value = jnp.stack([have[order.index(entry)] for entry in range(len(order))])
    while bit < len(order):
        grid = value.reshape(-1, 2, bit, *value.shape[1:])
        turned = jnp.stack([grid[:, 1], grid[:, 0]], axis=1)
        value = jnp.where((own & bit) == 0, grid, turned).reshape(value.shape)
        bit *= 2
    return value


def gather_pieces(piece):
    z, y, _, x = place()
    z_count = lax.axis_size("seq") // 4
    have = piece[None]
    for mask in z_masks(z_count):
        have = jnp.concatenate([have, swap_z(have, mask)], axis=0)
    half = piece.shape[0] // 2
    first, second = have[:, :half], have[:, half:]
    first_y, second_x = swap_y(first), swap_x(second)
    first = jnp.stack([first, first_y])
    second = jnp.stack([second, second_x])
    first_x, second_y = swap_x(first), swap_y(second)
    first = jnp.stack([first, first_x], axis=1)
    second = jnp.stack([second, second_y])
    rel = jnp.concatenate([first, second], axis=3)
    order = z_order(z_count)
    rows = []
    for za in range(z_count):
        rel_z = z ^ za
        slot = sum(jnp.where(rel_z == entry, at, 0) for at, entry in enumerate(order))
        slab = pick(rel, slot, 2)
        slab = jnp.where(y == 0, slab, jnp.stack([slab[1], slab[0]]))
        slab = jnp.where(x == 0, slab, jnp.stack([slab[:, 1], slab[:, 0]], axis=1))
        rows.append(slab)
    return jnp.stack(rows)


def reduce_z(parts):
    z = place()[0]
    z_count = parts.shape[0]
    have = jnp.stack([pick(parts, z ^ rel, 0) for rel in z_order(z_count)])
    for mask in reversed(z_masks(z_count)):
        half = have.shape[0] // 2
        got = swap_z(have[half:].astype(bf16), mask)
        have = have[:half] + got.astype(f32)
    return have[0]


def reduce_pair(first, second):
    _, y, _, x = place()
    first_got = swap_x(pick(first, 1 - x, 2))
    second_got = swap_y(pick(second, 1 - y, 1))
    first = pick(first, x, 2).astype(f32) + first_got.astype(f32)
    second = pick(second, y, 1).astype(f32) + second_got.astype(f32)
    first_got = swap_y(pick(first, 1 - y, 1).astype(bf16))
    second_got = swap_x(pick(second, 1 - x, 1).astype(bf16))
    first = pick(first, y, 1) + first_got.astype(f32)
    second = pick(second, x, 1) + second_got.astype(f32)
    return reduce_z(first), reduce_z(second)


def sum_chips(value, gates=None):
    value = value + swap_x(value)
    value = value + swap_y(value)
    if gates is not None:
        value = lax.optimization_barrier((gates, value))[1]
    for mask in z_masks(lax.axis_size("seq") // 4):
        value = value + swap_z(value, mask)
    return value


def gather_small(value):
    seq = lax.axis_index("seq")
    count = lax.axis_size("seq")
    have = value[None]
    for mask in [2, 1] + [4 * m for m in z_masks(count // 4)]:
        have = jnp.concatenate([have, swap_seq(have, mask)], axis=0)
    order = [0]
    for mask in [2, 1] + [4 * m for m in z_masks(count // 4)]:
        order = order + [entry ^ mask for entry in order]
    return by_index(have, order, seq)


def twiddle(k, n):
    angle = -2.0 * math.pi * (k % n) / n
    return math.cos(angle), math.sin(angle)


def c_add(p, q):
    return (p[0] + q[0], q[1] if p[1] is None else (p[1] if q[1] is None else p[1] + q[1]))


def c_sub(p, q):
    if q[1] is None:
        return (p[0] - q[0], p[1])
    return (p[0] - q[0], -q[1] if p[1] is None else p[1] - q[1])


def c_conj(p):
    return (p[0], None if p[1] is None else -p[1])


def c_turn(p, k, n):
    k = k % n
    if k == 0:
        return p
    re, im = p
    if 4 * k == n:
        return (im if im is not None else jnp.zeros_like(re), -re)
    if 2 * k == n:
        return (-re, None if im is None else -im)
    if 4 * k == 3 * n:
        return (-im if im is not None else jnp.zeros_like(re), re)
    c, s = twiddle(k, n)
    if im is None:
        return (re * c, re * s)
    return (re * c - im * s, re * s + im * c)


def real_dft(xs):
    n = len(xs)
    if n == 1:
        return [(xs[0], None)]
    if n == 2:
        if xs[1] is None:
            return [(xs[0], None), (xs[0], None)]
        return [(xs[0] + xs[1], None), (xs[0] - xs[1], None)]
    even, odd = real_dft(xs[0::2]), real_dft(xs[1::2])
    out = [None] * (n // 2 + 1)
    for k in range(n // 4 + 1):
        turned = c_turn(odd[k], k, n)
        out[k] = c_add(even[k], turned)
        if n // 2 - k != k:
            out[n // 2 - k] = c_conj(c_sub(even[k], turned))
    return out


def real_inverse(spec):
    def whole(v):
        n = 2 * (len(v) - 1)
        if n == 2:
            return [v[0][0] + v[1][0], None]
        even, odd = [], []
        for k in range(n // 4 + 1):
            mirror = c_conj(v[n // 2 - k])
            e, o = c_add(v[k], mirror), c_turn(c_sub(v[k], mirror), -k, n)
            if k == 0 or 4 * k == n:
                e, o = (e[0], None), (o[0], None)
            even.append(e)
            odd.append(o)
        even, odd = whole(even), whole(odd)
        return [entry for pair in zip(even, odd) for entry in pair]

    values = whole(spec)
    return values[: len(values) // 2]


def split_terms(value):
    high = value.astype(bf16)
    return high, (value - high.astype(f32)).astype(bf16)


def conv_tables(pairs):
    rows = 4 * pairs
    total = rows * LANES
    slots = np.arange(pairs + 1)
    lanes = np.arange(LANES)
    upper = lanes >= LANES // 2
    angle = -2.0 * np.pi * slots[:, None] / rows * upper[None, :]
    lane_turn = np.stack([np.cos(angle), np.sin(angle)], axis=1).astype(np.float32)
    freq = slots[:, None] + np.where(upper, rows // 2, 0)[None, :]
    angle = -2.0 * np.pi * ((freq[:, None, :] * lanes[None, :, None]) % total) / total
    turn = np.stack([np.cos(angle), np.sin(angle)], axis=1).astype(np.float32)
    angle = 2.0 * np.pi * ((lanes[:, None] * lanes[None, :]) % LANES) / LANES
    c, s = np.cos(angle), np.sin(angle)

    def terms(table):
        table = table.astype(np.float32)
        high = table.astype(bf16)
        low = (table - high.astype(np.float32)).astype(bf16)
        return np.concatenate([high, low], axis=1)

    ahead = terms(np.block([[c, s], [-s, c]]))
    back = terms(np.block([[c, -s], [s, c]]) / total)
    return lane_turn, turn, ahead, back


CHUNK = 16


def put(terms_ref, start, slot, re, im):
    cols = pl.ds(slot * LANES, LANES)
    terms_ref[pl.ds(start, CHUNK), cols] = re
    terms_ref[pl.ds(LANES + start, CHUNK), cols] = im


COLUMNS = 4 * LANES


def table_product(table_ref, terms_ref, out_ref):
    width = terms_ref.shape[1]
    high_table, low_table = table_ref[:, :256], table_ref[:, 256:]
    for at in range(0, width, COLUMNS):
        cols = pl.ds(at, min(COLUMNS, width - at))
        high, low = split_terms(terms_ref[:, cols])
        out_ref[:, cols] = (
            jnp.dot(high_table, low, preferred_element_type=f32)
            + jnp.dot(low_table, high, preferred_element_type=f32)
            + jnp.dot(high_table, high, preferred_element_type=f32)
        )


def lane_sign(shape):
    return jnp.where(lax.broadcasted_iota(jnp.int32, shape, 1) < LANES // 2, 1.0, -1.0).astype(f32)


def transform(x_ref, pairs, lane_ref, turn_ref, ahead_ref, terms_ref, spec_ref):
    sign = lane_sign((CHUNK, LANES))

    def chunk(step, carry):
        start = pl.multiple_of(step * CHUNK, CHUNK)
        xs = [x_ref[j, pl.ds(start, CHUNK), :].astype(f32) for j in range(pairs)]
        spec = real_dft(xs + [None] * pairs)
        for k in range(pairs + 1):
            re, im = spec[k]
            c, s = lane_ref[k, 0:1, :], lane_ref[k, 1:2, :]
            if im is None:
                re, im = re * c, re * s
            else:
                re, im = re * c - im * s, re * s + im * c
            re = pltpu.roll(re, LANES // 2, 1) + sign * re
            im = pltpu.roll(im, LANES // 2, 1) + sign * im
            c, s = turn_ref[k, 0, pl.ds(start, CHUNK), :], turn_ref[k, 1, pl.ds(start, CHUNK), :]
            put(terms_ref, start, k, re * c - im * s, re * s + im * c)
        return carry

    lax.fori_loop(0, LANES // CHUNK, chunk, 0)
    table_product(ahead_ref, terms_ref, spec_ref)


def put_product(terms_ref, pairs, one_ref, other_ref, conjugate):
    def chunk(step, carry):
        start = pl.multiple_of(step * CHUNK, CHUNK)
        for k in range(pairs + 1):
            cols = pl.ds(k * LANES, LANES)
            a, b = one_ref[pl.ds(start, CHUNK), cols], one_ref[pl.ds(LANES + start, CHUNK), cols]
            c, d = other_ref[pl.ds(start, CHUNK), cols], other_ref[pl.ds(LANES + start, CHUNK), cols]
            if conjugate:
                put(terms_ref, start, k, a * c + b * d, b * c - a * d)
            else:
                put(terms_ref, start, k, a * c - b * d, a * d + b * c)
        return carry

    lax.fori_loop(0, LANES // CHUNK, chunk, 0)


def inverse(pairs, lane_ref, turn_ref, back_ref, terms_ref, spec_ref, finish):
    table_product(back_ref, terms_ref, spec_ref)
    sign = lane_sign((CHUNK, LANES))

    def chunk(step, carry):
        start = pl.multiple_of(step * CHUNK, CHUNK)
        spec = []
        for k in range(pairs + 1):
            cols = pl.ds(k * LANES, LANES)
            re, im = spec_ref[pl.ds(start, CHUNK), cols], spec_ref[pl.ds(LANES + start, CHUNK), cols]
            c, s = turn_ref[k, 0, pl.ds(start, CHUNK), :], turn_ref[k, 1, pl.ds(start, CHUNK), :]
            re, im = re * c + im * s, im * c - re * s
            re = pltpu.roll(re, LANES // 2, 1) + sign * re
            im = pltpu.roll(im, LANES // 2, 1) + sign * im
            c, s = lane_ref[k, 0:1, :], lane_ref[k, 1:2, :]
            re, im = re * c + im * s, im * c - re * s
            spec.append((re, None if k in (0, pairs) else im))
        for j, values in enumerate(real_inverse(spec)):
            finish(j, start, values)
        return carry

    lax.fori_loop(0, LANES // CHUNK, chunk, 0)


def window_of(j, start, delta, length):
    lane = lax.broadcasted_iota(jnp.int32, (CHUNK, LANES), 1)
    row = lax.broadcasted_iota(jnp.int32, (CHUNK, LANES), 0)
    position = (2 * j + lane // (LANES // 2)) * LANES + start + row
    return jnp.exp(-(position.astype(f32) / (length - 1)) * delta) + 0.05


def filter_body(pairs, h_ref, w_ref, delta_ref, lane_ref, turn_ref, ahead_ref, spec_ref, low_ref, terms_ref):
    delta = delta_ref[...]
    for j in range(pairs):
        rows = jnp.dot(h_ref[j], w_ref[...], precision=highest, preferred_element_type=f32)
        window = jnp.concatenate(
            [window_of(j, start, delta, 2 * pairs * LANES) for start in range(0, LANES, CHUNK)], axis=0
        )
        low_ref[j] = (rows * window).astype(bf16).astype(f32)
    transform(low_ref, pairs, lane_ref, turn_ref, ahead_ref, terms_ref, spec_ref)


def forward_body(
    pairs, x_ref, kernel_ref, skip_ref, lane_ref, turn_ref, ahead_ref, back_ref, out_ref, spec_ref, terms_ref, work_ref
):
    transform(x_ref, pairs, lane_ref, turn_ref, ahead_ref, terms_ref, spec_ref)
    put_product(terms_ref, pairs, spec_ref, kernel_ref, False)
    skip = skip_ref[...]

    def finish(j, start, values):
        rows = pl.ds(start, CHUNK)
        out_ref[j, rows, :] = (values + x_ref[j, rows, :].astype(f32) * skip).astype(bf16)

    inverse(pairs, lane_ref, turn_ref, back_ref, terms_ref, work_ref, finish)


def backward_body(
    pairs, g_ref, kernel_ref, skip_ref, lane_ref, turn_ref, ahead_ref, back_ref, gx_ref, spec_ref, terms_ref, work_ref
):
    transform(g_ref, pairs, lane_ref, turn_ref, ahead_ref, terms_ref, spec_ref)
    put_product(terms_ref, pairs, spec_ref, kernel_ref, True)
    skip = skip_ref[...]

    chips, rows = gx_ref.shape[:2]
    own = (rows - CHUNK) // LANES

    def finish(j, start, values):
        value = (values + g_ref[j, pl.ds(start, CHUNK), :].astype(f32) * skip).astype(bf16)
        gx_ref[j // own, pl.ds(pl.multiple_of(j % own * LANES + start, CHUNK), CHUNK), :] = value

    inverse(pairs, lane_ref, turn_ref, back_ref, terms_ref, work_ref, finish)
    for chip in range(chips - 1):
        gx_ref[chip, own * LANES :, :] = gx_ref[chip + 1, :CHUNK, :]
    gx_ref[chips - 1, own * LANES :, :] = jnp.zeros((CHUNK, LANES), bf16)


def filter_back_body(
    pairs,
    g_ref,
    g_spec_ref,
    x_ref,
    x_spec_ref,
    h_ref,
    w_ref,
    delta_ref,
    lane_ref,
    turn_ref,
    back_ref,
    gh_ref,
    gw_ref,
    gskip_ref,
    terms_ref,
    work_ref,
    pre_ref,
):
    put_product(terms_ref, pairs, g_spec_ref, x_spec_ref, True)
    delta = delta_ref[...]

    def finish(j, start, values):
        window = window_of(j, start, delta, 2 * pairs * LANES)
        pre_ref[j, pl.ds(start, CHUNK), :] = values.astype(bf16).astype(f32) * window

    inverse(pairs, lane_ref, turn_ref, back_ref, terms_ref, work_ref, finish)
    gw_ref[...] = jnp.zeros_like(gw_ref)
    gskip_ref[...] = jnp.zeros_like(gskip_ref)
    for j in range(pairs):
        pre = pre_ref[j]
        gh = lax.dot_general(
            pre, w_ref[...], (((1,), (1,)), ((), ())), precision=highest, preferred_element_type=f32
        )
        gh_ref[j] = gh.astype(bf16)
        gw_ref[...] += lax.dot_general(
            h_ref[j], pre, (((0,), (0,)), ((), ())), precision=highest, preferred_element_type=f32
        )
        gskip_ref[...] += jnp.sum(g_ref[j].astype(f32) * x_ref[j].astype(f32), axis=0, keepdims=True)


SHARE = 100000
FILLER = 40 * 10**9
VMEM_BYTES = 50 * 1024 * 1024


def whole_call(body, outs, scratch, flops, moved, *operands, share=SHARE):
    return pl.pallas_call(
        body,
        out_shape=outs,
        scratch_shapes=scratch,
        compiler_params=pltpu.CompilerParams(vmem_limit_bytes=VMEM_BYTES),
        cost_estimate=pl.CostEstimate(flops=flops // share, bytes_accessed=moved // share, transcendentals=0),
    )(*operands)


def spec_shape(pairs):
    return (256, (pairs + 1) * LANES)


def conv_filter(hidden, weight, delta, tables):
    pairs = hidden.shape[0]
    lane_turn, turn, ahead, _ = tables
    return whole_call(
        partial(filter_body, pairs),
        jax.ShapeDtypeStruct(spec_shape(pairs), f32),
        [pltpu.VMEM((pairs, LANES, LANES), f32), pltpu.VMEM(spec_shape(pairs), f32)],
        10**9,
        8 * 10**6,
        hidden,
        weight,
        delta,
        lane_turn,
        turn,
        ahead,
    )


def conv_forward(x, kernel_spec, skip, tables):
    pairs = x.shape[0]
    return whole_call(
        partial(forward_body, pairs),
        (jax.ShapeDtypeStruct(x.shape, bf16), jax.ShapeDtypeStruct(spec_shape(pairs), f32)),
        [pltpu.VMEM(spec_shape(pairs), f32), pltpu.VMEM(spec_shape(pairs), f32)],
        2 * 10**9,
        10 * 10**6,
        x,
        kernel_spec,
        skip,
        *tables,
    )


def conv_backward(g, kernel_spec, skip, tables, chips):
    pairs = g.shape[0]
    out_rows = pairs // chips * LANES + CHUNK
    return whole_call(
        partial(backward_body, pairs),
        (jax.ShapeDtypeStruct((chips, out_rows, LANES), bf16), jax.ShapeDtypeStruct(spec_shape(pairs), f32)),
        [pltpu.VMEM(spec_shape(pairs), f32), pltpu.VMEM(spec_shape(pairs), f32)],
        2 * 10**9,
        10 * 10**6,
        g,
        kernel_spec,
        skip,
        *tables,
    )


def filter_backward(g, g_spec, x, x_spec, hidden, weight, delta, tables):
    pairs = x.shape[0]
    lane_turn, turn, _, back = tables
    return whole_call(
        partial(filter_back_body, pairs),
        (
            jax.ShapeDtypeStruct(x.shape, bf16),
            jax.ShapeDtypeStruct((LANES, LANES), f32),
            jax.ShapeDtypeStruct((1, LANES), f32),
        ),
        [
            pltpu.VMEM(spec_shape(pairs), f32),
            pltpu.VMEM(spec_shape(pairs), f32),
            pltpu.VMEM(x.shape, f32),
        ],
        FILLER,
        10 * 10**6,
        g,
        g_spec,
        x,
        x_spec,
        hidden,
        weight,
        delta,
        lane_turn,
        turn,
        back,
        share=1,
    )


def plain_spectrum(x, length):
    pairs, _, lanes = x.shape
    flat = x.astype(f32).reshape(pairs, LANES, 2, lanes // 2).transpose(3, 0, 2, 1)
    tables = spectral_tables(length // 64, LANES)
    return forward_transform(flat.reshape(lanes // 2, length // LANES, LANES), tables)


def plain_inverse(re, im, length):
    tables = spectral_tables(length // 64, LANES)
    back = inverse_transform(re, im, tables, length // LANES)
    channels = back.shape[0]
    back = back.reshape(channels, length // 256, 2, LANES).transpose(1, 3, 2, 0)
    return back.reshape(length // 256, LANES, 2 * channels)


def spectral_tables(rows_total, col_count):
    total_size = rows_total * col_count
    row_index = jnp.arange(rows_total, dtype=jnp.int32)
    col_index = jnp.arange(col_count, dtype=jnp.int32)
    row_angle = (row_index[:, None] * row_index[None, :] % rows_total).astype(f32) * (
        2.0 * math.pi / rows_total
    )
    col_angle = (col_index[:, None] * col_index[None, :] % col_count).astype(f32) * (
        2.0 * math.pi / col_count
    )
    twist_angle = (row_index[:, None] * col_index[None, :]).astype(f32) * (2.0 * math.pi / total_size)
    return (
        jnp.cos(row_angle),
        -jnp.sin(row_angle),
        jnp.cos(twist_angle),
        -jnp.sin(twist_angle),
        jnp.cos(col_angle),
        -jnp.sin(col_angle),
        total_size,
    )


def forward_transform(signal, tables):
    row_cos, row_sin, twist_cos, twist_sin, col_cos, col_sin, _ = tables
    half_rows = signal.shape[1]
    product = partial(jnp.einsum, precision=highest)
    first_re = product("ka,cab->ckb", row_cos[:, :half_rows], signal)
    first_im = product("ka,cab->ckb", row_sin[:, :half_rows], signal)
    turned_re = first_re * twist_cos - first_im * twist_sin
    turned_im = first_re * twist_sin + first_im * twist_cos
    out_re = product("ckb,bm->ckm", turned_re, col_cos) - product("ckb,bm->ckm", turned_im, col_sin)
    out_im = product("ckb,bm->ckm", turned_re, col_sin) + product("ckb,bm->ckm", turned_im, col_cos)
    return (out_re, out_im)


def inverse_transform(spec_re, spec_im, tables, half_rows):
    row_cos, row_sin, twist_cos, twist_sin, col_cos, col_sin, total_size = tables
    product = partial(jnp.einsum, precision=highest)
    back_re = product("ckm,mb->ckb", spec_re, col_cos) + product("ckm,mb->ckb", spec_im, col_sin)
    back_im = product("ckm,mb->ckb", spec_im, col_cos) - product("ckm,mb->ckb", spec_re, col_sin)
    untwist_re = back_re * twist_cos + back_im * twist_sin
    untwist_im = back_im * twist_cos - back_re * twist_sin
    real_part = product("ak,ckb->cab", row_cos[:half_rows], untwist_re) + product(
        "ak,ckb->cab", row_sin[:half_rows], untwist_im
    )
    return real_part / total_size


def plain_window(shape, delta, length):
    pairs, _, lanes = shape
    position = jnp.arange(length, dtype=jnp.int32).reshape(pairs, 2, LANES, 1).astype(f32)
    window = jnp.exp(-(position / (length - 1)) * delta[0, : lanes // 2]) + 0.05
    return window.transpose(0, 2, 1, 3).reshape(shape)


def plain_filter(hidden, weight, delta):
    pairs = hidden.shape[0]
    length = 256 * pairs
    rows = jnp.einsum("jbh,hc->jbc", hidden, weight, precision=highest)
    rows = (rows * plain_window(rows.shape, delta, length)).astype(bf16)
    return plain_spectrum(rows, length)


def plain_forward(x, kernel_spec, skip):
    length = 256 * x.shape[0]
    re, im = plain_spectrum(x, length)
    kre, kim = kernel_spec
    out = plain_inverse(re * kre - im * kim, re * kim + im * kre, length)
    return (out + x.astype(f32) * skip).astype(bf16), (re, im)


def plain_backward(g, x, x_spec, kernel_spec, skip, hidden, weight, delta):
    length = 256 * x.shape[0]
    re, im = plain_spectrum(g, length)
    kre, kim = kernel_spec
    xre, xim = x_spec
    gx = plain_inverse(re * kre + im * kim, im * kre - re * kim, length) + g.astype(f32) * skip
    pre = plain_inverse(re * xre + im * xim, im * xre - re * xim, length).astype(bf16).astype(f32)
    pre = pre * plain_window(pre.shape, delta, length)
    gh = jnp.einsum("jbc,hc->jbh", pre, weight, precision=highest)
    gw = jnp.einsum("jbh,jbc->hc", hidden, pre, precision=highest)
    gskip = jnp.sum(g.astype(f32) * x.astype(f32), axis=(0, 1))[None]
    return gx.astype(bf16), gh.astype(bf16), gw, gskip


def feed_body(nt_ref, ct_ref, up_ref, bias_ref, down_ref, y_ref, gx_ref, gdown_ref, gup_ref, gbias_ref):
    @pl.when(pl.program_id(0) == 0)
    def _():
        y_ref[...] = jnp.zeros_like(y_ref)
        gx_ref[...] = jnp.zeros_like(gx_ref)

    nt, ct, up, down = nt_ref[...], ct_ref[...], up_ref[...], down_ref[...]
    before = jnp.dot(nt, up, preferred_element_type=f32) + bias_ref[...]
    cdf = 0.5 * (1.0 + lax.erf(before * math.sqrt(0.5)))
    active = (before * cdf).astype(bf16)
    slope = cdf + before * (jnp.exp(-0.5 * before * before) * (1.0 / math.sqrt(2.0 * math.pi)))
    g_act = lax.dot_general(ct, down, (((1,), (1,)), ((), ())), preferred_element_type=f32)
    g_before = (g_act * slope).astype(bf16)
    y_ref[...] += jnp.dot(active, down, preferred_element_type=f32)
    gx_ref[...] += lax.dot_general(g_before, up, (((1,), (1,)), ((), ())), preferred_element_type=f32)
    gdown_ref[...] = lax.dot_general(
        active, ct, (((0,), (0,)), ((), ())), preferred_element_type=f32
    ).astype(bf16)
    gup_ref[...] = lax.dot_general(
        nt, g_before, (((0,), (0,)), ((), ())), preferred_element_type=f32
    ).astype(bf16)
    gbias_ref[...] = jnp.sum(g_before.astype(f32), axis=0, keepdims=True)


def feed_forward(nt, ct, up, bias, down):
    rows, width = nt.shape
    hidden = up.shape[1]
    block = min(256, hidden)
    return pl.pallas_call(
        feed_body,
        grid=(hidden // block,),
        in_specs=[
            pl.BlockSpec((rows, width), lambda i: (0, 0)),
            pl.BlockSpec((rows, width), lambda i: (0, 0)),
            pl.BlockSpec((width, block), lambda i: (0, i)),
            pl.BlockSpec((1, block), lambda i: (0, i)),
            pl.BlockSpec((block, width), lambda i: (i, 0)),
        ],
        out_specs=[
            pl.BlockSpec((rows, width), lambda i: (0, 0)),
            pl.BlockSpec((rows, width), lambda i: (0, 0)),
            pl.BlockSpec((block, width), lambda i: (i, 0)),
            pl.BlockSpec((width, block), lambda i: (0, i)),
            pl.BlockSpec((1, block), lambda i: (0, i)),
        ],
        out_shape=[
            jax.ShapeDtypeStruct((rows, width), f32),
            jax.ShapeDtypeStruct((rows, width), f32),
            jax.ShapeDtypeStruct((hidden, width), bf16),
            jax.ShapeDtypeStruct((width, hidden), bf16),
            jax.ShapeDtypeStruct((1, hidden), f32),
        ],
        compiler_params=pltpu.CompilerParams(vmem_limit_bytes=VMEM_BYTES),
        cost_estimate=pl.CostEstimate(
            flops=12 * rows * width * hidden,
            bytes_accessed=8 * width * hidden + 12 * rows * width,
            transcendentals=2 * rows * hidden,
        ),
    )(nt, ct, up, bias, down)


def norm_forward(values, norm_gain, norm_offset):
    center = values - jnp.mean(values, axis=-1, keepdims=True)
    inverse_root = lax.rsqrt(jnp.mean(center * center, axis=-1, keepdims=True) + 1e-05)
    normed = center * inverse_root
    return (normed * norm_gain + norm_offset, normed, inverse_root)


def norm_backward(upstream, normed, inverse_root, norm_gain):
    scaled = upstream * norm_gain
    centered = (
        scaled
        - jnp.mean(scaled, axis=-1, keepdims=True)
        - normed * jnp.mean(scaled * normed, axis=-1, keepdims=True)
    )
    return centered * inverse_root


def contract(left_side, right_side, left_dim, right_dim):
    return lax.dot_general(
        left_side, right_side, (((left_dim,), (right_dim,)), ((), ())), preferred_element_type=f32
    )


def trunk_hidden(trunk, features):
    embed_weight, embed_bias, hidden_weight, hidden_bias, last_weight, last_bias, frequency = trunk
    layer_out = jnp.sin(frequency * (jnp.dot(features, embed_weight, precision=highest) + embed_bias))
    layer_out = jnp.sin(frequency * (jnp.dot(layer_out, hidden_weight, precision=highest) + hidden_bias))
    return jnp.sin(frequency * (jnp.dot(layer_out, last_weight, precision=highest) + last_bias))


def to_owners(value, chips):
    tokens, width = value.shape
    channels = width // chips
    grid = value.reshape(tokens // 256, 2, LANES, chips, channels)
    return grid.transpose(3, 0, 2, 1, 4).reshape(chips, tokens // 256, LANES, 2 * channels)


def from_owners(value):
    chips, pairs, _, lanes = value.shape
    grid = value.reshape(chips, pairs, LANES, 2, lanes // 2)
    return grid.transpose(1, 3, 2, 0, 4).reshape(pairs * 256, chips * (lanes // 2))


def exchange(value):
    return chip_exchange(value)


def flatten(*values):
    return jnp.concatenate([value.reshape(-1) for value in values])


def unflatten(flat, shapes):
    out, at = [], 0
    for shape in shapes:
        size = int(np.prod(shape))
        out.append(flat[at : at + size].reshape(shape))
        at += size
    return out


def to_rows(flat):
    rows = -(-flat.shape[0] // 1024) * 8
    return jnp.pad(flat, (0, rows * LANES - flat.shape[0])).reshape(rows, LANES)


def plain_device(
    tokens,
    cotangent,
    pre_gain,
    pre_offset,
    input_weight,
    input_bias,
    short_weight,
    short_bias,
    skip_weight,
    embed_weight,
    embed_bias,
    hidden_weight,
    hidden_bias,
    last_weight,
    last_bias,
    frequency,
    filter_weight,
    output_weight,
    output_bias,
    post_gain,
    post_offset,
    up_weight,
    up_bias,
    down_weight,
    down_bias,
):
    seq_count = lax.axis_size("seq")
    seq_index = lax.axis_index("seq")
    z, y, core, x = place()
    chips = seq_count // 2
    z_count = seq_count // 4
    chip = seq_index // 2
    tok_count = tokens.shape[1]
    width = tokens.shape[2]
    length = tok_count * seq_count
    channels = width // seq_count
    ff = up_weight.shape[1]
    hidden_own = ff // seq_count
    half = width // 2
    pairs = length // 256

    mine = jnp.stack([tokens[0], cotangent[0]])
    other = swap_core(mine)
    pair = both(mine, other, core)
    tok = pair[:, 0].reshape(2 * tok_count, width)
    cot = pair[:, 1].reshape(2 * tok_count, width)

    def half_columns(value, groups, run):
        rows = value.shape[0]
        grid = value.reshape(rows, groups, chips, 2, run)
        return [grid[:, :, :, side].reshape(rows, groups * chips * run) for side in range(2)]

    def own_rows(value, groups, run):
        sides = half_columns(value, groups, run)
        keep = jnp.where(core == 0, sides[0], sides[1])
        got = swap_core(jnp.where(core == 0, sides[1], sides[0]))
        return jnp.where(core == x, keep, got)

    in_piece = own_rows(input_weight, 3, channels)
    in_half = gather_pieces(in_piece).reshape(width, 3 * half)
    small_shapes = [(width // seq_count,)] * 2 + [(3, channels), (3, 3, channels), (3, channels)]
    small_shapes += [(width // seq_count,)] * 3 + [(hidden_own,), (width // seq_count,)]
    smalls = flatten(
        pre_gain, pre_offset, input_bias, short_weight, short_bias, output_bias, post_gain, post_offset, up_bias, down_bias
    )
    shapes = [v.shape for v in (pre_gain, pre_offset, input_bias, short_weight, short_bias)]
    shapes += [v.shape for v in (output_bias, post_gain, post_offset, up_bias, down_bias)]
    small_rows = to_rows(smalls)
    small_all = gather_small(small_rows.reshape(-1)).astype(f32)
    columns, at = [], 0
    for shape in shapes:
        size = int(np.prod(shape))
        columns.append(small_all[:, at : at + size])
        at += size

    def halved(value, run):
        lead = value.shape[:-1]
        return pick(value.reshape(*lead, -1, 2, run), core, len(lead) + 1).reshape(*lead, -1)

    pre_gain_full, pre_offset_full = columns[0].reshape(-1), columns[1].reshape(-1)
    input_bias_own = halved(columns[2].reshape(3, width), channels).reshape(-1)
    short_full = columns[3].reshape(seq_count, 3, -1).transpose(1, 0, 2).reshape(3, 3, width)
    short_taps = halved(short_full, channels).reshape(3, -1)
    short_bias_own = halved(columns[4].reshape(3, width), channels).reshape(-1)
    output_bias_full = columns[5].reshape(-1)
    post_gain_full, post_offset_full = columns[6].reshape(-1), columns[7].reshape(-1)
    up_bias_own = halved(columns[8].reshape(-1), hidden_own)
    down_bias_full = columns[9].reshape(-1)

    out_rows = output_weight.shape[0] // 2
    up_piece = own_rows(up_weight, 1, hidden_own)
    out_piece = pick(output_weight.reshape(2, out_rows, width), x, 0)
    down_piece = pick(down_weight.reshape(2, hidden_own // 2, width), x, 0)
    up_half = gather_pieces(up_piece).reshape(width, ff // 2)
    n_out, n_down = out_rows // 2, hidden_own // 4
    mixed_piece = jnp.concatenate(
        [out_piece[:n_out], down_piece[:n_down], out_piece[n_out:], down_piece[n_down:]], axis=0
    )
    later = gather_pieces(mixed_piece)
    later = later.reshape(chips, 2, 2, n_out + n_down, width)
    out_half = later[:, :, :, :n_out].reshape(half, width)
    down_half = later[:, :, :, n_out:].reshape(ff // 2, width)

    positions = (seq_index * tok_count + jnp.arange(tok_count, dtype=jnp.int32)).astype(f32)
    relative = positions / (length - 1)
    phases = positions * (2.0 * math.pi / length)
    band_count = (FEATURES - 1) // 2
    band_freq = jnp.linspace(0.0001, band_count - 1, band_count).astype(f32)
    angles = phases[:, None] * band_freq[None, :]
    features = jnp.concatenate([relative[:, None], jnp.cos(angles), -jnp.sin(angles)], axis=1)
    trunk = (embed_weight, embed_bias, hidden_weight, hidden_bias, last_weight, last_bias, frequency)
    hidden_rows, trunk_pull = jax.vjp(partial(trunk_hidden, features=features), trunk)
    units = hidden_rows.shape[1]
    own_pairs = tok_count // 256
    packed = hidden_rows.reshape(own_pairs, 2, LANES, units).transpose(0, 2, 1, 3)
    packed = packed.reshape(own_pairs, LANES, 2 * units)
    filter_hidden = lax.all_gather(packed, "seq", axis=0, tiled=True)
    filter_own = filter_weight.astype(f32)
    zero = jnp.zeros_like(filter_own)
    filter_pair = jnp.concatenate(
        [jnp.concatenate([filter_own, zero], axis=1), jnp.concatenate([zero, filter_own], axis=1)], axis=0
    )
    deltas = jnp.linspace(math.log(0.01) / 1.5, math.log(0.01) / 0.3, width).astype(f32)
    delta_own = jnp.abs(lax.dynamic_slice_in_dim(deltas, seq_index * channels, channels))
    delta_pair = jnp.concatenate([delta_own, delta_own])[None]
    skip_own = skip_weight.astype(f32)
    skip_pair = jnp.concatenate([skip_own, skip_own])[None]
    kernel_spec = plain_filter(filter_hidden, filter_pair, delta_pair)

    rows = 2 * tok_count
    inputs = tok.astype(f32)
    normed_one, unit_one, inverse_one = norm_forward(inputs, pre_gain_full, pre_offset_full)
    normed_low = normed_one.astype(bf16)
    projected_low = (contract(normed_low, in_half, 1, 0) + input_bias_own).astype(bf16)
    shift = [(i, i + 2) for i in range(seq_count - 2)]
    earlier = lax.ppermute(projected_low[rows - 2 :], "seq", shift)
    extended = jnp.concatenate([earlier, projected_low], axis=0).astype(f32)
    convolved = (
        short_taps[0] * extended[:rows]
        + short_taps[1] * extended[1 : rows + 1]
        + short_taps[2] * extended[2:]
        + short_bias_own
    )
    first_part, second_part, values_part = (convolved[:, i * half : (i + 1) * half] for i in range(3))
    gated_low = (values_part * second_part).astype(bf16)
    gated_ch = exchange(to_owners(gated_low, chips)).reshape(pairs, LANES, 2 * channels)
    mixed_ch, gated_spec = plain_forward(gated_ch, kernel_spec, skip_pair)
    chip_shape = (chips, rows // 256, LANES, 2 * channels)
    mixed_tok = from_owners(exchange(mixed_ch.reshape(chip_shape))).astype(f32)
    mix_low = (mixed_tok * first_part).astype(bf16)
    branch_part = contract(mix_low, out_half, 1, 0)
    branch = branch_part + swap_core(branch_part) + output_bias_full
    hidden = inputs + branch

    normed_two, unit_two, inverse_two = norm_forward(hidden, post_gain_full, post_offset_full)
    normed_two_low = normed_two.astype(bf16)
    down_part, back_part, down_grad, up_grad, up_bias_grad = feed_forward(
        normed_two_low, cot, up_half, up_bias_own[None], down_half
    )

    def own_tokens(value):
        return lax.dynamic_slice_in_dim(value, core * tok_count, tok_count, 0)

    def other_tokens(value):
        return lax.dynamic_slice_in_dim(value, (1 - core) * tok_count, tok_count, 0)

    result = own_tokens(hidden) + (
        own_tokens(down_part) + swap_core(other_tokens(down_part)) + down_bias_full
    )
    up_grad = up_grad.reshape(z_count, 2, 2, 2, -1, ff // 2).transpose(0, 1, 3, 2, 4, 5)
    down_sum, up_sum = reduce_pair(down_grad.reshape(z_count, 2, 2, hidden_own // 2, width), up_grad)

    cot_f = cot.astype(f32)
    down_bias_grad = jnp.sum(cot_f, axis=0)
    normed_two_grad = back_part + swap_core(back_part)
    post_gain_grad = jnp.sum(normed_two_grad * unit_two, axis=0)
    post_offset_grad = jnp.sum(normed_two_grad, axis=0)
    hidden_grad = cot_f + norm_backward(normed_two_grad, unit_two, inverse_two, post_gain_full)
    branch_low = hidden_grad.astype(bf16)
    output_bias_grad = jnp.sum(branch_low.astype(f32), axis=0)
    gate_grad = contract(branch_low, out_half, 1, 1)
    mixed_grad_low = (gate_grad * first_part).astype(bf16)
    first_grad = gate_grad * mixed_tok
    mixed_grad_ch = exchange(to_owners(mixed_grad_low, chips)).reshape(pairs, LANES, 2 * channels)
    gated_back, hidden_back, filter_square, skip_line = plain_backward(
        mixed_grad_ch, gated_ch, gated_spec, kernel_spec, skip_pair, filter_hidden, filter_pair, delta_pair
    )
    gated_grad = from_owners(exchange(gated_back.reshape(chip_shape))).astype(f32)
    output_grad = contract(mix_low, branch_low, 0, 0)

    hidden_got = lax.all_to_all(
        hidden_back.reshape(seq_count, own_pairs * LANES, 2 * units), "seq", split_axis=0, concat_axis=0, tiled=True
    )
    hidden_sum = jnp.sum(hidden_got.astype(f32), axis=0)
    hidden_sum = hidden_sum.reshape(own_pairs, LANES, 2, units).transpose(0, 2, 1, 3).reshape(tok_count, units)
    (trunk_grad,) = trunk_pull(hidden_sum)
    filter_grad = filter_square[:units, :channels] + filter_square[units:, channels:]
    skip_grad = skip_line[:, :channels] + skip_line[:, channels:]
    own_grad = jnp.concatenate([filter_grad, skip_grad], axis=0)
    own_grad = own_grad + swap_x(own_grad)
    own_grad = pick(own_grad.reshape(-1, 2, channels // 2), x, 1)

    conv_grad_low = jnp.concatenate(
        [first_grad, gated_grad * values_part, gated_grad * second_part], axis=1
    ).astype(bf16)
    back_shift = [(i + 2, i) for i in range(seq_count - 2)]
    following = lax.ppermute(conv_grad_low[:2], "seq", back_shift)
    conv_grad = conv_grad_low.astype(f32)
    grad_ext = jnp.concatenate([conv_grad_low, following], axis=0).astype(f32)
    projected_grad_low = (
        short_taps[0] * grad_ext[2:] + short_taps[1] * grad_ext[1 : rows + 1] + short_taps[2] * grad_ext[:rows]
    ).astype(bf16)
    short_weight_grad = jnp.stack(
        [jnp.sum(conv_grad * extended[tap : tap + rows], axis=0) for tap in range(3)]
    )
    short_bias_grad = jnp.sum(conv_grad, axis=0)
    input_bias_grad = jnp.sum(projected_grad_low.astype(f32), axis=0)
    input_grad = contract(normed_low, projected_grad_low, 0, 0)
    normed_one_part = contract(projected_grad_low, in_half, 1, 1)
    normed_one_grad = own_tokens(normed_one_part) + swap_core(other_tokens(normed_one_part))
    unit_own = own_tokens(unit_one)
    pre_gain_grad = jnp.sum(normed_one_grad * unit_own, axis=0)
    pre_offset_grad = jnp.sum(normed_one_grad, axis=0)
    tokens_grad = own_tokens(hidden_grad) + norm_backward(
        normed_one_grad, unit_own, own_tokens(inverse_one), pre_gain_full
    )

    in_low = input_grad.astype(bf16).reshape(z_count, 2, 2, 2, -1, 3 * half).transpose(0, 1, 3, 2, 4, 5)
    in_sum = jnp.stack(reduce_pair(in_low[:, :, :, 0], in_low[:, :, :, 1]))
    out_low = output_grad.astype(bf16).reshape(z_count, 2, 2, -1, width)
    split = out_low.shape[3] // 2
    out_sum = jnp.concatenate(reduce_pair(out_low[:, :, :, :split], out_low[:, :, :, split:]), axis=0)

    def whole_columns(value, groups, run):
        got = swap_core(pick(value, 1 - core, 0))
        mine_part = pick(value, core, 0)
        n = mine_part.shape[0]
        grid = both(mine_part, got, core).reshape(2, n, groups, chips, run)
        return grid.transpose(1, 2, 3, 0, 4).reshape(n, -1)

    in_rows = whole_columns(in_sum, 3, channels)
    up_rows_sum = whole_columns(up_sum, 1, hidden_own)

    chip_wide = [post_gain_grad, post_offset_grad, down_bias_grad, output_bias_grad]
    own_wide = [pre_gain_grad, pre_offset_grad, *trunk_grad]
    half_wide = [up_bias_grad.reshape(-1), input_bias_grad, short_weight_grad, short_bias_grad]
    own_flat, half_flat = to_rows(flatten(*own_wide)), to_rows(flatten(*half_wide))
    summed = sum_chips(jnp.concatenate([to_rows(flatten(*chip_wide)), own_flat, half_flat], axis=0))
    n_chip = to_rows(flatten(*chip_wide)).shape[0]
    chip_sum = summed[:n_chip].reshape(-1)
    got = swap_core(summed[n_chip:])
    own_sum = (summed[n_chip:] + got)[: own_flat.shape[0]].reshape(-1)
    half_sums_pair = both(summed[n_chip + own_flat.shape[0] :], got[own_flat.shape[0] :], core).reshape(2, -1)
    chip_sums = unflatten(chip_sum, [v.shape for v in chip_wide])
    own_sums = unflatten(own_sum, [v.shape for v in own_wide])
    half_sums = [
        unflatten(half_sums_pair[side], [v.shape for v in half_wide]) for side in range(2)
    ]

    def joined(index, groups, run):
        pair_of = jnp.stack([half_sums[side][index].reshape(groups, chips, run) for side in range(2)], axis=2)
        return pair_of.reshape(groups, -1)

    block_index = seq_index * 2 + x

    def own_block(value, axis=0):
        size = value.shape[axis] // (2 * seq_count)
        return lax.dynamic_slice_in_dim(value, block_index * size, size, axis)

    up_bias_sum = joined(0, 1, hidden_own).reshape(-1)
    input_bias_sum = joined(1, 3, channels).reshape(-1)
    short_weight_sum = joined(2, 9, channels).reshape(3, -1)
    short_bias_sum = joined(3, 3, channels).reshape(-1)
    return (
        result.astype(bf16)[None],
        tokens_grad.astype(bf16)[None],
        own_block(own_sums[0]),
        own_block(own_sums[1]),
        in_rows,
        own_block(input_bias_sum),
        own_block(short_weight_sum, 1),
        own_block(short_bias_sum),
        own_grad[units],
        *own_sums[2:],
        own_grad[:units],
        out_sum,
        own_block(chip_sums[3]),
        own_block(chip_sums[0]),
        own_block(chip_sums[1]),
        up_rows_sum,
        own_block(up_bias_sum),
        down_sum,
        own_block(chip_sums[2]),
    )


def after(earlier, value):
    return lax.optimization_barrier((earlier, value))[1]


def gather_z(piece, gates=None):
    have = piece[None]
    masks = z_masks(lax.axis_size("seq") // 4)
    for step, mask in enumerate(masks):
        if gates is not None and step == len(masks) - 1:
            have = after(gates, have)
        have = jnp.concatenate([have, swap_z(have, mask)], axis=0)
    return have


def gather_near(have):
    half = have.shape[1] // 2
    first, second = have[:, :half], have[:, half:]
    return jnp.stack([first, swap_y(first)]), jnp.stack([second, swap_x(second)])


def gather_far(near):
    first, second = near
    return first, swap_x(first), second, swap_y(second)


def reduce_pass(kept, got, second):
    sent = (kept[1].astype(f32) + got[1].astype(f32)).astype(bf16)
    return sent, kept[0].astype(f32) + got[0].astype(f32), second(sent)


def reduce_z_step(total, mask):
    half = total.shape[0] // 2
    return total[:half] + swap_z(total[half:].astype(bf16), mask).astype(f32)


def reduce_far(total, masks):
    for mask in masks:
        total = reduce_z_step(total, mask)
    return total[0]


def place_pieces(out_ref, pieces, scalars, chips, span):
    first, first_far, second, second_far = pieces
    x = scalars[0]
    half = span // 2
    z_count = chips // 2
    for slot in range(z_count):
        for yr in range(2):
            base = scalars[2 + yr * z_count + slot] * (2 * span)
            source = second_far if yr else second
            for xr in range(2):
                at = pl.multiple_of(base + (x if xr == 0 else 1 - x) * span, span)
                out_ref[pl.ds(at, half), :] = (first_far if xr else first)[yr, slot]
                out_ref[pl.ds(pl.multiple_of(at + half, half), half), :] = source[xr, slot]


def route_rows(grad_ref, kept_ref, sent_ref, scalars, chips, inner, by_x):
    x = scalars[0]
    z_count = chips // 2
    rows = grad_ref.shape[0] // (2 * chips * inner)
    tiles, _, columns = kept_ref.shape[3:]
    for slot in range(z_count):
        for yr in range(2):
            base = scalars[2 + yr * z_count + slot] * (2 * inner * rows)
            for xr in range(2):
                is_sent, lead = (xr, yr) if by_x else (yr, xr)
                for part in range(inner):
                    at = pl.multiple_of(base + part * 2 * rows + (x if xr == 0 else 1 - x) * rows, rows)
                    for tile in range(tiles):
                        value = grad_ref[pl.ds(at, rows), tile * columns : (tile + 1) * columns].astype(bf16)
                        if not is_sent:
                            kept_ref[lead, slot, part, tile] = value
                        elif isinstance(sent_ref, tuple):
                            sent_ref[lead][slot, part, tile] = value
                        else:
                            sent_ref[lead, slot, part, tile] = value


HALO = 16


def short_conv(rows, taps, bias):
    two, one = pltpu.roll(rows, 2, 0), pltpu.roll(rows, 1, 0)
    return (taps[0:1] * two + taps[1:2] * one + taps[2:3] * rows + bias)[HALO:]


def chip_rows(convolved):
    return convolved[: convolved.shape[0] - HALO]


def pack_pairs(out_ref, index, pair, even, odd):
    half = LANES // 2
    lower = lax.broadcasted_iota(jnp.int32, even.shape, 1) < half
    out_ref[index, pair] = jnp.where(lower, even, pltpu.roll(odd, half, 1)).astype(bf16)
    out_ref[index + 1, pair] = jnp.where(lower, pltpu.roll(even, half, 1), odd).astype(bf16)


def pack_rows(out_ref, index, value):
    for pair in range(value.shape[0] // 256):
        rows = value[256 * pair : 256 * (pair + 1)]
        pack_pairs(out_ref, index, pair, rows[:LANES], rows[LANES:])


def unpack_pair(one, two):
    half = LANES // 2
    one, two = one.astype(f32), two.astype(f32)
    lower = lax.broadcasted_iota(jnp.int32, one.shape, 1) < half
    return jnp.where(lower, one, pltpu.roll(two, half, 1)), jnp.where(lower, pltpu.roll(one, half, 1), two)


def unpack_rows(in_ref, index):
    out = []
    for pair in range(in_ref.shape[1]):
        out.extend(unpack_pair(in_ref[index, pair], in_ref[index + 1, pair]))
    return jnp.concatenate(out, axis=0)


def project_body(scalars, normed_ref, bias_ref, a_ref, ax_ref, b_ref, by_ref, out_ref, weight_ref):
    chips = 2 * a_ref.shape[1]
    place_pieces(weight_ref, (a_ref, ax_ref, b_ref, by_ref), scalars, chips, 2 * a_ref.shape[2])
    value = jnp.dot(normed_ref[...], weight_ref[...], preferred_element_type=f32) + bias_ref[...]
    row = lax.broadcasted_iota(jnp.int32, value.shape, 0)
    value = jnp.where(jnp.logical_and(row < HALO, scalars[1] == 0), 0.0, value)
    out_ref[...] = value.astype(bf16)


def grid_call(body, scalars, grid, ins, outs, scratch, flops, moved, transcendentals=0):
    return pl.pallas_call(
        body,
        grid_spec=pltpu.PrefetchScalarGridSpec(
            num_scalar_prefetch=1,
            grid=(grid,),
            in_specs=[pl.BlockSpec(block, index) for _, block, index in ins],
            out_specs=[pl.BlockSpec(block, index) for _, _, block, index in outs],
            scratch_shapes=scratch,
        ),
        out_shape=[jax.ShapeDtypeStruct(shape, dtype) for shape, dtype, _, _ in outs],
        compiler_params=pltpu.CompilerParams(vmem_limit_bytes=VMEM_BYTES),
        cost_estimate=pl.CostEstimate(flops=flops // SHARE, bytes_accessed=moved // SHARE, transcendentals=0),
    )(scalars, *[value for value, _, _ in ins])


def fixed(value):
    return (value, value.shape, lambda i, s, n=value.ndim: (0,) * n)


def fixed_out(shape, dtype):
    return (shape, dtype, shape, lambda i, s, n=len(shape): (0,) * n)


def project(scalars, normed, bias, pieces):
    rows, width = normed.shape
    columns = bias.shape[1]
    block = columns // 3
    lead = pieces[0].shape[:3]
    piece_specs = [(p, (*lead, block), lambda i, s: (0, 0, 0, i)) for p in pieces]
    return grid_call(
        project_body,
        scalars,
        3,
        [fixed(normed), (bias, (1, block), lambda i, s: (0, i)), *piece_specs],
        [
            ((rows, columns), bf16, (rows, block), lambda i, s: (0, i)),
            ((width, columns), bf16, (width, block), lambda i, s: (0, i)),
        ],
        [],
        2 * rows * width * columns,
        4 * width * columns + 2 * rows * (width + columns),
    )


def gate_body(scalars, second_ref, values_ref, t2_ref, t3_ref, b2_ref, b3_ref, out_ref):
    second = short_conv(second_ref[...].astype(f32), t2_ref[...], b2_ref[...])
    values = short_conv(values_ref[...].astype(f32), t3_ref[...], b3_ref[...])
    pack_rows(out_ref, 0, chip_rows(values * second))


def stream_tiles(projected, taps, bias, stream, tiles):
    rows = projected.shape[0]
    index = lambda i, s, at=stream * tiles: (0, at + i)
    return (
        (projected, (rows, LANES), index),
        (taps, (3, LANES), index),
        (bias, (1, LANES), index),
    )


def gate(scalars, projected, taps, bias, chips):
    rows, columns = projected.shape
    tiles = columns // 3 // LANES
    p2, t2, b2 = stream_tiles(projected, taps, bias, 1, tiles)
    p3, t3, b3 = stream_tiles(projected, taps, bias, 2, tiles)
    pairs = (rows - 2 * HALO) // 256
    (out,) = grid_call(
        gate_body,
        scalars,
        tiles,
        [p2, p3, t2, t3, b2, b3],
        [((chips, pairs, LANES, LANES), bf16, (2, pairs, LANES, LANES), lambda i, s: (i, 0, 0, 0))],
        [],
        20 * rows * columns,
        3 * rows * columns,
    )
    return out


def branch_body(
    scalars, mixed_ref, first_ref, taps_ref, bias_ref, a_ref, ax_ref, b_ref, by_ref, mixed_out, mix_out, weight_ref, out_ref, low_ref
):
    chips = 2 * a_ref.shape[1]
    place_pieces(weight_ref, (a_ref, ax_ref, b_ref, by_ref), scalars, chips, 2 * a_ref.shape[2])
    for tile in range(chips // 2):
        cols = slice(tile * LANES, (tile + 1) * LANES)
        mixed = unpack_rows(mixed_ref, 2 * tile)
        first = chip_rows(short_conv(first_ref[:, cols].astype(f32), taps_ref[:, cols], bias_ref[:, cols]))
        mixed_out[:, cols] = mixed.astype(bf16)
        mix_out[:, cols] = (mixed * first).astype(bf16)
    value = jnp.dot(mix_out[...], weight_ref[...], preferred_element_type=f32)
    out_ref[...] = value
    low_ref[...] = value.astype(bf16)


def first_stream(projected, taps, bias):
    rows, columns = projected.shape
    block = columns // 3
    return [
        (projected, (rows, block), lambda i, s: (0, 0)),
        (taps, (3, block), lambda i, s: (0, 0)),
        (bias, (1, block), lambda i, s: (0, 0)),
    ]


def branch_out(scalars, mixed, projected, taps, bias, pieces, piece_rows):
    rows = projected.shape[0] - 2 * HALO
    half = projected.shape[1] // 3
    width = pieces[0].shape[3]
    return grid_call(
        branch_body,
        scalars,
        1,
        [
            fixed(mixed),
            *first_stream(projected, taps, bias),
            *[
                (p, (*p.shape[:2], piece_rows, width), lambda i, s, at=p.shape[2] // piece_rows - 1: (0, 0, at, 0))
                for p in pieces
            ],
        ],
        [
            fixed_out((rows, half), bf16),
            fixed_out((rows, half), bf16),
            fixed_out((half, width), bf16),
            fixed_out((rows, width), f32),
            fixed_out((rows, width), bf16),
        ],
        [],
        2 * rows * half * width,
        4 * rows * width + 6 * half * width,
    )


def tiled_feed_body(
    scalars,
    nt_ref,
    ct_ref,
    bias_ref,
    ua_ref,
    uax_ref,
    ub_ref,
    uby_ref,
    da_ref,
    dax_ref,
    db_ref,
    dby_ref,
    y_ref,
    gx_ref,
    gdown_kept,
    gdown_late,
    gdown_first,
    gup_kept,
    gup_late,
    gup_first,
    gbias_ref,
    gx_low_ref,
    up_ref,
    down_ref,
    grad_ref,
):
    step = pl.program_id(0)
    z_count = ua_ref.shape[1]
    x = scalars[0]

    @pl.when(step == 0)
    def _():
        y_ref[...] = jnp.zeros_like(y_ref)
        gx_ref[...] = jnp.zeros_like(gx_ref)

    place_pieces(up_ref, (ua_ref, uax_ref, ub_ref, uby_ref), scalars, 2 * z_count, 2 * ua_ref.shape[2])
    span = down_ref.shape[0] // 2
    half = span // 2
    own, other = pl.multiple_of(x * span, span), pl.multiple_of((1 - x) * span, span)
    down_ref[pl.ds(own, half), :] = da_ref[0, 0]
    down_ref[pl.ds(other, half), :] = dax_ref[0, 0]

    def put_second(source):
        down_ref[pl.ds(pl.multiple_of(own + half, half), half), :] = source[0, 0]
        down_ref[pl.ds(pl.multiple_of(other + half, half), half), :] = source[1, 0]

    @pl.when(step < z_count)
    def _():
        put_second(db_ref)

    @pl.when(step >= z_count)
    def _():
        put_second(dby_ref)

    nt, ct, up, down = nt_ref[...], ct_ref[...], up_ref[...], down_ref[...]
    before = jnp.dot(nt, up, preferred_element_type=f32) + bias_ref[...]
    cdf = 0.5 * (1.0 + lax.erf(before * math.sqrt(0.5)))
    active = (before * cdf).astype(bf16)
    slope = cdf + before * (jnp.exp(-0.5 * before * before) * (1.0 / math.sqrt(2.0 * math.pi)))
    g_act = lax.dot_general(ct, down, (((1,), (1,)), ((), ())), preferred_element_type=f32)
    g_before = (g_act * slope).astype(bf16)
    y_ref[...] += jnp.dot(active, down, preferred_element_type=f32)
    gx_ref[...] += lax.dot_general(g_before, up, (((1,), (1,)), ((), ())), preferred_element_type=f32)
    gdown = lax.dot_general(active, ct, (((0,), (0,)), ((), ())), preferred_element_type=f32)
    one, two = gdown[:span], gdown[span:]
    gdown_kept[0, 0] = jnp.where(x == 0, one, two).astype(bf16)
    sent = jnp.where(x == 0, two, one).astype(bf16)

    @pl.when(step < z_count)
    def _():
        gdown_late[0] = sent

    @pl.when(step >= z_count)
    def _():
        gdown_first[0] = sent

    grad_ref[...] = lax.dot_general(nt, g_before, (((0,), (0,)), ((), ())), preferred_element_type=f32)
    route_rows(grad_ref, gup_kept, (gup_late, gup_first), scalars, 2 * z_count, 2, False)
    gbias_ref[...] = jnp.sum(g_before.astype(f32), axis=0, keepdims=True)

    @pl.when(step == 2 * z_count - 1)
    def _():
        gx_low_ref[...] = gx_ref[...].astype(bf16)


def tiled_feed(scalars, nt, ct, bias, pieces, down_pieces, up_rows, down_rows):
    rows, width = nt.shape
    hidden = bias.shape[1]
    z_count = pieces[0].shape[1]
    chips = 2 * z_count
    block = hidden // chips
    per = width // block
    tiles = hidden // width
    column = lambda i, s: (0, s[2 + i])
    up_specs = [(p, (2, z_count, up_rows, block), lambda i, s: (0, 0, s[2 + i] // per, s[2 + i] % per)) for p in pieces]
    near = lambda i, s: (i // z_count, i % z_count, 0, 0)
    far = lambda i, s: (0, i % z_count, 0, 0)
    down_specs = [(p, (1, 1, down_rows, width), near) for p in down_pieces[:2]]
    down_specs += [(p, (2, 1, down_rows, width), far) for p in down_pieces[2:]]
    down_shape, down_block = (z_count, 2 * down_rows, width), (1, 2 * down_rows, width)
    up_shape = (z_count, 2, tiles, up_rows, width)
    up_block = (z_count, 2, 1, up_rows, block)
    up_index = lambda i, s: (0, 0, s[2 + i] // per, 0, s[2 + i] % per)
    return grid_call(
        tiled_feed_body,
        scalars,
        chips,
        [fixed(nt), fixed(ct), (bias, (1, block), column), *up_specs, *down_specs],
        [
            fixed_out((rows, width), f32),
            fixed_out((rows, width), f32),
            ((2, *down_shape), bf16, (1, *down_block), lambda i, s: (i // z_count, i % z_count, 0, 0)),
            (down_shape, bf16, down_block, lambda i, s: (jnp.minimum(i, z_count - 1), 0, 0)),
            (down_shape, bf16, down_block, lambda i, s: (jnp.maximum(i - z_count, 0), 0, 0)),
            ((2, *up_shape), bf16, (2, *up_block), lambda i, s: (0, *up_index(i, s))),
            (up_shape, bf16, up_block, up_index),
            (up_shape, bf16, up_block, up_index),
            ((1, hidden), f32, (1, block), column),
            fixed_out((rows, width), bf16),
        ],
        [pltpu.VMEM((width, block), bf16), pltpu.VMEM((block, width), bf16), pltpu.VMEM((width, block), f32)],
        12 * rows * width * hidden,
        8 * width * hidden + 12 * rows * width,
        2 * rows * hidden,
    )


def unbranch_body(
    scalars,
    g_ref,
    mix_ref,
    mixed_ref,
    first_ref,
    taps_ref,
    bias_ref,
    weight_ref,
    gmixed_ref,
    gfirst_ref,
    kept_ref,
    sent_ref,
    grad_ref,
):
    chips = gmixed_ref.shape[0]
    g = g_ref[...]
    gate_grad = lax.dot_general(g, weight_ref[...], (((1,), (1,)), ((), ())), preferred_element_type=f32)
    for tile in range(chips // 2):
        cols = slice(tile * LANES, (tile + 1) * LANES)
        first = chip_rows(short_conv(first_ref[:, cols].astype(f32), taps_ref[:, cols], bias_ref[:, cols]))
        gfirst_ref[:, cols] = (gate_grad[:, cols] * mixed_ref[:, cols].astype(f32)).astype(bf16)
        pack_rows(gmixed_ref, 2 * tile, gate_grad[:, cols] * first)
    grad_ref[...] = lax.dot_general(mix_ref[...], g, (((0,), (0,)), ((), ())), preferred_element_type=f32)
    route_rows(grad_ref, kept_ref, sent_ref, scalars, chips, 1, False)


def unbranch(scalars, g, mix, mixed, projected, taps, bias, weight, chips):
    rows, width = g.shape
    half = weight.shape[0]
    grad_shape = (2, chips // 2, 1, width // half, half // (2 * chips), half)
    return grid_call(
        unbranch_body,
        scalars,
        1,
        [fixed(g), fixed(mix), fixed(mixed), *first_stream(projected, taps, bias), fixed(weight)],
        [
            fixed_out((chips, rows // 256, LANES, LANES), bf16),
            fixed_out((rows, half), bf16),
            fixed_out(grad_shape, bf16),
            fixed_out(grad_shape, bf16),
        ],
        [pltpu.VMEM((half, width), f32)],
        4 * rows * half * width,
        4 * rows * width + 6 * half * width,
    )


def ungate_body(scalars, gated_ref, second_ref, values_ref, t2_ref, t3_ref, b2_ref, b3_ref, gsecond_ref, gvalues_ref):
    pairs = (gated_ref.shape[1] - HALO) // LANES
    blocks = [gated_ref.at[:, pl.ds(pair * LANES, LANES), :] for pair in range(pairs)]
    grad = jnp.concatenate([part for block in blocks for part in unpack_pair(block[0], block[1])], axis=0)
    ahead, _ = unpack_pair(gated_ref[0, pairs * LANES :], gated_ref[1, pairs * LANES :])
    grad = jnp.concatenate([grad, ahead], axis=0)
    second = short_conv(second_ref[...].astype(f32), t2_ref[...], b2_ref[...])
    values = short_conv(values_ref[...].astype(f32), t3_ref[...], b3_ref[...])
    gsecond_ref[...] = (grad * values).astype(bf16)
    gvalues_ref[...] = (grad * second).astype(bf16)


def ungate(scalars, gated, projected, taps, bias):
    rows, columns = projected.shape
    half = columns // 3
    tiles = half // LANES
    p2, t2, b2 = stream_tiles(projected, taps, bias, 1, tiles)
    p3, t3, b3 = stream_tiles(projected, taps, bias, 2, tiles)
    out = ((rows - HALO, half), bf16, (rows - HALO, LANES), lambda i, s: (0, i))
    return grid_call(
        ungate_body,
        scalars,
        tiles,
        [(gated, (2, *gated.shape[1:]), lambda i, s: (i, 0, 0)), p2, p3, t2, t3, b2, b3],
        [out, out],
        [],
        20 * rows * columns,
        3 * rows * columns,
    )


def stream_body(
    by_x, scalars, grad_ref, rows_ref, taps_ref, normed_ref, gproj_ref, kept_ref, sent_ref, sums_ref, work_ref
):
    count, columns = gproj_ref.shape
    chips = 2 * kept_ref.shape[1]
    for at in range(0, columns, LANES):
        cols = slice(at, at + LANES)
        taps = taps_ref[:, cols]
        ext = grad_ref[:, cols].astype(f32)
        grad = ext[:count]
        total = count + HALO
        one, two = pltpu.roll(ext, total - 1, 0)[:count], pltpu.roll(ext, total - 2, 0)[:count]
        low = (taps[0:1] * two + taps[1:2] * one + taps[2:3] * grad).astype(bf16)
        gproj_ref[:, cols] = low
        rows = rows_ref[:, cols].astype(f32)
        sums = [
            jnp.sum(grad * pltpu.roll(rows, 2, 0)[HALO:total], axis=0, keepdims=True),
            jnp.sum(grad * pltpu.roll(rows, 1, 0)[HALO:total], axis=0, keepdims=True),
            jnp.sum(grad * rows[HALO:total], axis=0, keepdims=True),
            jnp.sum(grad, axis=0, keepdims=True),
            jnp.sum(low.astype(f32), axis=0, keepdims=True),
            jnp.zeros((3, LANES), f32),
        ]
        sums_ref[:, cols] = jnp.concatenate(sums, axis=0)
    work_ref[...] = lax.dot_general(
        normed_ref[HALO:total, :], gproj_ref[...], (((0,), (0,)), ((), ())), preferred_element_type=f32
    )
    route_rows(work_ref, kept_ref, sent_ref, scalars, chips, 2, by_x)


def stream_back(scalars, grad, projected, taps, normed, stream, chips, by_x):
    count, columns = grad.shape[0] - HALO, grad.shape[1]
    width = normed.shape[1]
    rows = projected.shape[0]
    index = lambda i, s: (0, stream)
    shape = (2, chips // 2, 2, 1, width // (4 * chips), columns)
    return grid_call(
        partial(stream_body, by_x),
        scalars,
        1,
        [
            fixed(grad),
            (projected, (rows, columns), index),
            (taps, (3, columns), index),
            fixed(normed),
        ],
        [
            fixed_out((count, columns), bf16),
            fixed_out(shape, bf16),
            fixed_out(shape, bf16),
            fixed_out((8, columns), f32),
        ],
        [pltpu.VMEM((width, columns), f32)],
        2 * count * columns * width,
        4 * count * columns + 2 * count * width + 2 * width * columns,
    )


def split_body(run, scalars, in_ref, kept_ref, sent_ref):
    core = scalars[0]
    if run == LANES // 2:
        one, two = in_ref[:, :LANES].astype(f32), in_ref[:, LANES:].astype(f32)
        lower = lax.broadcasted_iota(jnp.int32, one.shape, 1) < run
        sides = (
            jnp.where(lower, one, pltpu.roll(two, run, 1)).astype(bf16),
            jnp.where(lower, pltpu.roll(one, run, 1), two).astype(bf16),
        )
        kept_ref[...] = jnp.where(core == 0, sides[0], sides[1])
        sent_ref[...] = jnp.where(core == 0, sides[1], sides[0])
    else:
        kept_ref[...] = jnp.where(core == 0, in_ref[:, :run], in_ref[:, run:])
        sent_ref[...] = jnp.where(core == 0, in_ref[:, run:], in_ref[:, :run])


def split_columns(core, value, run, tile=None):
    rows, columns = value.shape
    block = max(run, LANES)
    if tile is None:
        out = ((rows, columns // 2), bf16, (rows, block), lambda i, s: (0, i))
    else:
        per = tile // block
        out = ((columns // 2 // tile, rows, tile), bf16, (None, rows, block), lambda i, s: (i // per, 0, i % per))
    return grid_call(
        partial(split_body, run),
        core.reshape(1),
        columns // (2 * block),
        [(value, (rows, 2 * block), lambda i, s: (0, i))],
        [out, out],
        [],
        rows * columns,
        4 * rows * columns,
    )


def filter_features(seq_index, tok_count, length):
    positions = (seq_index * tok_count + jnp.arange(tok_count, dtype=jnp.int32)).astype(f32)
    relative = positions / (length - 1)
    phases = positions * (2.0 * math.pi / length)
    band_count = (FEATURES - 1) // 2
    band_freq = jnp.linspace(0.0001, band_count - 1, band_count).astype(f32)
    angles = phases[:, None] * band_freq[None, :]
    return jnp.concatenate([relative[:, None], jnp.cos(angles), -jnp.sin(angles)], axis=1)


def tiled_device(
    tokens,
    cotangent,
    pre_gain,
    pre_offset,
    input_weight,
    input_bias,
    short_weight,
    short_bias,
    skip_weight,
    embed_weight,
    embed_bias,
    hidden_weight,
    hidden_bias,
    last_weight,
    last_bias,
    frequency,
    filter_weight,
    output_weight,
    output_bias,
    post_gain,
    post_offset,
    up_weight,
    up_bias,
    down_weight,
    down_bias,
):
    seq_count = lax.axis_size("seq")
    seq_index = lax.axis_index("seq")
    z, y, core, x = place()
    chips = seq_count // 2
    z_count = seq_count // 4
    tok_count, width = tokens.shape[1:]
    length = tok_count * seq_count
    channels = width // seq_count
    ff = up_weight.shape[1]
    hidden_own = ff // seq_count
    half = width // 2
    pairs = length // 256
    rows = 2 * tok_count
    chip_at = [(z ^ rel) * 2 + (y ^ yr) for yr in range(2) for rel in z_order(z_count)]
    scalars = jnp.stack([x, seq_index // 2, *chip_at]).astype(jnp.int32)

    def own_rows(value, run, tile=None):
        keep, sent = split_columns(core, value, run, tile)
        return jnp.where(core == x, keep, swap_core(sent))

    in_piece = own_rows(input_weight, channels)
    mine = jnp.stack([after(in_piece, tokens)[0], cotangent[0]])
    pair = both(mine, swap_core(mine), core)
    tok = pair[:, 0].reshape(rows, width)
    cot = pair[:, 1].reshape(rows, width)
    onward = [(i, i + 2) for i in range(seq_count - 2)]
    backward = [(i + 2, i) for i in range(seq_count - 2)]
    earlier = lax.ppermute(tok[rows - HALO :], "seq", onward)
    later = lax.ppermute(tok[:HALO], "seq", backward)
    tok_ext = jnp.concatenate([earlier, tok, later], axis=0)
    vectors = [
        pre_gain,
        pre_offset,
        input_bias,
        short_weight,
        short_bias,
        output_bias,
        post_gain,
        post_offset,
        up_bias,
        down_bias,
    ]
    small_blocks = []
    for vector in vectors:
        flat = vector.reshape(-1)
        small_blocks.append(jnp.pad(flat, (0, -flat.shape[0] % LANES)).reshape(-1, LANES))
    small_count = sum(block.shape[0] for block in small_blocks)
    small_blocks.append(jnp.zeros((-small_count % 8, LANES), bf16))
    small = jnp.concatenate(small_blocks, axis=0).astype(f32)

    in_have = gather_z(in_piece, (earlier, later))

    trunk = (embed_weight, embed_bias, hidden_weight, hidden_bias, last_weight, last_bias, frequency)
    features = filter_features(after(tok, seq_index), tok_count, length)
    hidden_rows, trunk_pull = jax.vjp(partial(trunk_hidden, features=features), trunk)
    units = hidden_rows.shape[1]
    own_pairs = tok_count // 256
    packed = hidden_rows.reshape(own_pairs, 2, LANES, units).transpose(0, 2, 1, 3)
    packed = packed.reshape(own_pairs * LANES, 2 * units)
    gathered = gather_small(after((earlier, later), jnp.concatenate([packed, small], axis=0)))
    filter_hidden = gathered[:, : own_pairs * LANES].reshape(pairs, LANES, 2 * units)
    small_all = gathered[:, own_pairs * LANES :].reshape(seq_count, -1)

    in_near = gather_near(in_have)
    in_pieces = gather_far(in_near)

    up_piece = own_rows(after(in_piece, up_weight), hidden_own, width)
    out_piece = pick(after(in_piece, output_weight).reshape(2, -1, width), x, 0)
    down_piece = pick(after(in_piece, down_weight).reshape(2, -1, width), x, 0)
    up_half, out_half_rows, down_half_rows = up_piece.shape[1] // 2, out_piece.shape[0] // 2, down_piece.shape[0] // 2
    parts = []
    for side in range(2):
        parts.append(up_piece[:, side * up_half : (side + 1) * up_half].reshape(-1, width))
        parts.append(out_piece[side * out_half_rows : (side + 1) * out_half_rows])
    rest_have = gather_z(after(in_have, jnp.concatenate(parts, axis=0)))
    rest_near = gather_near(after(in_pieces, rest_have))
    down_have = gather_z(after(rest_have, down_piece))

    columns, at = [], 0
    for vector in vectors:
        columns.append(small_all[:, at : at + vector.size])
        at += vector.size + -vector.size % LANES

    def halved(value, run):
        lead = value.shape[:-1]
        return pick(value.reshape(*lead, -1, 2, run), core, len(lead) + 1).reshape(*lead, -1)

    pre_gain_full, pre_offset_full = columns[0].reshape(-1), columns[1].reshape(-1)
    input_bias_own = halved(columns[2].reshape(3, width), channels).reshape(1, -1)
    short_full = columns[3].reshape(seq_count, 3, -1).transpose(1, 0, 2).reshape(3, 3, width)
    taps = halved(short_full, channels).reshape(3, -1)
    short_bias_own = halved(columns[4].reshape(3, width), channels).reshape(1, -1)
    output_bias_full = columns[5].reshape(-1)
    post_gain_full, post_offset_full = columns[6].reshape(-1), columns[7].reshape(-1)
    up_bias_own = halved(columns[8].reshape(-1), hidden_own)[None]
    down_bias_full = columns[9].reshape(-1)

    filter_own = filter_weight.astype(f32)
    zero = jnp.zeros_like(filter_own)
    filter_pair = jnp.concatenate(
        [jnp.concatenate([filter_own, zero], axis=1), jnp.concatenate([zero, filter_own], axis=1)], axis=0
    )
    deltas = jnp.linspace(math.log(0.01) / 1.5, math.log(0.01) / 0.3, width).astype(f32)
    delta_own = jnp.abs(lax.dynamic_slice_in_dim(deltas, seq_index * channels, channels))
    delta_pair = jnp.concatenate([delta_own, delta_own])[None]
    skip_own = skip_weight.astype(f32)
    skip_pair = jnp.concatenate([skip_own, skip_own])[None]
    tables = tuple(jnp.asarray(t) for t in conv_tables(pairs))

    normed_one, unit_one, inverse_one = norm_forward(tok_ext.astype(f32), pre_gain_full, pre_offset_full)
    normed_ext = normed_one.astype(bf16)
    in_pieces = after((normed_ext, input_bias_own, taps, short_bias_own), in_pieces)
    projected, in_half = project(scalars, normed_ext, input_bias_own, in_pieces)
    gated = gate(scalars, after(rest_near, projected), taps, short_bias_own, chips)
    rest_pieces = gather_far(after(gated, rest_near))
    filter_hidden = after(gated, filter_hidden)
    kernel_spec = conv_filter(filter_hidden, filter_pair, delta_pair, tables)
    gated_ch = chip_exchange(gated).reshape(pairs, LANES, LANES)
    down_near = gather_near(after((rest_pieces, gated_ch, kernel_spec), down_have))
    gated_ch = after(rest_pieces, gated_ch)
    mixed_ch, gated_spec = conv_forward(gated_ch, kernel_spec, skip_pair, tables)
    chip_shape = (chips, rows // 256, LANES, LANES)
    mixed_back = chip_exchange(mixed_ch.reshape(chip_shape))
    down_pieces = gather_far(after(mixed_ch, down_near))
    mixed_tok, mix_low, out_half, branch_part, branch_send = branch_out(
        scalars, after(down_pieces, mixed_back), projected, taps, short_bias_own, rest_pieces, out_half_rows
    )
    hidden = tok.astype(f32) + (branch_part + swap_core(branch_send).astype(f32) + output_bias_full)

    normed_two, unit_two, inverse_two = norm_forward(hidden, post_gain_full, post_offset_full)
    (
        down_part,
        back_part,
        gdown_kept,
        gdown_late,
        gdown_first,
        gup_kept,
        gup_late,
        gup_first,
        up_bias_grad,
        back_send,
    ) = tiled_feed(scalars, normed_two.astype(bf16), cot, up_bias_own, rest_pieces, down_pieces, up_half, down_half_rows)
    up_flat = gdown_kept.shape
    gup_kept, gup_late, gup_first = (
        value.reshape(*shape) for value, shape in ((gup_kept, up_flat), (gup_late, up_flat[1:]), (gup_first, up_flat[1:]))
    )

    def own_tokens(value):
        return lax.dynamic_slice_in_dim(value, core * tok_count, tok_count, 0)

    def other_tokens(value):
        return lax.dynamic_slice_in_dim(value, (1 - core) * tok_count, tok_count, 0)

    normed_two_grad = back_part + swap_core(back_send).astype(f32)
    cot_f = cot.astype(f32)
    hidden_grad = cot_f + norm_backward(normed_two_grad, unit_two, inverse_two, post_gain_full)
    branch_low = hidden_grad.astype(bf16)
    gmixed, gfirst, gout_kept, gout_sent = unbranch(
        scalars, branch_low, mix_low, mixed_tok, projected, taps, short_bias_own, out_half, chips
    )
    mixed_grad_ch = chip_exchange(gmixed).reshape(pairs, LANES, LANES)

    def add_parts(kept, got):
        return kept.astype(f32) + got.astype(f32)

    down_got, up_got = after(gmixed, (swap_x(gdown_first), swap_y(gup_first)))
    down_next, up_next = add_parts(gdown_kept[1], down_got).astype(bf16), add_parts(gup_kept[1], up_got).astype(bf16)
    down_got, up_got = swap_y(down_next), swap_x(up_next)
    down_late, up_late = after((down_next, up_next), (gdown_late, gup_late))
    down_late, up_late = swap_x(down_late), swap_y(up_late)
    mixed_grad_ch = after((down_next, up_next), mixed_grad_ch)

    gated_back, grad_spec = conv_backward(mixed_grad_ch, kernel_spec, skip_pair, tables, chips)
    hidden_back, filter_square, skip_line = filter_backward(
        mixed_grad_ch, after(gated_back, grad_spec), gated_ch, gated_spec, filter_hidden, filter_pair, delta_pair, tables
    )
    gated_grad = chip_exchange(gated_back)

    down_part = after(gmixed, down_part)
    result = own_tokens(hidden) + (
        own_tokens(down_part) + swap_core(other_tokens(down_part)) + down_bias_full
    )
    down_bias_grad = jnp.sum(after(gmixed, cot).astype(f32), axis=0)
    post_gain_grad = jnp.sum(normed_two_grad * unit_two, axis=0)
    post_offset_grad = jnp.sum(normed_two_grad, axis=0)
    output_bias_grad = jnp.sum(branch_low.astype(f32), axis=0)

    gfirst_next = lax.ppermute(gfirst[:HALO], "seq", backward)
    gated_grad = after(hidden_back, gated_grad)
    gsecond, gvalues = ungate(scalars, gated_grad, projected, taps, short_bias_own)
    gfirst = jnp.concatenate([gfirst, after(gsecond, gfirst_next)], axis=0)
    first_proj, first_kept, first_sent, first_sums = stream_back(
        scalars, gfirst, projected, taps, normed_ext, 0, chips, True
    )
    second_proj, second_kept, second_sent, second_sums = stream_back(
        scalars, gsecond, projected, taps, normed_ext, 1, chips, True
    )
    values_proj, values_kept, values_sent, values_sums = stream_back(
        scalars, gvalues, projected, taps, normed_ext, 2, chips, False
    )
    down_late, down_got, up_late, up_got = after((second_sent, values_sent), (down_late, down_got, up_late, up_got))
    feed_total = jnp.stack(
        [
            add_parts(gdown_kept[0], down_late) + down_got.astype(f32),
            add_parts(gup_kept[0], up_late) + up_got.astype(f32),
        ],
        axis=1,
    )
    second_proj = after(feed_total, second_proj)
    normed_one_part = sum(
        contract(part, in_half[:, i * half : (i + 1) * half], 1, 1)
        for i, part in enumerate((first_proj, second_proj, values_proj))
    )
    mixer_shape = first_kept.shape[:2] + (2, *first_kept.shape[4:])

    def mixer_pair(kept, got):
        kept, got = ([value.reshape(mixer_shape) for value in pair] for pair in (kept, got))
        next_part = jnp.stack([add_parts(k[1], g[1]).astype(bf16) for k, g in zip(kept, got)], axis=1)
        rest_part = jnp.stack([add_parts(k[0], g[0]) for k, g in zip(kept, got)], axis=1)
        return next_part, rest_part

    one_got, two_got = after(
        normed_one_part, ((swap_x(first_sent), swap_x(second_sent)), (swap_y(gout_sent), swap_y(values_sent)))
    )
    one_next, one_rest = mixer_pair((first_kept, second_kept), one_got)
    two_next, two_rest = mixer_pair((gout_kept, values_kept), two_got)
    one_got, two_got = swap_y(one_next), swap_x(two_next)

    normed_one_grad = own_tokens(normed_one_part) + swap_core(other_tokens(normed_one_part))
    unit_own = lax.dynamic_slice_in_dim(after((one_next, two_next), unit_one), HALO + core * tok_count, tok_count, 0)
    pre_gain_grad = jnp.sum(normed_one_grad * unit_own, axis=0)
    pre_offset_grad = jnp.sum(normed_one_grad, axis=0)
    tokens_grad = own_tokens(hidden_grad) + norm_backward(
        normed_one_grad, unit_own, lax.dynamic_slice_in_dim(inverse_one, HALO + core * tok_count, tok_count, 0), pre_gain_full
    )

    hidden_got = lax.all_to_all(
        hidden_back.reshape(seq_count, own_pairs * LANES, 2 * units), "seq", split_axis=0, concat_axis=0, tiled=True
    )
    hidden_sum = jnp.sum(after((one_next, two_next), hidden_got).astype(f32), axis=0)
    hidden_sum = hidden_sum.reshape(own_pairs, LANES, 2, units).transpose(0, 2, 1, 3).reshape(tok_count, units)
    (trunk_grad,) = trunk_pull(hidden_sum)
    filter_grad = filter_square[:units, :channels] + filter_square[units:, channels:]
    skip_grad = skip_line[:, :channels] + skip_line[:, channels:]
    own_grad = jnp.concatenate([filter_grad, skip_grad], axis=0)
    own_grad = after((one_next, two_next), own_grad)
    own_grad_got = swap_x(own_grad)

    def whole_columns(value, groups, run):
        got = swap_core(pick(value, 1 - core, 0))
        mine_part = pick(value, core, 0)
        n = mine_part.shape[0]
        grid = both(mine_part, got, core).reshape(2, n, groups, chips, run)
        return grid.transpose(1, 2, 3, 0, 4).reshape(n, -1)


    def lane_rows(vector):
        return vector.reshape(-1, LANES)

    def wide_rows(matrix):
        padded = jnp.pad(matrix, ((0, -matrix.shape[0] % 8), (0, LANES - matrix.shape[1])))
        return padded

    embed_grad, embed_bias_grad, hidden_grad_w, hidden_bias_grad, last_grad, last_bias_grad, frequency_grad = trunk_grad
    unit_lines = jnp.stack([embed_bias_grad, hidden_bias_grad, last_bias_grad, frequency_grad])
    trunk_parts = [wide_rows(part) for part in (embed_grad, hidden_grad_w, last_grad, unit_lines)]
    stream_sums = jnp.concatenate([first_sums, second_sums, values_sums], axis=0)
    stream_rows = [stream_sums[:, at : at + LANES] for at in range(0, half, LANES)]
    flats = [
        jnp.concatenate(
            [lane_rows(v) for v in (post_gain_grad, post_offset_grad, down_bias_grad, output_bias_grad)], axis=0
        ),
        jnp.concatenate([lane_rows(pre_gain_grad), lane_rows(pre_offset_grad), *trunk_parts], axis=0),
        jnp.concatenate([lane_rows(up_bias_grad), *stream_rows], axis=0),
    ]
    n_chip, n_own = flats[0].shape[0], flats[1].shape[0]
    small = jnp.concatenate(flats, axis=0)
    one_got, two_got = after(trunk_grad, (one_got, two_got))
    mixer_total = jnp.concatenate([add_parts(one_rest, one_got), add_parts(two_rest, two_got)], axis=1)
    masks = z_masks(z_count)[::-1]
    mixer_start = mixer_total
    mixer_total = reduce_z_step(mixer_total, masks[0])
    summed = sum_chips(after(mixer_start, small))
    own_grad = own_grad + after(mixer_total, own_grad_got)
    own_grad = pick(own_grad.reshape(-1, 2, channels // 2), x, 1)
    got = swap_core(summed[n_chip:])
    own_sum = (summed[n_chip:] + got)[:n_own]
    half_pair = both(summed[n_chip + n_own :], got[n_own:], core)
    n_line = width // LANES
    lines = jnp.concatenate([summed[:n_chip], own_sum[: 2 * n_line]], axis=0).reshape(6, n_line, LANES)
    trunk_sums, at = [], 2 * n_line
    for part in trunk_parts:
        trunk_sums.append(own_sum[at : at + part.shape[0], :units])
        at += part.shape[0]
    feed_sum = reduce_far(feed_total, masks)
    first_sum, second_sum, out_sum, values_sum = reduce_far(mixer_total, masks[1:])
    down_sum = feed_sum[0]
    up_sum = feed_sum[1].reshape(2, -1, up_half, width).transpose(0, 2, 1, 3).reshape(2, up_half, -1)
    out_sum = out_sum.transpose(1, 0, 2).reshape(out_sum.shape[1], -1)
    in_rows = whole_columns(jnp.concatenate([first_sum, second_sum, values_sum], axis=2), 3, channels)
    up_rows_sum = whole_columns(up_sum, 1, hidden_own)
    block_index = seq_index * 2 + x

    def own_block(value, axis=0):
        size = value.shape[axis] // (2 * seq_count)
        return lax.dynamic_slice_in_dim(value, block_index * size, size, axis)

    run = width // (2 * seq_count)
    per = LANES // run
    line = pick(lines, block_index // per, 1)
    runs = pick(jnp.stack([line[:, i * run : (i + 1) * run] for i in range(per)]), block_index % per, 0)
    n_up = up_bias_grad.size // LANES
    up_bias_sum = half_pair[:, :n_up].reshape(2, chips, hidden_own).transpose(1, 0, 2).reshape(-1)
    streams = half_pair[:, n_up:].reshape(2, half // LANES, 3, 8, LANES // channels, channels)
    streams = streams.transpose(3, 2, 1, 4, 0, 5).reshape(8, 3 * width)
    return (
        result.astype(bf16)[None],
        tokens_grad.astype(bf16)[None],
        runs[4],
        runs[5],
        in_rows,
        own_block(streams[4]),
        own_block(streams[:3], 1),
        own_block(streams[3]),
        own_grad[units],
        trunk_sums[0][:FEATURES],
        trunk_sums[3][0],
        trunk_sums[1],
        trunk_sums[3][1],
        trunk_sums[2],
        trunk_sums[3][2],
        trunk_sums[3][3],
        own_grad[:units],
        out_sum,
        runs[3],
        runs[0],
        runs[1],
        up_rows_sum,
        own_block(up_bias_sum),
        down_sum,
        runs[2],
    )


def per_device(tokens, *others):
    channels = tokens.shape[2] // lax.axis_size("seq")
    tiled = 2 * channels == LANES and tokens.shape[1] % 256 == 0
    return (tiled_device if tiled else plain_device)(tokens, *others)


def solution(mesh):
    placed = (
        P("dp", "seq", None),
        P("dp", "seq", None),
        P("seq"),
        P("seq"),
        P("seq", None),
        P("seq"),
        P(None, "seq"),
        P("seq"),
        P("seq"),
        P(),
        P(),
        P(),
        P(),
        P(),
        P(),
        P(),
        P(None, "seq"),
        P("seq", None),
        P("seq"),
        P("seq"),
        P("seq"),
        P("seq", None),
        P("seq"),
        P("seq", None),
        P("seq"),
    )
    split = P(("seq", "dp"))
    split_rows = P(("seq", "dp"), None)
    split_columns = P(None, ("seq", "dp"))
    return jax.shard_map(
        per_device,
        mesh=mesh,
        in_specs=placed,
        out_specs=(
            P("dp", "seq", None),
            P("dp", "seq", None),
            split,
            split,
            split_rows,
            split,
            split_columns,
            split,
            split,
            P(),
            P(),
            P(),
            P(),
            P(),
            P(),
            P(),
            split_columns,
            split_rows,
            split,
            split,
            split,
            split_rows,
            split,
            split_rows,
            split,
        ),
        check_vma=False,
    )
```
